32 devices in a mesh: wide: 8 (over z, x), narrow: 4 (over y, core).
Axes of the slice: x: 2, y: 2, z: 4, core: 2. Of those that a mesh axis runs over, the one named last changes fastest.
Arguments:
- tokens: bfloat16 [8, 2048, 1024], P('narrow', 'wide'), may hold values from -6 to 6
- lengths: int32 [8], P('narrow'), may hold values from 128 to 2048, as said below
- value_ids: int32 [8, 2048, 4, 2], P('narrow', 'wide'), may hold values from 0 to 4, all different within a row
- out_ids: int32 [8, 2048, 4, 2], P('narrow', 'wide'), may hold values from 0 to 4, all different within a row
- mlp_ids: int32 [8, 2048, 16], P('narrow'), may hold values from 0 to 63, all different within a row
- w_query: bfloat16 [1024, 512], replicated, may hold values from -0.1875 to 0.1875
- w_key: bfloat16 [1024, 512], replicated, may hold values from -0.1875 to 0.1875
- w_value: bfloat16 [1024, 2560], replicated, may hold values from -0.1875 to 0.1875
- w_out: bfloat16 [4, 128, 5120], replicated, may hold values from -6 to 6
- sel_value: bfloat16 [1024, 20], replicated, may hold values from -0.125 to 0.125
- sel_out: bfloat16 [1024, 20], replicated, may hold values from -0.125 to 0.125
- gain_one: float32 [1024], replicated, may hold values from 0.5 to 1.5
- bias_one: float32 [1024], replicated, may hold values from -1.2 to 1.2
- gain_two: float32 [1024], replicated, may hold values from 0.5 to 1.5
- bias_two: float32 [1024], replicated, may hold values from -1.2 to 1.2
- w_select: bfloat16 [1024, 64], P(None, 'wide'), may hold values from -0.09375 to 0.09375
- w_up: bfloat16 [1024, 8192], P(None, 'wide'), may hold values from -0.1875 to 0.1875
- w_down: bfloat16 [8192, 1024], P('wide'), may hold values from -0.25 to 0.25
- cotangent: bfloat16 [8, 2048, 1024], P('narrow', 'wide'), may hold values from -6 to 6
Outputs:
- output: bfloat16 [8, 2048, 1024], P('narrow', 'wide')
- grad_tokens: bfloat16 [8, 2048, 1024], P('narrow', 'wide')
- grad_query: float32 [1024, 512], replicated
- grad_key: float32 [1024, 512], replicated
- grad_value: float32 [1024, 2560], replicated
- grad_out: float32 [4, 128, 5120], replicated
- grad_sel_value: float32 [1024, 20], replicated
- grad_sel_out: float32 [1024, 20], replicated
- grad_gain_one: float32 [1024], replicated
- grad_bias_one: float32 [1024], replicated
- grad_gain_two: float32 [1024], replicated
- grad_bias_two: float32 [1024], replicated
- grad_select: float32 [1024, 64], P(None, 'wide')
- grad_up: float32 [1024, 8192], P(None, 'wide')
- grad_down: float32 [8192, 1024], P('wide')
The draws below stay inside these ranges and needn't reach their ends.
Inputs may be any that keep to these rules, and one draw needn't show every extreme that they name: `lengths`: in each group of 2 consecutive sequences one has length 2048. `value_ids`: the 2 experts of a token and head are distinct. `out_ids`: the 2 experts of a token and head are distinct. `mlp_ids`: the 16 experts of a token are distinct.
All inputs are finite; a program needn't handle non-finite values.
Results may differ from the reference program's by a relative error of at most 0.017.
Values may be sent and summed in bfloat16 or wider, within the bound.
No kernel may reach another device: no remote copies, remote signals or barrier semaphores. Data moves between devices by JAX's collectives and lax.ppermute only.
A program may use at most 384 MiB of HBM per device.

```python
import jax
import jax.numpy as jnp
from jax import lax

D = 1024
HEADS = 4
HD = 128
VEXP = 5
VTOP = 2
HE = 128
TOP = 16
SEQ_LEN = 2048
SEQ_GRP = 2
EXPERTS = 64
SEQS = 8


def draw_lengths(key, part):
    key = jax.random.fold_in(key, 11)
    key_lengths, key_longest = jax.random.split(key)
    drawn = jax.random.randint(key_lengths, (SEQS,), SEQ_LEN // 16, SEQ_LEN + 1)
    longest = jax.random.randint(key_longest, (SEQS // SEQ_GRP,), 0, SEQ_GRP)
    indices = jnp.arange(SEQS)
    is_longest = indices % SEQ_GRP == longest[indices // SEQ_GRP]
    return jnp.where(is_longest, SEQ_LEN, drawn).astype(jnp.int32)


def steps_of(rng, dims, pieces, low, largest):
    level, own = 1.0, jax.random.fold_in(rng, 6)
    for dim, blocks in pieces:
        heights = jnp.exp(jax.random.uniform(jax.random.fold_in(own, dim), (blocks,), jnp.float32, low / len(pieces), largest / len(pieces)))
        level = level * jnp.repeat(heights, dims[dim] // blocks).reshape([-1 if axis == dim else 1 for axis in range(len(dims))])
    return level


def distinct(stream_key, rows, count, top, lift):
    order = jax.random.permutation(jax.random.fold_in(stream_key, 1), count)
    pull = order
    for power in range(3):
        pull = pull * pull // count
    pull = pull * lift // count
    tickets = jax.random.randint(jax.random.fold_in(stream_key, 2), (rows, count), 0, 4096) + pull
    sure = jax.random.permutation(jax.random.fold_in(stream_key, 3), rows)[jnp.arange(count) % rows]
    tickets = jnp.where(jnp.arange(rows)[:, None] == sure[None, :], 1 << 14, tickets)
    score = tickets * count + jnp.arange(count)
    return lax.top_k(score.astype(jnp.int32), top)[1].astype(jnp.int32)


def scatter_about(rng, dims, spread, bound, cuts=(), kind=jnp.bfloat16):
    values = spread * jax.random.normal(rng, dims, jnp.float32)
    if cuts:
        values = values * steps_of(rng, dims, cuts, -0.22, 0.18)
    return jnp.clip(values, -bound, bound).astype(kind)


def setup_inputs(seed: int = 0) -> dict:
    arg_keys = jax.random.split(jax.random.key(seed), 20)
    tokens = scatter_about(arg_keys[0], (SEQS, SEQ_LEN, D), 1.0, 6.0, ((0, 4), (1, 8)))
    lengths = draw_lengths(jax.random.fold_in(arg_keys[19], 71), 0)
    value_ids = distinct(arg_keys[2], SEQS * SEQ_LEN * HEADS, VEXP, VTOP, 0).reshape((SEQS, SEQ_LEN, HEADS, VTOP))
    out_ids = distinct(arg_keys[3], SEQS * SEQ_LEN * HEADS, VEXP, VTOP, 0).reshape((SEQS, SEQ_LEN, HEADS, VTOP))
    mlp_ids = distinct(arg_keys[4], SEQS * SEQ_LEN, EXPERTS, TOP, 2048).reshape((SEQS, SEQ_LEN, TOP))
    w_query = scatter_about(arg_keys[5], (D, HEADS * HD), D ** -0.5, 0.1875)
    w_key = scatter_about(arg_keys[6], (D, HEADS * HD), D ** -0.5, 0.1875)
    w_value = scatter_about(arg_keys[7], (D, HEADS * VEXP * HD), D ** -0.5, 0.1875)
    w_out = scatter_about(arg_keys[8], (HEADS, HD, VEXP * D), 1 ** -0.5, 6.0)
    sel_value = scatter_about(arg_keys[9], (D, HEADS * VEXP), (2 * D) ** -0.5, 0.125)
    sel_out = scatter_about(arg_keys[10], (D, HEADS * VEXP), (2 * D) ** -0.5, 0.125)
    gain_one = jnp.clip(1.0 + 0.1 * jax.random.normal(arg_keys[11], (D,), jnp.float32), 0.5, 1.5)
    bias_one = scatter_about(arg_keys[12], (D,), 0.2, 1.2, (), jnp.float32)
    gain_two = jnp.clip(1.0 + 0.1 * jax.random.normal(arg_keys[13], (D,), jnp.float32), 0.5, 1.5)
    bias_two = scatter_about(arg_keys[14], (D,), 0.2, 1.2, (), jnp.float32)
    w_select = scatter_about(arg_keys[15], (D, EXPERTS), (4 * D) ** -0.5, 0.09375, ((1, 8),))
    w_up = scatter_about(arg_keys[16], (D, EXPERTS * HE), D ** -0.5, 0.1875, ((1, 8),))
    w_down = scatter_about(arg_keys[17], (EXPERTS * HE, D), (TOP * HE // 4) ** -0.5, 0.25, ((0, 8),))
    cotangent = scatter_about(arg_keys[18], (SEQS, SEQ_LEN, D), 1.0, 6.0, ((0, 4), (1, 8)))
    return {"tokens": tokens, "lengths": lengths, "value_ids": value_ids, "out_ids": out_ids, "mlp_ids": mlp_ids, "w_query": w_query, "w_key": w_key, "w_value": w_value, "w_out": w_out, "sel_value": sel_value, "sel_out": sel_out, "gain_one": gain_one, "bias_one": bias_one, "gain_two": gain_two, "bias_two": bias_two, "w_select": w_select, "w_up": w_up, "w_down": w_down, "cotangent": cotangent}


EPSILON = 1e-05
PRECISE = lax.Precision.HIGHEST

@jax.custom_vjp
def low(v):
    return lax.optimization_barrier(v.astype(jnp.bfloat16)).astype(jnp.float32)

@jax.custom_vjp
def low_back(v):
    return v

def low_keep(v):
    return (low(v), None)

def low_pass(kept, grad):
    return (grad,)

def back_keep(v):
    return (v, None)

def back_low(kept, grad):
    return (low(grad),)
low.defvjp(low_keep, low_pass)
low_back.defvjp(back_keep, back_low)

def layer_norm(values_in, gain, bias):
    row_mean = lax.optimization_barrier(jnp.mean(values_in, axis=-1, keepdims=True))
    centred = values_in - row_mean
    variance = lax.optimization_barrier(jnp.mean(centred * centred, axis=-1, keepdims=True))
    return centred * lax.rsqrt(variance + EPSILON) * gain + bias

def rotate(values_in, positions):
    half_dim = values_in.shape[-1] // 2
    frequency = 10000.0 ** (-(jnp.arange(half_dim).astype(jnp.float32) * 2.0 / values_in.shape[-1]))
    angles = positions.astype(jnp.float32)[:, None] * frequency[None, :]
    cosine = jnp.cos(angles)[:, None, :]
    sine_part = jnp.sin(angles)[:, None, :]
    front_half = values_in[..., :half_dim]
    back_half = values_in[..., half_dim:]
    return jnp.concatenate([front_half * cosine - back_half * sine_part, front_half * sine_part + back_half * cosine], axis=-1)

def one_hot_sum(ids, count):
    return lax.optimization_barrier(jnp.sum((ids[..., None] == jnp.arange(count, dtype=jnp.int32)).astype(jnp.float32), axis=-2))

def project(left_op, right_op):
    return jnp.einsum('bsd,dk->bsk', left_op, right_op, precision=PRECISE)

def forward(params, tokens, lengths, value_ids, out_ids, mlp_ids):
    w_query, w_key, w_value, w_out, sel_value, sel_out, gain_one, bias_one, gain_two, bias_two, w_select, w_up, w_down = params
    seq_count, seq_length, model_width = tokens.shape
    head_count = w_out.shape[0]
    head_dim = w_out.shape[1]
    value_experts = sel_value.shape[1] // head_count
    expert_count = w_select.shape[1]
    hidden = w_up.shape[1] // expert_count
    positions = jnp.arange(seq_length, dtype=jnp.int32)
    normed = low(layer_norm(tokens, gain_one, bias_one))
    query_pre = low_back(project(normed, w_query)).reshape(seq_count, seq_length, head_count, head_dim)
    key_pre = low_back(project(normed, w_key)).reshape(seq_count, seq_length, head_count, head_dim)
    queries = low(rotate(query_pre, positions))
    keys = low(rotate(key_pre, positions))
    value_logit = low_back(project(normed, sel_value)).reshape(seq_count, seq_length, head_count, value_experts)
    value_gate = jax.nn.sigmoid(value_logit) * one_hot_sum(value_ids, value_experts)
    projected = low_back(project(tokens, w_value)).reshape(seq_count, seq_length, head_count, value_experts, head_dim)
    values = low(lax.optimization_barrier(jnp.sum(value_gate[..., None] * projected, axis=3)))
    scores = low_back(jnp.einsum('bphc,bshc->bhps', queries, keys, precision=PRECISE) * head_dim ** (-0.5))
    key_pos = positions
    allowed = (key_pos[None, :] <= positions[:, None])[None, None, :, :] & (key_pos[None, :] < lengths[:, None])[:, None, None, :]
    masked = jnp.where(allowed, scores, -1e+30)
    row_max = lax.optimization_barrier(jnp.max(masked, axis=-1, keepdims=True))
    exponent = jnp.exp(masked - row_max)
    attn_probs = low(exponent / lax.optimization_barrier(jnp.sum(exponent, axis=-1, keepdims=True)))
    attended = low_back(jnp.einsum('bhps,bshc->bphc', attn_probs, values, precision=PRECISE))
    live_rows = (positions[None, :] < lengths[:, None]).astype(jnp.float32)[:, :, None, None]
    mixed_out = low(attended * live_rows)
    out_logit = low_back(project(normed, sel_out)).reshape(seq_count, seq_length, head_count, value_experts)
    out_gate = jax.nn.sigmoid(out_logit) * one_hot_sum(out_ids, value_experts)
    expert_out = low_back(jnp.einsum('bphc,hcf->bphf', mixed_out, w_out, precision=PRECISE)).reshape(seq_count, seq_length, head_count, value_experts, model_width)
    after_attn = tokens + lax.optimization_barrier(jnp.sum(out_gate[..., None] * expert_out, axis=(2, 3)))
    rows_low = low(after_attn)
    normed_two = low(layer_norm(after_attn, gain_two, bias_two))
    select_logit = low_back(project(normed_two, w_select))
    mlp_gate = jax.nn.sigmoid(select_logit) * one_hot_sum(mlp_ids, expert_count)
    pre_act = low_back(project(rows_low, w_up))
    activated = jax.nn.gelu(pre_act).reshape(seq_count, seq_length, expert_count, hidden) * mlp_gate[..., None]
    inner_low = low(activated.reshape(seq_count, seq_length, expert_count * hidden))
    return after_attn + project(inner_low, w_down)

def reference(tokens, lengths, value_ids, out_ids, mlp_ids, w_query, w_key, w_value, w_out, sel_value, sel_out, gain_one, bias_one, gain_two, bias_two, w_select, w_up, w_down, cotangent):
    params = tuple((weight.astype(jnp.float32) for weight in (w_query, w_key, w_value, w_out, sel_value, sel_out, gain_one, bias_one, gain_two, bias_two, w_select, w_up, w_down)))
    group_count = SEQS // SEQ_GRP

    def regroup(array):
        return array.reshape((group_count, SEQ_GRP) + array.shape[1:])
    blocks = (regroup(tokens.astype(jnp.float32)), regroup(lengths), regroup(value_ids), regroup(out_ids), regroup(mlp_ids), regroup(cotangent.astype(jnp.float32)))

    def group_step(totals, block):
        block_tokens, block_lengths, block_value, block_out, block_mlp, block_cot = block

        def apply_layer(weights, inputs):
            return forward(weights, inputs, block_lengths, block_value, block_out, block_mlp)
        result, pull_back = jax.vjp(apply_layer, params, block_tokens)
        grad_params, grad_inputs = pull_back(block_cot)
        totals = tuple((running + fresh for running, fresh in zip(totals, grad_params)))
        return (totals, (result.astype(jnp.bfloat16), grad_inputs.astype(jnp.bfloat16)))
    zero_grads = tuple((jnp.zeros_like(weight) for weight in params))
    totals, (results, grad_rows) = lax.scan(group_step, zero_grads, blocks)
    grad_query, grad_key, grad_value, grad_out, grad_sel_value, grad_sel_out, grad_gain_one, grad_bias_one, grad_gain_two, grad_bias_two, grad_select, grad_up, grad_down = totals
    return (results.reshape(tokens.shape), grad_rows.reshape(tokens.shape), grad_query, grad_key, grad_value, grad_out, grad_sel_value, grad_sel_out, grad_gain_one, grad_bias_one, grad_gain_two, grad_bias_two, grad_select, grad_up, grad_down)
```

```python
import jax
import jax.numpy as jnp
from jax import lax
from jax.experimental import pallas as pl
from jax.experimental.pallas import tpu as pltpu
from jax.sharding import PartitionSpec as P

EPSILON = 1e-05
FULL_TYPE = jnp.float32
HALF_TYPE = jnp.bfloat16


def for_sending(value):

    def short(part):
        return part.astype(jnp.bfloat16) if part.dtype == jnp.float32 else part

    return jax.tree.map(short, value)


def norm_parts(values_in, gain, bias):
    row_mean = jnp.mean(values_in, axis=-1, keepdims=True)
    centred = values_in - row_mean
    inv_scale = lax.rsqrt(jnp.mean(centred * centred, axis=-1, keepdims=True) + EPSILON)
    normal = centred * inv_scale
    return (normal * gain + bias, normal, inv_scale)


def norm_back(grad_in, normal, inv_scale, gain):
    scaled = grad_in * gain
    return inv_scale * (
        scaled
        - jnp.mean(scaled, axis=-1, keepdims=True)
        - normal * jnp.mean(scaled * normal, axis=-1, keepdims=True)
    )


def rotate(values_in, positions, turn):
    half_dim = values_in.shape[-1] // 2
    frequency = 10000.0 ** (-(jnp.arange(half_dim).astype(FULL_TYPE) * 2.0 / values_in.shape[-1]))
    angles = positions.astype(FULL_TYPE)[:, None] * frequency[None, :]
    cosine = jnp.cos(angles)[:, None, :]
    sine_part = turn * jnp.sin(angles)[:, None, :]
    front_half = values_in[..., :half_dim]
    back_half = values_in[..., half_dim:]
    return jnp.concatenate(
        [front_half * cosine - back_half * sine_part, front_half * sine_part + back_half * cosine],
        axis=-1,
    )


def one_hot_sum(ids, wanted):
    return jnp.sum((ids[..., None] == wanted).astype(FULL_TYPE), axis=-2)


def matmul(left_op, right_op):
    return jnp.dot(left_op, right_op, preferred_element_type=FULL_TYPE)


def contract_rows(left_op, right_op):
    left_flat = left_op.reshape(-1, left_op.shape[-1])
    right_flat = right_op.reshape(-1, right_op.shape[-1])
    return lax.dot_general(
        left_flat, right_flat, (((0,), (0,)), ((), ())), preferred_element_type=FULL_TYPE
    )


def times_transpose(grad_in, weight):
    return lax.dot_general(
        grad_in, weight, (((grad_in.ndim - 1,), (1,)), ((), ())), preferred_element_type=FULL_TYPE
    )


def attend_forward(
    tokens,
    lengths,
    value_ids,
    out_ids,
    w_query,
    w_key,
    w_value,
    w_out,
    sel_value,
    sel_out,
    gain_one,
    bias_one,
    gain_two,
    bias_two,
):
    seq_count, row_count, model_width = tokens.shape
    head_count = w_out.shape[0]
    head_dim = w_out.shape[1]
    value_experts = sel_value.shape[1] // head_count
    positions = lax.axis_index("wide") * row_count + jnp.arange(row_count, dtype=jnp.int32)
    inputs = tokens.astype(FULL_TYPE)
    normed, normal_one, scale_one = norm_parts(inputs, gain_one, bias_one)
    normed_low = normed.astype(HALF_TYPE)
    query_pre = matmul(normed_low, w_query).reshape(seq_count, row_count, head_count, head_dim)
    key_pre = matmul(normed_low, w_key).reshape(seq_count, row_count, head_count, head_dim)
    queries = rotate(query_pre, positions, 1.0).astype(HALF_TYPE)
    key_low = rotate(key_pre, positions, 1.0).astype(HALF_TYPE)
    expert_ids = jnp.arange(value_experts, dtype=jnp.int32)
    value_choice = one_hot_sum(value_ids, expert_ids)
    value_sig = jax.nn.sigmoid(
        matmul(normed_low, sel_value).reshape(seq_count, row_count, head_count, value_experts)
    )
    value_gate = value_sig * value_choice
    projected = matmul(tokens, w_value).reshape(
        seq_count, row_count, head_count, value_experts, head_dim
    )
    values = jnp.sum(value_gate[..., None] * projected, axis=3).astype(HALF_TYPE)
    keys_all, values_all = (
        lax.all_gather(key_low, "wide", axis=1, tiled=True),
        lax.all_gather(values, "wide", axis=1, tiled=True),
    )
    span = keys_all.shape[1]
    key_pos = jnp.arange(span, dtype=jnp.int32)
    allowed = (key_pos[None, None, None, :] <= positions[None, None, :, None]) & (
        key_pos[None, None, None, :] < lengths[:, None, None, None]
    )
    scores = jnp.einsum(
        "bphc,bshc->bhps", queries, keys_all, preferred_element_type=FULL_TYPE
    ) * head_dim ** (-0.5)
    masked = jnp.where(allowed, scores, -1e30)
    row_max = jnp.max(masked, axis=-1, keepdims=True)
    exponent = jnp.exp(masked - row_max)
    row_total = jnp.sum(exponent, axis=-1, keepdims=True)
    attn_probs = exponent / row_total
    log_total = row_max + jnp.log(row_total)
    attended = jnp.einsum(
        "bhps,bshc->bphc",
        attn_probs.astype(HALF_TYPE),
        values_all,
        preferred_element_type=FULL_TYPE,
    )
    live_rows = (positions[None, :] < lengths[:, None]).astype(FULL_TYPE)[:, :, None, None]
    mixed_out = (attended * live_rows).astype(HALF_TYPE)
    out_choice = one_hot_sum(out_ids, expert_ids)
    out_sig = jax.nn.sigmoid(
        matmul(normed_low, sel_out).reshape(seq_count, row_count, head_count, value_experts)
    )
    out_gate = out_sig * out_choice
    expert_out = jnp.einsum(
        "bphc,hcf->bphf", mixed_out, w_out, preferred_element_type=FULL_TYPE
    ).reshape(seq_count, row_count, head_count, value_experts, model_width)
    after_attn = inputs + jnp.sum(out_gate[..., None] * expert_out, axis=(2, 3))
    normed_two, normal_two, scale_two = norm_parts(after_attn, gain_two, bias_two)
    return dict(
        positions=positions,
        normal_one=normal_one,
        scale_one=scale_one,
        normed_low=normed_low,
        queries=queries,
        keys_all=keys_all,
        values_all=values_all,
        allowed=allowed,
        log_total=log_total,
        live_rows=live_rows,
        mixed_out=mixed_out,
        value_choice=value_choice,
        value_sig=value_sig,
        value_gate=value_gate,
        projected=projected,
        out_choice=out_choice,
        out_sig=out_sig,
        out_gate=out_gate,
        expert_out=expert_out,
        after_attn=after_attn,
        normed_two=normed_two,
        normal_two=normal_two,
        scale_two=scale_two,
    )


def expert_forward(after_attn, normed_two, mlp_ids, w_select, w_up):
    rows_all, normed_all = (
        lax.all_gather(for_sending(after_attn.astype(HALF_TYPE)), "wide", axis=1, tiled=True),
        lax.all_gather(for_sending(normed_two.astype(HALF_TYPE)), "wide", axis=1, tiled=True),
    )
    local_count = w_select.shape[1]
    hidden = w_up.shape[1] // local_count
    seq_count, span = (rows_all.shape[0], rows_all.shape[1])
    owned_ids = lax.axis_index("wide") * local_count + jnp.arange(local_count, dtype=jnp.int32)
    chosen = one_hot_sum(mlp_ids, owned_ids)
    sigmoid_gate = jax.nn.sigmoid(matmul(normed_all, w_select))
    mlp_gate = sigmoid_gate * chosen
    pre_act = matmul(rows_all, w_up)
    activated = jax.nn.gelu(pre_act).reshape(seq_count, span, local_count, hidden)
    inner_low = (
        (activated * mlp_gate[..., None])
        .reshape(seq_count, span, local_count * hidden)
        .astype(HALF_TYPE)
    )
    return dict(
        rows_all=rows_all,
        normed_all=normed_all,
        chosen=chosen,
        sigmoid_gate=sigmoid_gate,
        mlp_gate=mlp_gate,
        pre_act=pre_act,
        activated=activated,
        inner_low=inner_low,
    )


def per_device(
    tokens,
    lengths,
    value_ids,
    out_ids,
    mlp_ids,
    w_query,
    w_key,
    w_value,
    w_out,
    sel_value,
    sel_out,
    gain_one,
    bias_one,
    gain_two,
    bias_two,
    w_select,
    w_up,
    w_down,
    cotangent,
):
    seq_count, row_count, model_width = tokens.shape
    head_count = w_out.shape[0]
    head_dim = w_out.shape[1]
    value_experts = sel_value.shape[1] // head_count
    saved = attend_forward(
        tokens,
        lengths,
        value_ids,
        out_ids,
        w_query,
        w_key,
        w_value,
        w_out,
        sel_value,
        sel_out,
        gain_one,
        bias_one,
        gain_two,
        bias_two,
    )
    expert_state = expert_forward(saved["after_attn"], saved["normed_two"], mlp_ids, w_select, w_up)
    branch_part = matmul(expert_state["inner_low"], w_down)
    branch_sum = lax.psum_scatter(
        branch_part.astype(jnp.bfloat16), "wide", scatter_dimension=1, tiled=True
    ).astype(jnp.float32)
    output = (saved["after_attn"] + branch_sum).astype(HALF_TYPE)
    saved = attend_forward(
        tokens,
        lengths,
        value_ids,
        out_ids,
        w_query,
        w_key,
        w_value,
        w_out,
        sel_value,
        sel_out,
        gain_one,
        bias_one,
        gain_two,
        bias_two,
    )
    expert_state = expert_forward(saved["after_attn"], saved["normed_two"], mlp_ids, w_select, w_up)
    cot_all = lax.all_gather(cotangent, "wide", axis=1, tiled=True)
    grad_down = contract_rows(expert_state["inner_low"], cot_all)
    d_inner = times_transpose(cot_all, w_down)
    activated = expert_state["activated"]
    d_inner_four = d_inner.reshape(activated.shape)
    d_mlp_gate = jnp.sum(d_inner_four * activated, axis=-1)
    mlp_gate = expert_state["mlp_gate"]
    gated_grad = (d_inner_four * mlp_gate[..., None]).reshape(expert_state["pre_act"].shape)
    unused_value, gelu_pull = jax.vjp(jax.nn.gelu, expert_state["pre_act"])
    d_pre = gelu_pull(gated_grad)[0].astype(HALF_TYPE)
    sigmoid_gate = expert_state["sigmoid_gate"]
    d_logit = (d_mlp_gate * expert_state["chosen"] * sigmoid_gate * (1.0 - sigmoid_gate)).astype(
        HALF_TYPE
    )
    grad_up = contract_rows(expert_state["rows_all"], d_pre)
    grad_select = contract_rows(expert_state["normed_all"], d_logit)
    row_part = times_transpose(d_pre, w_up)
    norm_part = times_transpose(d_logit, w_select)
    row_grad, norm_grad = (
        lax.psum_scatter(row_part, "wide", scatter_dimension=1, tiled=True),
        lax.psum_scatter(norm_part, "wide", scatter_dimension=1, tiled=True),
    )
    grad_gain_two = jnp.sum(norm_grad * saved["normal_two"], axis=(0, 1))
    grad_bias_two = jnp.sum(norm_grad, axis=(0, 1))
    d_after = (
        cotangent.astype(FULL_TYPE)
        + row_grad
        + norm_back(norm_grad, saved["normal_two"], saved["scale_two"], gain_two)
    )
    out_gate = saved["out_gate"]
    d_expert = (out_gate[..., None] * d_after[:, :, None, None, :]).astype(HALF_TYPE)
    d_out_gate = jnp.sum(saved["expert_out"] * d_after[:, :, None, None, :], axis=-1)
    d_expert_flat = d_expert.reshape(seq_count, row_count, head_count, value_experts * model_width)
    grad_out = jnp.einsum(
        "bphc,bphf->hcf", saved["mixed_out"], d_expert_flat, preferred_element_type=FULL_TYPE
    )
    d_mixed = jnp.einsum("bphf,hcf->bphc", d_expert_flat, w_out, preferred_element_type=FULL_TYPE)
    d_attended = (d_mixed * saved["live_rows"]).astype(HALF_TYPE)
    out_sig = saved["out_sig"]
    d_out_logit = (
        (d_out_gate * saved["out_choice"] * out_sig * (1.0 - out_sig))
        .astype(HALF_TYPE)
        .reshape(seq_count, row_count, head_count * value_experts)
    )
    queries = saved["queries"]
    keys_all = saved["keys_all"]
    values_all = saved["values_all"]
    score_scale = head_dim ** (-0.5)
    scores = (
        jnp.einsum("bphc,bshc->bhps", queries, keys_all, preferred_element_type=FULL_TYPE)
        * score_scale
    )
    attn_probs = jnp.where(saved["allowed"], jnp.exp(scores - saved["log_total"]), 0.0)
    d_values_part = jnp.einsum(
        "bhps,bphc->bshc",
        attn_probs.astype(HALF_TYPE),
        d_attended,
        preferred_element_type=FULL_TYPE,
    )
    d_probs = jnp.einsum(
        "bphc,bshc->bhps", d_attended, values_all, preferred_element_type=FULL_TYPE
    )
    row_inner = jnp.sum(attn_probs * d_probs, axis=-1, keepdims=True)
    d_scores = (attn_probs * (d_probs - row_inner)).astype(HALF_TYPE)
    d_queries = (
        jnp.einsum("bhps,bshc->bphc", d_scores, keys_all, preferred_element_type=FULL_TYPE)
        * score_scale
    )
    d_keys_part = (
        jnp.einsum("bhps,bphc->bshc", d_scores, queries, preferred_element_type=FULL_TYPE)
        * score_scale
    )
    d_keys, d_values = (
        lax.psum_scatter(
            d_keys_part.astype(jnp.bfloat16), "wide", scatter_dimension=1, tiled=True
        ).astype(jnp.float32),
        lax.psum_scatter(
            d_values_part.astype(jnp.bfloat16), "wide", scatter_dimension=1, tiled=True
        ).astype(jnp.float32),
    )
    positions = saved["positions"]
    d_query_pre = (
        rotate(d_queries, positions, -1.0)
        .astype(HALF_TYPE)
        .reshape(seq_count, row_count, head_count * head_dim)
    )
    d_key_pre = (
        rotate(d_keys, positions, -1.0)
        .astype(HALF_TYPE)
        .reshape(seq_count, row_count, head_count * head_dim)
    )
    d_projected = (
        (saved["value_gate"][..., None] * d_values[:, :, :, None, :])
        .astype(HALF_TYPE)
        .reshape(seq_count, row_count, head_count * value_experts * head_dim)
    )
    d_value_gate = jnp.sum(saved["projected"] * d_values[:, :, :, None, :], axis=-1)
    value_sig = saved["value_sig"]
    d_value_logit = (
        (d_value_gate * saved["value_choice"] * value_sig * (1.0 - value_sig))
        .astype(HALF_TYPE)
        .reshape(seq_count, row_count, head_count * value_experts)
    )
    normed_low = saved["normed_low"]
    grad_query = contract_rows(normed_low, d_query_pre)
    grad_key = contract_rows(normed_low, d_key_pre)
    grad_sel_value = contract_rows(normed_low, d_value_logit)
    grad_sel_out = contract_rows(normed_low, d_out_logit)
    grad_value = contract_rows(tokens, d_projected)
    d_normed = (
        times_transpose(d_query_pre, w_query)
        + times_transpose(d_key_pre, w_key)
        + times_transpose(d_value_logit, sel_value)
        + times_transpose(d_out_logit, sel_out)
    )
    grad_gain_one = jnp.sum(d_normed * saved["normal_one"], axis=(0, 1))
    grad_bias_one = jnp.sum(d_normed, axis=(0, 1))
    grad_tokens = (
        d_after
        + times_transpose(d_projected, w_value)
        + norm_back(d_normed, saved["normal_one"], saved["scale_one"], gain_one)
    ).astype(HALF_TYPE)
    (
        grad_query,
        grad_key,
        grad_value,
        grad_out,
        grad_sel_value,
        grad_sel_out,
        grad_gain_one,
        grad_bias_one,
        grad_gain_two,
        grad_bias_two,
    ) = lax.psum(
        (
            grad_query,
            grad_key,
            grad_value,
            grad_out,
            grad_sel_value,
            grad_sel_out,
            grad_gain_one,
            grad_bias_one,
            grad_gain_two,
            grad_bias_two,
        ),
        ("wide", "narrow"),
    )
    grad_select, grad_up, grad_down = (
        lax.psum(grad_select.astype(jnp.bfloat16), "narrow").astype(jnp.float32),
        lax.psum(grad_up.astype(jnp.bfloat16), "narrow").astype(jnp.float32),
        lax.psum(grad_down.astype(jnp.bfloat16), "narrow").astype(jnp.float32),
    )
    return (
        output,
        grad_tokens,
        grad_query,
        grad_key,
        grad_value,
        grad_out,
        grad_sel_value,
        grad_sel_out,
        grad_gain_one,
        grad_bias_one,
        grad_gain_two,
        grad_bias_two,
        grad_select,
        grad_up,
        grad_down,
    )


SELV = 72
SELO = 92
LANES = 128


def call(kernel, out_shape, *args, grid=None, in_specs=None, out_specs=None, scratch=(), flops=0, limit=56):
    moved = sum(a.size * a.dtype.itemsize for a in jax.tree.leaves((args, out_shape)))
    extra = {}
    if grid is not None:
        extra["grid"] = grid
        extra["in_specs"] = in_specs
        extra["out_specs"] = out_specs
    elif in_specs is not None:
        extra["in_specs"] = in_specs
    return pl.pallas_call(
        kernel,
        out_shape=out_shape,
        scratch_shapes=list(scratch),
        compiler_params=pltpu.CompilerParams(vmem_limit_bytes=limit * 1024 * 1024),
        cost_estimate=pl.CostEstimate(flops=int(flops), bytes_accessed=int(moved), transcendentals=0),
        **extra,
    )(*args)


def full(shape):
    rank = len(shape)
    return pl.BlockSpec(tuple(shape), lambda s: (0,) * rank)


def shaped(shape, dtype=HALF_TYPE):
    return jax.ShapeDtypeStruct(tuple(shape), dtype)


def nn(a, b):
    return lax.dot_general(a, b, (((1,), (0,)), ((), ())), preferred_element_type=FULL_TYPE)


def nt(a, b):
    return lax.dot_general(a, b, (((1,), (1,)), ((), ())), preferred_element_type=FULL_TYPE)


def tn(a, b):
    return lax.dot_general(a, b, (((0,), (0,)), ((), ())), preferred_element_type=FULL_TYPE)


def layer_stats(v):
    centred = v - jnp.mean(v, axis=-1, keepdims=True)
    inv = lax.rsqrt(jnp.mean(centred * centred, axis=-1, keepdims=True) + EPSILON)
    return centred * inv, inv


def turned(v, cos, sin):
    return v * cos + pltpu.roll(v, v.shape[-1] // 2, axis=v.ndim - 1) * sin


def lane_ids(shape, dim):
    return lax.broadcasted_iota(jnp.int32, shape, dim)


def pre_kernel(tok, gain, bias, wq, wk, wv, sel, vid, oid, cos, sin, qkv, proj, gate):
    heads = qkv.shape[0]
    experts = wv.shape[1] // (heads * LANES)
    low = tok[0]
    normal, _ = layer_stats(low.astype(FULL_TYPE))
    normed = (normal * gain[...] + bias[...]).astype(HALF_TYPE)
    for part, weight in ((0, wq), (1, wk)):
        pre = nn(normed, weight[...])
        for h in range(heads):
            qkv[h, part] = turned(pre[:, h * LANES:(h + 1) * LANES], cos[...], sin[...]).astype(HALF_TYPE)
    lanes = lane_ids((low.shape[0], LANES), 1)
    chosen = jnp.zeros((low.shape[0], LANES), FULL_TYPE)
    tops = vid.shape[2] // heads
    for h in range(heads):
        for k in range(tops):
            j = h * tops + k
            chosen += (lanes == vid[0, :, j:j + 1] + (SELV + experts * h)).astype(FULL_TYPE)
            chosen += (lanes == oid[0, :, j:j + 1] + (SELO + experts * h)).astype(FULL_TYPE)
    gates = jax.nn.sigmoid(nn(normed, sel[...])) * chosen
    gate[0] = gates
    for h in range(heads):
        at = h * experts * LANES
        block = nn(low, wv[:, at:at + experts * LANES])
        proj[0, :, at:at + experts * LANES] = block.astype(HALF_TYPE)
        total = None
        for e in range(experts):
            col = SELV + h * experts + e
            term = gates[:, col:col + 1] * block[:, e * LANES:(e + 1) * LANES]
            total = term if total is None else total + term
        qkv[h, 2] = total.astype(HALF_TYPE)


def limits_of(i, rows, length):
    position = i * rows + lane_ids((1, rows), 1)
    return jnp.minimum(position + 1, length), position


def attend_kernel(length, qkv, mixed, out_t, lse):
    blocks, _, rows, width = qkv.shape
    scale = width ** (-0.5)
    values_t = jnp.transpose(
        qkv[:, 2].reshape(blocks * rows, width).astype(FULL_TYPE)
    ).astype(HALF_TYPE)
    for i in range(blocks):
        n = (i + 1) * rows
        keys = qkv[0:i + 1, 1].reshape(n, width)
        limit, position = limits_of(i, rows, length[0])
        scores = nt(keys, qkv[i, 0]) * scale
        scores = jnp.where(lane_ids((n, rows), 0) < limit, scores, -1e30)
        top = jnp.max(scores, axis=0, keepdims=True)
        weights = jnp.exp(scores - top)
        total = jnp.sum(weights, axis=0, keepdims=True)
        attended = nn(values_t[:, :n], weights.astype(HALF_TYPE)) / total
        out_t[:, i * rows:(i + 1) * rows] = attended
        lse[:, i * rows:(i + 1) * rows] = top + jnp.log(total)
        live = (position < length[0]).astype(FULL_TYPE)
        mixed[i] = jnp.transpose(attended * live).astype(HALF_TYPE)


def attend_back_kernel(length, qkv, d_out, out_t, lse, cos, sin, d_qkv, d_keys, d_values):
    blocks, _, rows, width = qkv.shape
    scale = width ** (-0.5)
    keys_t = jnp.transpose(
        qkv[:, 1].reshape(blocks * rows, width).astype(FULL_TYPE)
    ).astype(HALF_TYPE)
    d_keys[...] = jnp.zeros_like(d_keys)
    d_values[...] = jnp.zeros_like(d_values)
    for i in range(blocks):
        n = (i + 1) * rows
        here = slice(i * rows, (i + 1) * rows)
        limit, _ = limits_of(i, rows, length[0])
        query = qkv[i, 0]
        d_att = d_out[i]
        delta = jnp.sum(jnp.transpose(d_att.astype(FULL_TYPE)) * out_t[:, here], axis=0, keepdims=True)
        scores = nt(qkv[0:i + 1, 1].reshape(n, width), query) * scale
        probs = jnp.where(lane_ids((n, rows), 0) < limit, jnp.exp(scores - lse[:, here]), 0.0)
        d_probs = nt(qkv[0:i + 1, 2].reshape(n, width), d_att)
        d_scores = (probs * (d_probs - delta)).astype(HALF_TYPE)
        d_values[0:n, :] += nn(probs.astype(HALF_TYPE), d_att)
        d_keys[0:n, :] += nn(d_scores, query)
        d_query = jnp.transpose(nn(keys_t[:, :n], d_scores)) * scale
        d_qkv[i, 0] = turned(d_query, cos[here, :], -sin[here, :]).astype(HALF_TYPE)
    for i in range(blocks):
        here = slice(i * rows, (i + 1) * rows)
        d_qkv[i, 1] = turned(d_keys[here, :] * scale, cos[here, :], -sin[here, :]).astype(HALF_TYPE)
        d_qkv[i, 2] = d_values[here, :].astype(HALF_TYPE)


def gated(mixed, gate, hp, e, experts):
    parts = []
    for h in (2 * hp, 2 * hp + 1):
        col = SELO + h * experts + e
        parts.append((gate[:, col:col + 1] * mixed[h].astype(FULL_TYPE)).astype(HALF_TYPE))
    return jnp.concatenate(parts, axis=1)


def out_block(w_out, hp, e, width):
    block = w_out[2 * hp:2 * hp + 2, :, e * width:(e + 1) * width]
    return block.reshape(2 * block.shape[1], width)


def post_kernel(mixed, gate, w_out, tok, gain, bias, w_sel, ids, eids, places, after, rows, gates, sent):
    width = tok.shape[2]
    heads = w_out.shape[0]
    experts = w_out.shape[2] // width
    total = tok[0].astype(FULL_TYPE)
    gate_here = gate[0]
    mixed_here = mixed[...]
    for hp in range(heads // 2):
        for e in range(experts):
            total += nn(gated(mixed_here, gate_here, hp, e, experts), out_block(w_out, hp, e, width))
    after[...] = total
    rows[...] = total.astype(HALF_TYPE)
    normal, _ = layer_stats(total)
    normed = (normal * gain[...] + bias[...]).astype(HALF_TYPE)
    chosen = jnp.zeros((eids.shape[0], ids.shape[2]), FULL_TYPE)
    for k in range(ids.shape[1]):
        chosen += (eids[...] == ids[0, k:k + 1, :]).astype(FULL_TYPE)
    values = jax.nn.sigmoid(nt(w_sel[...], normed)) * chosen
    gates[...] = values
    moved = nn(places[...], values.astype(HALF_TYPE)).astype(HALF_TYPE)
    sent[...] = moved.reshape(sent.shape)


def expand(count, cols, first):
    rows = lane_ids((count, cols), 0)
    cut = lane_ids((count, cols), 1)
    hit = None
    for i in range(cols // LANES):
        inside = (cut >= i * LANES) & (cut < (i + 1) * LANES) & (rows == first + i)
        hit = inside if hit is None else hit | inside
    return hit.astype(FULL_TYPE).astype(HALF_TYPE)


def experts_kernel(*refs):
    rows, cot, gate = refs[:3]
    ups, downs = refs[3:11], refs[11:19]
    d_rows, branch, d_gate, inner, d_pre = refs[19:]
    low, cot_low, gates = rows[...], cot[...], gate[...]
    row_total = branch_total = gate_total = None
    for p in range(8):
        w_up, w_down = ups[p][...], downs[p][...]
        cols = w_up.shape[1]
        spread = expand(gates.shape[0], cols, p * (cols // LANES))
        gate_wide = tn(gates, spread)
        pre = nn(low, w_up)
        d_in = nt(cot_low, w_down)
        root = 0.7978845608028654
        square = pre * pre
        tanh = jnp.tanh(root * pre * (1.0 + 0.044715 * square))
        half = 0.5 * (1.0 + tanh)
        act = pre * half
        slope = half + 0.5 * pre * (1.0 - tanh * tanh) * (root * (1.0 + 3 * 0.044715 * square))
        in_low = (act * gate_wide).astype(HALF_TYPE)
        pre_low = (slope * gate_wide * d_in).astype(HALF_TYPE)
        inner[:, p * cols:(p + 1) * cols] = in_low
        d_pre[:, p * cols:(p + 1) * cols] = pre_low
        g = nt(spread, (d_in * act).astype(HALF_TYPE))
        r = nt(pre_low, w_up)
        b = nn(in_low, w_down)
        gate_total = g if p == 0 else gate_total + g
        row_total = r if p == 0 else row_total + r
        branch_total = b if p == 0 else branch_total + b
    d_rows[...] = row_total.astype(HALF_TYPE)
    branch[...] = branch_total.astype(HALF_TYPE)
    d_gate[...] = gate_total.astype(HALF_TYPE)


def expert_grads_kernel(*refs):
    count = 4
    rows, cots = refs[0:count], refs[count:2 * count]
    pres, inners = refs[2 * count:3 * count], refs[3 * count:4 * count]
    up, down = refs[4 * count:]
    total = None
    for i in range(count):
        term = tn(rows[i][...], pres[i][...])
        total = term if i == 0 else total + term
    up[0] = total.astype(HALF_TYPE)
    for i in range(count):
        term = tn(inners[i][...], cots[i][...])
        total = term if i == 0 else total + term
    down[0] = total.astype(HALF_TYPE)


def mid_kernel(length, r0, r1, r2, r3, g0, g1, g2, g3, cot, after, gates, gain, bias, w_sel, places, order, w_out, gate, mixed,
               d_after, d_att, d_gate_out, small, acc):
    step = pl.program_id(0)
    width = cot.shape[2]
    heads = w_out.shape[0]
    experts = w_out.shape[2] // width
    row_count = cot.shape[1]
    d_rel = jnp.concatenate([g0[...], g1[...], g2[...], g3[...]], axis=0)
    d_gate = tn(places[...], d_rel)
    values = gates[...]
    d_logit = (d_gate * values * (1.0 - values)).astype(HALF_TYPE)
    normal, inv = layer_stats(after[...])
    normed = (normal * gain[...] + bias[...]).astype(HALF_TYPE)
    d_normed = tn(d_logit, w_sel[...])
    sel_part = nn(d_logit, normed)
    gain_part = jnp.sum(d_normed * normal, axis=0, keepdims=True)
    bias_part = jnp.sum(d_normed, axis=0, keepdims=True)
    count = sel_part.shape[0]

    @pl.when(step == 0)
    def _():
        acc[...] = jnp.zeros_like(acc)

    acc[0:count, :] += sel_part
    acc[count:count + 1, :] += gain_part
    acc[count + 1:count + 2, :] += bias_part
    d_row = (
        r0[...].astype(FULL_TYPE) + r1[...].astype(FULL_TYPE)
        + r2[...].astype(FULL_TYPE) + r3[...].astype(FULL_TYPE)
    )
    total = cot[0].astype(FULL_TYPE) + d_row + norm_back(d_normed, normal, inv, gain[...])
    d_after[...] = total
    total_low = total.astype(HALF_TYPE)
    mixed_here = mixed[...]
    gate_here = gate[0]
    lanes = lane_ids((2 * LANES, LANES), 1)
    second = (lane_ids((2 * LANES, LANES), 0) >= LANES).astype(jnp.int32)
    d_gates = jnp.zeros((row_count, LANES), FULL_TYPE)
    for hp in range(heads // 2):
        both = jnp.concatenate([mixed_here[2 * hp], mixed_here[2 * hp + 1]], axis=1).astype(FULL_TYPE)
        sums = [None, None]
        for e in range(experts):
            d_mixed = nt(total_low, out_block(w_out, hp, e, width))
            hit = (lanes == SELO + 2 * hp * experts + e + second * experts).astype(FULL_TYPE).astype(HALF_TYPE)
            d_gates += nn((both * d_mixed).astype(HALF_TYPE), hit)
            for i in range(2):
                col = SELO + (2 * hp + i) * experts + e
                term = gate_here[:, col:col + 1] * d_mixed[:, i * LANES:(i + 1) * LANES]
                sums[i] = term if e == 0 else sums[i] + term
        for i in range(2):
            position = length[1] + lane_ids((row_count, 1), 0)
            live = (position < length[2 + step]).astype(FULL_TYPE)
            d_att[2 * hp + i] = (sums[i] * live).astype(HALF_TYPE)
    d_gate_out[0] = d_gates

    @pl.when(step == pl.num_programs(0) - 1)
    def _():
        small[...] = tn(acc[...].astype(HALF_TYPE), order[...])


def out_grad_kernel(mixed, gate, d_after, out):
    heads, experts = 4, out.shape[1] // d_after.shape[1]
    width = d_after.shape[1]
    seqs, row_count = gate.shape[0], gate.shape[1]
    low = d_after[...].astype(HALF_TYPE)
    for hp in range(heads // 2):
        for e in range(experts):
            total = None
            for s in range(seqs):
                left = gated([mixed[s * heads + h] for h in range(heads)], gate[s], hp, e, experts)
                term = tn(left, low[s * row_count:(s + 1) * row_count, :])
                total = term if total is None else total + term
            out[2 * hp * LANES:(2 * hp + 2) * LANES, e * width:(e + 1) * width] = total.astype(HALF_TYPE)


def last_kernel(d_qkv, tok, gain, bias, wq, wk, sel, proj, gate, d_gate_out, small, d_after,
                grads, d_proj, part, d_qk, d_sel):
    seqs, row_count, width = tok.shape
    heads = 4
    experts = proj.shape[2] // (heads * LANES)
    lanes = lane_ids((LANES, LANES), 1)
    gain_sum = bias_sum = 0.0
    normed_t, tok_t = [], []
    for s in range(seqs):
        low = tok[s]
        normal, inv = layer_stats(low.astype(FULL_TYPE))
        normed = (normal * gain[...] + bias[...]).astype(HALF_TYPE)
        d_gates = d_gate_out[s]
        gate_here = gate[s]
        here = slice(s * row_count, (s + 1) * row_count)
        for h in range(heads):
            for part_id in range(2):
                at = part_id * heads * LANES + h * LANES
                d_qk[here, at:at + LANES] = d_qkv[s * heads + h, part_id]
            d_value = d_qkv[s * heads + h, 2].astype(FULL_TYPE)
            for e in range(experts):
                col = SELV + h * experts + e
                at = (h * experts + e) * LANES
                d_proj[here, at:at + LANES] = (gate_here[:, col:col + 1] * d_value).astype(HALF_TYPE)
                hit = (lanes == col).astype(FULL_TYPE).astype(HALF_TYPE)
                product = (proj[s, :, at:at + LANES].astype(FULL_TYPE) * d_value).astype(HALF_TYPE)
                d_gates += nn(product, hit)
        d_logit = (d_gates * gate_here * (1.0 - gate_here)).astype(HALF_TYPE)
        d_sel[here, :] = d_logit
        half = heads * LANES
        d_normed = (
            nt(d_qk[here, 0:half], wq[...]) + nt(d_qk[here, half:2 * half], wk[...]) + nt(d_logit, sel[...])
        )
        gain_sum += jnp.sum(d_normed * normal, axis=0, keepdims=True)
        bias_sum += jnp.sum(d_normed, axis=0, keepdims=True)
        part[here, :] = d_after[here, :] + norm_back(d_normed, normal, inv, gain[...])
        normed_t.append(jnp.transpose(normed.astype(FULL_TYPE)).astype(HALF_TYPE))
        tok_t.append(jnp.transpose(low.astype(FULL_TYPE)).astype(HALF_TYPE))
    normed_t = jnp.concatenate(normed_t, axis=1)
    tok_t = jnp.concatenate(tok_t, axis=1)
    size = 512
    at = 0
    for left, right in ((normed_t, d_qk), (tok_t, d_proj)):
        for b in range(right.shape[1] // size):
            grads[:, at:at + size] = nn(left, right[:, b * size:(b + 1) * size]).astype(HALF_TYPE)
            at += size
    rows = jnp.concatenate([gain_sum, bias_sum, jnp.zeros((14, width), FULL_TYPE)], axis=0).astype(HALF_TYPE)
    spot = (lane_ids((16, LANES), 1) == lane_ids((16, LANES), 0) + 66) & (lane_ids((16, LANES), 0) < 2)
    spread = tn(rows, spot.astype(FULL_TYPE).astype(HALF_TYPE))
    grads[:, at:at + LANES] = (small[...] + nn(normed_t, d_sel[...]) + spread).astype(HALF_TYPE)


def token_grad_kernel(part, d_proj, wv, out):
    out[...] = (part[...] + nt(d_proj[...], wv[...])).astype(HALF_TYPE)


def output_kernel(after, b0, b1, b2, b3, out):
    out[...] = (
        after[...] + b0[...].astype(FULL_TYPE) + b1[...].astype(FULL_TYPE)
        + b2[...].astype(FULL_TYPE) + b3[...].astype(FULL_TYPE)
    ).astype(HALF_TYPE)


class Place:
    def __init__(self):
        self.wide = lax.axis_index("wide")
        self.narrow = lax.axis_index("narrow")
        self.z, self.x = self.wide // 2, self.wide % 2
        self.y, self.c = self.narrow // 2, self.narrow % 2

    @staticmethod
    def pairs(move):
        every = []
        for z in range(4):
            for x in range(2):
                for y in range(2):
                    for c in range(2):
                        tz, tx, ty, tc = move(z, x, y, c)
                        every.append(((z * 2 + x) * 4 + y * 2 + c, (tz * 2 + tx) * 4 + ty * 2 + tc))
        return every

    def send(self, value, move):
        return lax.ppermute(value, ("wide", "narrow"), self.pairs(move))

    def swap_x(self, value):
        return self.send(value, lambda z, x, y, c: (z, 1 - x, y, c))

    def swap_y(self, value):
        return self.send(value, lambda z, x, y, c: (z, x, 1 - y, c))

    def swap_xy(self, value):
        return self.send(value, lambda z, x, y, c: (z, 1 - x, 1 - y, c))

    def swap_c(self, value):
        return self.send(value, lambda z, x, y, c: (z, x, y, 1 - c))

    def shift_z(self, value, k):
        return self.send(value, lambda z, x, y, c: ((z + k) % 4, x, y, c))


def pick(array, index):
    return lax.dynamic_index_in_dim(array, index, 0, keepdims=False)


def add(*terms):
    total = terms[0].astype(FULL_TYPE)
    for term in terms[1:]:
        total = total + term.astype(FULL_TYPE)
    return total.astype(HALF_TYPE)


def in_order(bit, mine, other):
    return jnp.stack([jnp.where(bit == 0, mine, other), jnp.where(bit == 0, other, mine)])


def sum_everywhere(place, array):
    rows, cols = array.shape
    parts = array.reshape(2, 2, 2, 2, 4, rows // 64, cols)
    bits = ((place.y, place.swap_y), (place.x, place.swap_x))

    def halve(bit, swap, value):
        return add(pick(value, bit), swap(pick(value, 1 - bit)))

    kept = halve(place.c, place.swap_c, parts)
    first = [halve(*bits[i], kept[i]) for i in range(2)]
    second = [halve(*bits[1 - i], first[i]) for i in range(2)]
    value = jnp.stack(second, axis=1)
    came = [place.shift_z(pick(value, (place.z + k) % 4), k) for k in (1, 2, 3)]
    done = add(pick(value, place.z), *came)
    around = [done] + [place.shift_z(done, k) for k in (1, 2, 3)]
    around = jnp.stack(around)
    ordered = jnp.stack([pick(around, (place.z - k) % 4) for k in range(4)])
    back = []
    for i in range(2):
        own = ordered[:, i]
        bit, swap = bits[1 - i]
        own = in_order(bit, own, swap(own))
        bit, swap = bits[i]
        back.append(in_order(bit, own, swap(own)))
    own = jnp.stack(back)
    whole = in_order(place.c, own, place.swap_c(own))
    return whole.reshape(rows, cols)


def tuned_device(
    tokens, lengths, value_ids, out_ids, mlp_ids, w_query, w_key, w_value, w_out, sel_value, sel_out,
    gain_one, bias_one, gain_two, bias_two, w_select, w_up, w_down, cotangent,
):
    seqs, row_count, width = tokens.shape
    heads, head_dim = w_out.shape[0], w_out.shape[1]
    experts = w_out.shape[2] // width
    pair_count = seqs * heads
    span = 8 * row_count
    all_rows = seqs * row_count
    place = Place()
    first_row = place.wide * row_count
    row = lambda v: v.reshape(1, -1)

    half = head_dim // 2
    frequency = 10000.0 ** (-(jnp.arange(half).astype(FULL_TYPE) * 2.0 / head_dim))
    angles = jnp.arange(span).astype(FULL_TYPE)[:, None] * frequency[None, :]
    cosine, sine = jnp.cos(angles), jnp.sin(angles)
    cosine = jnp.concatenate([cosine, cosine], axis=1)
    sine = jnp.concatenate([-sine, sine], axis=1)
    here = lambda t: lax.dynamic_slice_in_dim(t, first_row, row_count, 0)
    sel = jnp.concatenate(
        [
            jnp.zeros((width, SELV), HALF_TYPE), sel_value, sel_out,
            jnp.zeros((width, LANES - SELO - heads * experts), HALF_TYPE),
        ],
        axis=1,
    )
    value_flat = value_ids.reshape(seqs, row_count, -1)
    out_flat = out_ids.reshape(seqs, row_count, -1)

    local = w_up.shape[1] // 4
    my_up = lax.dynamic_slice_in_dim(w_up, place.narrow * local, local, 1)
    my_down = lax.dynamic_slice_in_dim(w_down, place.narrow * local, local, 0)
    peer = place.narrow + 1 - 2 * place.c
    ups = [my_up, lax.dynamic_slice_in_dim(w_up, peer * local, local, 1)]
    downs = [my_down, lax.dynamic_slice_in_dim(w_down, peer * local, local, 0)]
    for k in (1, 2, 3):
        up_k, down_k = place.shift_z(my_up, 4 - k), place.shift_z(my_down, 4 - k)
        ups += [up_k, place.swap_c(up_k)]
        downs += [down_k, place.swap_c(down_k)]

    own_select = jnp.transpose(w_select)
    select = jnp.concatenate(
        [own_select] + [lax.ppermute(own_select, "wide", [(i, i ^ k) for i in range(8)]) for k in range(1, 8)]
    )
    own_count = own_select.shape[0]
    select_ids = ((place.wide ^ jnp.arange(8))[:, None] * own_count + jnp.arange(own_count)[None, :]).reshape(-1)
    kind = place.x * 2 + place.y
    kinds = kind ^ jnp.arange(4)
    kx, ky = (kinds // 2)[:, None, None, None], (kinds % 2)[:, None, None, None]
    kz = ((place.z + jnp.arange(4)) % 4)[None, :, None, None]
    kc = (place.c ^ jnp.arange(2))[None, None, :, None]
    ki = jnp.arange(2)[None, None, None, :]
    sent_ids = ((kz * 2 + kx) * own_count + ky * 4 + kc * 2 + ki).reshape(-1)
    places = (sent_ids[:, None] == select_ids[None, :]).astype(HALF_TYPE)
    count = select_ids.shape[0]
    lanes = jnp.arange(LANES)
    targets = jnp.concatenate([select_ids, count + jnp.arange(LANES - count)])
    order = (targets[:, None] == lanes[None, :]).astype(HALF_TYPE)

    cot_own = cotangent.reshape(all_rows, width)
    cots = [cot_own, place.swap_y(cot_own), place.swap_x(cot_own), place.swap_xy(cot_own)]

    by_seq = lambda shape: pl.BlockSpec((1,) + tuple(shape[1:]), lambda s: (s,) + (0,) * (len(shape) - 1))
    split = lambda shape: pl.BlockSpec((shape[0] // seqs,) + tuple(shape[1:]), lambda s: (s,) + (0,) * (len(shape) - 1))
    wide_out = heads * experts * LANES
    qkv, projected, gate = call(
        pre_kernel,
        (
            shaped((pair_count, 3, row_count, head_dim)),
            shaped((seqs, row_count, wide_out)),
            shaped((seqs, row_count, LANES), FULL_TYPE),
        ),
        tokens, row(gain_one), row(bias_one), w_query, w_key, w_value, sel, value_flat, out_flat,
        here(cosine), here(sine),
        grid=(seqs,),
        in_specs=[
            by_seq(tokens.shape), full((1, width)), full((1, width)), full(w_query.shape), full(w_key.shape),
            full(w_value.shape), full(sel.shape), by_seq(value_flat.shape), by_seq(out_flat.shape),
            full((row_count, head_dim)), full((row_count, head_dim)),
        ],
        out_specs=(
            split((pair_count, 3, row_count, head_dim)), by_seq((seqs, row_count, wide_out)),
            by_seq((seqs, row_count, LANES)),
        ),
        flops=2 * all_rows * width * 3712,
    )
    qkv = lax.all_to_all(qkv, "wide", 0, 0, tiled=True)
    length = pick(lengths, place.wide // heads).reshape(1)
    smem = pl.BlockSpec(memory_space=pltpu.SMEM)
    vmem = pl.BlockSpec(memory_space=pltpu.VMEM)
    mixed, out_t, lse = call(
        attend_kernel,
        (
            shaped((8, row_count, head_dim)), shaped((head_dim, span), FULL_TYPE), shaped((1, span), FULL_TYPE),
        ),
        length, qkv,
        in_specs=[smem, vmem],
        flops=2 * span * span * head_dim,
    )
    mixed = lax.all_to_all(mixed, "wide", 0, 0, tiled=True)

    own_mlp = lax.dynamic_slice_in_dim(mlp_ids, first_row, row_count, 1)
    own_mlp = jnp.swapaxes(own_mlp, 1, 2)
    token_cols = lambda n: pl.BlockSpec((n, row_count), lambda s: (0, s))
    after, rows_own, gates, sent = call(
        post_kernel,
        (
            shaped((all_rows, width), FULL_TYPE), shaped((all_rows, width)),
            shaped((count, all_rows), FULL_TYPE), shaped((4, count // 4, all_rows)),
        ),
        mixed, gate, w_out, tokens, row(gain_two), row(bias_two), select, own_mlp,
        select_ids.reshape(-1, 1), places,
        grid=(seqs,),
        in_specs=[
            split(mixed.shape), by_seq(gate.shape), full(w_out.shape), by_seq(tokens.shape), full((1, width)),
            full((1, width)), full(select.shape), by_seq(own_mlp.shape), full((count, 1)), full(places.shape),
        ],
        out_specs=(
            split((all_rows, width)), split((all_rows, width)), token_cols(count),
            pl.BlockSpec((4, count // 4, row_count), lambda s: (0, 0, s)),
        ),
        flops=2 * all_rows * width * wide_out,
    )

    swaps = (lambda v: v, place.swap_y, place.swap_x, place.swap_xy)
    rows_in = [swaps[i](rows_own) for i in range(4)]
    gates_in = [swaps[i](sent[i]) for i in range(4)]
    hidden = 8 * local
    results = []
    for i in range(4):
        results.append(
            call(
                experts_kernel,
                (
                    shaped((all_rows, width)), shaped((all_rows, width)), shaped((count // 4, all_rows)),
                    shaped((all_rows, hidden)), shaped((all_rows, hidden)),
                ),
                rows_in[i], cots[i], gates_in[i], *ups, *downs,
                flops=8 * all_rows * width * hidden,
            )
        )
    d_rows = [swaps[i](results[i][0]) for i in range(4)]
    d_gates = [swaps[i](results[i][2]) for i in range(4)]
    branches = [swaps[i](results[i][1]) for i in range(4)]

    cols = lambda: pl.BlockSpec((all_rows, local), lambda p: (0, p))
    whole = lambda: pl.BlockSpec((all_rows, width), lambda p: (0, 0))
    grad_up, grad_down = call(
        expert_grads_kernel,
        (shaped((8, width, local)), shaped((8, local, width))),
        *rows_in, *cots, *[r[4] for r in results], *[r[3] for r in results],
        grid=(8,),
        in_specs=[whole() for _ in range(8)] + [cols() for _ in range(8)],
        out_specs=(
            pl.BlockSpec((1, width, local), lambda p: (p, 0, 0)), pl.BlockSpec((1, local, width), lambda p: (p, 0, 0)),
        ),
        flops=16 * all_rows * width * hidden,
    )

    live_info = jnp.concatenate([jnp.zeros((1,), jnp.int32), first_row.reshape(1).astype(jnp.int32), lengths])
    d_after, d_att, d_gate_out, small = call(
        mid_kernel,
        (
            shaped((all_rows, width), FULL_TYPE), shaped((pair_count, row_count, head_dim)),
            shaped((seqs, row_count, LANES), FULL_TYPE), shaped((width, LANES), FULL_TYPE),
        ),
        live_info, *d_rows, *d_gates, cotangent, after, gates, row(gain_two), row(bias_two), select, places, order,
        w_out, gate, mixed,
        grid=(seqs,),
        in_specs=[smem] + [split((all_rows, width))] * 4 + [token_cols(count // 4)] * 4 + [
            by_seq(cotangent.shape), split((all_rows, width)), token_cols(count), full((1, width)), full((1, width)),
            full(select.shape), full(places.shape), full(order.shape), full(w_out.shape), by_seq(gate.shape),
            split(mixed.shape),
        ],
        out_specs=(
            split((all_rows, width)), split((pair_count, row_count, head_dim)),
            by_seq((seqs, row_count, LANES)), full((width, LANES)),
        ),
        scratch=[pltpu.VMEM((LANES, width), FULL_TYPE)],
        flops=2 * all_rows * width * wide_out,
    )
    d_att = lax.all_to_all(d_att, "wide", 0, 0, tiled=True)
    d_qkv = call(
        attend_back_kernel,
        shaped((8, 3, row_count, head_dim)),
        length, qkv, d_att, out_t, lse, cosine, sine,
        in_specs=[smem] + [vmem] * 6,
        scratch=[pltpu.VMEM((span, head_dim), FULL_TYPE), pltpu.VMEM((span, head_dim), FULL_TYPE)],
        flops=5 * span * span * head_dim,
    )
    d_qkv = lax.all_to_all(d_qkv, "wide", 0, 0, tiled=True)

    grad_out = call(
        out_grad_kernel, shaped((heads * head_dim, experts * width)), mixed, gate, d_after,
        flops=2 * all_rows * width * wide_out,
    )
    output = call(output_kernel, shaped((all_rows, width)), after, *branches)

    grads, d_proj, part = call(
        last_kernel,
        (shaped((width, 2 * heads * head_dim + wide_out + LANES)), shaped((all_rows, wide_out)), shaped((all_rows, width), FULL_TYPE)),
        d_qkv, tokens, row(gain_one), row(bias_one), w_query, w_key, sel, projected, gate, d_gate_out, small, d_after,
        scratch=[pltpu.VMEM((all_rows, 2 * heads * head_dim), HALF_TYPE), pltpu.VMEM((all_rows, LANES), HALF_TYPE)],
        flops=2 * all_rows * width * 4700,
    )
    grad_tokens = call(token_grad_kernel, shaped((all_rows, width)), part, d_proj, w_value, flops=2 * all_rows * width * wide_out)

    grad_out = sum_everywhere(place, grad_out).astype(FULL_TYPE).reshape(heads, head_dim, -1)
    grads = sum_everywhere(place, grads).astype(FULL_TYPE)
    wide_qk = heads * head_dim
    grad_query, grad_key = grads[:, :wide_qk], grads[:, wide_qk:2 * wide_qk]
    grad_value = grads[:, 2 * wide_qk:2 * wide_qk + wide_out]
    small = grads[:, 2 * wide_qk + wide_out:]
    grad_select = lax.dynamic_slice_in_dim(small, place.wide * own_count, own_count, 1)
    grad_gain_two, grad_bias_two = small[:, count], small[:, count + 1]
    grad_gain_one, grad_bias_one = small[:, count + 2], small[:, count + 3]
    grad_sel_value = small[:, SELV:SELV + heads * experts]
    grad_sel_out = small[:, SELO:SELO + heads * experts]

    def experts_sum(pieces):
        by_z = [add(pieces[2 * k], place.swap_c(pieces[2 * k + 1])) for k in range(4)]
        mine = add(by_z[0], *[place.shift_z(by_z[k], k) for k in (1, 2, 3)])
        pair = in_order(place.c, mine, place.swap_c(mine))
        return in_order(place.y, pair, place.swap_y(pair)).reshape((4,) + mine.shape)

    up_sum = experts_sum(grad_up)
    down_sum = experts_sum(grad_down)
    grad_up = jnp.swapaxes(up_sum, 0, 1).reshape(width, -1).astype(FULL_TYPE)
    grad_down = down_sum.reshape(-1, width).astype(FULL_TYPE)
    return (
        output.reshape(tokens.shape), grad_tokens.reshape(tokens.shape), grad_query, grad_key, grad_value, grad_out,
        grad_sel_value, grad_sel_out, grad_gain_one, grad_bias_one, grad_gain_two, grad_bias_two, grad_select,
        grad_up, grad_down,
    )


def fits(mesh):
    return dict(mesh.shape) == {"wide": 8, "narrow": 4}


def solution(mesh):
    placed = (
        P("narrow", "wide", None),
        P("narrow"),
        P("narrow", "wide", None, None),
        P("narrow", "wide", None, None),
        P("narrow", None, None),
        P(),
        P(),
        P(),
        P(),
        P(),
        P(),
        P(),
        P(),
        P(),
        P(),
        P(None, "wide"),
        P(None, "wide"),
        P("wide", None),
        P("narrow", "wide", None),
    )
    return jax.shard_map(
        tuned_device if fits(mesh) else per_device,
        mesh=mesh,
        in_specs=placed,
        out_specs=(
            P("narrow", "wide", None),
            P("narrow", "wide", None),
            P(),
            P(),
            P(),
            P(),
            P(),
            P(),
            P(),
            P(),
            P(),
            P(),
            P(None, "wide"),
            P(None, "wide"),
            P("wide", None),
        ),
        check_vma=False,
    )
```

```python
import functools

import jax
import jax.numpy as jnp
import numpy as np
from jax import lax
from jax.experimental import pallas as pl
from jax.experimental.pallas import tpu as pltpu
from jax.sharding import PartitionSpec as P

EPSILON = 1e-05
FULL_TYPE = jnp.float32
HALF_TYPE = jnp.bfloat16


def for_sending(value):

    def short(part):
        return part.astype(jnp.bfloat16) if part.dtype == jnp.float32 else part

    return jax.tree.map(short, value)


def norm_parts(values_in, gain, bias):
    row_mean = jnp.mean(values_in, axis=-1, keepdims=True)
    centred = values_in - row_mean
    inv_scale = lax.rsqrt(jnp.mean(centred * centred, axis=-1, keepdims=True) + EPSILON)
    normal = centred * inv_scale
    return (normal * gain + bias, normal, inv_scale)


def norm_back(grad_in, normal, inv_scale, gain):
    scaled = grad_in * gain
    return inv_scale * (
        scaled
        - jnp.mean(scaled, axis=-1, keepdims=True)
        - normal * jnp.mean(scaled * normal, axis=-1, keepdims=True)
    )


def rotate(values_in, positions, turn):
    half_dim = values_in.shape[-1] // 2
    frequency = 10000.0 ** (-(jnp.arange(half_dim).astype(FULL_TYPE) * 2.0 / values_in.shape[-1]))
    angles = positions.astype(FULL_TYPE)[:, None] * frequency[None, :]
    cosine = jnp.cos(angles)[:, None, :]
    sine_part = turn * jnp.sin(angles)[:, None, :]
    front_half = values_in[..., :half_dim]
    back_half = values_in[..., half_dim:]
    return jnp.concatenate(
        [front_half * cosine - back_half * sine_part, front_half * sine_part + back_half * cosine],
        axis=-1,
    )


def one_hot_sum(ids, wanted):
    return jnp.sum((ids[..., None] == wanted).astype(FULL_TYPE), axis=-2)


def matmul(left_op, right_op):
    return jnp.dot(left_op, right_op, preferred_element_type=FULL_TYPE)


def contract_rows(left_op, right_op):
    left_flat = left_op.reshape(-1, left_op.shape[-1])
    right_flat = right_op.reshape(-1, right_op.shape[-1])
    return lax.dot_general(
        left_flat, right_flat, (((0,), (0,)), ((), ())), preferred_element_type=FULL_TYPE
    )


def times_transpose(grad_in, weight):
    return lax.dot_general(
        grad_in, weight, (((grad_in.ndim - 1,), (1,)), ((), ())), preferred_element_type=FULL_TYPE
    )


def attend_forward(
    tokens,
    lengths,
    value_ids,
    out_ids,
    w_query,
    w_key,
    w_value,
    w_out,
    sel_value,
    sel_out,
    gain_one,
    bias_one,
    gain_two,
    bias_two,
):
    seq_count, row_count, model_width = tokens.shape
    head_count = w_out.shape[0]
    head_dim = w_out.shape[1]
    value_experts = sel_value.shape[1] // head_count
    positions = lax.axis_index("wide") * row_count + jnp.arange(row_count, dtype=jnp.int32)
    inputs = tokens.astype(FULL_TYPE)
    normed, normal_one, scale_one = norm_parts(inputs, gain_one, bias_one)
    normed_low = normed.astype(HALF_TYPE)
    query_pre = matmul(normed_low, w_query).reshape(seq_count, row_count, head_count, head_dim)
    key_pre = matmul(normed_low, w_key).reshape(seq_count, row_count, head_count, head_dim)
    queries = rotate(query_pre, positions, 1.0).astype(HALF_TYPE)
    key_low = rotate(key_pre, positions, 1.0).astype(HALF_TYPE)
    expert_ids = jnp.arange(value_experts, dtype=jnp.int32)
    value_choice = one_hot_sum(value_ids, expert_ids)
    value_sig = jax.nn.sigmoid(
        matmul(normed_low, sel_value).reshape(seq_count, row_count, head_count, value_experts)
    )
    value_gate = value_sig * value_choice
    projected = matmul(tokens, w_value).reshape(
        seq_count, row_count, head_count, value_experts, head_dim
    )
    values = jnp.sum(value_gate[..., None] * projected, axis=3).astype(HALF_TYPE)
    keys_all, values_all = (
        lax.all_gather(key_low, "wide", axis=1, tiled=True),
        lax.all_gather(values, "wide", axis=1, tiled=True),
    )
    span = keys_all.shape[1]
    key_pos = jnp.arange(span, dtype=jnp.int32)
    allowed = (key_pos[None, None, None, :] <= positions[None, None, :, None]) & (
        key_pos[None, None, None, :] < lengths[:, None, None, None]
    )
    scores = jnp.einsum(
        "bphc,bshc->bhps", queries, keys_all, preferred_element_type=FULL_TYPE
    ) * head_dim ** (-0.5)
    masked = jnp.where(allowed, scores, -1e30)
    row_max = jnp.max(masked, axis=-1, keepdims=True)
    exponent = jnp.exp(masked - row_max)
    row_total = jnp.sum(exponent, axis=-1, keepdims=True)
    attn_probs = exponent / row_total
    log_total = row_max + jnp.log(row_total)
    attended = jnp.einsum(
        "bhps,bshc->bphc",
        attn_probs.astype(HALF_TYPE),
        values_all,
        preferred_element_type=FULL_TYPE,
    )
    live_rows = (positions[None, :] < lengths[:, None]).astype(FULL_TYPE)[:, :, None, None]
    mixed_out = (attended * live_rows).astype(HALF_TYPE)
    out_choice = one_hot_sum(out_ids, expert_ids)
    out_sig = jax.nn.sigmoid(
        matmul(normed_low, sel_out).reshape(seq_count, row_count, head_count, value_experts)
    )
    out_gate = out_sig * out_choice
    expert_out = jnp.einsum(
        "bphc,hcf->bphf", mixed_out, w_out, preferred_element_type=FULL_TYPE
    ).reshape(seq_count, row_count, head_count, value_experts, model_width)
    after_attn = inputs + jnp.sum(out_gate[..., None] * expert_out, axis=(2, 3))
    normed_two, normal_two, scale_two = norm_parts(after_attn, gain_two, bias_two)
    return dict(
        positions=positions,
        normal_one=normal_one,
        scale_one=scale_one,
        normed_low=normed_low,
        queries=queries,
        keys_all=keys_all,
        values_all=values_all,
        allowed=allowed,
        log_total=log_total,
        live_rows=live_rows,
        mixed_out=mixed_out,
        value_choice=value_choice,
        value_sig=value_sig,
        value_gate=value_gate,
        projected=projected,
        out_choice=out_choice,
        out_sig=out_sig,
        out_gate=out_gate,
        expert_out=expert_out,
        after_attn=after_attn,
        normed_two=normed_two,
        normal_two=normal_two,
        scale_two=scale_two,
    )


def expert_forward(after_attn, normed_two, mlp_ids, w_select, w_up):
    rows_all, normed_all = (
        lax.all_gather(for_sending(after_attn.astype(HALF_TYPE)), "wide", axis=1, tiled=True),
        lax.all_gather(for_sending(normed_two.astype(HALF_TYPE)), "wide", axis=1, tiled=True),
    )
    local_count = w_select.shape[1]
    hidden = w_up.shape[1] // local_count
    seq_count, span = (rows_all.shape[0], rows_all.shape[1])
    owned_ids = lax.axis_index("wide") * local_count + jnp.arange(local_count, dtype=jnp.int32)
    chosen = one_hot_sum(mlp_ids, owned_ids)
    sigmoid_gate = jax.nn.sigmoid(matmul(normed_all, w_select))
    mlp_gate = sigmoid_gate * chosen
    pre_act = matmul(rows_all, w_up)
    activated = jax.nn.gelu(pre_act).reshape(seq_count, span, local_count, hidden)
    inner_low = (
        (activated * mlp_gate[..., None])
        .reshape(seq_count, span, local_count * hidden)
        .astype(HALF_TYPE)
    )
    return dict(
        rows_all=rows_all,
        normed_all=normed_all,
        chosen=chosen,
        sigmoid_gate=sigmoid_gate,
        mlp_gate=mlp_gate,
        pre_act=pre_act,
        activated=activated,
        inner_low=inner_low,
    )


def per_device(
    tokens,
    lengths,
    value_ids,
    out_ids,
    mlp_ids,
    w_query,
    w_key,
    w_value,
    w_out,
    sel_value,
    sel_out,
    gain_one,
    bias_one,
    gain_two,
    bias_two,
    w_select,
    w_up,
    w_down,
    cotangent,
):
    seq_count, row_count, model_width = tokens.shape
    head_count = w_out.shape[0]
    head_dim = w_out.shape[1]
    value_experts = sel_value.shape[1] // head_count
    saved = attend_forward(
        tokens,
        lengths,
        value_ids,
        out_ids,
        w_query,
        w_key,
        w_value,
        w_out,
        sel_value,
        sel_out,
        gain_one,
        bias_one,
        gain_two,
        bias_two,
    )
    expert_state = expert_forward(saved["after_attn"], saved["normed_two"], mlp_ids, w_select, w_up)
    branch_part = matmul(expert_state["inner_low"], w_down)
    branch_sum = lax.psum_scatter(
        branch_part.astype(jnp.bfloat16), "wide", scatter_dimension=1, tiled=True
    ).astype(jnp.float32)
    output = (saved["after_attn"] + branch_sum).astype(HALF_TYPE)
    saved = attend_forward(
        tokens,
        lengths,
        value_ids,
        out_ids,
        w_query,
        w_key,
        w_value,
        w_out,
        sel_value,
        sel_out,
        gain_one,
        bias_one,
        gain_two,
        bias_two,
    )
    expert_state = expert_forward(saved["after_attn"], saved["normed_two"], mlp_ids, w_select, w_up)
    cot_all = lax.all_gather(cotangent, "wide", axis=1, tiled=True)
    grad_down = contract_rows(expert_state["inner_low"], cot_all)
    d_inner = times_transpose(cot_all, w_down)
    activated = expert_state["activated"]
    d_inner_four = d_inner.reshape(activated.shape)
    d_mlp_gate = jnp.sum(d_inner_four * activated, axis=-1)
    mlp_gate = expert_state["mlp_gate"]
    gated_grad = (d_inner_four * mlp_gate[..., None]).reshape(expert_state["pre_act"].shape)
    unused_value, gelu_pull = jax.vjp(jax.nn.gelu, expert_state["pre_act"])
    d_pre = gelu_pull(gated_grad)[0].astype(HALF_TYPE)
    sigmoid_gate = expert_state["sigmoid_gate"]
    d_logit = (d_mlp_gate * expert_state["chosen"] * sigmoid_gate * (1.0 - sigmoid_gate)).astype(
        HALF_TYPE
    )
    grad_up = contract_rows(expert_state["rows_all"], d_pre)
    grad_select = contract_rows(expert_state["normed_all"], d_logit)
    row_part = times_transpose(d_pre, w_up)
    norm_part = times_transpose(d_logit, w_select)
    row_grad, norm_grad = (
        lax.psum_scatter(row_part, "wide", scatter_dimension=1, tiled=True),
        lax.psum_scatter(norm_part, "wide", scatter_dimension=1, tiled=True),
    )
    grad_gain_two = jnp.sum(norm_grad * saved["normal_two"], axis=(0, 1))
    grad_bias_two = jnp.sum(norm_grad, axis=(0, 1))
    d_after = (
        cotangent.astype(FULL_TYPE)
        + row_grad
        + norm_back(norm_grad, saved["normal_two"], saved["scale_two"], gain_two)
    )
    out_gate = saved["out_gate"]
    d_expert = (out_gate[..., None] * d_after[:, :, None, None, :]).astype(HALF_TYPE)
    d_out_gate = jnp.sum(saved["expert_out"] * d_after[:, :, None, None, :], axis=-1)
    d_expert_flat = d_expert.reshape(seq_count, row_count, head_count, value_experts * model_width)
    grad_out = jnp.einsum(
        "bphc,bphf->hcf", saved["mixed_out"], d_expert_flat, preferred_element_type=FULL_TYPE
    )
    d_mixed = jnp.einsum("bphf,hcf->bphc", d_expert_flat, w_out, preferred_element_type=FULL_TYPE)
    d_attended = (d_mixed * saved["live_rows"]).astype(HALF_TYPE)
    out_sig = saved["out_sig"]
    d_out_logit = (
        (d_out_gate * saved["out_choice"] * out_sig * (1.0 - out_sig))
        .astype(HALF_TYPE)
        .reshape(seq_count, row_count, head_count * value_experts)
    )
    queries = saved["queries"]
    keys_all = saved["keys_all"]
    values_all = saved["values_all"]
    score_scale = head_dim ** (-0.5)
    scores = (
        jnp.einsum("bphc,bshc->bhps", queries, keys_all, preferred_element_type=FULL_TYPE)
        * score_scale
    )
    attn_probs = jnp.where(saved["allowed"], jnp.exp(scores - saved["log_total"]), 0.0)
    d_values_part = jnp.einsum(
        "bhps,bphc->bshc",
        attn_probs.astype(HALF_TYPE),
        d_attended,
        preferred_element_type=FULL_TYPE,
    )
    d_probs = jnp.einsum(
        "bphc,bshc->bhps", d_attended, values_all, preferred_element_type=FULL_TYPE
    )
    row_inner = jnp.sum(attn_probs * d_probs, axis=-1, keepdims=True)
    d_scores = (attn_probs * (d_probs - row_inner)).astype(HALF_TYPE)
    d_queries = (
        jnp.einsum("bhps,bshc->bphc", d_scores, keys_all, preferred_element_type=FULL_TYPE)
        * score_scale
    )
    d_keys_part = (
        jnp.einsum("bhps,bphc->bshc", d_scores, queries, preferred_element_type=FULL_TYPE)
        * score_scale
    )
    d_keys, d_values = (
        lax.psum_scatter(
            d_keys_part.astype(jnp.bfloat16), "wide", scatter_dimension=1, tiled=True
        ).astype(jnp.float32),
        lax.psum_scatter(
            d_values_part.astype(jnp.bfloat16), "wide", scatter_dimension=1, tiled=True
        ).astype(jnp.float32),
    )
    positions = saved["positions"]
    d_query_pre = (
        rotate(d_queries, positions, -1.0)
        .astype(HALF_TYPE)
        .reshape(seq_count, row_count, head_count * head_dim)
    )
    d_key_pre = (
        rotate(d_keys, positions, -1.0)
        .astype(HALF_TYPE)
        .reshape(seq_count, row_count, head_count * head_dim)
    )
    d_projected = (
        (saved["value_gate"][..., None] * d_values[:, :, :, None, :])
        .astype(HALF_TYPE)
        .reshape(seq_count, row_count, head_count * value_experts * head_dim)
    )
    d_value_gate = jnp.sum(saved["projected"] * d_values[:, :, :, None, :], axis=-1)
    value_sig = saved["value_sig"]
    d_value_logit = (
        (d_value_gate * saved["value_choice"] * value_sig * (1.0 - value_sig))
        .astype(HALF_TYPE)
        .reshape(seq_count, row_count, head_count * value_experts)
    )
    normed_low = saved["normed_low"]
    grad_query = contract_rows(normed_low, d_query_pre)
    grad_key = contract_rows(normed_low, d_key_pre)
    grad_sel_value = contract_rows(normed_low, d_value_logit)
    grad_sel_out = contract_rows(normed_low, d_out_logit)
    grad_value = contract_rows(tokens, d_projected)
    d_normed = (
        times_transpose(d_query_pre, w_query)
        + times_transpose(d_key_pre, w_key)
        + times_transpose(d_value_logit, sel_value)
        + times_transpose(d_out_logit, sel_out)
    )
    grad_gain_one = jnp.sum(d_normed * saved["normal_one"], axis=(0, 1))
    grad_bias_one = jnp.sum(d_normed, axis=(0, 1))
    grad_tokens = (
        d_after
        + times_transpose(d_projected, w_value)
        + norm_back(d_normed, saved["normal_one"], saved["scale_one"], gain_one)
    ).astype(HALF_TYPE)
    (
        grad_query,
        grad_key,
        grad_value,
        grad_out,
        grad_sel_value,
        grad_sel_out,
        grad_gain_one,
        grad_bias_one,
        grad_gain_two,
        grad_bias_two,
    ) = lax.psum(
        (
            grad_query,
            grad_key,
            grad_value,
            grad_out,
            grad_sel_value,
            grad_sel_out,
            grad_gain_one,
            grad_bias_one,
            grad_gain_two,
            grad_bias_two,
        ),
        ("wide", "narrow"),
    )
    grad_select, grad_up, grad_down = (
        lax.psum(grad_select.astype(jnp.bfloat16), "narrow").astype(jnp.float32),
        lax.psum(grad_up.astype(jnp.bfloat16), "narrow").astype(jnp.float32),
        lax.psum(grad_down.astype(jnp.bfloat16), "narrow").astype(jnp.float32),
    )
    return (
        output,
        grad_tokens,
        grad_query,
        grad_key,
        grad_value,
        grad_out,
        grad_sel_value,
        grad_sel_out,
        grad_gain_one,
        grad_bias_one,
        grad_gain_two,
        grad_bias_two,
        grad_select,
        grad_up,
        grad_down,
    )


SELV = 72
SELO = 92
LANES = 128


def call(
    kernel, out_shape, *args, grid=None, in_specs=None, out_specs=None, scratch=(), flops=0, limit=56, prefetch=0, aliases=None
):
    moved = sum(a.size * a.dtype.itemsize for a in jax.tree.leaves((args, out_shape)))
    extra = {}
    if prefetch:
        extra["grid_spec"] = pltpu.PrefetchScalarGridSpec(
            num_scalar_prefetch=prefetch, grid=grid, in_specs=in_specs, out_specs=out_specs, scratch_shapes=list(scratch)
        )
    else:
        extra["scratch_shapes"] = list(scratch)
        if grid is not None:
            extra["grid"] = grid
        if in_specs is not None:
            extra["in_specs"] = in_specs
        if out_specs is not None:
            extra["out_specs"] = out_specs
    return pl.pallas_call(
        kernel,
        out_shape=out_shape,
        input_output_aliases=aliases or {},
        compiler_params=pltpu.CompilerParams(vmem_limit_bytes=limit * 1024 * 1024),
        cost_estimate=pl.CostEstimate(flops=int(flops), bytes_accessed=int(moved), transcendentals=0),
        **extra,
    )(*args)


def full(shape):
    rank = len(shape)
    return pl.BlockSpec(tuple(shape), lambda *s: (0,) * rank)


def shaped(shape, dtype=HALF_TYPE):
    return jax.ShapeDtypeStruct(tuple(shape), dtype)


def nn(a, b):
    return lax.dot_general(a, b, (((1,), (0,)), ((), ())), preferred_element_type=FULL_TYPE)


def nt(a, b):
    return lax.dot_general(a, b, (((1,), (1,)), ((), ())), preferred_element_type=FULL_TYPE)


def tn(a, b):
    return lax.dot_general(a, b, (((0,), (0,)), ((), ())), preferred_element_type=FULL_TYPE)


def layer_stats(v):
    centred = v - jnp.mean(v, axis=-1, keepdims=True)
    inv = lax.rsqrt(jnp.mean(centred * centred, axis=-1, keepdims=True) + EPSILON)
    return centred * inv, inv


def turned(v, cos, sin):
    return v * cos + pltpu.roll(v, v.shape[-1] // 2, axis=v.ndim - 1) * sin


def lane_ids(shape, dim):
    return lax.broadcasted_iota(jnp.int32, shape, dim)


def pre_kernel(tok, gain, bias, wq, wk, wv, sel, vid, oid, cos, sin, select, qkv, proj, gate):
    heads = qkv.shape[0]
    experts = wv.shape[1] // (heads * LANES)
    low = tok[0]
    rows = low.shape[0]
    normal, _ = layer_stats(low.astype(FULL_TYPE))
    normed = (normal * gain[...] + bias[...]).astype(HALF_TYPE)
    for part, weight in ((0, wq), (1, wk)):
        pre = nn(normed, weight[...])
        for h in range(heads):
            head = turned(pre[:, h * LANES:(h + 1) * LANES], cos[...], sin[...])
            qkv[h, part * rows:(part + 1) * rows] = head.astype(HALF_TYPE)
    lanes = lane_ids((rows, LANES), 1)
    chosen = jnp.zeros((rows, LANES), FULL_TYPE)
    tops = vid.shape[2] // heads
    for h in range(heads):
        for k in range(tops):
            j = h * tops + k
            chosen += (lanes == vid[0, :, j:j + 1] + (SELV + experts * h)).astype(FULL_TYPE)
            chosen += (lanes == oid[0, :, j:j + 1] + (SELO + experts * h)).astype(FULL_TYPE)
    gates = jax.nn.sigmoid(nn(normed, sel[...])) * chosen
    gate[0] = gates
    gates_low = gates.astype(HALF_TYPE)
    for h in range(heads):
        at = h * experts * LANES
        block = nn(low, wv[:, at:at + experts * LANES])
        proj[0, :, at:at + experts * LANES] = block.astype(HALF_TYPE)
        total = None
        for e in range(experts):
            col = SELV + h * experts + e
            term = gates[:, col:col + 1] * block[:, e * LANES:(e + 1) * LANES]
            total = term if total is None else total + term
        qkv[h, 2 * rows:3 * rows] = total.astype(HALF_TYPE)
        first = SELV + h * experts
        row_id = lane_ids((8, LANES), 0)
        spot = (lane_ids((8, LANES), 1) == row_id + first) & (row_id < experts)
        turned_gates = nt(spot.astype(FULL_TYPE).astype(HALF_TYPE), gates_low)
        tail = jnp.concatenate([turned_gates[:, i * LANES:(i + 1) * LANES] for i in range(rows // LANES)], axis=0)
        last = 3 * rows + select.shape[0]
        qkv[h, 3 * rows:last] = select[...]
        qkv[h, last:last + tail.shape[0]] = tail.astype(HALF_TYPE)


def limits_of(i, rows, length):
    position = i * rows + lane_ids((1, rows), 1)
    return jnp.minimum(position + 1, length), position


def parts_of(ref, first, last, part, rows):
    block = ref[first:last, part * rows:(part + 1) * rows]
    return block.reshape((last - first) * rows, block.shape[2])


def attend_kernel(length, qkv, mixed, out_t, lse):
    blocks, rows, width = mixed.shape
    scale = width ** (-0.5)
    values_t = jnp.transpose(parts_of(qkv, 0, blocks, 2, rows).astype(FULL_TYPE)).astype(HALF_TYPE)
    for i in range(blocks):
        n = (i + 1) * rows
        keys = parts_of(qkv, 0, i + 1, 1, rows)
        limit, position = limits_of(i, rows, length[0])
        scores = nt(keys, qkv[i, 0:rows]) * scale
        scores = jnp.where(lane_ids((n, rows), 0) < limit, scores, -1e30)
        top = jnp.max(scores, axis=0, keepdims=True)
        weights = jnp.exp(scores - top)
        total = jnp.sum(weights, axis=0, keepdims=True)
        attended = nn(values_t[:, :n], weights.astype(HALF_TYPE)) / total
        out_t[:, i * rows:(i + 1) * rows] = attended
        lse[:, i * rows:(i + 1) * rows] = top + jnp.log(total)
        live = (position < length[0]).astype(FULL_TYPE)
        mixed[i] = jnp.transpose(attended * live).astype(HALF_TYPE)


def attend_back_kernel(length, qkv, d_out, out_t, lse, cos, sin, d_qkv, d_keys, d_values):
    blocks, rows, width = d_out.shape
    scale = width ** (-0.5)
    keys_t = jnp.transpose(parts_of(qkv, 0, blocks, 1, rows).astype(FULL_TYPE)).astype(HALF_TYPE)
    d_keys[...] = jnp.zeros_like(d_keys)
    d_values[...] = jnp.zeros_like(d_values)
    for i in range(blocks):
        n = (i + 1) * rows
        here = slice(i * rows, (i + 1) * rows)
        limit, _ = limits_of(i, rows, length[0])
        query = qkv[i, 0:rows]
        d_att = d_out[i]
        delta = jnp.sum(jnp.transpose(d_att.astype(FULL_TYPE)) * out_t[:, here], axis=0, keepdims=True)
        scores = nt(parts_of(qkv, 0, i + 1, 1, rows), query) * scale
        probs = jnp.where(lane_ids((n, rows), 0) < limit, jnp.exp(scores - lse[:, here]), 0.0)
        d_probs = nt(parts_of(qkv, 0, i + 1, 2, rows), d_att)
        d_scores = (probs * (d_probs - delta)).astype(HALF_TYPE)
        d_values[0:n, :] += nn(probs.astype(HALF_TYPE), d_att)
        d_keys[0:n, :] += nn(d_scores, query)
        d_query = jnp.transpose(nn(keys_t[:, :n], d_scores)) * scale
        d_qkv[i, 0:rows] = turned(d_query, cos[here, :], -sin[here, :]).astype(HALF_TYPE)
    for i in range(blocks):
        here = slice(i * rows, (i + 1) * rows)
        d_qkv[i, rows:2 * rows] = turned(d_keys[here, :] * scale, cos[here, :], -sin[here, :]).astype(HALF_TYPE)
        d_qkv[i, 2 * rows:3 * rows] = d_values[here, :].astype(HALF_TYPE)


def gated(mixed, gate, hp, e, experts):
    parts = []
    for h in (2 * hp, 2 * hp + 1):
        col = SELO + h * experts + e
        parts.append((gate[:, col:col + 1] * mixed[h].astype(FULL_TYPE)).astype(HALF_TYPE))
    return jnp.concatenate(parts, axis=1)


def out_block(w_out, hp, e, width):
    block = w_out[2 * hp:2 * hp + 2, :, e * width:(e + 1) * width]
    return block.reshape(2 * block.shape[1], width)


def post_kernel(mixed, gate, w_out, tok, gain, bias, columns, ids, places, after, gates, sent, select):
    width = tok.shape[2]
    heads = w_out.shape[0]
    experts = w_out.shape[2] // width
    row_count = tok.shape[1]
    total = tok[0].astype(FULL_TYPE)
    gate_here = gate[0]
    mixed_here = mixed[...]
    for hp in range(heads // 2):
        for e in range(experts):
            total += nn(gated(mixed_here, gate_here, hp, e, experts), out_block(w_out, hp, e, width))
    after[...] = total
    sent[0, 0:row_count] = total.astype(HALF_TYPE)
    normal, _ = layer_stats(total)
    normed = (normal * gain[...] + bias[...]).astype(HALF_TYPE)
    every = columns[...].astype(FULL_TYPE)
    count = every.shape[1]
    each = count // 8
    w_sel = jnp.concatenate(
        [every[:, j * each:(j + 1) * each].reshape(count, LANES) for j in range(8)], axis=1
    ).astype(HALF_TYPE)
    select[...] = w_sel
    row_id = lane_ids((count, row_count), 0)
    chosen = jnp.zeros((count, row_count), FULL_TYPE)
    for k in range(ids.shape[1]):
        chosen += (row_id == ids[0, k:k + 1, :]).astype(FULL_TYPE)
    values = jax.nn.sigmoid(nt(w_sel, normed)) * chosen
    gates[...] = values
    moved = nn(places[...], values.astype(HALF_TYPE)).astype(HALF_TYPE)
    quarter = count // 4
    for i in range(4):
        sent[0, row_count:row_count + quarter, i * row_count:(i + 1) * row_count] = moved[i * quarter:(i + 1) * quarter]


def weights_kernel(spots, up, down, out):
    out[0, 0] = up[...]
    out[0, 1] = jnp.transpose(down[...].astype(FULL_TYPE)).astype(HALF_TYPE)


def expand(count, cols, first):
    rows = lane_ids((count, cols), 0)
    cut = lane_ids((count, cols), 1)
    hit = None
    for i in range(cols // LANES):
        inside = (cut >= i * LANES) & (cut < (i + 1) * LANES) & (rows == first + i)
        hit = inside if hit is None else hit | inside
    return hit.astype(FULL_TYPE).astype(HALF_TYPE)


def experts_kernel(kind, halves, *refs):
    rows_in, cot, first = refs[:halves], refs[halves], refs[halves + 1]
    others = refs[halves + 2:halves + 8]
    back, inner, d_pre = refs[halves + 8:]
    seqs, tall, width = back.shape
    row_count = width // 4
    cols = first.shape[3]
    quarter = tall - row_count
    picked = [rows_in[0][s] if halves == 1 else rows_in[s][...] for s in range(seqs)]
    low = jnp.concatenate([block[0:row_count] for block in picked], axis=0)
    gates = jnp.concatenate(
        [block[row_count:tall, kind * row_count:(kind + 1) * row_count] for block in picked], axis=1
    )
    cot_low = cot[...]
    row_total = gate_total = None
    weight = lambda p, u: first[p, u] if p < 2 else others[p - 2][u]
    root, cube = 0.7978845608028654, 0.044715
    for p in range(8):
        spread = expand(quarter, cols, p * (cols // LANES))
        gate_wide = tn(gates, spread)
        pre = nn(low, weight(p, 0))
        d_in = nn(cot_low, weight(p, 1))
        square = pre * pre
        tanh = jnp.tanh(pre * (root + (root * cube) * square))
        half = 0.5 + 0.5 * tanh
        act = pre * half
        slope = half + act * (1.0 - tanh) * (root + (3 * root * cube) * square)
        d_pre[p] = (slope * gate_wide * d_in).astype(HALF_TYPE)
        inner[p] = (act * gate_wide).astype(HALF_TYPE)
        g = nt(spread, (d_in * act).astype(HALF_TYPE))
        gate_total = g if p == 0 else gate_total + g
    for p in range(8):
        r = nt(d_pre[p], weight(p, 0))
        row_total = r if p == 0 else row_total + r
    for s in range(seqs):
        here = slice(s * row_count, (s + 1) * row_count)
        back[s, 0:row_count] = row_total[here].astype(HALF_TYPE)
        back[s, row_count:tall] = jnp.zeros((quarter, width), HALF_TYPE)
        back[s, row_count:tall, 0:row_count] = gate_total[:, here].astype(HALF_TYPE)


def branch_kernel(*refs):
    inners, first, others, outs = refs[0:4], refs[4], refs[5:11], refs[11:15]
    downs = [first[0, 1], first[1, 1]] + [ref[1] for ref in others]
    for i in range(4):
        total = None
        for p in range(8):
            term = nt(inners[i][p], downs[p])
            total = term if p == 0 else total + term
        outs[i][...] = total.astype(HALF_TYPE)


def expert_grads_kernel(*refs):
    rows, cots, pres, inners = refs[0:5], refs[5:9], refs[9:13], refs[13:17]
    outs = refs[17:21]
    step = pl.program_id(0)
    row_count = pres[0].shape[1] // 2
    up = down = None
    for i in range(4):
        for s in range(2):
            block = rows[i][s, 0:row_count] if i < 3 else rows[3 + s][0:row_count]
            term = tn(block, pres[i][0, s * row_count:(s + 1) * row_count])
            up = term if up is None else up + term
        term = tn(cots[i][...], inners[i][0])
        down = term if down is None else down + term
    results = (up.astype(HALF_TYPE), down.astype(HALF_TYPE))
    for j in range(4):

        @pl.when(step // 2 == j)
        def _(j=j):
            for u in range(2):
                outs[j][0, u] = results[u]


def mid_kernel(length, r0, r1, r2, r3, cot, after, gates, gain, bias, w_sel, places, w_out, gate, mixed,
               d_after, d_att, d_gate_out, small, acc):
    step = pl.program_id(0)
    width = cot.shape[2]
    heads = w_out.shape[0]
    experts = w_out.shape[2] // width
    row_count = cot.shape[1]
    tall = r0.shape[1]
    d_rel = jnp.concatenate([r[0, row_count:tall, 0:row_count] for r in (r0, r1, r2, r3)], axis=0)
    d_gate = tn(places[...], d_rel)
    values = gates[...]
    d_logit = (d_gate * values * (1.0 - values)).astype(HALF_TYPE)
    normal, inv = layer_stats(after[...])
    normed = (normal * gain[...] + bias[...]).astype(HALF_TYPE)
    d_normed = tn(d_logit, w_sel[...])
    sel_part = nn(d_logit, normed)
    gain_part = jnp.sum(d_normed * normal, axis=0, keepdims=True)
    bias_part = jnp.sum(d_normed, axis=0, keepdims=True)
    count = sel_part.shape[0]

    @pl.when(step == 0)
    def _():
        acc[...] = jnp.zeros_like(acc)

    acc[0:count, :] += sel_part
    acc[count:count + 1, :] += gain_part
    acc[count + 1:count + 2, :] += bias_part
    d_row = sum(r[0, 0:row_count].astype(FULL_TYPE) for r in (r0, r1, r2, r3))
    total = cot[0].astype(FULL_TYPE) + d_row + norm_back(d_normed, normal, inv, gain[...])
    d_after[...] = total
    total_low = total.astype(HALF_TYPE)
    mixed_here = mixed[...]
    gate_here = gate[0]
    lanes = lane_ids((2 * LANES, LANES), 1)
    second = (lane_ids((2 * LANES, LANES), 0) >= LANES).astype(jnp.int32)
    d_gates = jnp.zeros((row_count, LANES), FULL_TYPE)
    for hp in range(heads // 2):
        both = jnp.concatenate([mixed_here[2 * hp], mixed_here[2 * hp + 1]], axis=1).astype(FULL_TYPE)
        sums = [None, None]
        for e in range(experts):
            d_mixed = nt(total_low, out_block(w_out, hp, e, width))
            hit = (lanes == SELO + 2 * hp * experts + e + second * experts).astype(FULL_TYPE).astype(HALF_TYPE)
            d_gates += nn((both * d_mixed).astype(HALF_TYPE), hit)
            for i in range(2):
                col = SELO + (2 * hp + i) * experts + e
                term = gate_here[:, col:col + 1] * d_mixed[:, i * LANES:(i + 1) * LANES]
                sums[i] = term if e == 0 else sums[i] + term
        for i in range(2):
            position = length[1] + lane_ids((row_count, 1), 0)
            live = (position < length[2 + step]).astype(FULL_TYPE)
            d_att[2 * hp + i] = (sums[i] * live).astype(HALF_TYPE)
    d_gate_out[0] = d_gates

    @pl.when(step == pl.num_programs(0) - 1)
    def _():
        spots = (lane_ids((LANES, LANES), 0) == lanes[0:LANES]).astype(FULL_TYPE).astype(HALF_TYPE)
        small[...] = tn(acc[...].astype(HALF_TYPE), spots)


def out_grad_kernel(mixed, gate, d_after, out):
    heads, experts = 4, out.shape[1] // d_after.shape[1]
    width = d_after.shape[1]
    seqs, row_count = gate.shape[0], gate.shape[1]
    low = d_after[...].astype(HALF_TYPE)
    for hp in range(heads // 2):
        for e in range(experts):
            total = None
            for s in range(seqs):
                left = gated([mixed[s * heads + h] for h in range(heads)], gate[s], hp, e, experts)
                term = tn(left, low[s * row_count:(s + 1) * row_count, :])
                total = term if total is None else total + term
            out[2 * hp * LANES:(2 * hp + 2) * LANES, e * width:(e + 1) * width] = total.astype(HALF_TYPE)


def last_kernel(d_qkv, tok, gain, bias, wq, wk, wv, sel, proj, gate, d_gate_out, small, d_after,
                out, sums, d_proj, acc):
    step = pl.program_id(0)
    row_count, width = tok.shape[1], tok.shape[2]
    heads = d_qkv.shape[0]
    experts = proj.shape[2] // (heads * LANES)
    lanes = lane_ids((LANES, LANES), 1)
    low = tok[0]
    normal, inv = layer_stats(low.astype(FULL_TYPE))
    normed = (normal * gain[...] + bias[...]).astype(HALF_TYPE)
    d_gates = d_gate_out[0]
    gate_here = gate[0]
    d_query = jnp.concatenate([d_qkv[h, 0:row_count] for h in range(heads)], axis=1)
    d_key = jnp.concatenate([d_qkv[h, row_count:2 * row_count] for h in range(heads)], axis=1)
    for h in range(heads):
        d_value = d_qkv[h, 2 * row_count:3 * row_count].astype(FULL_TYPE)
        for e in range(experts):
            col = SELV + h * experts + e
            at = (h * experts + e) * LANES
            d_proj[:, at:at + LANES] = (gate_here[:, col:col + 1] * d_value).astype(HALF_TYPE)
            hit = (lanes == col).astype(FULL_TYPE).astype(HALF_TYPE)
            product = (proj[0, :, at:at + LANES].astype(FULL_TYPE) * d_value).astype(HALF_TYPE)
            d_gates += nn(product, hit)
    d_logit = (d_gates * gate_here * (1.0 - gate_here)).astype(HALF_TYPE)
    d_normed = nt(d_query, wq[...]) + nt(d_key, wk[...]) + nt(d_logit, sel[...])
    total = d_after[...] + norm_back(d_normed, normal, inv, gain[...]) + nt(d_proj[...], wv[...])
    out[...] = total.astype(HALF_TYPE)
    gain_sum = jnp.sum(d_normed * normal, axis=0, keepdims=True)
    bias_sum = jnp.sum(d_normed, axis=0, keepdims=True)
    rows = jnp.concatenate([gain_sum, bias_sum, jnp.zeros((14, width), FULL_TYPE)], axis=0).astype(HALF_TYPE)
    spot = (lane_ids((16, LANES), 1) == lane_ids((16, LANES), 0) + 66) & (lane_ids((16, LANES), 0) < 2)
    spread = tn(rows, spot.astype(FULL_TYPE).astype(HALF_TYPE))
    part = tn(normed, d_logit) + spread

    @pl.when(step == 0)
    def _():
        acc[...] = small[...] + part

    @pl.when(step > 0)
    def _():
        acc[...] += part

    sums[...] = acc[...].astype(HALF_TYPE)


def turn_kernel(near, far, gain, bias, tok_t, norm_t):
    step = pl.program_id(0)

    def turn(low):
        normal, _ = layer_stats(low.astype(FULL_TYPE))
        tok_t[0] = jnp.transpose(low.astype(FULL_TYPE)).astype(HALF_TYPE)
        normed = (normal * gain[...] + bias[...]).astype(HALF_TYPE)
        norm_t[0] = jnp.transpose(normed.astype(FULL_TYPE)).astype(HALF_TYPE)

    @pl.when(step < 4)
    def _():
        turn(near[0])

    @pl.when(step >= 4)
    def _():
        turn(far[0])


def head_grads_kernel(spot, tok_t, norm_t, d_qkv, gate, out, acc):
    step = pl.program_id(0)
    rows = tok_t.shape[2]
    experts = out.shape[1] // LANES - 2
    both = jnp.concatenate([d_qkv[0, 0:rows], d_qkv[0, rows:2 * rows]], axis=1)
    wide = experts * LANES
    spread = expand(8, wide, 0)
    tail = gate[0]
    gates = jnp.concatenate([tn(tail[i * 8:(i + 1) * 8], spread) for i in range(rows // LANES)], axis=0)
    d_value = d_qkv[0, 2 * rows:3 * rows].astype(FULL_TYPE)
    d_proj = (gates * jnp.concatenate([d_value] * experts, axis=1)).astype(HALF_TYPE)
    first = nn(norm_t[0], both)
    second = nn(tok_t[0], d_proj)

    @pl.when(step == 0)
    def _():
        acc[:, 0:2 * LANES] = first
        acc[:, 2 * LANES:] = second

    @pl.when(step > 0)
    def _():
        acc[:, 0:2 * LANES] += first
        acc[:, 2 * LANES:] += second

    @pl.when(step == pl.num_programs(0) - 1)
    def _():
        out[...] = acc[...].astype(HALF_TYPE)


def place_heads_kernel(bits, *refs):
    sources = refs[:4]
    query, key, value = refs[-3:]
    step = pl.program_id(0)
    part = step // 4
    x, low = bits[1], bits[3]
    wide = value.shape[1] // 4

    def put(block, head):
        at = pl.multiple_of(head * LANES, LANES)
        query[:, pl.ds(at, LANES)] = block[:, 0:LANES].astype(FULL_TYPE)
        key[:, pl.ds(at, LANES)] = block[:, LANES:2 * LANES].astype(FULL_TYPE)
        value[:, pl.ds(pl.multiple_of(head * wide, LANES), wide)] = block[:, 2 * LANES:].astype(FULL_TYPE)

    for y in range(2):

        @pl.when((part == 0) & ((step // 2) % 2 == y))
        def _(y=y):
            for i in range(2):
                for b in range(2):
                    put(sources[y][i, b, 0], (low ^ b) * 2 + (x ^ i))

    @pl.when(part == 1)
    def _():
        for i in range(2):
            for b in range(2):
                put(sources[2 + i][0, b, 0], (low ^ b) * 2 + (x ^ i))


def place_out_kernel(spot, mine, peer, out):
    step = pl.program_id(0)

    @pl.when(step < 2)
    def _():
        out[0] = mine[...].astype(FULL_TYPE)

    @pl.when(step >= 2)
    def _():
        out[0] = peer[...].astype(FULL_TYPE)


def place_small_kernel(first, small, select, value, out, rows):
    low = small[...]

    def rows_of(count, start):
        hit = lane_ids((count, LANES), 1) == lane_ids((count, LANES), 0) + start
        return nt(hit.astype(FULL_TYPE).astype(HALF_TYPE), low)

    select[...] = rows_of(select.shape[0], first[0])
    value[...] = rows_of(value.shape[0], SELV)
    out[...] = rows_of(out.shape[0], SELO)
    spots = (lane_ids((8, LANES), 1) == lane_ids((8, LANES), 0) + 64) & (lane_ids((8, LANES), 0) < 4)
    rows[...] = nt(spots.astype(FULL_TYPE).astype(HALF_TYPE), low)


def place_experts_kernel(spots, *refs):
    up, down = refs[4:]
    step = pl.program_id(0)
    for i in range(4):

        @pl.when(step == i)
        def _(i=i):
            up[...] = refs[i][0].astype(FULL_TYPE)
            down[...] = jnp.transpose(refs[i][1].astype(FULL_TYPE))


def output_kernel(after, b0, b1, b2, b3, out):
    out[...] = (
        after[...] + b0[...].astype(FULL_TYPE) + b1[...].astype(FULL_TYPE)
        + b2[...].astype(FULL_TYPE) + b3[...].astype(FULL_TYPE)
    ).astype(HALF_TYPE)


class Place:
    def __init__(self):
        self.wide = lax.axis_index("wide")
        self.narrow = lax.axis_index("narrow")
        self.z, self.x = self.wide // 2, self.wide % 2
        self.y, self.c = self.narrow // 2, self.narrow % 2
        self.high, self.low = self.z // 2, self.z % 2

    @staticmethod
    def pairs(move):
        every = []
        for z in range(4):
            for x in range(2):
                for y in range(2):
                    for c in range(2):
                        tz, tx, ty, tc = move(z, x, y, c)
                        every.append(((z * 2 + x) * 4 + y * 2 + c, (tz * 2 + tx) * 4 + ty * 2 + tc))
        return every

    def send(self, value, move):
        return lax.ppermute(value, ("wide", "narrow"), self.pairs(move))

    def swap_x(self, value):
        return self.send(value, lambda z, x, y, c: (z, 1 - x, y, c))

    def swap_y(self, value):
        return self.send(value, lambda z, x, y, c: (z, x, 1 - y, c))

    def swap_xy(self, value):
        return self.send(value, lambda z, x, y, c: (z, 1 - x, 1 - y, c))

    def swap_c(self, value):
        return self.send(value, lambda z, x, y, c: (z, x, y, 1 - c))

    def swap_low(self, value):
        return self.send(value, lambda z, x, y, c: (z ^ 1, x, y, c))

    def swap_high(self, value):
        return self.send(value, lambda z, x, y, c: (z ^ 2, x, y, c))


def pick(array, index):
    return lax.dynamic_index_in_dim(array, index, 0, keepdims=False)


def add(*terms):
    total = terms[0].astype(FULL_TYPE)
    for term in terms[1:]:
        total = total + term.astype(FULL_TYPE)
    return total.astype(HALF_TYPE)


def in_order(bit, mine, other):
    return jnp.stack([jnp.where(bit == 0, mine, other), jnp.where(bit == 0, other, mine)])


def tie(value, *others):
    return lax.optimization_barrier((value,) + others)[0]


def halve(bit, swap, value):
    return add(pick(value, bit), swap(pick(value, 1 - bit)))


def place_heads(place, sources, core, heads, rows, begun):
    size, cols = sources[0].shape[3:]

    def block(j):
        part, y = j // 2, j % 2

        def at(s, bits):
            a = s % 2
            active = (s // 4) == part
            if part == 0:
                active = active & ((s // 2) % 2 == y)
                return (0, 0, jnp.where(active, a, 0), 0, 0)
            return (jnp.where(active, (s // 2) % 2, 0), 0, jnp.where(active, a, 0), 0, 0)

        return pl.BlockSpec((2 if part == 0 else 1, 2, 1, size, cols), at)

    def row_block(s, bits):
        part, i, a = s // 4, (s // 2) % 2, s % 2
        y, high = bits[0] ^ i, bits[2] ^ a
        inside = jnp.where(part == 0, y * 2 + high, high * 2 + y)
        return (((bits[4] ^ core) * 2 + part) * 4 + inside, 0)

    wide = cols - 2 * LANES
    more = () if begun is None else tuple(begun)
    return call(
        place_heads_kernel,
        (
            shaped((rows, heads * LANES), FULL_TYPE), shaped((rows, heads * LANES), FULL_TYPE),
            shaped((rows, heads * wide), FULL_TYPE),
        ),
        jnp.stack([place.y, place.x, place.high, place.low, place.c]).astype(jnp.int32), *sources, *more,
        grid=(8,), prefetch=1,
        in_specs=[block(j) for j in range(4)] + [pl.BlockSpec(memory_space=pl.ANY)] * len(more),
        out_specs=(
            pl.BlockSpec((size, heads * LANES), row_block), pl.BlockSpec((size, heads * LANES), row_block),
            pl.BlockSpec((size, heads * wide), row_block),
        ),
        aliases={5 + i: i for i in range(len(more))},
    )


def turn_tables(span, head_dim):
    half = head_dim // 2
    frequency = np.float32(10000.0) ** (-(np.arange(half).astype(np.float32) * np.float32(2.0) / np.float32(head_dim)))
    angles = np.arange(span).astype(np.float32)[:, None] * frequency[None, :].astype(np.float32)
    cosine, sine = np.cos(angles.astype(np.float64)), np.sin(angles.astype(np.float64))
    return (
        jnp.asarray(np.concatenate([cosine, cosine], axis=1).astype(np.float32)),
        jnp.asarray(np.concatenate([-sine, sine], axis=1).astype(np.float32)),
    )


def tuned_device(
    tokens, lengths, value_ids, out_ids, mlp_ids, w_query, w_key, w_value, w_out, sel_value, sel_out,
    gain_one, bias_one, gain_two, bias_two, w_select, w_up, w_down, cotangent,
):
    seqs, row_count, width = tokens.shape
    heads, head_dim = w_out.shape[0], w_out.shape[1]
    experts = w_out.shape[2] // width
    pair_count = seqs * heads
    span = 8 * row_count
    all_rows = seqs * row_count
    wide_out = heads * experts * LANES
    local = w_up.shape[1] // 4
    hidden = 8 * local
    own_count = w_select.shape[1]
    count = 8 * own_count
    quarter = count // 4
    tall = row_count + quarter
    place = Place()
    first_row = place.wide * row_count
    row = lambda v: v.reshape(1, -1)
    smem = pl.BlockSpec(memory_space=pltpu.SMEM)
    vmem = pl.BlockSpec(memory_space=pltpu.VMEM)
    hbm = pl.BlockSpec(memory_space=pl.ANY)
    by_seq = lambda shape: pl.BlockSpec((1,) + tuple(shape[1:]), lambda s: (s,) + (0,) * (len(shape) - 1))
    split = lambda shape: pl.BlockSpec((shape[0] // seqs,) + tuple(shape[1:]), lambda s: (s,) + (0,) * (len(shape) - 1))
    token_cols = lambda n: pl.BlockSpec((n, row_count), lambda s: (0, s))

    own_select = jnp.transpose(w_select).reshape(own_count, 8, -1).swapaxes(0, 1).reshape(-1, LANES)

    own_weights = call(
        weights_kernel,
        shaped((2, 2, width, local)),
        jnp.stack([place.narrow, place.narrow + 1 - 2 * place.c]).astype(jnp.int32), w_up, w_down,
        grid=(2,), prefetch=1,
        in_specs=[
            pl.BlockSpec((width, local), lambda s, spots: (0, spots[s])),
            pl.BlockSpec((local, width), lambda s, spots: (spots[s], 0)),
        ],
        out_specs=pl.BlockSpec((1, 2, width, local), lambda s, spots: (s, 0, 0, 0)),
    )
    weights_far = place.swap_high(own_weights[0])
    weights_near = place.swap_low(own_weights[0])

    cot_own = cotangent.reshape(all_rows, width)
    cots = [cot_own, place.swap_y(cot_own), place.swap_x(cot_own), place.swap_xy(cot_own)]

    cosine, sine = turn_tables(span, head_dim)
    here = lambda t: lax.dynamic_slice_in_dim(t, first_row, row_count, 0)
    sel = jnp.concatenate(
        [
            jnp.zeros((width, SELV), HALF_TYPE), sel_value, sel_out,
            jnp.zeros((width, LANES - SELO - heads * experts), HALF_TYPE),
        ],
        axis=1,
    )
    value_flat = value_ids.reshape(seqs, row_count, -1)
    out_flat = out_ids.reshape(seqs, row_count, -1)
    payload = 3 * row_count + own_select.shape[0] + 16
    qkv, projected, gate = call(
        pre_kernel,
        (
            shaped((pair_count, payload, head_dim)),
            shaped((seqs, row_count, wide_out)),
            shaped((seqs, row_count, LANES), FULL_TYPE),
        ),
        tokens, row(gain_one), row(bias_one), w_query, w_key, w_value, sel, value_flat, out_flat,
        here(cosine), here(sine), own_select,
        grid=(seqs,),
        in_specs=[
            by_seq(tokens.shape), full((1, width)), full((1, width)), full(w_query.shape), full(w_key.shape),
            full(w_value.shape), full(sel.shape), by_seq(value_flat.shape), by_seq(out_flat.shape),
            full((row_count, head_dim)), full((row_count, head_dim)),
            full(own_select.shape),
        ],
        out_specs=(
            split((pair_count, payload, head_dim)), by_seq((seqs, row_count, wide_out)),
            by_seq((seqs, row_count, LANES)),
        ),
        flops=2 * all_rows * width * 3712,
    )
    qkv = lax.all_to_all(qkv, "wide", 0, 0, tiled=True)
    qkv, weights_far, weights_near, cots[1], cots[2], cots[3] = lax.optimization_barrier(
        (qkv, weights_far, weights_near, cots[1], cots[2], cots[3])
    )
    tokens_x = place.swap_x(tie(tokens, qkv))
    weights_last = place.swap_low(weights_far)
    seq_here = place.wide // heads
    length = pick(lengths, seq_here).reshape(1)
    mixed, out_t, lse = call(
        attend_kernel,
        (
            shaped((8, row_count, head_dim)), shaped((head_dim, span), FULL_TYPE), shaped((1, span), FULL_TYPE),
        ),
        length, qkv,
        in_specs=[smem, vmem],
        flops=2 * span * span * head_dim,
    )
    mixed = lax.all_to_all(mixed, "wide", 0, 0, tiled=True)
    mixed, weights_last, tokens_x = lax.optimization_barrier((mixed, weights_last, tokens_x))

    kinds = (place.x * 2 + place.y) ^ jnp.arange(4)
    kx, ky = (kinds // 2)[:, None, None, None], (kinds % 2)[:, None, None, None]
    kz = (place.z ^ jnp.arange(4))[None, :, None, None]
    kc = (place.c ^ jnp.arange(2))[None, None, :, None]
    ki = jnp.arange(2)[None, None, None, :]
    sent_ids = ((kz * 2 + kx) * own_count + ky * 4 + kc * 2 + ki).reshape(-1)
    places = (sent_ids[:, None] == jnp.arange(count)[None, :]).astype(HALF_TYPE)

    own_mlp = lax.dynamic_slice_in_dim(mlp_ids, first_row, row_count, 1)
    own_mlp = jnp.swapaxes(own_mlp, 1, 2)
    after, gates, rows_own, select = call(
        post_kernel,
        (
            shaped((all_rows, width), FULL_TYPE), shaped((count, all_rows), FULL_TYPE), shaped((seqs, tall, width)),
            shaped((count, width)),
        ),
        mixed, gate, w_out, tokens, row(gain_two), row(bias_two), qkv, own_mlp, places,
        grid=(seqs,),
        in_specs=[
            split(mixed.shape), by_seq(gate.shape), full(w_out.shape), by_seq(tokens.shape), full((1, width)),
            full((1, width)), pl.BlockSpec((8, 8 * own_count, LANES), lambda s: (0, 3 * row_count // (8 * own_count), 0)),
            by_seq(own_mlp.shape), full(places.shape),
        ],
        out_specs=(
            split((all_rows, width)), token_cols(count), by_seq((seqs, tall, width)), full((count, width)),
        ),
        flops=2 * all_rows * width * wide_out,
    )

    rows_y, rows_x = place.swap_y(rows_own), place.swap_x(rows_own)
    rows_d = (place.swap_x(rows_y[0]), place.swap_y(rows_x[1]))
    rows_in = [(rows_own,), (rows_y,), (rows_x,), rows_d]
    weights = [own_weights]
    for piece in (weights_near, weights_far, weights_last):
        weights += [piece, place.swap_c(piece)]
    results = []
    for i in range(4):
        if i:
            cots[i] = tie(cots[i], results[-1][1])
        results.append(
            call(
                functools.partial(experts_kernel, i, len(rows_in[i])),
                (
                    shaped((seqs, tall, width)), shaped((8, all_rows, local)), shaped((8, all_rows, local)),
                ),
                *rows_in[i], cots[i], *weights,
                flops=6 * all_rows * width * hidden,
            )
        )
    swaps = (lambda v: v, place.swap_y, place.swap_x, place.swap_xy)
    d_rows = [swaps[i](results[i][0]) for i in range(4)]
    inners = [r[1] for r in results]

    own_two = jnp.stack([pick(tokens, seq_here), pick(tokens_x, seq_here)])
    other_two = jnp.stack([pick(tokens, 1 - seq_here), pick(tokens_x, 1 - seq_here)])
    near_four = jnp.concatenate([own_two, tie(place.swap_high(tie(other_two, rows_own)), results[1][1])])
    far_four = place.swap_low(near_four)

    whole = lambda shape: pl.BlockSpec(tuple(shape), lambda p: (0,) * len(shape))
    piece = lambda: pl.BlockSpec((1, all_rows, local), lambda p: (2 * (2 * (p % 2) + (p // 2) % 2) + p // 4, 0, 0))
    grads_out = [
        pl.BlockSpec((1, 2, width, local), lambda p, j=j: (jnp.clip(p - 2 * j, 0, 1), 0, 0, 0)) for j in range(4)
    ]
    grad_near, grad_far, peer_near, peer_far = call(
        expert_grads_kernel,
        (shaped((2, 2, width, local)),) * 4,
        tie(rows_own, d_rows[1], d_rows[2]), rows_y, rows_x, *rows_d, *cots, *[r[2] for r in results], *inners,
        grid=(8,),
        in_specs=[whole((seqs, tall, width))] * 3 + [whole((tall, width))] * 2 + [whole((all_rows, width))] * 4
        + [piece() for _ in range(8)],
        out_specs=tuple(grads_out),
        flops=16 * all_rows * width * hidden,
    )
    d_rows[3], peer_far, peer_near, far_four = lax.optimization_barrier(
        (tie(d_rows[3], grad_near), peer_far, peer_near, far_four)
    )
    came_far, came_near = place.swap_c(peer_far), place.swap_c(peer_near)

    live_info = jnp.concatenate([jnp.zeros((1,), jnp.int32), first_row.reshape(1).astype(jnp.int32), lengths])
    d_after, d_att, d_gate_out, small = call(
        mid_kernel,
        (
            shaped((all_rows, width), FULL_TYPE), shaped((pair_count, row_count, head_dim)),
            shaped((seqs, row_count, LANES), FULL_TYPE), shaped((width, LANES), FULL_TYPE),
        ),
        live_info, *d_rows, cotangent, after, gates, row(gain_two), row(bias_two), select, places,
        w_out, gate, mixed,
        grid=(seqs,),
        in_specs=[smem] + [by_seq((seqs, tall, width))] * 4 + [
            by_seq(cotangent.shape), split((all_rows, width)), token_cols(count), full((1, width)), full((1, width)),
            full(select.shape), full(places.shape), full(w_out.shape), by_seq(gate.shape),
            split(mixed.shape),
        ],
        out_specs=(
            split((all_rows, width)), split((pair_count, row_count, head_dim)),
            by_seq((seqs, row_count, LANES)), full((width, LANES)),
        ),
        scratch=[pltpu.VMEM((LANES, width), FULL_TYPE)],
        flops=2 * all_rows * width * wide_out,
    )
    d_att_all = lax.all_to_all(d_att, "wide", 0, 0, tiled=True)

    to_low = add(grad_far, came_far)
    passed = place.swap_low(to_low)
    near_four = tie(near_four, d_att, to_low)
    tok_t, norm_t = call(
        turn_kernel,
        (shaped((8, width, row_count)), shaped((8, width, row_count))),
        near_four, far_four, row(gain_one), row(bias_one),
        grid=(8,),
        in_specs=[
            pl.BlockSpec((1, row_count, width), lambda i: (jnp.minimum(i, 3), 0, 0)),
            pl.BlockSpec((1, row_count, width), lambda i: (jnp.maximum(i - 4, 0), 0, 0)),
            full((1, width)), full((1, width)),
        ],
        out_specs=(
            pl.BlockSpec((1, width, row_count), lambda i: (i, 0, 0)),
            pl.BlockSpec((1, width, row_count), lambda i: (i, 0, 0)),
        ),
    )
    grad_out = call(
        out_grad_kernel, shaped((heads * head_dim, experts * width)), tie(mixed, d_att, came_far, came_near), gate, d_after,
        flops=2 * all_rows * width * wide_out,
    )
    rows_out, cols_out = grad_out.shape
    flat = ((place.y, place.swap_y), (place.x, place.swap_x))
    out_parts = halve(place.c, place.swap_c, grad_out.reshape(2, 2, 2, 2, 2, 2, rows_out // 64, cols_out))

    d_att_all, tok_t, out_parts = lax.optimization_barrier((d_att_all, tok_t, out_parts))
    out_parts = [halve(*flat[i], out_parts[i]) for i in range(2)]
    d_qkv = call(
        attend_back_kernel,
        shaped((8, 3 * row_count, head_dim)),
        length, qkv, d_att_all, out_t, lse, cosine, sine,
        in_specs=[smem] + [vmem] * 6,
        scratch=[pltpu.VMEM((span, head_dim), FULL_TYPE), pltpu.VMEM((span, head_dim), FULL_TYPE)],
        flops=5 * span * span * head_dim,
    )

    d_qkv, out_parts[0], out_parts[1] = lax.optimization_barrier((d_qkv, *out_parts))
    out_parts = [halve(*flat[1 - i], out_parts[i]) for i in range(2)]

    block_of = lambda i, spot: spot[0] ^ ((i & 1) | ((i & 2) << 1) | ((i & 4) >> 1))
    head_cols = (2 + experts) * LANES
    head_grads = call(
        head_grads_kernel,
        shaped((width, head_cols)),
        place.wide.reshape(1).astype(jnp.int32), tok_t, norm_t, d_qkv, qkv,
        grid=(8,), prefetch=1,
        in_specs=[
            pl.BlockSpec((1, width, row_count), lambda i, spot: (i, 0, 0)),
            pl.BlockSpec((1, width, row_count), lambda i, spot: (i, 0, 0)),
            pl.BlockSpec((1, 3 * row_count, head_dim), lambda i, spot: (block_of(i, spot), 0, 0)),
            pl.BlockSpec((1, 16, head_dim), lambda i, spot: (block_of(i, spot), payload // 16 - 1, 0)),
        ],
        out_specs=pl.BlockSpec((width, head_cols), lambda i, spot: (0, 0)),
        scratch=[pltpu.VMEM((width, head_cols), FULL_TYPE)],
        flops=2 * span * width * head_cols,
    )
    d_qkv_rows = lax.all_to_all(d_qkv, "wide", 0, 0, tiled=True)
    bits = ((place.y, place.swap_y), (place.high, place.swap_high))
    rows_head = width // 16
    head_grads, out_sum, passed = lax.optimization_barrier((head_grads, jnp.stack(out_parts, axis=2), passed))
    branches = call(
        branch_kernel,
        (shaped((all_rows, width)),) * 4,
        tie(inners[0], head_grads), *inners[1:], *weights,
        flops=8 * all_rows * width * hidden,
    )
    b0, b1, b2, b3 = branches
    b1, b2 = place.swap_y(b1), place.swap_x(b2)
    mine = add(grad_near[0], came_near[0], passed[0])
    mine_far = place.swap_high(add(grad_near[1], came_near[1], passed[1]))
    kept = halve(place.c, place.swap_c, head_grads.reshape(2, 2, 2, 2, rows_head, head_cols))
    out_sum = halve(place.low, place.swap_low, out_sum)
    kept, out_sum, b3 = lax.optimization_barrier((kept, out_sum, b3))
    value = [halve(*bits[i], kept[i]) for i in range(2)]
    out_sum = halve(place.high, place.swap_high, out_sum)
    value[0], value[1], out_sum, d_qkv_rows, b1, b2 = lax.optimization_barrier(
        (value[0], value[1], out_sum, d_qkv_rows, b1, b2)
    )
    b3 = place.swap_xy(tie(b3, b1))
    value = [halve(*bits[1 - i], value[i]) for i in range(2)]
    out_sum = in_order(place.high, out_sum, place.swap_high(out_sum))
    grad_tokens, small = call(
        last_kernel,
        (shaped((all_rows, width)), shaped((width, LANES))),
        d_qkv_rows, tokens, row(gain_one), row(bias_one), w_query, w_key, w_value, sel, projected, gate, d_gate_out,
        small, d_after,
        grid=(seqs,),
        in_specs=[
            split(d_qkv.shape), by_seq(tokens.shape), full((1, width)), full((1, width)), full(w_query.shape),
            full(w_key.shape), full(w_value.shape), full(sel.shape), by_seq(projected.shape), by_seq(gate.shape),
            by_seq(d_gate_out.shape), full(small.shape), split(d_after.shape),
        ],
        out_specs=(split((all_rows, width)), full((width, LANES))),
        scratch=[pltpu.VMEM((row_count, wide_out), HALF_TYPE), pltpu.VMEM((width, LANES), FULL_TYPE)],
        flops=2 * all_rows * width * 3712,
    )
    done, small, out_sum = lax.optimization_barrier((jnp.stack(value), small, out_sum))
    far = place.swap_high(done)
    out_sum = in_order(place.low, out_sum, place.swap_low(out_sum))
    everywhere = ("wide", "narrow")
    small = lax.all_to_all(small, everywhere, 0, 0, tiled=True).reshape(32, -1, LANES)
    far, small, out_sum, mine_far, b3 = lax.optimization_barrier((far, small, out_sum, mine_far, b3))
    mine = add(mine, mine_far)
    mine_y = place.swap_y(mine)
    near = [place.swap_low(done), place.swap_low(far)]
    sets = [
        jnp.stack([jnp.stack([done[i], far[i]]), jnp.stack([near[0][i], near[1][i]])]) for i in range(2)
    ]
    small = jnp.sum(small.astype(FULL_TYPE), axis=0).astype(HALF_TYPE)
    small = lax.all_to_all(jnp.broadcast_to(small[None], (32,) + small.shape), everywhere, 0, 0, tiled=True)
    back = [in_order(flat[1 - i][0], out_sum[:, :, i], flat[1 - i][1](out_sum[:, :, i])) for i in range(2)]
    sets[0], sets[1], small, back[0], back[1] = lax.optimization_barrier((sets[0], sets[1], small, back[0], back[1]))
    back = [in_order(flat[i][0], back[i], flat[i][1](back[i])) for i in range(2)]
    first = jnp.stack([sets[0], place.swap_x(sets[0])])
    second = jnp.stack([sets[1], place.swap_y(sets[1])])
    out_half = jnp.stack(back).reshape(rows_out // 2, cols_out)
    first, second, out_half, mine_y = lax.optimization_barrier((first, second, out_half, mine_y))
    sources = [first, place.swap_y(first), second, place.swap_x(second)]
    out_peer = place.swap_c(out_half)
    mine_c, mine_yc = place.swap_c(mine), place.swap_c(mine_y)
    output = call(output_kernel, shaped((all_rows, width)), after, b0, b1, b2, b3)
    spots = jnp.stack(
        [place.narrow, place.narrow ^ 2, place.narrow ^ 1, place.narrow ^ 3]
    ).astype(jnp.int32)
    grad_up, grad_down = call(
        place_experts_kernel,
        (shaped((width, 4 * local), FULL_TYPE), shaped((4 * local, width), FULL_TYPE)),
        spots, mine, mine_y, mine_c, mine_yc,
        grid=(4,), prefetch=1,
        in_specs=[full((2, width, local))] * 4,
        out_specs=(
            pl.BlockSpec((width, local), lambda s, spots: (0, spots[s])),
            pl.BlockSpec((local, width), lambda s, spots: (spots[s], 0)),
        ),
    )
    half_spec = lambda mine: pl.BlockSpec((head_dim, cols_out), lambda s, spot: (jnp.where((s < 2) == mine, s % 2, 1), 0))
    grad_out = call(
        place_out_kernel,
        shaped((heads, head_dim, cols_out), FULL_TYPE),
        place.c.reshape(1).astype(jnp.int32), out_half, out_peer,
        grid=(4,), prefetch=1,
        in_specs=[half_spec(True), half_spec(False)],
        out_specs=pl.BlockSpec((1, head_dim, cols_out), lambda s, spot: (2 * (spot[0] ^ (s // 2)) + s % 2, 0, 0)),
    )
    small = small.reshape(width, LANES)
    grad_select, grad_sel_value, grad_sel_out, rows_four = call(
        place_small_kernel,
        (
            shaped((own_count, width), FULL_TYPE), shaped((heads * experts, width), FULL_TYPE),
            shaped((heads * experts, width), FULL_TYPE), shaped((8, width), FULL_TYPE),
        ),
        (place.wide * own_count).reshape(1).astype(jnp.int32), small,
        in_specs=[smem, vmem],
    )
    peers = [place.swap_c(first), None, place.swap_c(second), None]
    (sources[1], sources[3], peers[0], peers[2], output, grad_up, grad_down, grad_out, grad_select, grad_sel_value,
     grad_sel_out, rows_four) = lax.optimization_barrier(
        (sources[1], sources[3], peers[0], peers[2], output, grad_up, grad_down, grad_out, grad_select, grad_sel_value,
         grad_sel_out, rows_four)
    )
    peers[1], peers[3] = place.swap_c(sources[1]), place.swap_c(sources[3])
    grad_heads = place_heads(place, sources, 0, heads, width, None)
    grad_query, grad_key, grad_value = place_heads(place, peers, 1, heads, width, grad_heads)
    grad_select, grad_sel_value, grad_sel_out = grad_select.T, grad_sel_value.T, grad_sel_out.T
    grad_gain_two, grad_bias_two, grad_gain_one, grad_bias_one = (rows_four[i] for i in range(4))
    return (
        output.reshape(tokens.shape), grad_tokens.reshape(tokens.shape), grad_query, grad_key, grad_value, grad_out,
        grad_sel_value, grad_sel_out, grad_gain_one, grad_bias_one, grad_gain_two, grad_bias_two, grad_select,
        grad_up, grad_down,
    )


def fits(mesh):
    return dict(mesh.shape) == {"wide": 8, "narrow": 4}


def solution(mesh):
    placed = (
        P("narrow", "wide", None),
        P("narrow"),
        P("narrow", "wide", None, None),
        P("narrow", "wide", None, None),
        P("narrow", None, None),
        P(),
        P(),
        P(),
        P(),
        P(),
        P(),
        P(),
        P(),
        P(),
        P(),
        P(None, "wide"),
        P(None, "wide"),
        P("wide", None),
        P("narrow", "wide", None),
    )
    return jax.shard_map(
        tuned_device if fits(mesh) else per_device,
        mesh=mesh,
        in_specs=placed,
        out_specs=(
            P("narrow", "wide", None),
            P("narrow", "wide", None),
            P(),
            P(),
            P(),
            P(),
            P(),
            P(),
            P(),
            P(),
            P(),
            P(),
            P(None, "wide"),
            P(None, "wide"),
            P("wide", None),
        ),
        check_vma=False,
    )
```

```python
import functools

import jax
import jax.numpy as jnp
import numpy as np
from jax import lax
from jax.experimental import pallas as pl
from jax.experimental.pallas import tpu as pltpu
from jax.sharding import PartitionSpec as P

EPSILON = 1e-05
FULL_TYPE = jnp.float32
HALF_TYPE = jnp.bfloat16


def for_sending(value):

    def short(part):
        return part.astype(jnp.bfloat16) if part.dtype == jnp.float32 else part

    return jax.tree.map(short, value)


def norm_parts(values_in, gain, bias):
    row_mean = jnp.mean(values_in, axis=-1, keepdims=True)
    centred = values_in - row_mean
    inv_scale = lax.rsqrt(jnp.mean(centred * centred, axis=-1, keepdims=True) + EPSILON)
    normal = centred * inv_scale
    return (normal * gain + bias, normal, inv_scale)


def norm_back(grad_in, normal, inv_scale, gain):
    scaled = grad_in * gain
    return inv_scale * (
        scaled
        - jnp.mean(scaled, axis=-1, keepdims=True)
        - normal * jnp.mean(scaled * normal, axis=-1, keepdims=True)
    )


def rotate(values_in, positions, turn):
    half_dim = values_in.shape[-1] // 2
    frequency = 10000.0 ** (-(jnp.arange(half_dim).astype(FULL_TYPE) * 2.0 / values_in.shape[-1]))
    angles = positions.astype(FULL_TYPE)[:, None] * frequency[None, :]
    cosine = jnp.cos(angles)[:, None, :]
    sine_part = turn * jnp.sin(angles)[:, None, :]
    front_half = values_in[..., :half_dim]
    back_half = values_in[..., half_dim:]
    return jnp.concatenate(
        [front_half * cosine - back_half * sine_part, front_half * sine_part + back_half * cosine],
        axis=-1,
    )


def one_hot_sum(ids, wanted):
    return jnp.sum((ids[..., None] == wanted).astype(FULL_TYPE), axis=-2)


def matmul(left_op, right_op):
    return jnp.dot(left_op, right_op, preferred_element_type=FULL_TYPE)


def contract_rows(left_op, right_op):
    left_flat = left_op.reshape(-1, left_op.shape[-1])
    right_flat = right_op.reshape(-1, right_op.shape[-1])
    return lax.dot_general(
        left_flat, right_flat, (((0,), (0,)), ((), ())), preferred_element_type=FULL_TYPE
    )


def times_transpose(grad_in, weight):
    return lax.dot_general(
        grad_in, weight, (((grad_in.ndim - 1,), (1,)), ((), ())), preferred_element_type=FULL_TYPE
    )


def attend_forward(
    tokens,
    lengths,
    value_ids,
    out_ids,
    w_query,
    w_key,
    w_value,
    w_out,
    sel_value,
    sel_out,
    gain_one,
    bias_one,
    gain_two,
    bias_two,
):
    seq_count, row_count, model_width = tokens.shape
    head_count = w_out.shape[0]
    head_dim = w_out.shape[1]
    value_experts = sel_value.shape[1] // head_count
    positions = lax.axis_index("wide") * row_count + jnp.arange(row_count, dtype=jnp.int32)
    inputs = tokens.astype(FULL_TYPE)
    normed, normal_one, scale_one = norm_parts(inputs, gain_one, bias_one)
    normed_low = normed.astype(HALF_TYPE)
    query_pre = matmul(normed_low, w_query).reshape(seq_count, row_count, head_count, head_dim)
    key_pre = matmul(normed_low, w_key).reshape(seq_count, row_count, head_count, head_dim)
    queries = rotate(query_pre, positions, 1.0).astype(HALF_TYPE)
    key_low = rotate(key_pre, positions, 1.0).astype(HALF_TYPE)
    expert_ids = jnp.arange(value_experts, dtype=jnp.int32)
    value_choice = one_hot_sum(value_ids, expert_ids)
    value_sig = jax.nn.sigmoid(
        matmul(normed_low, sel_value).reshape(seq_count, row_count, head_count, value_experts)
    )
    value_gate = value_sig * value_choice
    projected = matmul(tokens, w_value).reshape(
        seq_count, row_count, head_count, value_experts, head_dim
    )
    values = jnp.sum(value_gate[..., None] * projected, axis=3).astype(HALF_TYPE)
    keys_all, values_all = (
        lax.all_gather(key_low, "wide", axis=1, tiled=True),
        lax.all_gather(values, "wide", axis=1, tiled=True),
    )
    span = keys_all.shape[1]
    key_pos = jnp.arange(span, dtype=jnp.int32)
    allowed = (key_pos[None, None, None, :] <= positions[None, None, :, None]) & (
        key_pos[None, None, None, :] < lengths[:, None, None, None]
    )
    scores = jnp.einsum(
        "bphc,bshc->bhps", queries, keys_all, preferred_element_type=FULL_TYPE
    ) * head_dim ** (-0.5)
    masked = jnp.where(allowed, scores, -1e30)
    row_max = jnp.max(masked, axis=-1, keepdims=True)
    exponent = jnp.exp(masked - row_max)
    row_total = jnp.sum(exponent, axis=-1, keepdims=True)
    attn_probs = exponent / row_total
    log_total = row_max + jnp.log(row_total)
    attended = jnp.einsum(
        "bhps,bshc->bphc",
        attn_probs.astype(HALF_TYPE),
        values_all,
        preferred_element_type=FULL_TYPE,
    )
    live_rows = (positions[None, :] < lengths[:, None]).astype(FULL_TYPE)[:, :, None, None]
    mixed_out = (attended * live_rows).astype(HALF_TYPE)
    out_choice = one_hot_sum(out_ids, expert_ids)
    out_sig = jax.nn.sigmoid(
        matmul(normed_low, sel_out).reshape(seq_count, row_count, head_count, value_experts)
    )
    out_gate = out_sig * out_choice
    expert_out = jnp.einsum(
        "bphc,hcf->bphf", mixed_out, w_out, preferred_element_type=FULL_TYPE
    ).reshape(seq_count, row_count, head_count, value_experts, model_width)
    after_attn = inputs + jnp.sum(out_gate[..., None] * expert_out, axis=(2, 3))
    normed_two, normal_two, scale_two = norm_parts(after_attn, gain_two, bias_two)
    return dict(
        positions=positions,
        normal_one=normal_one,
        scale_one=scale_one,
        normed_low=normed_low,
        queries=queries,
        keys_all=keys_all,
        values_all=values_all,
        allowed=allowed,
        log_total=log_total,
        live_rows=live_rows,
        mixed_out=mixed_out,
        value_choice=value_choice,
        value_sig=value_sig,
        value_gate=value_gate,
        projected=projected,
        out_choice=out_choice,
        out_sig=out_sig,
        out_gate=out_gate,
        expert_out=expert_out,
        after_attn=after_attn,
        normed_two=normed_two,
        normal_two=normal_two,
        scale_two=scale_two,
    )


def expert_forward(after_attn, normed_two, mlp_ids, w_select, w_up):
    rows_all, normed_all = (
        lax.all_gather(for_sending(after_attn.astype(HALF_TYPE)), "wide", axis=1, tiled=True),
        lax.all_gather(for_sending(normed_two.astype(HALF_TYPE)), "wide", axis=1, tiled=True),
    )
    local_count = w_select.shape[1]
    hidden = w_up.shape[1] // local_count
    seq_count, span = (rows_all.shape[0], rows_all.shape[1])
    owned_ids = lax.axis_index("wide") * local_count + jnp.arange(local_count, dtype=jnp.int32)
    chosen = one_hot_sum(mlp_ids, owned_ids)
    sigmoid_gate = jax.nn.sigmoid(matmul(normed_all, w_select))
    mlp_gate = sigmoid_gate * chosen
    pre_act = matmul(rows_all, w_up)
    activated = jax.nn.gelu(pre_act).reshape(seq_count, span, local_count, hidden)
    inner_low = (
        (activated * mlp_gate[..., None])
        .reshape(seq_count, span, local_count * hidden)
        .astype(HALF_TYPE)
    )
    return dict(
        rows_all=rows_all,
        normed_all=normed_all,
        chosen=chosen,
        sigmoid_gate=sigmoid_gate,
        mlp_gate=mlp_gate,
        pre_act=pre_act,
        activated=activated,
        inner_low=inner_low,
    )


def per_device(
    tokens,
    lengths,
    value_ids,
    out_ids,
    mlp_ids,
    w_query,
    w_key,
    w_value,
    w_out,
    sel_value,
    sel_out,
    gain_one,
    bias_one,
    gain_two,
    bias_two,
    w_select,
    w_up,
    w_down,
    cotangent,
):
    seq_count, row_count, model_width = tokens.shape
    head_count = w_out.shape[0]
    head_dim = w_out.shape[1]
    value_experts = sel_value.shape[1] // head_count
    saved = attend_forward(
        tokens,
        lengths,
        value_ids,
        out_ids,
        w_query,
        w_key,
        w_value,
        w_out,
        sel_value,
        sel_out,
        gain_one,
        bias_one,
        gain_two,
        bias_two,
    )
    expert_state = expert_forward(saved["after_attn"], saved["normed_two"], mlp_ids, w_select, w_up)
    branch_part = matmul(expert_state["inner_low"], w_down)
    branch_sum = lax.psum_scatter(
        branch_part.astype(jnp.bfloat16), "wide", scatter_dimension=1, tiled=True
    ).astype(jnp.float32)
    output = (saved["after_attn"] + branch_sum).astype(HALF_TYPE)
    saved = attend_forward(
        tokens,
        lengths,
        value_ids,
        out_ids,
        w_query,
        w_key,
        w_value,
        w_out,
        sel_value,
        sel_out,
        gain_one,
        bias_one,
        gain_two,
        bias_two,
    )
    expert_state = expert_forward(saved["after_attn"], saved["normed_two"], mlp_ids, w_select, w_up)
    cot_all = lax.all_gather(cotangent, "wide", axis=1, tiled=True)
    grad_down = contract_rows(expert_state["inner_low"], cot_all)
    d_inner = times_transpose(cot_all, w_down)
    activated = expert_state["activated"]
    d_inner_four = d_inner.reshape(activated.shape)
    d_mlp_gate = jnp.sum(d_inner_four * activated, axis=-1)
    mlp_gate = expert_state["mlp_gate"]
    gated_grad = (d_inner_four * mlp_gate[..., None]).reshape(expert_state["pre_act"].shape)
    unused_value, gelu_pull = jax.vjp(jax.nn.gelu, expert_state["pre_act"])
    d_pre = gelu_pull(gated_grad)[0].astype(HALF_TYPE)
    sigmoid_gate = expert_state["sigmoid_gate"]
    d_logit = (d_mlp_gate * expert_state["chosen"] * sigmoid_gate * (1.0 - sigmoid_gate)).astype(
        HALF_TYPE
    )
    grad_up = contract_rows(expert_state["rows_all"], d_pre)
    grad_select = contract_rows(expert_state["normed_all"], d_logit)
    row_part = times_transpose(d_pre, w_up)
    norm_part = times_transpose(d_logit, w_select)
    row_grad, norm_grad = (
        lax.psum_scatter(row_part, "wide", scatter_dimension=1, tiled=True),
        lax.psum_scatter(norm_part, "wide", scatter_dimension=1, tiled=True),
    )
    grad_gain_two = jnp.sum(norm_grad * saved["normal_two"], axis=(0, 1))
    grad_bias_two = jnp.sum(norm_grad, axis=(0, 1))
    d_after = (
        cotangent.astype(FULL_TYPE)
        + row_grad
        + norm_back(norm_grad, saved["normal_two"], saved["scale_two"], gain_two)
    )
    out_gate = saved["out_gate"]
    d_expert = (out_gate[..., None] * d_after[:, :, None, None, :]).astype(HALF_TYPE)
    d_out_gate = jnp.sum(saved["expert_out"] * d_after[:, :, None, None, :], axis=-1)
    d_expert_flat = d_expert.reshape(seq_count, row_count, head_count, value_experts * model_width)
    grad_out = jnp.einsum(
        "bphc,bphf->hcf", saved["mixed_out"], d_expert_flat, preferred_element_type=FULL_TYPE
    )
    d_mixed = jnp.einsum("bphf,hcf->bphc", d_expert_flat, w_out, preferred_element_type=FULL_TYPE)
    d_attended = (d_mixed * saved["live_rows"]).astype(HALF_TYPE)
    out_sig = saved["out_sig"]
    d_out_logit = (
        (d_out_gate * saved["out_choice"] * out_sig * (1.0 - out_sig))
        .astype(HALF_TYPE)
        .reshape(seq_count, row_count, head_count * value_experts)
    )
    queries = saved["queries"]
    keys_all = saved["keys_all"]
    values_all = saved["values_all"]
    score_scale = head_dim ** (-0.5)
    scores = (
        jnp.einsum("bphc,bshc->bhps", queries, keys_all, preferred_element_type=FULL_TYPE)
        * score_scale
    )
    attn_probs = jnp.where(saved["allowed"], jnp.exp(scores - saved["log_total"]), 0.0)
    d_values_part = jnp.einsum(
        "bhps,bphc->bshc",
        attn_probs.astype(HALF_TYPE),
        d_attended,
        preferred_element_type=FULL_TYPE,
    )
    d_probs = jnp.einsum(
        "bphc,bshc->bhps", d_attended, values_all, preferred_element_type=FULL_TYPE
    )
    row_inner = jnp.sum(attn_probs * d_probs, axis=-1, keepdims=True)
    d_scores = (attn_probs * (d_probs - row_inner)).astype(HALF_TYPE)
    d_queries = (
        jnp.einsum("bhps,bshc->bphc", d_scores, keys_all, preferred_element_type=FULL_TYPE)
        * score_scale
    )
    d_keys_part = (
        jnp.einsum("bhps,bphc->bshc", d_scores, queries, preferred_element_type=FULL_TYPE)
        * score_scale
    )
    d_keys, d_values = (
        lax.psum_scatter(
            d_keys_part.astype(jnp.bfloat16), "wide", scatter_dimension=1, tiled=True
        ).astype(jnp.float32),
        lax.psum_scatter(
            d_values_part.astype(jnp.bfloat16), "wide", scatter_dimension=1, tiled=True
        ).astype(jnp.float32),
    )
    positions = saved["positions"]
    d_query_pre = (
        rotate(d_queries, positions, -1.0)
        .astype(HALF_TYPE)
        .reshape(seq_count, row_count, head_count * head_dim)
    )
    d_key_pre = (
        rotate(d_keys, positions, -1.0)
        .astype(HALF_TYPE)
        .reshape(seq_count, row_count, head_count * head_dim)
    )
    d_projected = (
        (saved["value_gate"][..., None] * d_values[:, :, :, None, :])
        .astype(HALF_TYPE)
        .reshape(seq_count, row_count, head_count * value_experts * head_dim)
    )
    d_value_gate = jnp.sum(saved["projected"] * d_values[:, :, :, None, :], axis=-1)
    value_sig = saved["value_sig"]
    d_value_logit = (
        (d_value_gate * saved["value_choice"] * value_sig * (1.0 - value_sig))
        .astype(HALF_TYPE)
        .reshape(seq_count, row_count, head_count * value_experts)
    )
    normed_low = saved["normed_low"]
    grad_query = contract_rows(normed_low, d_query_pre)
    grad_key = contract_rows(normed_low, d_key_pre)
    grad_sel_value = contract_rows(normed_low, d_value_logit)
    grad_sel_out = contract_rows(normed_low, d_out_logit)
    grad_value = contract_rows(tokens, d_projected)
    d_normed = (
        times_transpose(d_query_pre, w_query)
        + times_transpose(d_key_pre, w_key)
        + times_transpose(d_value_logit, sel_value)
        + times_transpose(d_out_logit, sel_out)
    )
    grad_gain_one = jnp.sum(d_normed * saved["normal_one"], axis=(0, 1))
    grad_bias_one = jnp.sum(d_normed, axis=(0, 1))
    grad_tokens = (
        d_after
        + times_transpose(d_projected, w_value)
        + norm_back(d_normed, saved["normal_one"], saved["scale_one"], gain_one)
    ).astype(HALF_TYPE)
    (
        grad_query,
        grad_key,
        grad_value,
        grad_out,
        grad_sel_value,
        grad_sel_out,
        grad_gain_one,
        grad_bias_one,
        grad_gain_two,
        grad_bias_two,
    ) = lax.psum(
        (
            grad_query,
            grad_key,
            grad_value,
            grad_out,
            grad_sel_value,
            grad_sel_out,
            grad_gain_one,
            grad_bias_one,
            grad_gain_two,
            grad_bias_two,
        ),
        ("wide", "narrow"),
    )
    grad_select, grad_up, grad_down = (
        lax.psum(grad_select.astype(jnp.bfloat16), "narrow").astype(jnp.float32),
        lax.psum(grad_up.astype(jnp.bfloat16), "narrow").astype(jnp.float32),
        lax.psum(grad_down.astype(jnp.bfloat16), "narrow").astype(jnp.float32),
    )
    return (
        output,
        grad_tokens,
        grad_query,
        grad_key,
        grad_value,
        grad_out,
        grad_sel_value,
        grad_sel_out,
        grad_gain_one,
        grad_bias_one,
        grad_gain_two,
        grad_bias_two,
        grad_select,
        grad_up,
        grad_down,
    )


SELV = 72
SELO = 92
LANES = 128


def call(
    kernel, out_shape, *args, grid=None, in_specs=None, out_specs=None, scratch=(), flops=0, limit=56, prefetch=0, aliases=None
):
    moved = sum(a.size * a.dtype.itemsize for a in jax.tree.leaves((args, out_shape)))
    extra = {}
    if prefetch:
        extra["grid_spec"] = pltpu.PrefetchScalarGridSpec(
            num_scalar_prefetch=prefetch, grid=grid, in_specs=in_specs, out_specs=out_specs, scratch_shapes=list(scratch)
        )
    else:
        extra["scratch_shapes"] = list(scratch)
        if grid is not None:
            extra["grid"] = grid
        if in_specs is not None:
            extra["in_specs"] = in_specs
        if out_specs is not None:
            extra["out_specs"] = out_specs
    return pl.pallas_call(
        kernel,
        out_shape=out_shape,
        input_output_aliases=aliases or {},
        compiler_params=pltpu.CompilerParams(vmem_limit_bytes=limit * 1024 * 1024),
        cost_estimate=pl.CostEstimate(flops=int(flops), bytes_accessed=int(moved), transcendentals=0),
        **extra,
    )(*args)


def full(shape):
    rank = len(shape)
    return pl.BlockSpec(tuple(shape), lambda *s: (0,) * rank)


def shaped(shape, dtype=HALF_TYPE):
    return jax.ShapeDtypeStruct(tuple(shape), dtype)


def nn(a, b):
    return lax.dot_general(a, b, (((1,), (0,)), ((), ())), preferred_element_type=FULL_TYPE)


def nt(a, b):
    return lax.dot_general(a, b, (((1,), (1,)), ((), ())), preferred_element_type=FULL_TYPE)


def tn(a, b):
    return lax.dot_general(a, b, (((0,), (0,)), ((), ())), preferred_element_type=FULL_TYPE)


def layer_stats(v):
    centred = v - jnp.mean(v, axis=-1, keepdims=True)
    inv = lax.rsqrt(jnp.mean(centred * centred, axis=-1, keepdims=True) + EPSILON)
    return centred * inv, inv


def turned(v, cos, sin):
    return v * cos + pltpu.roll(v, v.shape[-1] // 2, axis=v.ndim - 1) * sin


def lane_ids(shape, dim):
    return lax.broadcasted_iota(jnp.int32, shape, dim)


def pre_kernel(tok, gain, bias, wq, wk, wv, sel, vid, oid, cos, sin, select, qkv, proj, gate):
    heads = qkv.shape[0]
    experts = wv.shape[1] // (heads * LANES)
    low = tok[0]
    rows = low.shape[0]
    normal, _ = layer_stats(low.astype(FULL_TYPE))
    normed = (normal * gain[...] + bias[...]).astype(HALF_TYPE)
    for part, weight in ((0, wq), (1, wk)):
        pre = nn(normed, weight[...])
        for h in range(heads):
            head = turned(pre[:, h * LANES:(h + 1) * LANES], cos[...], sin[...])
            qkv[h, part * rows:(part + 1) * rows] = head.astype(HALF_TYPE)
    lanes = lane_ids((rows, LANES), 1)
    chosen = jnp.zeros((rows, LANES), FULL_TYPE)
    tops = vid.shape[2] // heads
    for h in range(heads):
        for k in range(tops):
            j = h * tops + k
            chosen += (lanes == vid[0, :, j:j + 1] + (SELV + experts * h)).astype(FULL_TYPE)
            chosen += (lanes == oid[0, :, j:j + 1] + (SELO + experts * h)).astype(FULL_TYPE)
    gates = jax.nn.sigmoid(nn(normed, sel[...])) * chosen
    gate[0] = gates
    gates_low = gates.astype(HALF_TYPE)
    for h in range(heads):
        at = h * experts * LANES
        block = nn(low, wv[:, at:at + experts * LANES])
        proj[0, :, at:at + experts * LANES] = block.astype(HALF_TYPE)
        total = None
        for e in range(experts):
            col = SELV + h * experts + e
            term = gates[:, col:col + 1] * block[:, e * LANES:(e + 1) * LANES]
            total = term if total is None else total + term
        qkv[h, 2 * rows:3 * rows] = total.astype(HALF_TYPE)
        first = SELV + h * experts
        row_id = lane_ids((8, LANES), 0)
        spot = (lane_ids((8, LANES), 1) == row_id + first) & (row_id < experts)
        turned_gates = nt(spot.astype(FULL_TYPE).astype(HALF_TYPE), gates_low)
        tail = jnp.concatenate([turned_gates[:, i * LANES:(i + 1) * LANES] for i in range(rows // LANES)], axis=0)
        last = 3 * rows + select.shape[0]
        qkv[h, 3 * rows:last] = select[...]
        qkv[h, last:last + tail.shape[0]] = tail.astype(HALF_TYPE)


def limits_of(i, rows, length):
    position = i * rows + lane_ids((1, rows), 1)
    return jnp.minimum(position + 1, length), position


def parts_of(ref, first, last, part, rows):
    block = ref[first:last, part * rows:(part + 1) * rows]
    return block.reshape((last - first) * rows, block.shape[2])


def attend_kernel(length, qkv, mixed, out_t, lse):
    blocks, rows, width = mixed.shape
    scale = width ** (-0.5)
    values_t = jnp.transpose(parts_of(qkv, 0, blocks, 2, rows).astype(FULL_TYPE)).astype(HALF_TYPE)
    for i in range(blocks):
        n = (i + 1) * rows
        keys = parts_of(qkv, 0, i + 1, 1, rows)
        limit, position = limits_of(i, rows, length[0])
        scores = nt(keys, qkv[i, 0:rows]) * scale
        scores = jnp.where(lane_ids((n, rows), 0) < limit, scores, -1e30)
        top = jnp.max(scores, axis=0, keepdims=True)
        weights = jnp.exp(scores - top)
        total = jnp.sum(weights, axis=0, keepdims=True)
        attended = nn(values_t[:, :n], weights.astype(HALF_TYPE)) / total
        out_t[:, i * rows:(i + 1) * rows] = attended
        lse[:, i * rows:(i + 1) * rows] = top + jnp.log(total)
        live = (position < length[0]).astype(FULL_TYPE)
        mixed[i] = jnp.transpose(attended * live).astype(HALF_TYPE)


def attend_back_kernel(length, qkv, d_out, out_t, lse, cos, sin, d_qkv, d_keys, d_values):
    blocks, rows, width = d_out.shape
    scale = width ** (-0.5)
    keys_t = jnp.transpose(parts_of(qkv, 0, blocks, 1, rows).astype(FULL_TYPE)).astype(HALF_TYPE)
    d_keys[...] = jnp.zeros_like(d_keys)
    d_values[...] = jnp.zeros_like(d_values)
    for i in range(blocks):
        n = (i + 1) * rows
        here = slice(i * rows, (i + 1) * rows)
        limit, _ = limits_of(i, rows, length[0])
        query = qkv[i, 0:rows]
        d_att = d_out[i]
        delta = jnp.sum(jnp.transpose(d_att.astype(FULL_TYPE)) * out_t[:, here], axis=0, keepdims=True)
        scores = nt(parts_of(qkv, 0, i + 1, 1, rows), query) * scale
        probs = jnp.where(lane_ids((n, rows), 0) < limit, jnp.exp(scores - lse[:, here]), 0.0)
        d_probs = nt(parts_of(qkv, 0, i + 1, 2, rows), d_att)
        d_scores = (probs * (d_probs - delta)).astype(HALF_TYPE)
        d_values[0:n, :] += nn(probs.astype(HALF_TYPE), d_att)
        d_keys[0:n, :] += nn(d_scores, query)
        d_query = jnp.transpose(nn(keys_t[:, :n], d_scores)) * scale
        d_qkv[i, 0:rows] = turned(d_query, cos[here, :], -sin[here, :]).astype(HALF_TYPE)
    for i in range(blocks):
        here = slice(i * rows, (i + 1) * rows)
        d_qkv[i, rows:2 * rows] = turned(d_keys[here, :] * scale, cos[here, :], -sin[here, :]).astype(HALF_TYPE)
        d_qkv[i, 2 * rows:3 * rows] = d_values[here, :].astype(HALF_TYPE)


def gated(mixed, gate, hp, e, experts):
    parts = []
    for h in (2 * hp, 2 * hp + 1):
        col = SELO + h * experts + e
        parts.append((gate[:, col:col + 1] * mixed[h].astype(FULL_TYPE)).astype(HALF_TYPE))
    return jnp.concatenate(parts, axis=1)


def out_block(w_out, hp, e, width):
    block = w_out[2 * hp:2 * hp + 2, :, e * width:(e + 1) * width]
    return block.reshape(2 * block.shape[1], width)


def post_kernel(mixed, gate, w_out, tok, gain, bias, columns, ids, places, after, gates, sent, select):
    width = tok.shape[2]
    heads = w_out.shape[0]
    experts = w_out.shape[2] // width
    row_count = tok.shape[1]
    total = tok[0].astype(FULL_TYPE)
    gate_here = gate[0]
    mixed_here = mixed[...]
    for hp in range(heads // 2):
        for e in range(experts):
            total += nn(gated(mixed_here, gate_here, hp, e, experts), out_block(w_out, hp, e, width))
    after[...] = total
    sent[0, 0:row_count] = total.astype(HALF_TYPE)
    normal, _ = layer_stats(total)
    normed = (normal * gain[...] + bias[...]).astype(HALF_TYPE)
    every = columns[...].astype(FULL_TYPE)
    count = every.shape[1]
    each = count // 8
    w_sel = jnp.concatenate(
        [every[:, j * each:(j + 1) * each].reshape(count, LANES) for j in range(8)], axis=1
    ).astype(HALF_TYPE)
    select[...] = w_sel
    row_id = lane_ids((count, row_count), 0)
    chosen = jnp.zeros((count, row_count), FULL_TYPE)
    for k in range(ids.shape[1]):
        chosen += (row_id == ids[0, k:k + 1, :]).astype(FULL_TYPE)
    values = jax.nn.sigmoid(nt(w_sel, normed)) * chosen
    gates[...] = values
    moved = nn(places[...], values.astype(HALF_TYPE)).astype(HALF_TYPE)
    quarter = count // 4
    for i in range(4):
        sent[0, row_count:row_count + quarter, i * row_count:(i + 1) * row_count] = moved[i * quarter:(i + 1) * quarter]


def weights_kernel(spots, up, down, mine, peer):
    for s, out in enumerate((mine, peer)):

        @pl.when(pl.program_id(0) == s)
        def _(out=out):
            out[0] = up[...]
            out[1] = jnp.transpose(down[...].astype(FULL_TYPE)).astype(HALF_TYPE)


def expand(count, cols, first):
    rows = lane_ids((count, cols), 0)
    cut = lane_ids((count, cols), 1)
    hit = None
    for i in range(cols // LANES):
        inside = (cut >= i * LANES) & (cut < (i + 1) * LANES) & (rows == first + i)
        hit = inside if hit is None else hit | inside
    return hit.astype(FULL_TYPE).astype(HALF_TYPE)


def experts_kernel(kind, halves, *refs):
    rows_in, cot, pieces = refs[:halves], refs[halves], refs[halves + 1:halves + 9]
    back, inner, d_pre = refs[halves + 9:]
    seqs, tall, width = back.shape
    row_count = width // 4
    cols = pieces[0].shape[2]
    quarter = tall - row_count
    picked = [rows_in[0][s] if halves == 1 else rows_in[s][...] for s in range(seqs)]
    low = jnp.concatenate([block[0:row_count] for block in picked], axis=0)
    gates = jnp.concatenate(
        [block[row_count:tall, kind * row_count:(kind + 1) * row_count] for block in picked], axis=1
    )
    cot_low = cot[...]
    row_total = gate_total = None
    weight = lambda p, u: pieces[p][u]
    root, cube = 0.7978845608028654, 0.044715
    for p in range(8):
        spread = expand(quarter, cols, p * (cols // LANES))
        gate_wide = tn(gates, spread)
        pre = nn(low, weight(p, 0))
        d_in = nn(cot_low, weight(p, 1))
        square = pre * pre
        tanh = jnp.tanh(pre * (root + (root * cube) * square))
        half = 0.5 + 0.5 * tanh
        act = pre * half
        slope = half + act * (1.0 - tanh) * (root + (3 * root * cube) * square)
        d_pre[p] = (slope * gate_wide * d_in).astype(HALF_TYPE)
        inner[p] = (act * gate_wide).astype(HALF_TYPE)
        g = nt(spread, (d_in * act).astype(HALF_TYPE))
        gate_total = g if p == 0 else gate_total + g
    for p in range(8):
        r = nt(d_pre[p], weight(p, 0))
        row_total = r if p == 0 else row_total + r
    for s in range(seqs):
        here = slice(s * row_count, (s + 1) * row_count)
        back[s, 0:row_count] = row_total[here].astype(HALF_TYPE)
        back[s, row_count:tall] = jnp.zeros((quarter, width), HALF_TYPE)
        back[s, row_count:tall, 0:row_count] = gate_total[:, here].astype(HALF_TYPE)


def branch_kernel(*refs):
    inners, pieces, outs = refs[0:4], refs[4:12], refs[12:16]
    downs = [ref[1] for ref in pieces]
    for i in range(4):
        total = None
        for p in range(8):
            term = nt(inners[i][p], downs[p])
            total = term if p == 0 else total + term
        outs[i][...] = total.astype(HALF_TYPE)


def expert_grads_kernel(*refs):
    rows, cots, pres, inners = refs[0:5], refs[5:9], refs[9:13], refs[13:17]
    outs = refs[17:21]
    step = pl.program_id(0)
    row_count = pres[0].shape[1] // 2
    up = down = None
    for i in range(4):
        for s in range(2):
            block = rows[i][s, 0:row_count] if i < 3 else rows[3 + s][0:row_count]
            term = tn(block, pres[i][0, s * row_count:(s + 1) * row_count])
            up = term if up is None else up + term
        term = tn(cots[i][...], inners[i][0])
        down = term if down is None else down + term
    results = (up.astype(HALF_TYPE), down.astype(HALF_TYPE))
    for j in range(4):

        @pl.when(step // 2 == j)
        def _(j=j):
            for u in range(2):
                outs[j][0, u] = results[u]


def mid_kernel(length, r0, r1, r2, r3, cot, after, gates, gain, bias, w_sel, places, w_out, gate, mixed,
               d_after, d_att, d_gate_out, small, acc):
    step = pl.program_id(0)
    width = cot.shape[2]
    heads = w_out.shape[0]
    experts = w_out.shape[2] // width
    row_count = cot.shape[1]
    tall = r0.shape[1]
    d_rel = jnp.concatenate([r[0, row_count:tall, 0:row_count] for r in (r0, r1, r2, r3)], axis=0)
    d_gate = tn(places[...], d_rel)
    values = gates[...]
    d_logit = (d_gate * values * (1.0 - values)).astype(HALF_TYPE)
    normal, inv = layer_stats(after[...])
    normed = (normal * gain[...] + bias[...]).astype(HALF_TYPE)
    d_normed = tn(d_logit, w_sel[...])
    sel_part = nn(d_logit, normed)
    gain_part = jnp.sum(d_normed * normal, axis=0, keepdims=True)
    bias_part = jnp.sum(d_normed, axis=0, keepdims=True)
    count = sel_part.shape[0]

    @pl.when(step == 0)
    def _():
        acc[...] = jnp.zeros_like(acc)

    acc[0:count, :] += sel_part
    acc[count:count + 1, :] += gain_part
    acc[count + 1:count + 2, :] += bias_part
    d_row = sum(r[0, 0:row_count].astype(FULL_TYPE) for r in (r0, r1, r2, r3))
    total = cot[0].astype(FULL_TYPE) + d_row + norm_back(d_normed, normal, inv, gain[...])
    d_after[...] = total
    total_low = total.astype(HALF_TYPE)
    mixed_here = mixed[...]
    gate_here = gate[0]
    lanes = lane_ids((2 * LANES, LANES), 1)
    second = (lane_ids((2 * LANES, LANES), 0) >= LANES).astype(jnp.int32)
    d_gates = jnp.zeros((row_count, LANES), FULL_TYPE)
    for hp in range(heads // 2):
        both = jnp.concatenate([mixed_here[2 * hp], mixed_here[2 * hp + 1]], axis=1).astype(FULL_TYPE)
        sums = [None, None]
        for e in range(experts):
            d_mixed = nt(total_low, out_block(w_out, hp, e, width))
            hit = (lanes == SELO + 2 * hp * experts + e + second * experts).astype(FULL_TYPE).astype(HALF_TYPE)
            d_gates += nn((both * d_mixed).astype(HALF_TYPE), hit)
            for i in range(2):
                col = SELO + (2 * hp + i) * experts + e
                term = gate_here[:, col:col + 1] * d_mixed[:, i * LANES:(i + 1) * LANES]
                sums[i] = term if e == 0 else sums[i] + term
        for i in range(2):
            position = length[1] + lane_ids((row_count, 1), 0)
            live = (position < length[2 + step]).astype(FULL_TYPE)
            d_att[2 * hp + i] = (sums[i] * live).astype(HALF_TYPE)
    d_gate_out[0] = d_gates

    @pl.when(step == pl.num_programs(0) - 1)
    def _():
        spots = (lane_ids((LANES, LANES), 0) == lanes[0:LANES]).astype(FULL_TYPE).astype(HALF_TYPE)
        small[...] = tn(acc[...].astype(HALF_TYPE), spots)


def out_grad_kernel(mixed, gate, d_after, out):
    heads, experts = 4, out.shape[1] // d_after.shape[1]
    width = d_after.shape[1]
    seqs, row_count = gate.shape[0], gate.shape[1]
    low = d_after[...].astype(HALF_TYPE)
    for hp in range(heads // 2):
        for e in range(experts):
            total = None
            for s in range(seqs):
                left = gated([mixed[s * heads + h] for h in range(heads)], gate[s], hp, e, experts)
                term = tn(left, low[s * row_count:(s + 1) * row_count, :])
                total = term if total is None else total + term
            out[2 * hp * LANES:(2 * hp + 2) * LANES, e * width:(e + 1) * width] = total.astype(HALF_TYPE)


def last_kernel(d_qkv, tok, gain, bias, wq, wk, wv, sel, proj, gate, d_gate_out, small, d_after,
                out, sums, d_proj, acc):
    step = pl.program_id(0)
    row_count, width = tok.shape[1], tok.shape[2]
    heads = d_qkv.shape[0]
    experts = proj.shape[2] // (heads * LANES)
    lanes = lane_ids((LANES, LANES), 1)
    low = tok[0]
    normal, inv = layer_stats(low.astype(FULL_TYPE))
    normed = (normal * gain[...] + bias[...]).astype(HALF_TYPE)
    d_gates = d_gate_out[0]
    gate_here = gate[0]
    d_query = jnp.concatenate([d_qkv[h, 0:row_count] for h in range(heads)], axis=1)
    d_key = jnp.concatenate([d_qkv[h, row_count:2 * row_count] for h in range(heads)], axis=1)
    for h in range(heads):
        d_value = d_qkv[h, 2 * row_count:3 * row_count].astype(FULL_TYPE)
        for e in range(experts):
            col = SELV + h * experts + e
            at = (h * experts + e) * LANES
            d_proj[:, at:at + LANES] = (gate_here[:, col:col + 1] * d_value).astype(HALF_TYPE)
            hit = (lanes == col).astype(FULL_TYPE).astype(HALF_TYPE)
            product = (proj[0, :, at:at + LANES].astype(FULL_TYPE) * d_value).astype(HALF_TYPE)
            d_gates += nn(product, hit)
    d_logit = (d_gates * gate_here * (1.0 - gate_here)).astype(HALF_TYPE)
    d_normed = nt(d_query, wq[...]) + nt(d_key, wk[...]) + nt(d_logit, sel[...])
    total = d_after[...] + norm_back(d_normed, normal, inv, gain[...]) + nt(d_proj[...], wv[...])
    out[...] = total.astype(HALF_TYPE)
    gain_sum = jnp.sum(d_normed * normal, axis=0, keepdims=True)
    bias_sum = jnp.sum(d_normed, axis=0, keepdims=True)
    rows = jnp.concatenate([gain_sum, bias_sum, jnp.zeros((14, width), FULL_TYPE)], axis=0).astype(HALF_TYPE)
    spot = (lane_ids((16, LANES), 1) == lane_ids((16, LANES), 0) + 66) & (lane_ids((16, LANES), 0) < 2)
    spread = tn(rows, spot.astype(FULL_TYPE).astype(HALF_TYPE))
    part = tn(normed, d_logit) + spread

    @pl.when(step == 0)
    def _():
        acc[...] = small[...] + part

    @pl.when(step > 0)
    def _():
        acc[...] += part

    sums[...] = acc[...].astype(HALF_TYPE)


def turn_kernel(near, far, gain, bias, tok_t, norm_t):
    step = pl.program_id(0)

    def turn(low):
        normal, _ = layer_stats(low.astype(FULL_TYPE))
        tok_t[0] = jnp.transpose(low.astype(FULL_TYPE)).astype(HALF_TYPE)
        normed = (normal * gain[...] + bias[...]).astype(HALF_TYPE)
        norm_t[0] = jnp.transpose(normed.astype(FULL_TYPE)).astype(HALF_TYPE)

    @pl.when(step < 4)
    def _():
        turn(near[0])

    @pl.when(step >= 4)
    def _():
        turn(far[0])


def head_grads_kernel(spot, tok_t, norm_t, d_qkv, gate, out, acc):
    step = pl.program_id(0)
    rows = tok_t.shape[2]
    experts = out.shape[1] // LANES - 2
    both = jnp.concatenate([d_qkv[0, 0:rows], d_qkv[0, rows:2 * rows]], axis=1)
    wide = experts * LANES
    spread = expand(8, wide, 0)
    tail = gate[0]
    gates = jnp.concatenate([tn(tail[i * 8:(i + 1) * 8], spread) for i in range(rows // LANES)], axis=0)
    d_value = d_qkv[0, 2 * rows:3 * rows].astype(FULL_TYPE)
    d_proj = (gates * jnp.concatenate([d_value] * experts, axis=1)).astype(HALF_TYPE)
    first = nn(norm_t[0], both)
    second = nn(tok_t[0], d_proj)

    @pl.when(step == 0)
    def _():
        acc[:, 0:2 * LANES] = first
        acc[:, 2 * LANES:] = second

    @pl.when(step > 0)
    def _():
        acc[:, 0:2 * LANES] += first
        acc[:, 2 * LANES:] += second

    @pl.when(step == pl.num_programs(0) - 1)
    def _():
        out[...] = acc[...].astype(HALF_TYPE)


def place_heads_kernel(bits, *refs):
    sources = refs[:4]
    query, key, value = refs[-3:]
    step = pl.program_id(0)
    part = step // 4
    x, low = bits[1], bits[3]
    wide = value.shape[1] // 4

    def put(block, head):
        at = pl.multiple_of(head * LANES, LANES)
        query[:, pl.ds(at, LANES)] = block[:, 0:LANES].astype(FULL_TYPE)
        key[:, pl.ds(at, LANES)] = block[:, LANES:2 * LANES].astype(FULL_TYPE)
        value[:, pl.ds(pl.multiple_of(head * wide, LANES), wide)] = block[:, 2 * LANES:].astype(FULL_TYPE)

    for y in range(2):

        @pl.when((part == 0) & ((step // 2) % 2 == y))
        def _(y=y):
            for i in range(2):
                for b in range(2):
                    put(sources[y][i, b, 0], (low ^ b) * 2 + (x ^ i))

    @pl.when(part == 1)
    def _():
        for i in range(2):
            for b in range(2):
                put(sources[2 + i][0, b, 0], (low ^ b) * 2 + (x ^ i))


def place_out_kernel(spot, mine, *rest):
    rest[-1][0] = mine[...].astype(FULL_TYPE)


def place_small_kernel(first, small, select, value, out, rows):
    low = small[...]

    def rows_of(count, start):
        hit = lane_ids((count, LANES), 1) == lane_ids((count, LANES), 0) + start
        return nt(hit.astype(FULL_TYPE).astype(HALF_TYPE), low)

    select[...] = rows_of(select.shape[0], first[0])
    value[...] = rows_of(value.shape[0], SELV)
    out[...] = rows_of(out.shape[0], SELO)
    spots = (lane_ids((8, LANES), 1) == lane_ids((8, LANES), 0) + 64) & (lane_ids((8, LANES), 0) < 4)
    rows[...] = nt(spots.astype(FULL_TYPE).astype(HALF_TYPE), low)


def place_experts_kernel(spots, mine, mine_y, *rest):
    up, down = rest[-2:]
    for i, ref in enumerate((mine, mine_y)):

        @pl.when(pl.program_id(0) == i)
        def _(ref=ref):
            up[...] = ref[0].astype(FULL_TYPE)
            down[...] = jnp.transpose(ref[1].astype(FULL_TYPE))


def output_kernel(after, b0, b1, b2, b3, out):
    out[...] = (
        after[...] + b0[...].astype(FULL_TYPE) + b1[...].astype(FULL_TYPE)
        + b2[...].astype(FULL_TYPE) + b3[...].astype(FULL_TYPE)
    ).astype(HALF_TYPE)


class Place:
    def __init__(self):
        self.wide = lax.axis_index("wide")
        self.narrow = lax.axis_index("narrow")
        self.z, self.x = self.wide // 2, self.wide % 2
        self.y, self.c = self.narrow // 2, self.narrow % 2
        self.high, self.low = self.z // 2, self.z % 2

    @staticmethod
    def pairs(move):
        every = []
        for z in range(4):
            for x in range(2):
                for y in range(2):
                    for c in range(2):
                        tz, tx, ty, tc = move(z, x, y, c)
                        every.append(((z * 2 + x) * 4 + y * 2 + c, (tz * 2 + tx) * 4 + ty * 2 + tc))
        return every

    def send(self, value, move):
        return lax.ppermute(value, ("wide", "narrow"), self.pairs(move))

    def swap_x(self, value):
        return self.send(value, lambda z, x, y, c: (z, 1 - x, y, c))

    def swap_y(self, value):
        return self.send(value, lambda z, x, y, c: (z, x, 1 - y, c))

    def swap_xy(self, value):
        return self.send(value, lambda z, x, y, c: (z, 1 - x, 1 - y, c))

    def swap_c(self, value):
        return self.send(value, lambda z, x, y, c: (z, x, y, 1 - c))

    def swap_low(self, value):
        return self.send(value, lambda z, x, y, c: (z ^ 1, x, y, c))

    def swap_high(self, value):
        return self.send(value, lambda z, x, y, c: (z ^ 2, x, y, c))


def pick(array, index):
    return lax.dynamic_index_in_dim(array, index, 0, keepdims=False)


def add(*terms):
    total = terms[0].astype(FULL_TYPE)
    for term in terms[1:]:
        total = total + term.astype(FULL_TYPE)
    return total.astype(HALF_TYPE)


def in_order(bit, mine, other):
    return jnp.stack([jnp.where(bit == 0, mine, other), jnp.where(bit == 0, other, mine)])


def tie(value, *others):
    return lax.optimization_barrier((value,) + others)[0]


def halve(bit, swap, value):
    return add(pick(value, bit), swap(pick(value, 1 - bit)))


def place_out(place, half, core, heads, begun):
    rows, cols = half.shape
    size = 2 * rows // heads
    more = begun or ()
    return call(
        place_out_kernel,
        shaped((heads, size, cols), FULL_TYPE),
        (place.c ^ core).reshape(1).astype(jnp.int32), half, *more,
        grid=(heads // 2,), prefetch=1,
        in_specs=[pl.BlockSpec((size, cols), lambda s, spot: (s, 0))] + [pl.BlockSpec(memory_space=pl.ANY)] * len(more),
        out_specs=pl.BlockSpec((1, size, cols), lambda s, spot: (spot[0] * (heads // 2) + s, 0, 0)),
        aliases={2 + i: i for i in range(len(more))},
    )


def place_experts(place, mine, mine_y, core, begun):
    width, local = mine.shape[1:]
    more = begun or ()
    return call(
        place_experts_kernel,
        (shaped((width, 4 * local), FULL_TYPE), shaped((4 * local, width), FULL_TYPE)),
        jnp.stack([place.narrow ^ core, place.narrow ^ core ^ 2]).astype(jnp.int32), mine, mine_y, *more,
        grid=(2,), prefetch=1,
        in_specs=[full(mine.shape)] * 2 + [pl.BlockSpec(memory_space=pl.ANY)] * len(more),
        out_specs=(
            pl.BlockSpec((width, local), lambda s, spots: (0, spots[s])),
            pl.BlockSpec((local, width), lambda s, spots: (spots[s], 0)),
        ),
        aliases={3 + i: i for i in range(len(more))},
    )


def place_heads(place, sources, core, heads, rows, begun):
    size, cols = sources[0].shape[3:]

    def block(j):
        part, y = j // 2, j % 2

        def at(s, bits):
            a = s % 2
            active = (s // 4) == part
            if part == 0:
                active = active & ((s // 2) % 2 == y)
                return (0, 0, jnp.where(active, a, 0), 0, 0)
            return (jnp.where(active, (s // 2) % 2, 0), 0, jnp.where(active, a, 0), 0, 0)

        return pl.BlockSpec((2 if part == 0 else 1, 2, 1, size, cols), at)

    def row_block(s, bits):
        part, i, a = s // 4, (s // 2) % 2, s % 2
        y, high = bits[0] ^ i, bits[2] ^ a
        inside = jnp.where(part == 0, y * 2 + high, high * 2 + y)
        return (((bits[4] ^ core) * 2 + part) * 4 + inside, 0)

    wide = cols - 2 * LANES
    more = () if begun is None else tuple(begun)
    return call(
        place_heads_kernel,
        (
            shaped((rows, heads * LANES), FULL_TYPE), shaped((rows, heads * LANES), FULL_TYPE),
            shaped((rows, heads * wide), FULL_TYPE),
        ),
        jnp.stack([place.y, place.x, place.high, place.low, place.c]).astype(jnp.int32), *sources, *more,
        grid=(8,), prefetch=1,
        in_specs=[block(j) for j in range(4)] + [pl.BlockSpec(memory_space=pl.ANY)] * len(more),
        out_specs=(
            pl.BlockSpec((size, heads * LANES), row_block), pl.BlockSpec((size, heads * LANES), row_block),
            pl.BlockSpec((size, heads * wide), row_block),
        ),
        aliases={5 + i: i for i in range(len(more))},
    )


def turn_tables(span, head_dim):
    half = head_dim // 2
    frequency = np.float32(10000.0) ** (-(np.arange(half).astype(np.float32) * np.float32(2.0) / np.float32(head_dim)))
    angles = np.arange(span).astype(np.float32)[:, None] * frequency[None, :].astype(np.float32)
    cosine, sine = np.cos(angles.astype(np.float64)), np.sin(angles.astype(np.float64))
    return (
        jnp.asarray(np.concatenate([cosine, cosine], axis=1).astype(np.float32)),
        jnp.asarray(np.concatenate([-sine, sine], axis=1).astype(np.float32)),
    )


def tuned_device(
    tokens, lengths, value_ids, out_ids, mlp_ids, w_query, w_key, w_value, w_out, sel_value, sel_out,
    gain_one, bias_one, gain_two, bias_two, w_select, w_up, w_down, cotangent,
):
    seqs, row_count, width = tokens.shape
    heads, head_dim = w_out.shape[0], w_out.shape[1]
    experts = w_out.shape[2] // width
    pair_count = seqs * heads
    span = 8 * row_count
    all_rows = seqs * row_count
    wide_out = heads * experts * LANES
    local = w_up.shape[1] // 4
    hidden = 8 * local
    own_count = w_select.shape[1]
    count = 8 * own_count
    quarter = count // 4
    tall = row_count + quarter
    place = Place()
    first_row = place.wide * row_count
    row = lambda v: v.reshape(1, -1)
    smem = pl.BlockSpec(memory_space=pltpu.SMEM)
    vmem = pl.BlockSpec(memory_space=pltpu.VMEM)
    hbm = pl.BlockSpec(memory_space=pl.ANY)
    by_seq = lambda shape: pl.BlockSpec((1,) + tuple(shape[1:]), lambda s: (s,) + (0,) * (len(shape) - 1))
    split = lambda shape: pl.BlockSpec((shape[0] // seqs,) + tuple(shape[1:]), lambda s: (s,) + (0,) * (len(shape) - 1))
    token_cols = lambda n: pl.BlockSpec((n, row_count), lambda s: (0, s))

    own_select = jnp.transpose(w_select).reshape(own_count, 8, -1).swapaxes(0, 1).reshape(-1, LANES)

    mine_peer = jnp.stack([place.narrow, place.narrow + 1 - 2 * place.c]).astype(jnp.int32)
    weights_mine, weights_peer = call(
        weights_kernel,
        (shaped((2, width, local)), shaped((2, width, local))),
        mine_peer, w_up, w_down,
        grid=(2,), prefetch=1,
        in_specs=[
            pl.BlockSpec((width, local), lambda s, spots: (0, spots[s])),
            pl.BlockSpec((local, width), lambda s, spots: (spots[s], 0)),
        ],
        out_specs=(full((2, width, local)), full((2, width, local))),
    )

    cot_own = cotangent.reshape(all_rows, width)
    cots = [cot_own, place.swap_y(cot_own)]
    tokens_x = place.swap_x(tokens)

    cosine, sine = turn_tables(span, head_dim)
    here = lambda t: lax.dynamic_slice_in_dim(t, first_row, row_count, 0)
    sel = jnp.concatenate(
        [
            jnp.zeros((width, SELV), HALF_TYPE), sel_value, sel_out,
            jnp.zeros((width, LANES - SELO - heads * experts), HALF_TYPE),
        ],
        axis=1,
    )
    value_flat = value_ids.reshape(seqs, row_count, -1)
    out_flat = out_ids.reshape(seqs, row_count, -1)
    payload = 3 * row_count + own_select.shape[0] + 16
    qkv, projected, gate = call(
        pre_kernel,
        (
            shaped((pair_count, payload, head_dim)),
            shaped((seqs, row_count, wide_out)),
            shaped((seqs, row_count, LANES), FULL_TYPE),
        ),
        tokens, row(gain_one), row(bias_one), w_query, w_key, w_value, sel, value_flat, out_flat,
        here(cosine), here(sine), own_select,
        grid=(seqs,),
        in_specs=[
            by_seq(tokens.shape), full((1, width)), full((1, width)), full(w_query.shape), full(w_key.shape),
            full(w_value.shape), full(sel.shape), by_seq(value_flat.shape), by_seq(out_flat.shape),
            full((row_count, head_dim)), full((row_count, head_dim)),
            full(own_select.shape),
        ],
        out_specs=(
            split((pair_count, payload, head_dim)), by_seq((seqs, row_count, wide_out)),
            by_seq((seqs, row_count, LANES)),
        ),
        flops=2 * all_rows * width * 3712,
    )
    qkv = lax.all_to_all(qkv, "wide", 0, 0, tiled=True)
    qkv, cots[1], tokens_x, weights_mine = lax.optimization_barrier((qkv, cots[1], tokens_x, weights_mine))
    weights_far, weights_near = place.swap_high(weights_mine), place.swap_low(weights_mine)
    cot_later = tie(cot_own, qkv)
    cots += [place.swap_x(cot_later), place.swap_xy(cot_later)]
    seq_here = place.wide // heads
    length = pick(lengths, seq_here).reshape(1)
    mixed, out_t, lse = call(
        attend_kernel,
        (
            shaped((8, row_count, head_dim)), shaped((head_dim, span), FULL_TYPE), shaped((1, span), FULL_TYPE),
        ),
        length, qkv,
        in_specs=[smem, vmem],
        flops=2 * span * span * head_dim,
    )
    mixed = lax.all_to_all(mixed, "wide", 0, 0, tiled=True)
    mixed, weights_far, weights_near, cots[2], cots[3] = lax.optimization_barrier(
        (mixed, weights_far, weights_near, cots[2], cots[3])
    )
    weights_last = place.swap_low(weights_far)

    kinds = (place.x * 2 + place.y) ^ jnp.arange(4)
    kx, ky = (kinds // 2)[:, None, None, None], (kinds % 2)[:, None, None, None]
    kz = (place.z ^ jnp.arange(4))[None, :, None, None]
    kc = (place.c ^ jnp.arange(2))[None, None, :, None]
    ki = jnp.arange(2)[None, None, None, :]
    sent_ids = ((kz * 2 + kx) * own_count + ky * 4 + kc * 2 + ki).reshape(-1)
    places = (sent_ids[:, None] == jnp.arange(count)[None, :]).astype(HALF_TYPE)

    own_mlp = lax.dynamic_slice_in_dim(mlp_ids, first_row, row_count, 1)
    own_mlp = jnp.swapaxes(own_mlp, 1, 2)
    after, gates, rows_own, select = call(
        post_kernel,
        (
            shaped((all_rows, width), FULL_TYPE), shaped((count, all_rows), FULL_TYPE), shaped((seqs, tall, width)),
            shaped((count, width)),
        ),
        mixed, gate, w_out, tokens, row(gain_two), row(bias_two), qkv, own_mlp, places,
        grid=(seqs,),
        in_specs=[
            split(mixed.shape), by_seq(gate.shape), full(w_out.shape), by_seq(tokens.shape), full((1, width)),
            full((1, width)), pl.BlockSpec((8, 8 * own_count, LANES), lambda s: (0, 3 * row_count // (8 * own_count), 0)),
            by_seq(own_mlp.shape), full(places.shape),
        ],
        out_specs=(
            split((all_rows, width)), token_cols(count), by_seq((seqs, tall, width)), full((count, width)),
        ),
        flops=2 * all_rows * width * wide_out,
    )

    rows_y, rows_x = place.swap_y(rows_own), place.swap_x(rows_own)
    rows_d = (place.swap_x(rows_y[0]), place.swap_y(rows_x[1]))
    rows_in = [(rows_own,), (rows_y,), (rows_x,), rows_d]
    weights = [weights_mine, weights_peer]
    for piece in (weights_near, weights_far, weights_last):
        weights += [piece, place.swap_c(piece)]
    own_two = jnp.stack([pick(tokens, seq_here), pick(tokens_x, seq_here)])
    other_two = jnp.stack([pick(tokens, 1 - seq_here), pick(tokens_x, 1 - seq_here)])
    other_two = place.swap_high(tie(other_two, rows_own))
    results = {}
    for i, before in ((1, None), (2, 1), (3, 2), (0, 3)):
        if before is not None:
            cots[i] = tie(cots[i], results[before][1])
        results[i] = call(
                functools.partial(experts_kernel, i, len(rows_in[i])),
                (
                    shaped((seqs, tall, width)), shaped((8, all_rows, local)), shaped((8, all_rows, local)),
                ),
                *rows_in[i], cots[i], *weights,
                flops=8 * all_rows * width * hidden,
            )
    swaps = (lambda v: v, place.swap_y, place.swap_x, place.swap_xy)
    d_rows = [swaps[i](results[i][0]) for i in range(4)]
    inners = [results[i][1] for i in range(4)]
    near_four = jnp.concatenate([own_two, tie(other_two, results[2][1])])
    far_four = place.swap_low(near_four)

    whole = lambda shape: pl.BlockSpec(tuple(shape), lambda p: (0,) * len(shape))
    piece = lambda: pl.BlockSpec((1, all_rows, local), lambda p: (2 * (2 * (p % 2) + (p // 2) % 2) + p // 4, 0, 0))
    grad_near, grad_far, peer_near, peer_far = call(
        expert_grads_kernel,
        (shaped((2, 2, width, local)),) * 4,
        rows_own, rows_y, rows_x, *rows_d, *cots, *[results[i][2] for i in range(4)], *inners,
        grid=(8,),
        in_specs=[whole((seqs, tall, width))] * 3 + [whole((tall, width))] * 2 + [whole((all_rows, width))] * 4
        + [piece() for _ in range(8)],
        out_specs=tuple(
            pl.BlockSpec((1, 2, width, local), lambda p, j=j: (jnp.clip(p - 2 * j, 0, 1), 0, 0, 0)) for j in range(4)
        ),
        flops=16 * all_rows * width * hidden,
    )
    d_rows[1], d_rows[2], d_rows[3], peer_far, peer_near, far_four = lax.optimization_barrier(
        (d_rows[1], d_rows[2], tie(d_rows[3], grad_near), peer_far, peer_near, far_four)
    )
    came_far, came_near = place.swap_c(peer_far), place.swap_c(peer_near)

    live_info = jnp.concatenate([jnp.zeros((1,), jnp.int32), first_row.reshape(1).astype(jnp.int32), lengths])
    d_after, d_att, d_gate_out, small = call(
        mid_kernel,
        (
            shaped((all_rows, width), FULL_TYPE), shaped((pair_count, row_count, head_dim)),
            shaped((seqs, row_count, LANES), FULL_TYPE), shaped((width, LANES), FULL_TYPE),
        ),
        live_info, *d_rows, cotangent, after, gates, row(gain_two), row(bias_two), select, places,
        w_out, gate, mixed,
        grid=(seqs,),
        in_specs=[smem] + [by_seq((seqs, tall, width))] * 4 + [
            by_seq(cotangent.shape), split((all_rows, width)), token_cols(count), full((1, width)), full((1, width)),
            full(select.shape), full(places.shape), full(w_out.shape), by_seq(gate.shape),
            split(mixed.shape),
        ],
        out_specs=(
            split((all_rows, width)), split((pair_count, row_count, head_dim)),
            by_seq((seqs, row_count, LANES)), full((width, LANES)),
        ),
        scratch=[pltpu.VMEM((LANES, width), FULL_TYPE)],
        flops=2 * all_rows * width * wide_out,
    )
    d_att_all = lax.all_to_all(d_att, "wide", 0, 0, tiled=True)

    to_low = [add(grad_far[a], came_far[a]) for a in range(2)]
    passed = [None, place.swap_low(to_low[1])]
    passed[0] = place.swap_low(to_low[0])
    near_four = tie(near_four, d_att, *to_low)
    tok_t, norm_t = call(
        turn_kernel,
        (shaped((8, width, row_count)), shaped((8, width, row_count))),
        near_four, far_four, row(gain_one), row(bias_one),
        grid=(8,),
        in_specs=[
            pl.BlockSpec((1, row_count, width), lambda i: (jnp.minimum(i, 3), 0, 0)),
            pl.BlockSpec((1, row_count, width), lambda i: (jnp.maximum(i - 4, 0), 0, 0)),
            full((1, width)), full((1, width)),
        ],
        out_specs=(
            pl.BlockSpec((1, width, row_count), lambda i: (i, 0, 0)),
            pl.BlockSpec((1, width, row_count), lambda i: (i, 0, 0)),
        ),
    )
    grad_out = call(
        out_grad_kernel, shaped((heads * head_dim, experts * width)), tie(mixed, d_att, came_near, came_far), gate, d_after,
        flops=2 * all_rows * width * wide_out,
    )
    rows_out, cols_out = grad_out.shape
    flat = ((place.y, place.swap_y), (place.x, place.swap_x))
    out_parts = halve(place.c, place.swap_c, grad_out.reshape(2, 2, 2, 2, 2, 2, rows_out // 64, cols_out))

    d_att_all, tok_t, out_parts = lax.optimization_barrier((d_att_all, tok_t, out_parts))
    out_parts = [halve(*flat[i], out_parts[i]) for i in range(2)]
    d_qkv = call(
        attend_back_kernel,
        shaped((8, 3 * row_count, head_dim)),
        length, qkv, d_att_all, out_t, lse, cosine, sine,
        in_specs=[smem] + [vmem] * 6,
        scratch=[pltpu.VMEM((span, head_dim), FULL_TYPE), pltpu.VMEM((span, head_dim), FULL_TYPE)],
        flops=5 * span * span * head_dim,
    )

    d_qkv, out_parts[0], out_parts[1] = lax.optimization_barrier((d_qkv, *out_parts))
    out_parts = [halve(*flat[1 - i], out_parts[i]) for i in range(2)]

    block_of = lambda i, spot: spot[0] ^ ((i & 1) | ((i & 2) << 1) | ((i & 4) >> 1))
    head_cols = (2 + experts) * LANES
    head_grads = call(
        head_grads_kernel,
        shaped((width, head_cols)),
        place.wide.reshape(1).astype(jnp.int32), tok_t, norm_t, d_qkv, qkv,
        grid=(8,), prefetch=1,
        in_specs=[
            pl.BlockSpec((1, width, row_count), lambda i, spot: (i, 0, 0)),
            pl.BlockSpec((1, width, row_count), lambda i, spot: (i, 0, 0)),
            pl.BlockSpec((1, 3 * row_count, head_dim), lambda i, spot: (block_of(i, spot), 0, 0)),
            pl.BlockSpec((1, 16, head_dim), lambda i, spot: (block_of(i, spot), payload // 16 - 1, 0)),
        ],
        out_specs=pl.BlockSpec((width, head_cols), lambda i, spot: (0, 0)),
        scratch=[pltpu.VMEM((width, head_cols), FULL_TYPE)],
        flops=2 * span * width * head_cols,
    )
    d_qkv_rows = lax.all_to_all(d_qkv, "wide", 0, 0, tiled=True)
    bits = ((place.y, place.swap_y), (place.high, place.swap_high))
    rows_head = width // 16
    head_grads, out_sum, passed[0], passed[1] = lax.optimization_barrier((head_grads, jnp.stack(out_parts, axis=2), *passed))
    kept = halve(place.c, place.swap_c, head_grads.reshape(2, 2, 2, 2, rows_head, head_cols))
    out_sum = halve(place.low, place.swap_low, out_sum)
    kept = tie(kept, d_qkv)
    branches = call(
        branch_kernel,
        (shaped((all_rows, width)),) * 4,
        tie(inners[0], kept), *inners[1:], *weights,
        flops=8 * all_rows * width * hidden,
    )
    b0, b1, b2, b3 = branches
    value = [halve(*bits[i], kept[i]) for i in range(2)]
    value[0], value[1], d_qkv_rows, out_sum, b1, b2, b3 = lax.optimization_barrier(
        (value[0], value[1], d_qkv_rows, out_sum, b1, b2, b3)
    )
    b1, b2 = place.swap_y(b1), place.swap_x(b2)
    value = [halve(*bits[1 - i], value[i]) for i in range(2)]
    out_sum = halve(place.high, place.swap_high, out_sum)
    grad_tokens, small = call(
        last_kernel,
        (shaped((all_rows, width)), shaped((width, LANES))),
        d_qkv_rows, tokens, row(gain_one), row(bias_one), w_query, w_key, w_value, sel, projected, gate, d_gate_out,
        small, d_after,
        grid=(seqs,),
        in_specs=[
            split(d_qkv.shape), by_seq(tokens.shape), full((1, width)), full((1, width)), full(w_query.shape),
            full(w_key.shape), full(w_value.shape), full(sel.shape), by_seq(projected.shape), by_seq(gate.shape),
            by_seq(d_gate_out.shape), full(small.shape), split(d_after.shape),
        ],
        out_specs=(split((all_rows, width)), full((width, LANES))),
        scratch=[pltpu.VMEM((row_count, wide_out), HALF_TYPE), pltpu.VMEM((width, LANES), FULL_TYPE)],
        flops=2 * all_rows * width * 3712,
    )
    done, small, out_sum = lax.optimization_barrier((jnp.stack(value), small, out_sum))
    mine = add(grad_near[0], came_near[0], passed[0])
    far = place.swap_high(done)
    out_sum = in_order(place.high, out_sum, place.swap_high(out_sum))
    everywhere = ("wide", "narrow")
    small = lax.all_to_all(small, everywhere, 0, 0, tiled=True).reshape(32, -1, LANES)
    far, out_sum, b1, b2, b3 = lax.optimization_barrier((far, out_sum, b1, b2, b3))
    b3 = place.swap_xy(b3)
    out_sum = in_order(place.low, out_sum, place.swap_low(out_sum))
    near = [place.swap_low(done), place.swap_low(far)]
    sets = [
        jnp.stack([jnp.stack([done[i], far[i]]), jnp.stack([near[0][i], near[1][i]])]) for i in range(2)
    ]
    to_high = add(grad_near[1], came_near[1], passed[1])
    sets[0], sets[1], small, out_sum, b3, to_high = lax.optimization_barrier(
        (sets[0], sets[1], small, out_sum, b3, to_high)
    )
    mine_far = place.swap_high(to_high)
    small = jnp.sum(small.astype(FULL_TYPE), axis=0).astype(HALF_TYPE)
    small = lax.all_to_all(jnp.broadcast_to(small[None], (32,) + small.shape), everywhere, 0, 0, tiled=True)
    back = [in_order(flat[1 - i][0], out_sum[:, :, i], flat[1 - i][1](out_sum[:, :, i])) for i in range(2)]
    first = jnp.stack([sets[0], place.swap_x(sets[0])])
    second = jnp.stack([sets[1], place.swap_y(sets[1])])
    first, second, back[0], back[1] = lax.optimization_barrier((first, second, *back))
    sources = [first, place.swap_y(first), second, place.swap_x(second)]
    back = [in_order(flat[i][0], back[i], flat[i][1](back[i])) for i in range(2)]
    out_half = jnp.stack(back).reshape(rows_out // 2, cols_out)
    output = call(output_kernel, shaped((all_rows, width)), after, b0, b1, b2, b3)
    small = small.reshape(width, LANES)
    grad_select, grad_sel_value, grad_sel_out, rows_four = call(
        place_small_kernel,
        (
            shaped((own_count, width), FULL_TYPE), shaped((heads * experts, width), FULL_TYPE),
            shaped((heads * experts, width), FULL_TYPE), shaped((8, width), FULL_TYPE),
        ),
        (place.wide * own_count).reshape(1).astype(jnp.int32), small,
        in_specs=[smem, vmem],
    )
    peers = [place.swap_c(first), None, place.swap_c(second), None]
    (sources[1], sources[3], peers[0], peers[2], output, out_half, mine_far, grad_select, grad_sel_value,
     grad_sel_out, rows_four) = lax.optimization_barrier(
        (sources[1], sources[3], peers[0], peers[2], output, out_half, mine_far, grad_select, grad_sel_value,
         grad_sel_out, rows_four)
    )
    mine = add(mine, mine_far)
    mine_y = place.swap_y(mine)
    peers[1], peers[3] = place.swap_c(sources[1]), place.swap_c(sources[3])
    out_peer = place.swap_c(out_half)
    grad_heads = place_heads(place, sources, 0, heads, width, None)
    grad_out = place_out(place, out_half, 0, heads, None)
    grad_heads = lax.optimization_barrier((*grad_heads, grad_out, *peers, out_peer, mine_y))
    grad_heads, grad_out, peers, out_peer, mine_y = (
        grad_heads[:3], grad_heads[3], grad_heads[4:8], grad_heads[8], grad_heads[9]
    )
    mine_c, mine_yc = place.swap_c(mine), place.swap_c(mine_y)
    grad_experts = place_experts(place, mine, mine_y, 0, None)
    grad_query, grad_key, grad_value = place_heads(place, list(peers), 1, heads, width, grad_heads)
    grad_out = place_out(place, out_peer, 1, heads, (grad_out,))
    grad_up, grad_down = place_experts(place, mine_c, mine_yc, 1, grad_experts)
    grad_select, grad_sel_value, grad_sel_out = grad_select.T, grad_sel_value.T, grad_sel_out.T
    grad_gain_two, grad_bias_two, grad_gain_one, grad_bias_one = (rows_four[i] for i in range(4))
    return (
        output.reshape(tokens.shape), grad_tokens.reshape(tokens.shape), grad_query, grad_key, grad_value, grad_out,
        grad_sel_value, grad_sel_out, grad_gain_one, grad_bias_one, grad_gain_two, grad_bias_two, grad_select,
        grad_up, grad_down,
    )


def fits(mesh):
    return dict(mesh.shape) == {"wide": 8, "narrow": 4}


def solution(mesh):
    placed = (
        P("narrow", "wide", None),
        P("narrow"),
        P("narrow", "wide", None, None),
        P("narrow", "wide", None, None),
        P("narrow", None, None),
        P(),
        P(),
        P(),
        P(),
        P(),
        P(),
        P(),
        P(),
        P(),
        P(),
        P(None, "wide"),
        P(None, "wide"),
        P("wide", None),
        P("narrow", "wide", None),
    )
    return jax.shard_map(
        tuned_device if fits(mesh) else per_device,
        mesh=mesh,
        in_specs=placed,
        out_specs=(
            P("narrow", "wide", None),
            P("narrow", "wide", None),
            P(),
            P(),
            P(),
            P(),
            P(),
            P(),
            P(),
            P(),
            P(),
            P(),
            P(None, "wide"),
            P(None, "wide"),
            P("wide", None),
        ),
        check_vma=False,
    )
```

```python
import functools

import jax
import jax.numpy as jnp
import numpy as np
from jax import lax
from jax.experimental import pallas as pl
from jax.experimental.pallas import tpu as pltpu
from jax.sharding import PartitionSpec as P

EPSILON = 1e-05
FULL_TYPE = jnp.float32
HALF_TYPE = jnp.bfloat16


def for_sending(value):

    def short(part):
        return part.astype(jnp.bfloat16) if part.dtype == jnp.float32 else part

    return jax.tree.map(short, value)


def norm_parts(values_in, gain, bias):
    row_mean = jnp.mean(values_in, axis=-1, keepdims=True)
    centred = values_in - row_mean
    inv_scale = lax.rsqrt(jnp.mean(centred * centred, axis=-1, keepdims=True) + EPSILON)
    normal = centred * inv_scale
    return (normal * gain + bias, normal, inv_scale)


def norm_back(grad_in, normal, inv_scale, gain):
    scaled = grad_in * gain
    return inv_scale * (
        scaled
        - jnp.mean(scaled, axis=-1, keepdims=True)
        - normal * jnp.mean(scaled * normal, axis=-1, keepdims=True)
    )


def rotate(values_in, positions, turn):
    half_dim = values_in.shape[-1] // 2
    frequency = 10000.0 ** (-(jnp.arange(half_dim).astype(FULL_TYPE) * 2.0 / values_in.shape[-1]))
    angles = positions.astype(FULL_TYPE)[:, None] * frequency[None, :]
    cosine = jnp.cos(angles)[:, None, :]
    sine_part = turn * jnp.sin(angles)[:, None, :]
    front_half = values_in[..., :half_dim]
    back_half = values_in[..., half_dim:]
    return jnp.concatenate(
        [front_half * cosine - back_half * sine_part, front_half * sine_part + back_half * cosine],
        axis=-1,
    )


def one_hot_sum(ids, wanted):
    return jnp.sum((ids[..., None] == wanted).astype(FULL_TYPE), axis=-2)


def matmul(left_op, right_op):
    return jnp.dot(left_op, right_op, preferred_element_type=FULL_TYPE)


def contract_rows(left_op, right_op):
    left_flat = left_op.reshape(-1, left_op.shape[-1])
    right_flat = right_op.reshape(-1, right_op.shape[-1])
    return lax.dot_general(
        left_flat, right_flat, (((0,), (0,)), ((), ())), preferred_element_type=FULL_TYPE
    )


def times_transpose(grad_in, weight):
    return lax.dot_general(
        grad_in, weight, (((grad_in.ndim - 1,), (1,)), ((), ())), preferred_element_type=FULL_TYPE
    )


def attend_forward(
    tokens,
    lengths,
    value_ids,
    out_ids,
    w_query,
    w_key,
    w_value,
    w_out,
    sel_value,
    sel_out,
    gain_one,
    bias_one,
    gain_two,
    bias_two,
):
    seq_count, row_count, model_width = tokens.shape
    head_count = w_out.shape[0]
    head_dim = w_out.shape[1]
    value_experts = sel_value.shape[1] // head_count
    positions = lax.axis_index("wide") * row_count + jnp.arange(row_count, dtype=jnp.int32)
    inputs = tokens.astype(FULL_TYPE)
    normed, normal_one, scale_one = norm_parts(inputs, gain_one, bias_one)
    normed_low = normed.astype(HALF_TYPE)
    query_pre = matmul(normed_low, w_query).reshape(seq_count, row_count, head_count, head_dim)
    key_pre = matmul(normed_low, w_key).reshape(seq_count, row_count, head_count, head_dim)
    queries = rotate(query_pre, positions, 1.0).astype(HALF_TYPE)
    key_low = rotate(key_pre, positions, 1.0).astype(HALF_TYPE)
    expert_ids = jnp.arange(value_experts, dtype=jnp.int32)
    value_choice = one_hot_sum(value_ids, expert_ids)
    value_sig = jax.nn.sigmoid(
        matmul(normed_low, sel_value).reshape(seq_count, row_count, head_count, value_experts)
    )
    value_gate = value_sig * value_choice
    projected = matmul(tokens, w_value).reshape(
        seq_count, row_count, head_count, value_experts, head_dim
    )
    values = jnp.sum(value_gate[..., None] * projected, axis=3).astype(HALF_TYPE)
    keys_all, values_all = (
        lax.all_gather(key_low, "wide", axis=1, tiled=True),
        lax.all_gather(values, "wide", axis=1, tiled=True),
    )
    span = keys_all.shape[1]
    key_pos = jnp.arange(span, dtype=jnp.int32)
    allowed = (key_pos[None, None, None, :] <= positions[None, None, :, None]) & (
        key_pos[None, None, None, :] < lengths[:, None, None, None]
    )
    scores = jnp.einsum(
        "bphc,bshc->bhps", queries, keys_all, preferred_element_type=FULL_TYPE
    ) * head_dim ** (-0.5)
    masked = jnp.where(allowed, scores, -1e30)
    row_max = jnp.max(masked, axis=-1, keepdims=True)
    exponent = jnp.exp(masked - row_max)
    row_total = jnp.sum(exponent, axis=-1, keepdims=True)
    attn_probs = exponent / row_total
    log_total = row_max + jnp.log(row_total)
    attended = jnp.einsum(
        "bhps,bshc->bphc",
        attn_probs.astype(HALF_TYPE),
        values_all,
        preferred_element_type=FULL_TYPE,
    )
    live_rows = (positions[None, :] < lengths[:, None]).astype(FULL_TYPE)[:, :, None, None]
    mixed_out = (attended * live_rows).astype(HALF_TYPE)
    out_choice = one_hot_sum(out_ids, expert_ids)
    out_sig = jax.nn.sigmoid(
        matmul(normed_low, sel_out).reshape(seq_count, row_count, head_count, value_experts)
    )
    out_gate = out_sig * out_choice
    expert_out = jnp.einsum(
        "bphc,hcf->bphf", mixed_out, w_out, preferred_element_type=FULL_TYPE
    ).reshape(seq_count, row_count, head_count, value_experts, model_width)
    after_attn = inputs + jnp.sum(out_gate[..., None] * expert_out, axis=(2, 3))
    normed_two, normal_two, scale_two = norm_parts(after_attn, gain_two, bias_two)
    return dict(
        positions=positions,
        normal_one=normal_one,
        scale_one=scale_one,
        normed_low=normed_low,
        queries=queries,
        keys_all=keys_all,
        values_all=values_all,
        allowed=allowed,
        log_total=log_total,
        live_rows=live_rows,
        mixed_out=mixed_out,
        value_choice=value_choice,
        value_sig=value_sig,
        value_gate=value_gate,
        projected=projected,
        out_choice=out_choice,
        out_sig=out_sig,
        out_gate=out_gate,
        expert_out=expert_out,
        after_attn=after_attn,
        normed_two=normed_two,
        normal_two=normal_two,
        scale_two=scale_two,
    )


def expert_forward(after_attn, normed_two, mlp_ids, w_select, w_up):
    rows_all, normed_all = (
        lax.all_gather(for_sending(after_attn.astype(HALF_TYPE)), "wide", axis=1, tiled=True),
        lax.all_gather(for_sending(normed_two.astype(HALF_TYPE)), "wide", axis=1, tiled=True),
    )
    local_count = w_select.shape[1]
    hidden = w_up.shape[1] // local_count
    seq_count, span = (rows_all.shape[0], rows_all.shape[1])
    owned_ids = lax.axis_index("wide") * local_count + jnp.arange(local_count, dtype=jnp.int32)
    chosen = one_hot_sum(mlp_ids, owned_ids)
    sigmoid_gate = jax.nn.sigmoid(matmul(normed_all, w_select))
    mlp_gate = sigmoid_gate * chosen
    pre_act = matmul(rows_all, w_up)
    activated = jax.nn.gelu(pre_act).reshape(seq_count, span, local_count, hidden)
    inner_low = (
        (activated * mlp_gate[..., None])
        .reshape(seq_count, span, local_count * hidden)
        .astype(HALF_TYPE)
    )
    return dict(
        rows_all=rows_all,
        normed_all=normed_all,
        chosen=chosen,
        sigmoid_gate=sigmoid_gate,
        mlp_gate=mlp_gate,
        pre_act=pre_act,
        activated=activated,
        inner_low=inner_low,
    )


def per_device(
    tokens,
    lengths,
    value_ids,
    out_ids,
    mlp_ids,
    w_query,
    w_key,
    w_value,
    w_out,
    sel_value,
    sel_out,
    gain_one,
    bias_one,
    gain_two,
    bias_two,
    w_select,
    w_up,
    w_down,
    cotangent,
):
    seq_count, row_count, model_width = tokens.shape
    head_count = w_out.shape[0]
    head_dim = w_out.shape[1]
    value_experts = sel_value.shape[1] // head_count
    saved = attend_forward(
        tokens,
        lengths,
        value_ids,
        out_ids,
        w_query,
        w_key,
        w_value,
        w_out,
        sel_value,
        sel_out,
        gain_one,
        bias_one,
        gain_two,
        bias_two,
    )
    expert_state = expert_forward(saved["after_attn"], saved["normed_two"], mlp_ids, w_select, w_up)
    branch_part = matmul(expert_state["inner_low"], w_down)
    branch_sum = lax.psum_scatter(
        branch_part.astype(jnp.bfloat16), "wide", scatter_dimension=1, tiled=True
    ).astype(jnp.float32)
    output = (saved["after_attn"] + branch_sum).astype(HALF_TYPE)
    saved = attend_forward(
        tokens,
        lengths,
        value_ids,
        out_ids,
        w_query,
        w_key,
        w_value,
        w_out,
        sel_value,
        sel_out,
        gain_one,
        bias_one,
        gain_two,
        bias_two,
    )
    expert_state = expert_forward(saved["after_attn"], saved["normed_two"], mlp_ids, w_select, w_up)
    cot_all = lax.all_gather(cotangent, "wide", axis=1, tiled=True)
    grad_down = contract_rows(expert_state["inner_low"], cot_all)
    d_inner = times_transpose(cot_all, w_down)
    activated = expert_state["activated"]
    d_inner_four = d_inner.reshape(activated.shape)
    d_mlp_gate = jnp.sum(d_inner_four * activated, axis=-1)
    mlp_gate = expert_state["mlp_gate"]
    gated_grad = (d_inner_four * mlp_gate[..., None]).reshape(expert_state["pre_act"].shape)
    unused_value, gelu_pull = jax.vjp(jax.nn.gelu, expert_state["pre_act"])
    d_pre = gelu_pull(gated_grad)[0].astype(HALF_TYPE)
    sigmoid_gate = expert_state["sigmoid_gate"]
    d_logit = (d_mlp_gate * expert_state["chosen"] * sigmoid_gate * (1.0 - sigmoid_gate)).astype(
        HALF_TYPE
    )
    grad_up = contract_rows(expert_state["rows_all"], d_pre)
    grad_select = contract_rows(expert_state["normed_all"], d_logit)
    row_part = times_transpose(d_pre, w_up)
    norm_part = times_transpose(d_logit, w_select)
    row_grad, norm_grad = (
        lax.psum_scatter(row_part, "wide", scatter_dimension=1, tiled=True),
        lax.psum_scatter(norm_part, "wide", scatter_dimension=1, tiled=True),
    )
    grad_gain_two = jnp.sum(norm_grad * saved["normal_two"], axis=(0, 1))
    grad_bias_two = jnp.sum(norm_grad, axis=(0, 1))
    d_after = (
        cotangent.astype(FULL_TYPE)
        + row_grad
        + norm_back(norm_grad, saved["normal_two"], saved["scale_two"], gain_two)
    )
    out_gate = saved["out_gate"]
    d_expert = (out_gate[..., None] * d_after[:, :, None, None, :]).astype(HALF_TYPE)
    d_out_gate = jnp.sum(saved["expert_out"] * d_after[:, :, None, None, :], axis=-1)
    d_expert_flat = d_expert.reshape(seq_count, row_count, head_count, value_experts * model_width)
    grad_out = jnp.einsum(
        "bphc,bphf->hcf", saved["mixed_out"], d_expert_flat, preferred_element_type=FULL_TYPE
    )
    d_mixed = jnp.einsum("bphf,hcf->bphc", d_expert_flat, w_out, preferred_element_type=FULL_TYPE)
    d_attended = (d_mixed * saved["live_rows"]).astype(HALF_TYPE)
    out_sig = saved["out_sig"]
    d_out_logit = (
        (d_out_gate * saved["out_choice"] * out_sig * (1.0 - out_sig))
        .astype(HALF_TYPE)
        .reshape(seq_count, row_count, head_count * value_experts)
    )
    queries = saved["queries"]
    keys_all = saved["keys_all"]
    values_all = saved["values_all"]
    score_scale = head_dim ** (-0.5)
    scores = (
        jnp.einsum("bphc,bshc->bhps", queries, keys_all, preferred_element_type=FULL_TYPE)
        * score_scale
    )
    attn_probs = jnp.where(saved["allowed"], jnp.exp(scores - saved["log_total"]), 0.0)
    d_values_part = jnp.einsum(
        "bhps,bphc->bshc",
        attn_probs.astype(HALF_TYPE),
        d_attended,
        preferred_element_type=FULL_TYPE,
    )
    d_probs = jnp.einsum(
        "bphc,bshc->bhps", d_attended, values_all, preferred_element_type=FULL_TYPE
    )
    row_inner = jnp.sum(attn_probs * d_probs, axis=-1, keepdims=True)
    d_scores = (attn_probs * (d_probs - row_inner)).astype(HALF_TYPE)
    d_queries = (
        jnp.einsum("bhps,bshc->bphc", d_scores, keys_all, preferred_element_type=FULL_TYPE)
        * score_scale
    )
    d_keys_part = (
        jnp.einsum("bhps,bphc->bshc", d_scores, queries, preferred_element_type=FULL_TYPE)
        * score_scale
    )
    d_keys, d_values = (
        lax.psum_scatter(
            d_keys_part.astype(jnp.bfloat16), "wide", scatter_dimension=1, tiled=True
        ).astype(jnp.float32),
        lax.psum_scatter(
            d_values_part.astype(jnp.bfloat16), "wide", scatter_dimension=1, tiled=True
        ).astype(jnp.float32),
    )
    positions = saved["positions"]
    d_query_pre = (
        rotate(d_queries, positions, -1.0)
        .astype(HALF_TYPE)
        .reshape(seq_count, row_count, head_count * head_dim)
    )
    d_key_pre = (
        rotate(d_keys, positions, -1.0)
        .astype(HALF_TYPE)
        .reshape(seq_count, row_count, head_count * head_dim)
    )
    d_projected = (
        (saved["value_gate"][..., None] * d_values[:, :, :, None, :])
        .astype(HALF_TYPE)
        .reshape(seq_count, row_count, head_count * value_experts * head_dim)
    )
    d_value_gate = jnp.sum(saved["projected"] * d_values[:, :, :, None, :], axis=-1)
    value_sig = saved["value_sig"]
    d_value_logit = (
        (d_value_gate * saved["value_choice"] * value_sig * (1.0 - value_sig))
        .astype(HALF_TYPE)
        .reshape(seq_count, row_count, head_count * value_experts)
    )
    normed_low = saved["normed_low"]
    grad_query = contract_rows(normed_low, d_query_pre)
    grad_key = contract_rows(normed_low, d_key_pre)
    grad_sel_value = contract_rows(normed_low, d_value_logit)
    grad_sel_out = contract_rows(normed_low, d_out_logit)
    grad_value = contract_rows(tokens, d_projected)
    d_normed = (
        times_transpose(d_query_pre, w_query)
        + times_transpose(d_key_pre, w_key)
        + times_transpose(d_value_logit, sel_value)
        + times_transpose(d_out_logit, sel_out)
    )
    grad_gain_one = jnp.sum(d_normed * saved["normal_one"], axis=(0, 1))
    grad_bias_one = jnp.sum(d_normed, axis=(0, 1))
    grad_tokens = (
        d_after
        + times_transpose(d_projected, w_value)
        + norm_back(d_normed, saved["normal_one"], saved["scale_one"], gain_one)
    ).astype(HALF_TYPE)
    (
        grad_query,
        grad_key,
        grad_value,
        grad_out,
        grad_sel_value,
        grad_sel_out,
        grad_gain_one,
        grad_bias_one,
        grad_gain_two,
        grad_bias_two,
    ) = lax.psum(
        (
            grad_query,
            grad_key,
            grad_value,
            grad_out,
            grad_sel_value,
            grad_sel_out,
            grad_gain_one,
            grad_bias_one,
            grad_gain_two,
            grad_bias_two,
        ),
        ("wide", "narrow"),
    )
    grad_select, grad_up, grad_down = (
        lax.psum(grad_select.astype(jnp.bfloat16), "narrow").astype(jnp.float32),
        lax.psum(grad_up.astype(jnp.bfloat16), "narrow").astype(jnp.float32),
        lax.psum(grad_down.astype(jnp.bfloat16), "narrow").astype(jnp.float32),
    )
    return (
        output,
        grad_tokens,
        grad_query,
        grad_key,
        grad_value,
        grad_out,
        grad_sel_value,
        grad_sel_out,
        grad_gain_one,
        grad_bias_one,
        grad_gain_two,
        grad_bias_two,
        grad_select,
        grad_up,
        grad_down,
    )


SELV = 72
SELO = 92
LANES = 128


def call(
    kernel, out_shape, *args, grid=None, in_specs=None, out_specs=None, scratch=(), flops=0, limit=56, prefetch=0, aliases=None
):
    moved = sum(a.size * a.dtype.itemsize for a in jax.tree.leaves((args, out_shape)))
    extra = {}
    if prefetch:
        extra["grid_spec"] = pltpu.PrefetchScalarGridSpec(
            num_scalar_prefetch=prefetch, grid=grid, in_specs=in_specs, out_specs=out_specs, scratch_shapes=list(scratch)
        )
    else:
        extra["scratch_shapes"] = list(scratch)
        if grid is not None:
            extra["grid"] = grid
        if in_specs is not None:
            extra["in_specs"] = in_specs
        if out_specs is not None:
            extra["out_specs"] = out_specs
    return pl.pallas_call(
        kernel,
        out_shape=out_shape,
        input_output_aliases=aliases or {},
        compiler_params=pltpu.CompilerParams(vmem_limit_bytes=limit * 1024 * 1024),
        cost_estimate=pl.CostEstimate(flops=int(flops), bytes_accessed=int(moved), transcendentals=0),
        **extra,
    )(*args)


def full(shape):
    rank = len(shape)
    return pl.BlockSpec(tuple(shape), lambda *s: (0,) * rank)


def shaped(shape, dtype=HALF_TYPE):
    return jax.ShapeDtypeStruct(tuple(shape), dtype)


def nn(a, b):
    return lax.dot_general(a, b, (((1,), (0,)), ((), ())), preferred_element_type=FULL_TYPE)


def nt(a, b):
    return lax.dot_general(a, b, (((1,), (1,)), ((), ())), preferred_element_type=FULL_TYPE)


def tn(a, b):
    return lax.dot_general(a, b, (((0,), (0,)), ((), ())), preferred_element_type=FULL_TYPE)


def layer_stats(v):
    centred = v - jnp.mean(v, axis=-1, keepdims=True)
    inv = lax.rsqrt(jnp.mean(centred * centred, axis=-1, keepdims=True) + EPSILON)
    return centred * inv, inv


def turned(v, cos, sin):
    return v * cos + pltpu.roll(v, v.shape[-1] // 2, axis=v.ndim - 1) * sin


def lane_ids(shape, dim):
    return lax.broadcasted_iota(jnp.int32, shape, dim)


def pre_kernel(tok, gain, bias, wq, wk, wv, sel, vid, oid, cos, sin, select, qkv, proj, gate):
    heads = qkv.shape[0]
    experts = wv.shape[1] // (heads * LANES)
    low = tok[0]
    rows = low.shape[0]
    normal, _ = layer_stats(low.astype(FULL_TYPE))
    normed = (normal * gain[...] + bias[...]).astype(HALF_TYPE)
    for part, weight in ((0, wq), (1, wk)):
        pre = nn(normed, weight[...])
        for h in range(heads):
            head = turned(pre[:, h * LANES:(h + 1) * LANES], cos[...], sin[...])
            qkv[h, part * rows:(part + 1) * rows] = head.astype(HALF_TYPE)
    lanes = lane_ids((rows, LANES), 1)
    chosen = jnp.zeros((rows, LANES), FULL_TYPE)
    tops = vid.shape[2] // heads
    for h in range(heads):
        for k in range(tops):
            j = h * tops + k
            chosen += (lanes == vid[0, :, j:j + 1] + (SELV + experts * h)).astype(FULL_TYPE)
            chosen += (lanes == oid[0, :, j:j + 1] + (SELO + experts * h)).astype(FULL_TYPE)
    gates = jax.nn.sigmoid(nn(normed, sel[...])) * chosen
    gate[0] = gates
    gates_low = gates.astype(HALF_TYPE)
    for h in range(heads):
        at = h * experts * LANES
        block = nn(low, wv[:, at:at + experts * LANES])
        proj[0, :, at:at + experts * LANES] = block.astype(HALF_TYPE)
        total = None
        for e in range(experts):
            col = SELV + h * experts + e
            term = gates[:, col:col + 1] * block[:, e * LANES:(e + 1) * LANES]
            total = term if total is None else total + term
        qkv[h, 2 * rows:3 * rows] = total.astype(HALF_TYPE)
        first = SELV + h * experts
        row_id = lane_ids((8, LANES), 0)
        spot = (lane_ids((8, LANES), 1) == row_id + first) & (row_id < experts)
        turned_gates = nt(spot.astype(FULL_TYPE).astype(HALF_TYPE), gates_low)
        tail = jnp.concatenate([turned_gates[:, i * LANES:(i + 1) * LANES] for i in range(rows // LANES)], axis=0)
        last = 3 * rows + select.shape[0]
        qkv[h, 3 * rows:last] = select[...]
        qkv[h, last:last + tail.shape[0]] = tail.astype(HALF_TYPE)


def limits_of(i, rows, length):
    position = i * rows + lane_ids((1, rows), 1)
    return jnp.minimum(position + 1, length), position


def parts_of(ref, first, last, part, rows):
    block = ref[first:last, part * rows:(part + 1) * rows]
    return block.reshape((last - first) * rows, block.shape[2])


def attend_kernel(length, qkv, mixed, out_t, lse):
    blocks, rows, width = mixed.shape
    scale = width ** (-0.5)
    values_t = jnp.transpose(parts_of(qkv, 0, blocks, 2, rows).astype(FULL_TYPE)).astype(HALF_TYPE)
    for i in range(blocks):
        n = (i + 1) * rows
        keys = parts_of(qkv, 0, i + 1, 1, rows)
        limit, position = limits_of(i, rows, length[0])
        scores = nt(keys, qkv[i, 0:rows]) * scale
        scores = jnp.where(lane_ids((n, rows), 0) < limit, scores, -1e30)
        top = jnp.max(scores, axis=0, keepdims=True)
        weights = jnp.exp(scores - top)
        total = jnp.sum(weights, axis=0, keepdims=True)
        attended = nn(values_t[:, :n], weights.astype(HALF_TYPE)) / total
        out_t[:, i * rows:(i + 1) * rows] = attended
        lse[:, i * rows:(i + 1) * rows] = top + jnp.log(total)
        live = (position < length[0]).astype(FULL_TYPE)
        mixed[i] = jnp.transpose(attended * live).astype(HALF_TYPE)


def attend_back_kernel(length, qkv, d_out, out_t, lse, cos, sin, d_qkv, d_keys, d_values):
    blocks, rows, width = d_out.shape
    scale = width ** (-0.5)
    keys_t = jnp.transpose(parts_of(qkv, 0, blocks, 1, rows).astype(FULL_TYPE)).astype(HALF_TYPE)
    d_keys[...] = jnp.zeros_like(d_keys)
    d_values[...] = jnp.zeros_like(d_values)
    for i in range(blocks):
        n = (i + 1) * rows
        here = slice(i * rows, (i + 1) * rows)
        limit, _ = limits_of(i, rows, length[0])
        query = qkv[i, 0:rows]
        d_att = d_out[i]
        delta = jnp.sum(jnp.transpose(d_att.astype(FULL_TYPE)) * out_t[:, here], axis=0, keepdims=True)
        scores = nt(parts_of(qkv, 0, i + 1, 1, rows), query) * scale
        probs = jnp.where(lane_ids((n, rows), 0) < limit, jnp.exp(scores - lse[:, here]), 0.0)
        d_probs = nt(parts_of(qkv, 0, i + 1, 2, rows), d_att)
        d_scores = (probs * (d_probs - delta)).astype(HALF_TYPE)
        d_values[0:n, :] += nn(probs.astype(HALF_TYPE), d_att)
        d_keys[0:n, :] += nn(d_scores, query)
        d_query = jnp.transpose(nn(keys_t[:, :n], d_scores)) * scale
        d_qkv[i, 0:rows] = turned(d_query, cos[here, :], -sin[here, :]).astype(HALF_TYPE)
    for i in range(blocks):
        here = slice(i * rows, (i + 1) * rows)
        d_qkv[i, rows:2 * rows] = turned(d_keys[here, :] * scale, cos[here, :], -sin[here, :]).astype(HALF_TYPE)
        d_qkv[i, 2 * rows:3 * rows] = d_values[here, :].astype(HALF_TYPE)


def gated(mixed, gate, hp, e, experts):
    parts = []
    for h in (2 * hp, 2 * hp + 1):
        col = SELO + h * experts + e
        parts.append((gate[:, col:col + 1] * mixed[h].astype(FULL_TYPE)).astype(HALF_TYPE))
    return jnp.concatenate(parts, axis=1)


def out_block(w_out, hp, e, width):
    block = w_out[2 * hp:2 * hp + 2, :, e * width:(e + 1) * width]
    return block.reshape(2 * block.shape[1], width)


def post_kernel(mixed, gate, w_out, tok, gain, bias, columns, ids, places, after, gates, sent, select):
    width = tok.shape[2]
    heads = w_out.shape[0]
    experts = w_out.shape[2] // width
    row_count = tok.shape[1]
    total = tok[0].astype(FULL_TYPE)
    gate_here = gate[0]
    mixed_here = mixed[...]
    for hp in range(heads // 2):
        for e in range(experts):
            total += nn(gated(mixed_here, gate_here, hp, e, experts), out_block(w_out, hp, e, width))
    after[...] = total
    sent[0, 0:row_count] = total.astype(HALF_TYPE)
    normal, _ = layer_stats(total)
    normed = (normal * gain[...] + bias[...]).astype(HALF_TYPE)
    every = columns[...].astype(FULL_TYPE)
    count = every.shape[1]
    each = count // 8
    w_sel = jnp.concatenate(
        [every[:, j * each:(j + 1) * each].reshape(count, LANES) for j in range(8)], axis=1
    ).astype(HALF_TYPE)
    select[...] = w_sel
    row_id = lane_ids((count, row_count), 0)
    chosen = jnp.zeros((count, row_count), FULL_TYPE)
    for k in range(ids.shape[1]):
        chosen += (row_id == ids[0, k:k + 1, :]).astype(FULL_TYPE)
    values = jax.nn.sigmoid(nt(w_sel, normed)) * chosen
    gates[...] = values
    moved = nn(places[...], values.astype(HALF_TYPE)).astype(HALF_TYPE)
    quarter = count // 4
    for i in range(4):
        sent[0, row_count:row_count + quarter, i * row_count:(i + 1) * row_count] = moved[i * quarter:(i + 1) * quarter]


def weights_kernel(spots, up, down, mine, peer):
    for s, out in enumerate((mine, peer)):

        @pl.when(pl.program_id(0) == s)
        def _(out=out):
            out[0] = up[...]
            out[1] = jnp.transpose(down[...].astype(FULL_TYPE)).astype(HALF_TYPE)


def expand(count, cols, first):
    rows = lane_ids((count, cols), 0)
    cut = lane_ids((count, cols), 1)
    hit = None
    for i in range(cols // LANES):
        inside = (cut >= i * LANES) & (cut < (i + 1) * LANES) & (rows == first + i)
        hit = inside if hit is None else hit | inside
    return hit.astype(FULL_TYPE).astype(HALF_TYPE)


def experts_kernel(kind, halves, *refs):
    rows_in, cot, pieces = refs[:halves], refs[halves], refs[halves + 1:halves + 9]
    back, inner, d_pre = refs[halves + 9:]
    seqs, tall, width = back.shape
    row_count = width // 4
    cols = pieces[0].shape[2]
    quarter = tall - row_count
    picked = [rows_in[0][s] if halves == 1 else rows_in[s][...] for s in range(seqs)]
    low = jnp.concatenate([block[0:row_count] for block in picked], axis=0)
    gates = jnp.concatenate(
        [block[row_count:tall, kind * row_count:(kind + 1) * row_count] for block in picked], axis=1
    )
    cot_low = cot[...]
    row_total = gate_total = None
    weight = lambda p, u: pieces[p][u]
    root, cube = 0.7978845608028654, 0.044715
    for p in range(8):
        spread = expand(quarter, cols, p * (cols // LANES))
        gate_wide = tn(gates, spread)
        pre = nn(low, weight(p, 0))
        d_in = nn(cot_low, weight(p, 1))
        square = pre * pre
        tanh = jnp.tanh(pre * (root + (root * cube) * square))
        half = 0.5 + 0.5 * tanh
        act = pre * half
        slope = half + act * (1.0 - tanh) * (root + (3 * root * cube) * square)
        d_pre[p] = (slope * gate_wide * d_in).astype(HALF_TYPE)
        inner[p] = (act * gate_wide).astype(HALF_TYPE)
        g = nt(spread, (d_in * act).astype(HALF_TYPE))
        gate_total = g if p == 0 else gate_total + g
    for p in range(8):
        r = nt(d_pre[p], weight(p, 0))
        row_total = r if p == 0 else row_total + r
    for s in range(seqs):
        here = slice(s * row_count, (s + 1) * row_count)
        back[s, 0:row_count] = row_total[here].astype(HALF_TYPE)
        back[s, row_count:tall] = jnp.zeros((quarter, width), HALF_TYPE)
        back[s, row_count:tall, 0:row_count] = gate_total[:, here].astype(HALF_TYPE)


def branch_kernel(*refs):
    inners, pieces, outs = refs[0:4], refs[4:12], refs[12:16]
    downs = [ref[1] for ref in pieces]
    for i in range(4):
        total = None
        for p in range(8):
            term = nt(inners[i][p], downs[p])
            total = term if p == 0 else total + term
        outs[i][...] = total.astype(HALF_TYPE)


def expert_grads_kernel(*refs):
    rows, cots, pres, inners = refs[0:5], refs[5:9], refs[9:13], refs[13:17]
    outs = refs[17:21]
    step = pl.program_id(0)
    row_count = pres[0].shape[1] // 2
    up = down = None
    for i in range(4):
        for s in range(2):
            block = rows[i][s, 0:row_count] if i < 3 else rows[3 + s][0:row_count]
            term = tn(block, pres[i][0, s * row_count:(s + 1) * row_count])
            up = term if up is None else up + term
        term = tn(cots[i][...], inners[i][0])
        down = term if down is None else down + term
    results = (up.astype(HALF_TYPE), down.astype(HALF_TYPE))
    for j in range(4):

        @pl.when(step // 2 == j)
        def _(j=j):
            for u in range(2):
                outs[j][0, u] = results[u]


def mid_kernel(length, r0, r1, r2, r3, cot, after, gates, gain, bias, w_sel, places, w_out, gate, mixed,
               d_after, d_att, d_gate_out, small, acc):
    step = pl.program_id(0)
    width = cot.shape[2]
    heads = w_out.shape[0]
    experts = w_out.shape[2] // width
    row_count = cot.shape[1]
    tall = r0.shape[1]
    d_rel = jnp.concatenate([r[0, row_count:tall, 0:row_count] for r in (r0, r1, r2, r3)], axis=0)
    d_gate = tn(places[...], d_rel)
    values = gates[...]
    d_logit = (d_gate * values * (1.0 - values)).astype(HALF_TYPE)
    normal, inv = layer_stats(after[...])
    normed = (normal * gain[...] + bias[...]).astype(HALF_TYPE)
    d_normed = tn(d_logit, w_sel[...])
    sel_part = nn(d_logit, normed)
    gain_part = jnp.sum(d_normed * normal, axis=0, keepdims=True)
    bias_part = jnp.sum(d_normed, axis=0, keepdims=True)
    count = sel_part.shape[0]

    @pl.when(step == 0)
    def _():
        acc[...] = jnp.zeros_like(acc)

    acc[0:count, :] += sel_part
    acc[count:count + 1, :] += gain_part
    acc[count + 1:count + 2, :] += bias_part
    d_row = sum(r[0, 0:row_count].astype(FULL_TYPE) for r in (r0, r1, r2, r3))
    total = cot[0].astype(FULL_TYPE) + d_row + norm_back(d_normed, normal, inv, gain[...])
    d_after[...] = total
    total_low = total.astype(HALF_TYPE)
    mixed_here = mixed[...]
    gate_here = gate[0]
    lanes = lane_ids((2 * LANES, LANES), 1)
    second = (lane_ids((2 * LANES, LANES), 0) >= LANES).astype(jnp.int32)
    d_gates = jnp.zeros((row_count, LANES), FULL_TYPE)
    for hp in range(heads // 2):
        both = jnp.concatenate([mixed_here[2 * hp], mixed_here[2 * hp + 1]], axis=1).astype(FULL_TYPE)
        sums = [None, None]
        for e in range(experts):
            d_mixed = nt(total_low, out_block(w_out, hp, e, width))
            hit = (lanes == SELO + 2 * hp * experts + e + second * experts).astype(FULL_TYPE).astype(HALF_TYPE)
            d_gates += nn((both * d_mixed).astype(HALF_TYPE), hit)
            for i in range(2):
                col = SELO + (2 * hp + i) * experts + e
                term = gate_here[:, col:col + 1] * d_mixed[:, i * LANES:(i + 1) * LANES]
                sums[i] = term if e == 0 else sums[i] + term
        for i in range(2):
            position = length[1] + lane_ids((row_count, 1), 0)
            live = (position < length[2 + step]).astype(FULL_TYPE)
            d_att[2 * hp + i] = (sums[i] * live).astype(HALF_TYPE)
    d_gate_out[0] = d_gates

    @pl.when(step == pl.num_programs(0) - 1)
    def _():
        spots = (lane_ids((LANES, LANES), 0) == lanes[0:LANES]).astype(FULL_TYPE).astype(HALF_TYPE)
        small[...] = tn(acc[...].astype(HALF_TYPE), spots)


def out_grad_kernel(mixed, gate, d_after, out):
    heads, experts = 4, out.shape[1] // d_after.shape[1]
    width = d_after.shape[1]
    seqs, row_count = gate.shape[0], gate.shape[1]
    low = d_after[...].astype(HALF_TYPE)
    for hp in range(heads // 2):
        for e in range(experts):
            total = None
            for s in range(seqs):
                left = gated([mixed[s * heads + h] for h in range(heads)], gate[s], hp, e, experts)
                term = tn(left, low[s * row_count:(s + 1) * row_count, :])
                total = term if total is None else total + term
            out[2 * hp * LANES:(2 * hp + 2) * LANES, e * width:(e + 1) * width] = total.astype(HALF_TYPE)


def last_kernel(d_qkv, tok, gain, bias, wq, wk, wv, sel, proj, gate, d_gate_out, small, d_after,
                out, sums, d_proj, acc):
    step = pl.program_id(0)
    row_count, width = tok.shape[1], tok.shape[2]
    heads = d_qkv.shape[0]
    experts = proj.shape[2] // (heads * LANES)
    lanes = lane_ids((LANES, LANES), 1)
    low = tok[0]
    normal, inv = layer_stats(low.astype(FULL_TYPE))
    normed = (normal * gain[...] + bias[...]).astype(HALF_TYPE)
    d_gates = d_gate_out[0]
    gate_here = gate[0]
    d_query = jnp.concatenate([d_qkv[h, 0:row_count] for h in range(heads)], axis=1)
    d_key = jnp.concatenate([d_qkv[h, row_count:2 * row_count] for h in range(heads)], axis=1)
    for h in range(heads):
        d_value = d_qkv[h, 2 * row_count:3 * row_count].astype(FULL_TYPE)
        for e in range(experts):
            col = SELV + h * experts + e
            at = (h * experts + e) * LANES
            d_proj[:, at:at + LANES] = (gate_here[:, col:col + 1] * d_value).astype(HALF_TYPE)
            hit = (lanes == col).astype(FULL_TYPE).astype(HALF_TYPE)
            product = (proj[0, :, at:at + LANES].astype(FULL_TYPE) * d_value).astype(HALF_TYPE)
            d_gates += nn(product, hit)
    d_logit = (d_gates * gate_here * (1.0 - gate_here)).astype(HALF_TYPE)
    d_normed = nt(d_query, wq[...]) + nt(d_key, wk[...]) + nt(d_logit, sel[...])
    total = d_after[...] + norm_back(d_normed, normal, inv, gain[...]) + nt(d_proj[...], wv[...])
    out[...] = total.astype(HALF_TYPE)
    gain_sum = jnp.sum(d_normed * normal, axis=0, keepdims=True)
    bias_sum = jnp.sum(d_normed, axis=0, keepdims=True)
    rows = jnp.concatenate([gain_sum, bias_sum, jnp.zeros((14, width), FULL_TYPE)], axis=0).astype(HALF_TYPE)
    spot = (lane_ids((16, LANES), 1) == lane_ids((16, LANES), 0) + 66) & (lane_ids((16, LANES), 0) < 2)
    spread = tn(rows, spot.astype(FULL_TYPE).astype(HALF_TYPE))
    part = tn(normed, d_logit) + spread

    @pl.when(step == 0)
    def _():
        acc[...] = small[...] + part

    @pl.when(step > 0)
    def _():
        acc[...] += part

    sums[...] = acc[...].astype(HALF_TYPE)


def turn_kernel(near, far, gain, bias, tok_t, norm_t):
    step = pl.program_id(0)

    def turn(low):
        normal, _ = layer_stats(low.astype(FULL_TYPE))
        tok_t[0] = jnp.transpose(low.astype(FULL_TYPE)).astype(HALF_TYPE)
        normed = (normal * gain[...] + bias[...]).astype(HALF_TYPE)
        norm_t[0] = jnp.transpose(normed.astype(FULL_TYPE)).astype(HALF_TYPE)

    @pl.when(step < 4)
    def _():
        turn(near[0])

    @pl.when(step >= 4)
    def _():
        turn(far[0])


def head_grads_kernel(spot, tok_t, norm_t, d_qkv, gate, out, acc):
    step = pl.program_id(0)
    rows = tok_t.shape[2]
    experts = out.shape[1] // LANES - 2
    both = jnp.concatenate([d_qkv[0, 0:rows], d_qkv[0, rows:2 * rows]], axis=1)
    wide = experts * LANES
    spread = expand(8, wide, 0)
    tail = gate[0]
    gates = jnp.concatenate([tn(tail[i * 8:(i + 1) * 8], spread) for i in range(rows // LANES)], axis=0)
    d_value = d_qkv[0, 2 * rows:3 * rows].astype(FULL_TYPE)
    d_proj = (gates * jnp.concatenate([d_value] * experts, axis=1)).astype(HALF_TYPE)
    first = nn(norm_t[0], both)
    second = nn(tok_t[0], d_proj)

    @pl.when(step == 0)
    def _():
        acc[:, 0:2 * LANES] = first
        acc[:, 2 * LANES:] = second

    @pl.when(step > 0)
    def _():
        acc[:, 0:2 * LANES] += first
        acc[:, 2 * LANES:] += second

    @pl.when(step == pl.num_programs(0) - 1)
    def _():
        out[...] = acc[...].astype(HALF_TYPE)


def place_heads_kernel(bits, *refs):
    sources = refs[:4]
    query, key, value = refs[-3:]
    step = pl.program_id(0)
    part = step // 4
    x, low = bits[1], bits[3]
    wide = value.shape[1] // 4

    def put(block, head):
        at = pl.multiple_of(head * LANES, LANES)
        query[:, pl.ds(at, LANES)] = block[:, 0:LANES].astype(FULL_TYPE)
        key[:, pl.ds(at, LANES)] = block[:, LANES:2 * LANES].astype(FULL_TYPE)
        value[:, pl.ds(pl.multiple_of(head * wide, LANES), wide)] = block[:, 2 * LANES:].astype(FULL_TYPE)

    for y in range(2):

        @pl.when((part == 0) & ((step // 2) % 2 == y))
        def _(y=y):
            for i in range(2):
                for b in range(2):
                    put(sources[y][i, b, 0], (low ^ b) * 2 + (x ^ i))

    @pl.when(part == 1)
    def _():
        for i in range(2):
            for b in range(2):
                put(sources[2 + i][0, b, 0], (low ^ b) * 2 + (x ^ i))


def place_out_kernel(spot, mine, *rest):
    rest[-1][0] = mine[...].astype(FULL_TYPE)


def place_small_kernel(first, small, select, value, out, rows):
    low = small[...]

    def rows_of(count, start):
        hit = lane_ids((count, LANES), 1) == lane_ids((count, LANES), 0) + start
        return nt(hit.astype(FULL_TYPE).astype(HALF_TYPE), low)

    select[...] = rows_of(select.shape[0], first[0])
    value[...] = rows_of(value.shape[0], SELV)
    out[...] = rows_of(out.shape[0], SELO)
    spots = (lane_ids((8, LANES), 1) == lane_ids((8, LANES), 0) + 64) & (lane_ids((8, LANES), 0) < 4)
    rows[...] = nt(spots.astype(FULL_TYPE).astype(HALF_TYPE), low)


def place_experts_kernel(spots, mine, mine_y, *rest):
    up, down = rest[-2:]
    for i, ref in enumerate((mine, mine_y)):

        @pl.when(pl.program_id(0) == i)
        def _(ref=ref):
            up[...] = ref[0].astype(FULL_TYPE)
            down[...] = jnp.transpose(ref[1].astype(FULL_TYPE))


def output_kernel(after, own, first, last, out):
    out[...] = (
        after[...] + own[...].astype(FULL_TYPE) + first[...].astype(FULL_TYPE) + last[...].astype(FULL_TYPE)
    ).astype(HALF_TYPE)


class Place:
    def __init__(self):
        self.wide = lax.axis_index("wide")
        self.narrow = lax.axis_index("narrow")
        self.z, self.x = self.wide // 2, self.wide % 2
        self.y, self.c = self.narrow // 2, self.narrow % 2
        self.high, self.low = self.z // 2, self.z % 2

    @staticmethod
    def pairs(move):
        every = []
        for z in range(4):
            for x in range(2):
                for y in range(2):
                    for c in range(2):
                        tz, tx, ty, tc = move(z, x, y, c)
                        every.append(((z * 2 + x) * 4 + y * 2 + c, (tz * 2 + tx) * 4 + ty * 2 + tc))
        return every

    def send(self, value, move):
        return lax.ppermute(value, ("wide", "narrow"), self.pairs(move))

    def swap_x(self, value):
        return self.send(value, lambda z, x, y, c: (z, 1 - x, y, c))

    def swap_y(self, value):
        return self.send(value, lambda z, x, y, c: (z, x, 1 - y, c))

    def swap_xy(self, value):
        return self.send(value, lambda z, x, y, c: (z, 1 - x, 1 - y, c))

    def swap_c(self, value):
        return self.send(value, lambda z, x, y, c: (z, x, y, 1 - c))

    def swap_low(self, value):
        return self.send(value, lambda z, x, y, c: (z ^ 1, x, y, c))

    def swap_high(self, value):
        return self.send(value, lambda z, x, y, c: (z ^ 2, x, y, c))


def pick(array, index):
    return lax.dynamic_index_in_dim(array, index, 0, keepdims=False)


def add(*terms):
    total = terms[0].astype(FULL_TYPE)
    for term in terms[1:]:
        total = total + term.astype(FULL_TYPE)
    return total.astype(HALF_TYPE)


def in_order(bit, mine, other):
    return jnp.stack([jnp.where(bit == 0, mine, other), jnp.where(bit == 0, other, mine)])


def tie(value, *others):
    return lax.optimization_barrier((value,) + others)[0]


def halve(bit, swap, value):
    return add(pick(value, bit), swap(pick(value, 1 - bit)))


def place_out(place, half, core, heads, begun):
    rows, cols = half.shape
    size = 2 * rows // heads
    more = begun or ()
    return call(
        place_out_kernel,
        shaped((heads, size, cols), FULL_TYPE),
        (place.c ^ core).reshape(1).astype(jnp.int32), half, *more,
        grid=(heads // 2,), prefetch=1,
        in_specs=[pl.BlockSpec((size, cols), lambda s, spot: (s, 0))] + [pl.BlockSpec(memory_space=pl.ANY)] * len(more),
        out_specs=pl.BlockSpec((1, size, cols), lambda s, spot: (spot[0] * (heads // 2) + s, 0, 0)),
        aliases={2 + i: i for i in range(len(more))},
    )


def place_experts(place, mine, mine_y, core, begun):
    width, local = mine.shape[1:]
    more = begun or ()
    return call(
        place_experts_kernel,
        (shaped((width, 4 * local), FULL_TYPE), shaped((4 * local, width), FULL_TYPE)),
        jnp.stack([place.narrow ^ core, place.narrow ^ core ^ 2]).astype(jnp.int32), mine, mine_y, *more,
        grid=(2,), prefetch=1,
        in_specs=[full(mine.shape)] * 2 + [pl.BlockSpec(memory_space=pl.ANY)] * len(more),
        out_specs=(
            pl.BlockSpec((width, local), lambda s, spots: (0, spots[s])),
            pl.BlockSpec((local, width), lambda s, spots: (spots[s], 0)),
        ),
        aliases={3 + i: i for i in range(len(more))},
    )


def place_heads(place, sources, core, heads, rows, begun):
    size, cols = sources[0].shape[3:]

    def block(j):
        part, y = j // 2, j % 2

        def at(s, bits):
            a = s % 2
            active = (s // 4) == part
            if part == 0:
                active = active & ((s // 2) % 2 == y)
                return (0, 0, jnp.where(active, a, 0), 0, 0)
            return (jnp.where(active, (s // 2) % 2, 0), 0, jnp.where(active, a, 0), 0, 0)

        return pl.BlockSpec((2 if part == 0 else 1, 2, 1, size, cols), at)

    def row_block(s, bits):
        part, i, a = s // 4, (s // 2) % 2, s % 2
        y, high = bits[0] ^ i, bits[2] ^ a
        inside = jnp.where(part == 0, y * 2 + high, high * 2 + y)
        return (((bits[4] ^ core) * 2 + part) * 4 + inside, 0)

    wide = cols - 2 * LANES
    more = () if begun is None else tuple(begun)
    return call(
        place_heads_kernel,
        (
            shaped((rows, heads * LANES), FULL_TYPE), shaped((rows, heads * LANES), FULL_TYPE),
            shaped((rows, heads * wide), FULL_TYPE),
        ),
        jnp.stack([place.y, place.x, place.high, place.low, place.c]).astype(jnp.int32), *sources, *more,
        grid=(8,), prefetch=1,
        in_specs=[block(j) for j in range(4)] + [pl.BlockSpec(memory_space=pl.ANY)] * len(more),
        out_specs=(
            pl.BlockSpec((size, heads * LANES), row_block), pl.BlockSpec((size, heads * LANES), row_block),
            pl.BlockSpec((size, heads * wide), row_block),
        ),
        aliases={5 + i: i for i in range(len(more))},
    )


def turn_tables(span, head_dim):
    half = head_dim // 2
    frequency = np.float32(10000.0) ** (-(np.arange(half).astype(np.float32) * np.float32(2.0) / np.float32(head_dim)))
    angles = np.arange(span).astype(np.float32)[:, None] * frequency[None, :].astype(np.float32)
    cosine, sine = np.cos(angles.astype(np.float64)), np.sin(angles.astype(np.float64))
    return (
        jnp.asarray(np.concatenate([cosine, cosine], axis=1).astype(np.float32)),
        jnp.asarray(np.concatenate([-sine, sine], axis=1).astype(np.float32)),
    )


def tuned_device(
    tokens, lengths, value_ids, out_ids, mlp_ids, w_query, w_key, w_value, w_out, sel_value, sel_out,
    gain_one, bias_one, gain_two, bias_two, w_select, w_up, w_down, cotangent,
):
    seqs, row_count, width = tokens.shape
    heads, head_dim = w_out.shape[0], w_out.shape[1]
    experts = w_out.shape[2] // width
    pair_count = seqs * heads
    span = 8 * row_count
    all_rows = seqs * row_count
    wide_out = heads * experts * LANES
    local = w_up.shape[1] // 4
    hidden = 8 * local
    own_count = w_select.shape[1]
    count = 8 * own_count
    quarter = count // 4
    tall = row_count + quarter
    place = Place()
    first_row = place.wide * row_count
    row = lambda v: v.reshape(1, -1)
    smem = pl.BlockSpec(memory_space=pltpu.SMEM)
    vmem = pl.BlockSpec(memory_space=pltpu.VMEM)
    hbm = pl.BlockSpec(memory_space=pl.ANY)
    by_seq = lambda shape: pl.BlockSpec((1,) + tuple(shape[1:]), lambda s: (s,) + (0,) * (len(shape) - 1))
    split = lambda shape: pl.BlockSpec((shape[0] // seqs,) + tuple(shape[1:]), lambda s: (s,) + (0,) * (len(shape) - 1))
    token_cols = lambda n: pl.BlockSpec((n, row_count), lambda s: (0, s))

    own_select = jnp.transpose(w_select).reshape(own_count, 8, -1).swapaxes(0, 1).reshape(-1, LANES)

    mine_peer = jnp.stack([place.narrow, place.narrow + 1 - 2 * place.c]).astype(jnp.int32)
    weights_mine, weights_peer = call(
        weights_kernel,
        (shaped((2, width, local)), shaped((2, width, local))),
        mine_peer, w_up, w_down,
        grid=(2,), prefetch=1,
        in_specs=[
            pl.BlockSpec((width, local), lambda s, spots: (0, spots[s])),
            pl.BlockSpec((local, width), lambda s, spots: (spots[s], 0)),
        ],
        out_specs=(full((2, width, local)), full((2, width, local))),
    )

    cot_own = cotangent.reshape(all_rows, width)
    cots = [cot_own, place.swap_y(cot_own)]
    tokens_x = place.swap_x(tokens)

    cosine, sine = turn_tables(span, head_dim)
    here = lambda t: lax.dynamic_slice_in_dim(t, first_row, row_count, 0)
    sel = jnp.concatenate(
        [
            jnp.zeros((width, SELV), HALF_TYPE), sel_value, sel_out,
            jnp.zeros((width, LANES - SELO - heads * experts), HALF_TYPE),
        ],
        axis=1,
    )
    value_flat = value_ids.reshape(seqs, row_count, -1)
    out_flat = out_ids.reshape(seqs, row_count, -1)
    payload = 3 * row_count + own_select.shape[0] + 16
    qkv, projected, gate = call(
        pre_kernel,
        (
            shaped((pair_count, payload, head_dim)),
            shaped((seqs, row_count, wide_out)),
            shaped((seqs, row_count, LANES), FULL_TYPE),
        ),
        tokens, row(gain_one), row(bias_one), w_query, w_key, w_value, sel, value_flat, out_flat,
        here(cosine), here(sine), own_select,
        grid=(seqs,),
        in_specs=[
            by_seq(tokens.shape), full((1, width)), full((1, width)), full(w_query.shape), full(w_key.shape),
            full(w_value.shape), full(sel.shape), by_seq(value_flat.shape), by_seq(out_flat.shape),
            full((row_count, head_dim)), full((row_count, head_dim)),
            full(own_select.shape),
        ],
        out_specs=(
            split((pair_count, payload, head_dim)), by_seq((seqs, row_count, wide_out)),
            by_seq((seqs, row_count, LANES)),
        ),
        flops=2 * all_rows * width * 3712,
    )
    qkv = lax.all_to_all(qkv, "wide", 0, 0, tiled=True)
    qkv, cots[1], tokens_x, weights_mine = lax.optimization_barrier((qkv, cots[1], tokens_x, weights_mine))
    weights_far, weights_near = place.swap_high(weights_mine), place.swap_low(weights_mine)
    cot_later = tie(cot_own, qkv)
    cots += [place.swap_x(cot_later), place.swap_xy(cot_later)]
    seq_here = place.wide // heads
    length = pick(lengths, seq_here).reshape(1)
    mixed, out_t, lse = call(
        attend_kernel,
        (
            shaped((8, row_count, head_dim)), shaped((head_dim, span), FULL_TYPE), shaped((1, span), FULL_TYPE),
        ),
        length, qkv,
        in_specs=[smem, vmem],
        flops=2 * span * span * head_dim,
    )
    mixed = lax.all_to_all(mixed, "wide", 0, 0, tiled=True)
    mixed, weights_far, weights_near, cots[2], cots[3] = lax.optimization_barrier(
        (mixed, weights_far, weights_near, cots[2], cots[3])
    )
    weights_last = place.swap_low(weights_far)

    kinds = (place.x * 2 + place.y) ^ jnp.arange(4)
    kx, ky = (kinds // 2)[:, None, None, None], (kinds % 2)[:, None, None, None]
    kz = (place.z ^ jnp.arange(4))[None, :, None, None]
    kc = (place.c ^ jnp.arange(2))[None, None, :, None]
    ki = jnp.arange(2)[None, None, None, :]
    sent_ids = ((kz * 2 + kx) * own_count + ky * 4 + kc * 2 + ki).reshape(-1)
    places = (sent_ids[:, None] == jnp.arange(count)[None, :]).astype(HALF_TYPE)

    own_mlp = lax.dynamic_slice_in_dim(mlp_ids, first_row, row_count, 1)
    own_mlp = jnp.swapaxes(own_mlp, 1, 2)
    after, gates, rows_own, select = call(
        post_kernel,
        (
            shaped((all_rows, width), FULL_TYPE), shaped((count, all_rows), FULL_TYPE), shaped((seqs, tall, width)),
            shaped((count, width)),
        ),
        mixed, gate, w_out, tokens, row(gain_two), row(bias_two), qkv, own_mlp, places,
        grid=(seqs,),
        in_specs=[
            split(mixed.shape), by_seq(gate.shape), full(w_out.shape), by_seq(tokens.shape), full((1, width)),
            full((1, width)), pl.BlockSpec((8, 8 * own_count, LANES), lambda s: (0, 3 * row_count // (8 * own_count), 0)),
            by_seq(own_mlp.shape), full(places.shape),
        ],
        out_specs=(
            split((all_rows, width)), token_cols(count), by_seq((seqs, tall, width)), full((count, width)),
        ),
        flops=2 * all_rows * width * wide_out,
    )

    rows_y, rows_x = place.swap_y(rows_own), place.swap_x(rows_own)
    rows_d = (place.swap_x(rows_y[0]), place.swap_y(rows_x[1]))
    rows_in = [(rows_own,), (rows_y,), (rows_x,), rows_d]
    weights = [weights_mine, weights_peer]
    for piece in (weights_near, weights_far, weights_last):
        weights += [piece, place.swap_c(piece)]
    own_two = jnp.stack([pick(tokens, seq_here), pick(tokens_x, seq_here)])
    other_two = jnp.stack([pick(tokens, 1 - seq_here), pick(tokens_x, 1 - seq_here)])
    other_two = place.swap_high(tie(other_two, rows_own))
    results = {}
    for i, before in ((1, None), (2, 1), (3, 2), (0, 3)):
        if before is not None:
            cots[i] = tie(cots[i], results[before][1])
        results[i] = call(
                functools.partial(experts_kernel, i, len(rows_in[i])),
                (
                    shaped((seqs, tall, width)), shaped((8, all_rows, local)), shaped((8, all_rows, local)),
                ),
                *rows_in[i], cots[i], *weights,
                flops=8 * all_rows * width * hidden,
            )
    swaps = (lambda v: v, place.swap_y, place.swap_x, place.swap_xy)
    d_rows = [swaps[i](results[i][0]) for i in range(4)]
    inners = [results[i][1] for i in range(4)]
    near_four = jnp.concatenate([own_two, tie(other_two, results[2][1])])
    far_four = place.swap_low(near_four)

    whole = lambda shape: pl.BlockSpec(tuple(shape), lambda p: (0,) * len(shape))
    piece = lambda: pl.BlockSpec((1, all_rows, local), lambda p: (2 * (2 * (p % 2) + (p // 2) % 2) + p // 4, 0, 0))
    grad_near, grad_far, peer_near, peer_far = call(
        expert_grads_kernel,
        (shaped((2, 2, width, local)),) * 4,
        rows_own, rows_y, rows_x, *rows_d, *cots, *[results[i][2] for i in range(4)], *inners,
        grid=(8,),
        in_specs=[whole((seqs, tall, width))] * 3 + [whole((tall, width))] * 2 + [whole((all_rows, width))] * 4
        + [piece() for _ in range(8)],
        out_specs=tuple(
            pl.BlockSpec((1, 2, width, local), lambda p, j=j: (jnp.clip(p - 2 * j, 0, 1), 0, 0, 0)) for j in range(4)
        ),
        flops=16 * all_rows * width * hidden,
    )
    d_rows[1], d_rows[2], d_rows[3], peer_far, peer_near, far_four = lax.optimization_barrier(
        (d_rows[1], d_rows[2], tie(d_rows[3], grad_near), peer_far, peer_near, far_four)
    )
    came_far, came_near = place.swap_c(peer_far), place.swap_c(peer_near)

    live_info = jnp.concatenate([jnp.zeros((1,), jnp.int32), first_row.reshape(1).astype(jnp.int32), lengths])
    d_after, d_att, d_gate_out, small = call(
        mid_kernel,
        (
            shaped((all_rows, width), FULL_TYPE), shaped((pair_count, row_count, head_dim)),
            shaped((seqs, row_count, LANES), FULL_TYPE), shaped((width, LANES), FULL_TYPE),
        ),
        live_info, *d_rows, cotangent, after, gates, row(gain_two), row(bias_two), select, places,
        w_out, gate, mixed,
        grid=(seqs,),
        in_specs=[smem] + [by_seq((seqs, tall, width))] * 4 + [
            by_seq(cotangent.shape), split((all_rows, width)), token_cols(count), full((1, width)), full((1, width)),
            full(select.shape), full(places.shape), full(w_out.shape), by_seq(gate.shape),
            split(mixed.shape),
        ],
        out_specs=(
            split((all_rows, width)), split((pair_count, row_count, head_dim)),
            by_seq((seqs, row_count, LANES)), full((width, LANES)),
        ),
        scratch=[pltpu.VMEM((LANES, width), FULL_TYPE)],
        flops=2 * all_rows * width * wide_out,
    )
    d_att_all = lax.all_to_all(d_att, "wide", 0, 0, tiled=True)

    to_low = [add(grad_far[a], came_far[a]) for a in range(2)]
    passed = [None, place.swap_low(to_low[1])]
    near_four = tie(near_four, d_att, *to_low)
    tok_t, norm_t = call(
        turn_kernel,
        (shaped((8, width, row_count)), shaped((8, width, row_count))),
        near_four, far_four, row(gain_one), row(bias_one),
        grid=(8,),
        in_specs=[
            pl.BlockSpec((1, row_count, width), lambda i: (jnp.minimum(i, 3), 0, 0)),
            pl.BlockSpec((1, row_count, width), lambda i: (jnp.maximum(i - 4, 0), 0, 0)),
            full((1, width)), full((1, width)),
        ],
        out_specs=(
            pl.BlockSpec((1, width, row_count), lambda i: (i, 0, 0)),
            pl.BlockSpec((1, width, row_count), lambda i: (i, 0, 0)),
        ),
    )
    grad_out = call(
        out_grad_kernel, shaped((heads * head_dim, experts * width)), tie(mixed, d_att, tok_t), gate, d_after,
        flops=2 * all_rows * width * wide_out,
    )
    rows_out, cols_out = grad_out.shape
    flat = ((place.y, place.swap_y), (place.x, place.swap_x))
    d_att_all, tok_t, grad_out = lax.optimization_barrier((d_att_all, tok_t, grad_out))
    out_parts = halve(place.c, place.swap_c, grad_out.reshape(2, 2, 2, 2, 2, 2, rows_out // 64, cols_out))

    d_qkv = call(
        attend_back_kernel,
        shaped((8, 3 * row_count, head_dim)),
        length, qkv, d_att_all, out_t, lse, cosine, sine,
        in_specs=[smem] + [vmem] * 6,
        scratch=[pltpu.VMEM((span, head_dim), FULL_TYPE), pltpu.VMEM((span, head_dim), FULL_TYPE)],
        flops=5 * span * span * head_dim,
    )

    d_qkv, out_parts = lax.optimization_barrier((d_qkv, out_parts))
    out_parts = [halve(*flat[i], out_parts[i]) for i in range(2)]

    block_of = lambda i, spot: spot[0] ^ ((i & 1) | ((i & 2) << 1) | ((i & 4) >> 1))
    head_cols = (2 + experts) * LANES
    head_grads = call(
        head_grads_kernel,
        shaped((width, head_cols)),
        place.wide.reshape(1).astype(jnp.int32), tok_t, norm_t, d_qkv, qkv,
        grid=(8,), prefetch=1,
        in_specs=[
            pl.BlockSpec((1, width, row_count), lambda i, spot: (i, 0, 0)),
            pl.BlockSpec((1, width, row_count), lambda i, spot: (i, 0, 0)),
            pl.BlockSpec((1, 3 * row_count, head_dim), lambda i, spot: (block_of(i, spot), 0, 0)),
            pl.BlockSpec((1, 16, head_dim), lambda i, spot: (block_of(i, spot), payload // 16 - 1, 0)),
        ],
        out_specs=pl.BlockSpec((width, head_cols), lambda i, spot: (0, 0)),
        scratch=[pltpu.VMEM((width, head_cols), FULL_TYPE)],
        flops=2 * span * width * head_cols,
    )
    d_qkv_rows = lax.all_to_all(d_qkv, "wide", 0, 0, tiled=True)
    bits = ((place.y, place.swap_y), (place.high, place.swap_high))
    rows_head = width // 16
    head_grads, out_parts[0], out_parts[1] = lax.optimization_barrier((head_grads, *out_parts))
    out_parts = [halve(*flat[1 - i], out_parts[i]) for i in range(2)]
    kept = halve(place.c, place.swap_c, head_grads.reshape(2, 2, 2, 2, rows_head, head_cols))
    branches = call(
        branch_kernel,
        (shaped((all_rows, width)),) * 4,
        tie(inners[0], head_grads), *inners[1:], *weights,
        flops=8 * all_rows * width * hidden,
    )
    b0, b1, b2, b3 = branches
    kept, out_sum, b1, b2, b3 = lax.optimization_barrier((kept, jnp.stack(out_parts, axis=2), b1, b2, b3))
    b3 = place.swap_x(b3)
    out_sum = halve(place.low, place.swap_low, out_sum)
    value = [halve(*bits[i], kept[i]) for i in range(2)]
    value[0], value[1], d_qkv_rows, out_sum = lax.optimization_barrier((value[0], value[1], d_qkv_rows, out_sum))
    value = [halve(*bits[1 - i], value[i]) for i in range(2)]
    out_sum = halve(place.high, place.swap_high, out_sum)
    grad_tokens, small = call(
        last_kernel,
        (shaped((all_rows, width)), shaped((width, LANES))),
        d_qkv_rows, tokens, row(gain_one), row(bias_one), w_query, w_key, w_value, sel, projected, gate, d_gate_out,
        small, d_after,
        grid=(seqs,),
        in_specs=[
            split(d_qkv.shape), by_seq(tokens.shape), full((1, width)), full((1, width)), full(w_query.shape),
            full(w_key.shape), full(w_value.shape), full(sel.shape), by_seq(projected.shape), by_seq(gate.shape),
            by_seq(d_gate_out.shape), full(small.shape), split(d_after.shape),
        ],
        out_specs=(split((all_rows, width)), full((width, LANES))),
        scratch=[pltpu.VMEM((row_count, wide_out), HALF_TYPE), pltpu.VMEM((width, LANES), FULL_TYPE)],
        flops=2 * all_rows * width * 3712,
    )
    done, small, out_sum, b3 = lax.optimization_barrier((jnp.stack(value), small, out_sum, b3))
    b1 = place.swap_y(add(b1, b3))
    b2 = place.swap_x(tie(b2, b3))
    far = place.swap_high(done)
    out_sum = in_order(place.high, out_sum, place.swap_high(out_sum))
    everywhere = ("wide", "narrow")
    small = lax.all_to_all(small, everywhere, 0, 0, tiled=True).reshape(32, -1, LANES)
    far, out_sum = lax.optimization_barrier((far, out_sum))
    out_sum = in_order(place.low, out_sum, place.swap_low(out_sum))
    near = [place.swap_low(done), place.swap_low(far)]
    sets = [
        jnp.stack([jnp.stack([done[i], far[i]]), jnp.stack([near[0][i], near[1][i]])]) for i in range(2)
    ]
    passed[0] = place.swap_low(tie(to_low[0], near[1]))
    to_high = add(grad_near[1], came_near[1], tie(passed[1], done))
    sets[0], sets[1], small, out_sum, b1, b2, to_high = lax.optimization_barrier(
        (sets[0], sets[1], small, out_sum, b1, b2, to_high)
    )
    mine_far = place.swap_high(to_high)
    small = jnp.sum(small.astype(FULL_TYPE), axis=0).astype(HALF_TYPE)
    small = lax.all_to_all(jnp.broadcast_to(small[None], (32,) + small.shape), everywhere, 0, 0, tiled=True)
    back = [in_order(flat[1 - i][0], out_sum[:, :, i], flat[1 - i][1](out_sum[:, :, i])) for i in range(2)]
    first = jnp.stack([sets[0], place.swap_x(sets[0])])
    second = jnp.stack([sets[1], place.swap_y(sets[1])])
    first, second, back[0], back[1] = lax.optimization_barrier((first, second, *back))
    sources = [first, place.swap_y(first), second, place.swap_x(second)]
    back = [in_order(flat[i][0], back[i], flat[i][1](back[i])) for i in range(2)]
    out_half = jnp.stack(back).reshape(rows_out // 2, cols_out)
    output = call(output_kernel, shaped((all_rows, width)), after, b0, b2, b1)
    sources[1], sources[3], output, out_half, mine_far, small, passed[0] = lax.optimization_barrier(
        (sources[1], sources[3], output, out_half, mine_far, small, passed[0])
    )
    mine = add(grad_near[0], came_near[0], passed[0], mine_far)
    mine_y = place.swap_y(mine)
    peers = [place.swap_c(first), None, place.swap_c(second), None]
    peers[1], peers[3] = place.swap_c(sources[1]), place.swap_c(sources[3])
    out_peer = place.swap_c(out_half)
    grad_heads = place_heads(place, sources, 0, heads, width, None)
    grad_out = place_out(place, out_half, 0, heads, None)
    grad_heads = lax.optimization_barrier((*grad_heads, grad_out, *peers, out_peer))
    grad_heads, grad_out, peers, out_peer = grad_heads[:3], grad_heads[3], grad_heads[4:8], grad_heads[8]
    small = small.reshape(width, LANES)
    grad_select, grad_sel_value, grad_sel_out, rows_four = call(
        place_small_kernel,
        (
            shaped((own_count, width), FULL_TYPE), shaped((heads * experts, width), FULL_TYPE),
            shaped((heads * experts, width), FULL_TYPE), shaped((8, width), FULL_TYPE),
        ),
        (place.wide * own_count).reshape(1).astype(jnp.int32), small,
        in_specs=[smem, vmem],
    )
    grad_query, grad_key, grad_value = place_heads(place, list(peers), 1, heads, width, grad_heads)
    grad_out = place_out(place, out_peer, 1, heads, (grad_out,))
    mine, mine_y, grad_query, grad_out, rows_four = lax.optimization_barrier((mine, mine_y, grad_query, grad_out, rows_four))
    mine_c, mine_yc = place.swap_c(mine), place.swap_c(mine_y)
    grad_experts = place_experts(place, mine, mine_y, 0, None)
    grad_up, grad_down = place_experts(place, mine_c, mine_yc, 1, grad_experts)
    grad_select, grad_sel_value, grad_sel_out = grad_select.T, grad_sel_value.T, grad_sel_out.T
    grad_gain_two, grad_bias_two, grad_gain_one, grad_bias_one = (rows_four[i] for i in range(4))
    return (
        output.reshape(tokens.shape), grad_tokens.reshape(tokens.shape), grad_query, grad_key, grad_value, grad_out,
        grad_sel_value, grad_sel_out, grad_gain_one, grad_bias_one, grad_gain_two, grad_bias_two, grad_select,
        grad_up, grad_down,
    )


def fits(mesh):
    return dict(mesh.shape) == {"wide": 8, "narrow": 4}


def solution(mesh):
    placed = (
        P("narrow", "wide", None),
        P("narrow"),
        P("narrow", "wide", None, None),
        P("narrow", "wide", None, None),
        P("narrow", None, None),
        P(),
        P(),
        P(),
        P(),
        P(),
        P(),
        P(),
        P(),
        P(),
        P(),
        P(None, "wide"),
        P(None, "wide"),
        P("wide", None),
        P("narrow", "wide", None),
    )
    return jax.shard_map(
        tuned_device if fits(mesh) else per_device,
        mesh=mesh,
        in_specs=placed,
        out_specs=(
            P("narrow", "wide", None),
            P("narrow", "wide", None),
            P(),
            P(),
            P(),
            P(),
            P(),
            P(),
            P(),
            P(),
            P(),
            P(),
            P(None, "wide"),
            P(None, "wide"),
            P("wide", None),
        ),
        check_vma=False,
    )
```

```python
import functools

import jax
import jax.numpy as jnp
import numpy as np
from jax import lax
from jax.experimental import pallas as pl
from jax.experimental.pallas import tpu as pltpu
from jax.sharding import PartitionSpec as P

EPSILON = 1e-05
FULL_TYPE = jnp.float32
HALF_TYPE = jnp.bfloat16


def for_sending(value):

    def short(part):
        return part.astype(jnp.bfloat16) if part.dtype == jnp.float32 else part

    return jax.tree.map(short, value)


def norm_parts(values_in, gain, bias):
    row_mean = jnp.mean(values_in, axis=-1, keepdims=True)
    centred = values_in - row_mean
    inv_scale = lax.rsqrt(jnp.mean(centred * centred, axis=-1, keepdims=True) + EPSILON)
    normal = centred * inv_scale
    return (normal * gain + bias, normal, inv_scale)


def norm_back(grad_in, normal, inv_scale, gain):
    scaled = grad_in * gain
    return inv_scale * (
        scaled
        - jnp.mean(scaled, axis=-1, keepdims=True)
        - normal * jnp.mean(scaled * normal, axis=-1, keepdims=True)
    )


def rotate(values_in, positions, turn):
    half_dim = values_in.shape[-1] // 2
    frequency = 10000.0 ** (-(jnp.arange(half_dim).astype(FULL_TYPE) * 2.0 / values_in.shape[-1]))
    angles = positions.astype(FULL_TYPE)[:, None] * frequency[None, :]
    cosine = jnp.cos(angles)[:, None, :]
    sine_part = turn * jnp.sin(angles)[:, None, :]
    front_half = values_in[..., :half_dim]
    back_half = values_in[..., half_dim:]
    return jnp.concatenate(
        [front_half * cosine - back_half * sine_part, front_half * sine_part + back_half * cosine],
        axis=-1,
    )


def one_hot_sum(ids, wanted):
    return jnp.sum((ids[..., None] == wanted).astype(FULL_TYPE), axis=-2)


def matmul(left_op, right_op):
    return jnp.dot(left_op, right_op, preferred_element_type=FULL_TYPE)


def contract_rows(left_op, right_op):
    left_flat = left_op.reshape(-1, left_op.shape[-1])
    right_flat = right_op.reshape(-1, right_op.shape[-1])
    return lax.dot_general(
        left_flat, right_flat, (((0,), (0,)), ((), ())), preferred_element_type=FULL_TYPE
    )


def times_transpose(grad_in, weight):
    return lax.dot_general(
        grad_in, weight, (((grad_in.ndim - 1,), (1,)), ((), ())), preferred_element_type=FULL_TYPE
    )


def attend_forward(
    tokens,
    lengths,
    value_ids,
    out_ids,
    w_query,
    w_key,
    w_value,
    w_out,
    sel_value,
    sel_out,
    gain_one,
    bias_one,
    gain_two,
    bias_two,
):
    seq_count, row_count, model_width = tokens.shape
    head_count = w_out.shape[0]
    head_dim = w_out.shape[1]
    value_experts = sel_value.shape[1] // head_count
    positions = lax.axis_index("wide") * row_count + jnp.arange(row_count, dtype=jnp.int32)
    inputs = tokens.astype(FULL_TYPE)
    normed, normal_one, scale_one = norm_parts(inputs, gain_one, bias_one)
    normed_low = normed.astype(HALF_TYPE)
    query_pre = matmul(normed_low, w_query).reshape(seq_count, row_count, head_count, head_dim)
    key_pre = matmul(normed_low, w_key).reshape(seq_count, row_count, head_count, head_dim)
    queries = rotate(query_pre, positions, 1.0).astype(HALF_TYPE)
    key_low = rotate(key_pre, positions, 1.0).astype(HALF_TYPE)
    expert_ids = jnp.arange(value_experts, dtype=jnp.int32)
    value_choice = one_hot_sum(value_ids, expert_ids)
    value_sig = jax.nn.sigmoid(
        matmul(normed_low, sel_value).reshape(seq_count, row_count, head_count, value_experts)
    )
    value_gate = value_sig * value_choice
    projected = matmul(tokens, w_value).reshape(
        seq_count, row_count, head_count, value_experts, head_dim
    )
    values = jnp.sum(value_gate[..., None] * projected, axis=3).astype(HALF_TYPE)
    keys_all, values_all = (
        lax.all_gather(key_low, "wide", axis=1, tiled=True),
        lax.all_gather(values, "wide", axis=1, tiled=True),
    )
    span = keys_all.shape[1]
    key_pos = jnp.arange(span, dtype=jnp.int32)
    allowed = (key_pos[None, None, None, :] <= positions[None, None, :, None]) & (
        key_pos[None, None, None, :] < lengths[:, None, None, None]
    )
    scores = jnp.einsum(
        "bphc,bshc->bhps", queries, keys_all, preferred_element_type=FULL_TYPE
    ) * head_dim ** (-0.5)
    masked = jnp.where(allowed, scores, -1e30)
    row_max = jnp.max(masked, axis=-1, keepdims=True)
    exponent = jnp.exp(masked - row_max)
    row_total = jnp.sum(exponent, axis=-1, keepdims=True)
    attn_probs = exponent / row_total
    log_total = row_max + jnp.log(row_total)
    attended = jnp.einsum(
        "bhps,bshc->bphc",
        attn_probs.astype(HALF_TYPE),
        values_all,
        preferred_element_type=FULL_TYPE,
    )
    live_rows = (positions[None, :] < lengths[:, None]).astype(FULL_TYPE)[:, :, None, None]
    mixed_out = (attended * live_rows).astype(HALF_TYPE)
    out_choice = one_hot_sum(out_ids, expert_ids)
    out_sig = jax.nn.sigmoid(
        matmul(normed_low, sel_out).reshape(seq_count, row_count, head_count, value_experts)
    )
    out_gate = out_sig * out_choice
    expert_out = jnp.einsum(
        "bphc,hcf->bphf", mixed_out, w_out, preferred_element_type=FULL_TYPE
    ).reshape(seq_count, row_count, head_count, value_experts, model_width)
    after_attn = inputs + jnp.sum(out_gate[..., None] * expert_out, axis=(2, 3))
    normed_two, normal_two, scale_two = norm_parts(after_attn, gain_two, bias_two)
    return dict(
        positions=positions,
        normal_one=normal_one,
        scale_one=scale_one,
        normed_low=normed_low,
        queries=queries,
        keys_all=keys_all,
        values_all=values_all,
        allowed=allowed,
        log_total=log_total,
        live_rows=live_rows,
        mixed_out=mixed_out,
        value_choice=value_choice,
        value_sig=value_sig,
        value_gate=value_gate,
        projected=projected,
        out_choice=out_choice,
        out_sig=out_sig,
        out_gate=out_gate,
        expert_out=expert_out,
        after_attn=after_attn,
        normed_two=normed_two,
        normal_two=normal_two,
        scale_two=scale_two,
    )


def expert_forward(after_attn, normed_two, mlp_ids, w_select, w_up):
    rows_all, normed_all = (
        lax.all_gather(for_sending(after_attn.astype(HALF_TYPE)), "wide", axis=1, tiled=True),
        lax.all_gather(for_sending(normed_two.astype(HALF_TYPE)), "wide", axis=1, tiled=True),
    )
    local_count = w_select.shape[1]
    hidden = w_up.shape[1] // local_count
    seq_count, span = (rows_all.shape[0], rows_all.shape[1])
    owned_ids = lax.axis_index("wide") * local_count + jnp.arange(local_count, dtype=jnp.int32)
    chosen = one_hot_sum(mlp_ids, owned_ids)
    sigmoid_gate = jax.nn.sigmoid(matmul(normed_all, w_select))
    mlp_gate = sigmoid_gate * chosen
    pre_act = matmul(rows_all, w_up)
    activated = jax.nn.gelu(pre_act).reshape(seq_count, span, local_count, hidden)
    inner_low = (
        (activated * mlp_gate[..., None])
        .reshape(seq_count, span, local_count * hidden)
        .astype(HALF_TYPE)
    )
    return dict(
        rows_all=rows_all,
        normed_all=normed_all,
        chosen=chosen,
        sigmoid_gate=sigmoid_gate,
        mlp_gate=mlp_gate,
        pre_act=pre_act,
        activated=activated,
        inner_low=inner_low,
    )


def per_device(
    tokens,
    lengths,
    value_ids,
    out_ids,
    mlp_ids,
    w_query,
    w_key,
    w_value,
    w_out,
    sel_value,
    sel_out,
    gain_one,
    bias_one,
    gain_two,
    bias_two,
    w_select,
    w_up,
    w_down,
    cotangent,
):
    seq_count, row_count, model_width = tokens.shape
    head_count = w_out.shape[0]
    head_dim = w_out.shape[1]
    value_experts = sel_value.shape[1] // head_count
    saved = attend_forward(
        tokens,
        lengths,
        value_ids,
        out_ids,
        w_query,
        w_key,
        w_value,
        w_out,
        sel_value,
        sel_out,
        gain_one,
        bias_one,
        gain_two,
        bias_two,
    )
    expert_state = expert_forward(saved["after_attn"], saved["normed_two"], mlp_ids, w_select, w_up)
    branch_part = matmul(expert_state["inner_low"], w_down)
    branch_sum = lax.psum_scatter(
        branch_part.astype(jnp.bfloat16), "wide", scatter_dimension=1, tiled=True
    ).astype(jnp.float32)
    output = (saved["after_attn"] + branch_sum).astype(HALF_TYPE)
    saved = attend_forward(
        tokens,
        lengths,
        value_ids,
        out_ids,
        w_query,
        w_key,
        w_value,
        w_out,
        sel_value,
        sel_out,
        gain_one,
        bias_one,
        gain_two,
        bias_two,
    )
    expert_state = expert_forward(saved["after_attn"], saved["normed_two"], mlp_ids, w_select, w_up)
    cot_all = lax.all_gather(cotangent, "wide", axis=1, tiled=True)
    grad_down = contract_rows(expert_state["inner_low"], cot_all)
    d_inner = times_transpose(cot_all, w_down)
    activated = expert_state["activated"]
    d_inner_four = d_inner.reshape(activated.shape)
    d_mlp_gate = jnp.sum(d_inner_four * activated, axis=-1)
    mlp_gate = expert_state["mlp_gate"]
    gated_grad = (d_inner_four * mlp_gate[..., None]).reshape(expert_state["pre_act"].shape)
    unused_value, gelu_pull = jax.vjp(jax.nn.gelu, expert_state["pre_act"])
    d_pre = gelu_pull(gated_grad)[0].astype(HALF_TYPE)
    sigmoid_gate = expert_state["sigmoid_gate"]
    d_logit = (d_mlp_gate * expert_state["chosen"] * sigmoid_gate * (1.0 - sigmoid_gate)).astype(
        HALF_TYPE
    )
    grad_up = contract_rows(expert_state["rows_all"], d_pre)
    grad_select = contract_rows(expert_state["normed_all"], d_logit)
    row_part = times_transpose(d_pre, w_up)
    norm_part = times_transpose(d_logit, w_select)
    row_grad, norm_grad = (
        lax.psum_scatter(row_part, "wide", scatter_dimension=1, tiled=True),
        lax.psum_scatter(norm_part, "wide", scatter_dimension=1, tiled=True),
    )
    grad_gain_two = jnp.sum(norm_grad * saved["normal_two"], axis=(0, 1))
    grad_bias_two = jnp.sum(norm_grad, axis=(0, 1))
    d_after = (
        cotangent.astype(FULL_TYPE)
        + row_grad
        + norm_back(norm_grad, saved["normal_two"], saved["scale_two"], gain_two)
    )
    out_gate = saved["out_gate"]
    d_expert = (out_gate[..., None] * d_after[:, :, None, None, :]).astype(HALF_TYPE)
    d_out_gate = jnp.sum(saved["expert_out"] * d_after[:, :, None, None, :], axis=-1)
    d_expert_flat = d_expert.reshape(seq_count, row_count, head_count, value_experts * model_width)
    grad_out = jnp.einsum(
        "bphc,bphf->hcf", saved["mixed_out"], d_expert_flat, preferred_element_type=FULL_TYPE
    )
    d_mixed = jnp.einsum("bphf,hcf->bphc", d_expert_flat, w_out, preferred_element_type=FULL_TYPE)
    d_attended = (d_mixed * saved["live_rows"]).astype(HALF_TYPE)
    out_sig = saved["out_sig"]
    d_out_logit = (
        (d_out_gate * saved["out_choice"] * out_sig * (1.0 - out_sig))
        .astype(HALF_TYPE)
        .reshape(seq_count, row_count, head_count * value_experts)
    )
    queries = saved["queries"]
    keys_all = saved["keys_all"]
    values_all = saved["values_all"]
    score_scale = head_dim ** (-0.5)
    scores = (
        jnp.einsum("bphc,bshc->bhps", queries, keys_all, preferred_element_type=FULL_TYPE)
        * score_scale
    )
    attn_probs = jnp.where(saved["allowed"], jnp.exp(scores - saved["log_total"]), 0.0)
    d_values_part = jnp.einsum(
        "bhps,bphc->bshc",
        attn_probs.astype(HALF_TYPE),
        d_attended,
        preferred_element_type=FULL_TYPE,
    )
    d_probs = jnp.einsum(
        "bphc,bshc->bhps", d_attended, values_all, preferred_element_type=FULL_TYPE
    )
    row_inner = jnp.sum(attn_probs * d_probs, axis=-1, keepdims=True)
    d_scores = (attn_probs * (d_probs - row_inner)).astype(HALF_TYPE)
    d_queries = (
        jnp.einsum("bhps,bshc->bphc", d_scores, keys_all, preferred_element_type=FULL_TYPE)
        * score_scale
    )
    d_keys_part = (
        jnp.einsum("bhps,bphc->bshc", d_scores, queries, preferred_element_type=FULL_TYPE)
        * score_scale
    )
    d_keys, d_values = (
        lax.psum_scatter(
            d_keys_part.astype(jnp.bfloat16), "wide", scatter_dimension=1, tiled=True
        ).astype(jnp.float32),
        lax.psum_scatter(
            d_values_part.astype(jnp.bfloat16), "wide", scatter_dimension=1, tiled=True
        ).astype(jnp.float32),
    )
    positions = saved["positions"]
    d_query_pre = (
        rotate(d_queries, positions, -1.0)
        .astype(HALF_TYPE)
        .reshape(seq_count, row_count, head_count * head_dim)
    )
    d_key_pre = (
        rotate(d_keys, positions, -1.0)
        .astype(HALF_TYPE)
        .reshape(seq_count, row_count, head_count * head_dim)
    )
    d_projected = (
        (saved["value_gate"][..., None] * d_values[:, :, :, None, :])
        .astype(HALF_TYPE)
        .reshape(seq_count, row_count, head_count * value_experts * head_dim)
    )
    d_value_gate = jnp.sum(saved["projected"] * d_values[:, :, :, None, :], axis=-1)
    value_sig = saved["value_sig"]
    d_value_logit = (
        (d_value_gate * saved["value_choice"] * value_sig * (1.0 - value_sig))
        .astype(HALF_TYPE)
        .reshape(seq_count, row_count, head_count * value_experts)
    )
    normed_low = saved["normed_low"]
    grad_query = contract_rows(normed_low, d_query_pre)
    grad_key = contract_rows(normed_low, d_key_pre)
    grad_sel_value = contract_rows(normed_low, d_value_logit)
    grad_sel_out = contract_rows(normed_low, d_out_logit)
    grad_value = contract_rows(tokens, d_projected)
    d_normed = (
        times_transpose(d_query_pre, w_query)
        + times_transpose(d_key_pre, w_key)
        + times_transpose(d_value_logit, sel_value)
        + times_transpose(d_out_logit, sel_out)
    )
    grad_gain_one = jnp.sum(d_normed * saved["normal_one"], axis=(0, 1))
    grad_bias_one = jnp.sum(d_normed, axis=(0, 1))
    grad_tokens = (
        d_after
        + times_transpose(d_projected, w_value)
        + norm_back(d_normed, saved["normal_one"], saved["scale_one"], gain_one)
    ).astype(HALF_TYPE)
    (
        grad_query,
        grad_key,
        grad_value,
        grad_out,
        grad_sel_value,
        grad_sel_out,
        grad_gain_one,
        grad_bias_one,
        grad_gain_two,
        grad_bias_two,
    ) = lax.psum(
        (
            grad_query,
            grad_key,
            grad_value,
            grad_out,
            grad_sel_value,
            grad_sel_out,
            grad_gain_one,
            grad_bias_one,
            grad_gain_two,
            grad_bias_two,
        ),
        ("wide", "narrow"),
    )
    grad_select, grad_up, grad_down = (
        lax.psum(grad_select.astype(jnp.bfloat16), "narrow").astype(jnp.float32),
        lax.psum(grad_up.astype(jnp.bfloat16), "narrow").astype(jnp.float32),
        lax.psum(grad_down.astype(jnp.bfloat16), "narrow").astype(jnp.float32),
    )
    return (
        output,
        grad_tokens,
        grad_query,
        grad_key,
        grad_value,
        grad_out,
        grad_sel_value,
        grad_sel_out,
        grad_gain_one,
        grad_bias_one,
        grad_gain_two,
        grad_bias_two,
        grad_select,
        grad_up,
        grad_down,
    )


SELV = 72
SELO = 92
LANES = 128


def call(
    kernel, out_shape, *args, grid=None, in_specs=None, out_specs=None, scratch=(), flops=0, limit=56, prefetch=0, aliases=None
):
    moved = sum(a.size * a.dtype.itemsize for a in jax.tree.leaves((args, out_shape)))
    extra = {}
    if prefetch:
        extra["grid_spec"] = pltpu.PrefetchScalarGridSpec(
            num_scalar_prefetch=prefetch, grid=grid, in_specs=in_specs, out_specs=out_specs, scratch_shapes=list(scratch)
        )
    else:
        extra["scratch_shapes"] = list(scratch)
        if grid is not None:
            extra["grid"] = grid
        if in_specs is not None:
            extra["in_specs"] = in_specs
        if out_specs is not None:
            extra["out_specs"] = out_specs
    return pl.pallas_call(
        kernel,
        out_shape=out_shape,
        input_output_aliases=aliases or {},
        compiler_params=pltpu.CompilerParams(vmem_limit_bytes=limit * 1024 * 1024),
        cost_estimate=pl.CostEstimate(flops=int(flops), bytes_accessed=int(moved), transcendentals=0),
        **extra,
    )(*args)


def full(shape):
    rank = len(shape)
    return pl.BlockSpec(tuple(shape), lambda *s: (0,) * rank)


def shaped(shape, dtype=HALF_TYPE):
    return jax.ShapeDtypeStruct(tuple(shape), dtype)


def nn(a, b):
    return lax.dot_general(a, b, (((1,), (0,)), ((), ())), preferred_element_type=FULL_TYPE)


def nt(a, b):
    return lax.dot_general(a, b, (((1,), (1,)), ((), ())), preferred_element_type=FULL_TYPE)


def tn(a, b):
    return lax.dot_general(a, b, (((0,), (0,)), ((), ())), preferred_element_type=FULL_TYPE)


def layer_stats(v):
    centred = v - jnp.mean(v, axis=-1, keepdims=True)
    inv = lax.rsqrt(jnp.mean(centred * centred, axis=-1, keepdims=True) + EPSILON)
    return centred * inv, inv


def turned(v, cos, sin):
    return v * cos + pltpu.roll(v, v.shape[-1] // 2, axis=v.ndim - 1) * sin


def lane_ids(shape, dim):
    return lax.broadcasted_iota(jnp.int32, shape, dim)


def pre_kernel(spot, tok, gain, bias, wq, wk, wv, sel, vid, oid, cos, sin, select, qkv, proj, gate):
    heads = qkv.shape[0]
    experts = wv.shape[1] // (heads * LANES)
    low = tok[0]
    rows = low.shape[0]
    normal, _ = layer_stats(low.astype(FULL_TYPE))
    normed = (normal * gain[...] + bias[...]).astype(HALF_TYPE)
    for part, weight in ((0, wq), (1, wk)):
        pre = nn(normed, weight[...])
        for h in range(heads):
            head = turned(pre[:, h * LANES:(h + 1) * LANES], cos[...], sin[...])
            qkv[h, part * rows:(part + 1) * rows] = head.astype(HALF_TYPE)
    ids = lane_ids((LANES, rows), 0)
    chosen = jnp.zeros((LANES, rows), FULL_TYPE)
    tops = vid.shape[1] // heads
    for h in range(heads):
        for k in range(tops):
            j = h * tops + k
            chosen += (ids == vid[0, j:j + 1, :] + (SELV + experts * h)).astype(FULL_TYPE)
            chosen += (ids == oid[0, j:j + 1, :] + (SELO + experts * h)).astype(FULL_TYPE)
    gates = jax.nn.sigmoid(nt(normed, sel[...])) * jnp.transpose(chosen)
    gate[0] = gates
    gates_low = gates.astype(HALF_TYPE)
    for h in range(heads):
        at = h * experts * LANES
        block = nn(low, wv[:, at:at + experts * LANES])
        proj[0, :, at:at + experts * LANES] = block.astype(HALF_TYPE)
        total = None
        for e in range(experts):
            col = SELV + h * experts + e
            term = gates[:, col:col + 1] * block[:, e * LANES:(e + 1) * LANES]
            total = term if total is None else total + term
        qkv[h, 2 * rows:3 * rows] = total.astype(HALF_TYPE)
        first = SELV + h * experts
        row_id = lane_ids((8, LANES), 0)
        spot = (lane_ids((8, LANES), 1) == row_id + first) & (row_id < experts)
        turned_gates = nt(spot.astype(FULL_TYPE).astype(HALF_TYPE), gates_low)
        tail = jnp.concatenate([turned_gates[:, i * LANES:(i + 1) * LANES] for i in range(rows // LANES)], axis=0)
        last = 3 * rows + select.shape[0]
        qkv[h, 3 * rows:last] = select[...]
        qkv[h, last:last + tail.shape[0]] = tail.astype(HALF_TYPE)


def limits_of(i, rows, length):
    position = i * rows + lane_ids((1, rows), 1)
    return jnp.minimum(position + 1, length), position


def parts_of(ref, first, last, part, rows):
    block = ref[first:last, part * rows:(part + 1) * rows]
    return block.reshape((last - first) * rows, block.shape[2])


def attend_kernel(length, qkv, mixed, out_t, lse):
    blocks, rows, width = mixed.shape
    scale = width ** (-0.5)
    values_t = jnp.transpose(parts_of(qkv, 0, blocks, 2, rows).astype(FULL_TYPE)).astype(HALF_TYPE)
    for i in range(blocks):
        n = (i + 1) * rows
        keys = parts_of(qkv, 0, i + 1, 1, rows)
        limit, position = limits_of(i, rows, length[0])
        scores = nt(keys, qkv[i, 0:rows]) * scale
        scores = jnp.where(lane_ids((n, rows), 0) < limit, scores, -1e30)
        top = jnp.max(scores, axis=0, keepdims=True)
        weights = jnp.exp(scores - top)
        total = jnp.sum(weights, axis=0, keepdims=True)
        attended = nn(values_t[:, :n], weights.astype(HALF_TYPE)) / total
        out_t[:, i * rows:(i + 1) * rows] = attended
        lse[:, i * rows:(i + 1) * rows] = top + jnp.log(total)
        live = (position < length[0]).astype(FULL_TYPE)
        mixed[i] = jnp.transpose(attended * live).astype(HALF_TYPE)


def attend_back_kernel(length, qkv, d_out, out_t, lse, cos, sin, d_qkv, d_keys, d_values):
    blocks, rows, width = d_out.shape
    scale = width ** (-0.5)
    keys_t = jnp.transpose(parts_of(qkv, 0, blocks, 1, rows).astype(FULL_TYPE)).astype(HALF_TYPE)
    d_keys[...] = jnp.zeros_like(d_keys)
    d_values[...] = jnp.zeros_like(d_values)
    for i in range(blocks):
        n = (i + 1) * rows
        here = slice(i * rows, (i + 1) * rows)
        limit, _ = limits_of(i, rows, length[0])
        query = qkv[i, 0:rows]
        d_att = d_out[i]
        delta = jnp.sum(jnp.transpose(d_att.astype(FULL_TYPE)) * out_t[:, here], axis=0, keepdims=True)
        scores = nt(parts_of(qkv, 0, i + 1, 1, rows), query) * scale
        probs = jnp.where(lane_ids((n, rows), 0) < limit, jnp.exp(scores - lse[:, here]), 0.0)
        d_probs = nt(parts_of(qkv, 0, i + 1, 2, rows), d_att)
        d_scores = (probs * (d_probs - delta)).astype(HALF_TYPE)
        d_values[0:n, :] += nn(probs.astype(HALF_TYPE), d_att)
        d_keys[0:n, :] += nn(d_scores, query)
        d_query = jnp.transpose(nn(keys_t[:, :n], d_scores)) * scale
        d_qkv[i, 0:rows] = turned(d_query, cos[here, :], -sin[here, :]).astype(HALF_TYPE)
    for i in range(blocks):
        here = slice(i * rows, (i + 1) * rows)
        d_qkv[i, rows:2 * rows] = turned(d_keys[here, :] * scale, cos[here, :], -sin[here, :]).astype(HALF_TYPE)
        d_qkv[i, 2 * rows:3 * rows] = d_values[here, :].astype(HALF_TYPE)


def gated(mixed, gate, hp, e, experts):
    parts = []
    for h in (2 * hp, 2 * hp + 1):
        col = SELO + h * experts + e
        parts.append((gate[:, col:col + 1] * mixed[h].astype(FULL_TYPE)).astype(HALF_TYPE))
    return jnp.concatenate(parts, axis=1)


def out_block(w_out, hp, e, width):
    block = w_out[2 * hp:2 * hp + 2, :, e * width:(e + 1) * width]
    return block.reshape(2 * block.shape[1], width)


def post_kernel(mixed, gate, w_out, tok, gain, bias, columns, ids, places, after, gates, sent, select):
    width = tok.shape[2]
    heads = w_out.shape[0]
    experts = w_out.shape[2] // width
    row_count = tok.shape[1]
    total = tok[0].astype(FULL_TYPE)
    gate_here = gate[0]
    mixed_here = mixed[...]
    for hp in range(heads // 2):
        for e in range(experts):
            total += nn(gated(mixed_here, gate_here, hp, e, experts), out_block(w_out, hp, e, width))
    after[...] = total
    sent[0, 0:row_count] = total.astype(HALF_TYPE)
    normal, _ = layer_stats(total)
    normed = (normal * gain[...] + bias[...]).astype(HALF_TYPE)
    every = columns[...].astype(FULL_TYPE)
    count = every.shape[1]
    each = count // 8
    w_sel = jnp.concatenate(
        [every[:, j * each:(j + 1) * each].reshape(count, LANES) for j in range(8)], axis=1
    ).astype(HALF_TYPE)
    select[...] = w_sel
    row_id = lane_ids((count, row_count), 0)
    chosen = jnp.zeros((count, row_count), FULL_TYPE)
    for k in range(ids.shape[1]):
        chosen += (row_id == ids[0, k:k + 1, :]).astype(FULL_TYPE)
    values = jax.nn.sigmoid(nt(w_sel, normed)) * chosen
    gates[...] = values
    moved = nn(places[...], values.astype(HALF_TYPE)).astype(HALF_TYPE)
    quarter = count // 4
    for i in range(4):
        sent[0, row_count:row_count + quarter, i * row_count:(i + 1) * row_count] = moved[i * quarter:(i + 1) * quarter]


def weights_kernel(spots, up, down, mine, peer):
    for s, out in enumerate((mine, peer)):

        @pl.when(pl.program_id(0) == s)
        def _(out=out):
            out[0] = up[...]
            out[1] = jnp.transpose(down[...].astype(FULL_TYPE)).astype(HALF_TYPE)


def expand(count, cols, first):
    rows = lane_ids((count, cols), 0)
    cut = lane_ids((count, cols), 1)
    hit = None
    for i in range(cols // LANES):
        inside = (cut >= i * LANES) & (cut < (i + 1) * LANES) & (rows == first + i)
        hit = inside if hit is None else hit | inside
    return hit.astype(FULL_TYPE).astype(HALF_TYPE)


def experts_kernel(kind, halves, *refs):
    rows_in, cot, pieces = refs[:halves], refs[halves], refs[halves + 1:halves + 9]
    back, inner, d_pre = refs[halves + 9:]
    seqs, tall, width = back.shape
    row_count = width // 4
    cols = pieces[0].shape[2]
    quarter = tall - row_count
    picked = [rows_in[0][s] if halves == 1 else rows_in[s][...] for s in range(seqs)]
    low = jnp.concatenate([block[0:row_count] for block in picked], axis=0)
    gates = jnp.concatenate(
        [block[row_count:tall, kind * row_count:(kind + 1) * row_count] for block in picked], axis=1
    )
    cot_low = cot[...]
    row_total = gate_total = None
    weight = lambda p, u: pieces[p][u]
    root, cube = 0.7978845608028654, 0.044715
    for p in range(8):
        spread = expand(quarter, cols, p * (cols // LANES))
        gate_wide = tn(gates, spread)
        pre = nn(low, weight(p, 0))
        d_in = nn(cot_low, weight(p, 1))
        square = pre * pre
        tanh = jnp.tanh(pre * (root + (root * cube) * square))
        half = 0.5 + 0.5 * tanh
        act = pre * half
        slope = half + act * (1.0 - tanh) * (root + (3 * root * cube) * square)
        d_pre[p] = (slope * gate_wide * d_in).astype(HALF_TYPE)
        inner[p] = (act * gate_wide).astype(HALF_TYPE)
        g = nt(spread, (d_in * act).astype(HALF_TYPE))
        gate_total = g if p == 0 else gate_total + g
    for p in range(8):
        r = nt(d_pre[p], weight(p, 0))
        row_total = r if p == 0 else row_total + r
    for s in range(seqs):
        here = slice(s * row_count, (s + 1) * row_count)
        back[s, 0:row_count] = row_total[here].astype(HALF_TYPE)
        back[s, row_count:tall] = jnp.zeros((quarter, width), HALF_TYPE)
        back[s, row_count:tall, 0:row_count] = gate_total[:, here].astype(HALF_TYPE)


def branch_kernel(*refs):
    inners, pieces, outs = refs[0:4], refs[4:12], refs[12:16]
    downs = [ref[1] for ref in pieces]
    for i in range(4):
        total = None
        for p in range(8):
            term = nt(inners[i][p], downs[p])
            total = term if p == 0 else total + term
        outs[i][...] = total.astype(HALF_TYPE)


def expert_grads_kernel(*refs):
    rows, cots, pres, inners = refs[0:5], refs[5:9], refs[9:13], refs[13:17]
    outs = refs[17:21]
    step = pl.program_id(0)
    row_count = pres[0].shape[1] // 2
    up = down = None
    for i in range(4):
        for s in range(2):
            block = rows[i][s, 0:row_count] if i < 3 else rows[3 + s][0:row_count]
            term = tn(block, pres[i][0, s * row_count:(s + 1) * row_count])
            up = term if up is None else up + term
        term = tn(cots[i][...], inners[i][0])
        down = term if down is None else down + term
    results = (up.astype(HALF_TYPE), down.astype(HALF_TYPE))
    for j in range(4):

        @pl.when(step // 2 == j)
        def _(j=j):
            for u in range(2):
                outs[j][0, u] = results[u]


def mid_kernel(length, r0, r1, r2, r3, cot, after, gates, gain, bias, w_sel, places, w_out, gate, mixed,
               d_after, d_att, d_gate_out, small, acc):
    step = pl.program_id(0)
    width = cot.shape[2]
    heads = w_out.shape[0]
    experts = w_out.shape[2] // width
    row_count = cot.shape[1]
    tall = r0.shape[1]
    d_rel = jnp.concatenate([r[0, row_count:tall, 0:row_count] for r in (r0, r1, r2, r3)], axis=0)
    d_gate = tn(places[...], d_rel)
    values = gates[...]
    d_logit = (d_gate * values * (1.0 - values)).astype(HALF_TYPE)
    normal, inv = layer_stats(after[...])
    normed = (normal * gain[...] + bias[...]).astype(HALF_TYPE)
    d_normed = tn(d_logit, w_sel[...])
    sel_part = nn(d_logit, normed)
    gain_part = jnp.sum(d_normed * normal, axis=0, keepdims=True)
    bias_part = jnp.sum(d_normed, axis=0, keepdims=True)
    count = sel_part.shape[0]

    @pl.when(step == 0)
    def _():
        acc[...] = jnp.zeros_like(acc)

    acc[0:count, :] += sel_part
    acc[count:count + 1, :] += gain_part
    acc[count + 1:count + 2, :] += bias_part
    d_row = sum(r[0, 0:row_count].astype(FULL_TYPE) for r in (r0, r1, r2, r3))
    total = cot[0].astype(FULL_TYPE) + d_row + norm_back(d_normed, normal, inv, gain[...])
    d_after[...] = total
    total_low = total.astype(HALF_TYPE)
    mixed_here = mixed[...]
    gate_here = gate[0]
    lanes = lane_ids((2 * LANES, LANES), 1)
    second = (lane_ids((2 * LANES, LANES), 0) >= LANES).astype(jnp.int32)
    d_gates = jnp.zeros((row_count, LANES), FULL_TYPE)
    for hp in range(heads // 2):
        both = jnp.concatenate([mixed_here[2 * hp], mixed_here[2 * hp + 1]], axis=1).astype(FULL_TYPE)
        sums = [None, None]
        for e in range(experts):
            d_mixed = nt(total_low, out_block(w_out, hp, e, width))
            hit = (lanes == SELO + 2 * hp * experts + e + second * experts).astype(FULL_TYPE).astype(HALF_TYPE)
            d_gates += nn((both * d_mixed).astype(HALF_TYPE), hit)
            for i in range(2):
                col = SELO + (2 * hp + i) * experts + e
                term = gate_here[:, col:col + 1] * d_mixed[:, i * LANES:(i + 1) * LANES]
                sums[i] = term if e == 0 else sums[i] + term
        for i in range(2):
            position = length[1] + lane_ids((row_count, 1), 0)
            live = (position < length[2 + step]).astype(FULL_TYPE)
            d_att[2 * hp + i] = (sums[i] * live).astype(HALF_TYPE)
    d_gate_out[0] = d_gates

    @pl.when(step == pl.num_programs(0) - 1)
    def _():
        spots = (lane_ids((LANES, LANES), 0) == lanes[0:LANES]).astype(FULL_TYPE).astype(HALF_TYPE)
        small[...] = tn(acc[...].astype(HALF_TYPE), spots)


def out_grad_kernel(mixed, gate, d_after, out):
    heads, experts = 4, out.shape[1] // d_after.shape[1]
    width = d_after.shape[1]
    seqs, row_count = gate.shape[0], gate.shape[1]
    low = d_after[...].astype(HALF_TYPE)
    for hp in range(heads // 2):
        for e in range(experts):
            total = None
            for s in range(seqs):
                left = gated([mixed[s * heads + h] for h in range(heads)], gate[s], hp, e, experts)
                term = tn(left, low[s * row_count:(s + 1) * row_count, :])
                total = term if total is None else total + term
            out[2 * hp * LANES:(2 * hp + 2) * LANES, e * width:(e + 1) * width] = total.astype(HALF_TYPE)


def last_kernel(d_qkv, tok, gain, bias, wq, wk, wv, sel, proj, gate, d_gate_out, small, d_after,
                out, sums, d_proj, acc):
    step = pl.program_id(0)
    row_count, width = tok.shape[1], tok.shape[2]
    heads = d_qkv.shape[0]
    experts = proj.shape[2] // (heads * LANES)
    lanes = lane_ids((LANES, LANES), 1)
    low = tok[0]
    normal, inv = layer_stats(low.astype(FULL_TYPE))
    normed = (normal * gain[...] + bias[...]).astype(HALF_TYPE)
    d_gates = d_gate_out[0]
    gate_here = gate[0]
    d_query = jnp.concatenate([d_qkv[h, 0:row_count] for h in range(heads)], axis=1)
    d_key = jnp.concatenate([d_qkv[h, row_count:2 * row_count] for h in range(heads)], axis=1)
    for h in range(heads):
        d_value = d_qkv[h, 2 * row_count:3 * row_count].astype(FULL_TYPE)
        for e in range(experts):
            col = SELV + h * experts + e
            at = (h * experts + e) * LANES
            d_proj[:, at:at + LANES] = (gate_here[:, col:col + 1] * d_value).astype(HALF_TYPE)
            hit = (lanes == col).astype(FULL_TYPE).astype(HALF_TYPE)
            product = (proj[0, :, at:at + LANES].astype(FULL_TYPE) * d_value).astype(HALF_TYPE)
            d_gates += nn(product, hit)
    d_logit = (d_gates * gate_here * (1.0 - gate_here)).astype(HALF_TYPE)
    d_normed = nt(d_query, wq[...]) + nt(d_key, wk[...]) + nn(d_logit, sel[...])
    total = d_after[...] + norm_back(d_normed, normal, inv, gain[...]) + nt(d_proj[...], wv[...])
    out[...] = total.astype(HALF_TYPE)
    gain_sum = jnp.sum(d_normed * normal, axis=0, keepdims=True)
    bias_sum = jnp.sum(d_normed, axis=0, keepdims=True)
    rows = jnp.concatenate([gain_sum, bias_sum, jnp.zeros((14, width), FULL_TYPE)], axis=0).astype(HALF_TYPE)
    spot = (lane_ids((16, LANES), 1) == lane_ids((16, LANES), 0) + 66) & (lane_ids((16, LANES), 0) < 2)
    spread = tn(rows, spot.astype(FULL_TYPE).astype(HALF_TYPE))
    part = tn(normed, d_logit) + spread

    @pl.when(step == 0)
    def _():
        acc[...] = small[...] + part

    @pl.when(step > 0)
    def _():
        acc[...] += part

    sums[...] = acc[...].astype(HALF_TYPE)


def turn_kernel(near, far, gain, bias, tok_t, norm_t):
    step = pl.program_id(0)

    def turn(low):
        normal, _ = layer_stats(low.astype(FULL_TYPE))
        tok_t[0] = jnp.transpose(low.astype(FULL_TYPE)).astype(HALF_TYPE)
        normed = (normal * gain[...] + bias[...]).astype(HALF_TYPE)
        norm_t[0] = jnp.transpose(normed.astype(FULL_TYPE)).astype(HALF_TYPE)

    @pl.when(step < 4)
    def _():
        turn(near[0])

    @pl.when(step >= 4)
    def _():
        turn(far[0])


def head_grads_kernel(spot, tok_t, norm_t, d_qkv, gate, out, acc):
    step = pl.program_id(0)
    rows = tok_t.shape[2]
    experts = out.shape[1] // LANES - 2
    both = jnp.concatenate([d_qkv[0, 0:rows], d_qkv[0, rows:2 * rows]], axis=1)
    wide = experts * LANES
    spread = expand(8, wide, 0)
    tail = gate[0]
    gates = jnp.concatenate([tn(tail[i * 8:(i + 1) * 8], spread) for i in range(rows // LANES)], axis=0)
    d_value = d_qkv[0, 2 * rows:3 * rows].astype(FULL_TYPE)
    d_proj = (gates * jnp.concatenate([d_value] * experts, axis=1)).astype(HALF_TYPE)
    first = nn(norm_t[0], both)
    second = nn(tok_t[0], d_proj)

    @pl.when(step == 0)
    def _():
        acc[:, 0:2 * LANES] = first
        acc[:, 2 * LANES:] = second

    @pl.when(step > 0)
    def _():
        acc[:, 0:2 * LANES] += first
        acc[:, 2 * LANES:] += second

    @pl.when(step == pl.num_programs(0) - 1)
    def _():
        out[...] = acc[...].astype(HALF_TYPE)


def place_heads_kernel(bits, *refs):
    sources = refs[:4]
    query, key, value = refs[-3:]
    step = pl.program_id(0)
    y, x, high, low = bits[0], bits[1], bits[2], bits[3]
    wide = value.shape[1] // 4
    size = value.shape[0] // 2

    def put(block, head, place):
        here = pl.ds(pl.multiple_of(place * size, size), size)
        at = pl.multiple_of(head * LANES, LANES)
        query[here, pl.ds(at, LANES)] = block[:, 0:LANES].astype(FULL_TYPE)
        key[here, pl.ds(at, LANES)] = block[:, LANES:2 * LANES].astype(FULL_TYPE)
        value[here, pl.ds(pl.multiple_of(head * wide, LANES), wide)] = block[:, 2 * LANES:].astype(FULL_TYPE)

    for j in range(2):

        @pl.when(step == j)
        def _(j=j):
            for i in range(2):
                for b in range(2):
                    for a in range(2):
                        put(sources[j][i, b, a], (low ^ b) * 2 + (x ^ i), high ^ a)

    @pl.when(step >= 2)
    def _():
        for j in range(2):
            for i in range(2):
                for b in range(2):
                    put(sources[2 + j][i, b, 0], (low ^ b) * 2 + (x ^ j), y ^ i)


def place_out_kernel(spot, mine, *rest):
    rest[-1][0] = mine[...].astype(FULL_TYPE)


def place_small_kernel(first, small, select, value, out, rows):
    low = small[...]

    def rows_of(count, start):
        hit = lane_ids((count, LANES), 1) == lane_ids((count, LANES), 0) + start
        return nt(hit.astype(FULL_TYPE).astype(HALF_TYPE), low)

    select[...] = rows_of(select.shape[0], first[0])
    value[...] = rows_of(value.shape[0], SELV)
    out[...] = rows_of(out.shape[0], SELO)
    spots = (lane_ids((8, LANES), 1) == lane_ids((8, LANES), 0) + 64) & (lane_ids((8, LANES), 0) < 4)
    rows[...] = nt(spots.astype(FULL_TYPE).astype(HALF_TYPE), low)


def place_experts_kernel(spots, mine, mine_y, *rest):
    up, down = rest[-2:]
    for i, ref in enumerate((mine, mine_y)):

        @pl.when(pl.program_id(0) == i)
        def _(ref=ref):
            up[...] = ref[0].astype(FULL_TYPE)
            down[...] = jnp.transpose(ref[1].astype(FULL_TYPE))


def output_kernel(after, own, first, last, out):
    out[...] = (
        after[...] + own[...].astype(FULL_TYPE) + first[...].astype(FULL_TYPE) + last[...].astype(FULL_TYPE)
    ).astype(HALF_TYPE)


class Place:
    def __init__(self):
        self.wide = lax.axis_index("wide")
        self.narrow = lax.axis_index("narrow")
        self.z, self.x = self.wide // 2, self.wide % 2
        self.y, self.c = self.narrow // 2, self.narrow % 2
        self.high, self.low = self.z // 2, self.z % 2

    @staticmethod
    def pairs(move):
        every = []
        for z in range(4):
            for x in range(2):
                for y in range(2):
                    for c in range(2):
                        tz, tx, ty, tc = move(z, x, y, c)
                        every.append(((z * 2 + x) * 4 + y * 2 + c, (tz * 2 + tx) * 4 + ty * 2 + tc))
        return every

    def send(self, value, move):
        return lax.ppermute(value, ("wide", "narrow"), self.pairs(move))

    def swap_x(self, value):
        return self.send(value, lambda z, x, y, c: (z, 1 - x, y, c))

    def swap_y(self, value):
        return self.send(value, lambda z, x, y, c: (z, x, 1 - y, c))

    def swap_xy(self, value):
        return self.send(value, lambda z, x, y, c: (z, 1 - x, 1 - y, c))

    def swap_c(self, value):
        return self.send(value, lambda z, x, y, c: (z, x, y, 1 - c))

    def swap_low(self, value):
        return self.send(value, lambda z, x, y, c: (z ^ 1, x, y, c))

    def swap_high(self, value):
        return self.send(value, lambda z, x, y, c: (z ^ 2, x, y, c))


def pick(array, index):
    return lax.dynamic_index_in_dim(array, index, 0, keepdims=False)


def add(*terms):
    total = terms[0].astype(FULL_TYPE)
    for term in terms[1:]:
        total = total + term.astype(FULL_TYPE)
    return total.astype(HALF_TYPE)


def in_order(bit, mine, other):
    return jnp.stack([jnp.where(bit == 0, mine, other), jnp.where(bit == 0, other, mine)])


def tie(value, *others):
    return lax.optimization_barrier((value,) + others)[0]


def halve(bit, swap, value):
    return add(pick(value, bit), swap(pick(value, 1 - bit)))


def place_out(place, half, core, heads, begun):
    rows, cols = half.shape
    size = 2 * rows // heads
    more = begun or ()
    return call(
        place_out_kernel,
        shaped((heads, size, cols), FULL_TYPE),
        (place.c ^ core).reshape(1).astype(jnp.int32), half, *more,
        grid=(heads // 2,), prefetch=1,
        in_specs=[pl.BlockSpec((size, cols), lambda s, spot: (s, 0))] + [pl.BlockSpec(memory_space=pl.ANY)] * len(more),
        out_specs=pl.BlockSpec((1, size, cols), lambda s, spot: (spot[0] * (heads // 2) + s, 0, 0)),
        aliases={2 + i: i for i in range(len(more))},
    )


def place_experts(place, mine, mine_y, core, begun):
    width, local = mine.shape[1:]
    more = begun or ()
    return call(
        place_experts_kernel,
        (shaped((width, 4 * local), FULL_TYPE), shaped((4 * local, width), FULL_TYPE)),
        jnp.stack([place.narrow ^ core, place.narrow ^ core ^ 2]).astype(jnp.int32), mine, mine_y, *more,
        grid=(2,), prefetch=1,
        in_specs=[full(mine.shape)] * 2 + [pl.BlockSpec(memory_space=pl.ANY)] * len(more),
        out_specs=(
            pl.BlockSpec((width, local), lambda s, spots: (0, spots[s])),
            pl.BlockSpec((local, width), lambda s, spots: (spots[s], 0)),
        ),
        aliases={3 + i: i for i in range(len(more))},
    )


def place_heads(place, sources, core, heads, rows, begun):
    size, cols = sources[0].shape[3:]

    def block(j):
        if j < 2:
            return pl.BlockSpec((2, 2, 2, size, cols), lambda s, bits: (0, 0, 0, 0, 0))
        return pl.BlockSpec((2, 2, 1, size, cols), lambda s, bits: (0, 0, jnp.where(s < 2, 0, s % 2), 0, 0))

    def row_block(s, bits):
        inside = jnp.where(s < 2, bits[0], bits[2]) ^ (s % 2)
        return (((bits[4] ^ core) * 2 + s // 2) * 2 + inside, 0)

    wide = cols - 2 * LANES
    more = () if begun is None else tuple(begun)
    return call(
        place_heads_kernel,
        (
            shaped((rows, heads * LANES), FULL_TYPE), shaped((rows, heads * LANES), FULL_TYPE),
            shaped((rows, heads * wide), FULL_TYPE),
        ),
        jnp.stack([place.y, place.x, place.high, place.low, place.c]).astype(jnp.int32), *sources, *more,
        grid=(4,), prefetch=1,
        in_specs=[block(j) for j in range(4)] + [pl.BlockSpec(memory_space=pl.ANY)] * len(more),
        out_specs=(
            pl.BlockSpec((2 * size, heads * LANES), row_block), pl.BlockSpec((2 * size, heads * LANES), row_block),
            pl.BlockSpec((2 * size, heads * wide), row_block),
        ),
        aliases={5 + i: i for i in range(len(more))},
    )


def turn_tables(span, head_dim):
    half = head_dim // 2
    frequency = np.float32(10000.0) ** (-(np.arange(half).astype(np.float32) * np.float32(2.0) / np.float32(head_dim)))
    angles = np.arange(span).astype(np.float32)[:, None] * frequency[None, :].astype(np.float32)
    cosine, sine = np.cos(angles.astype(np.float64)), np.sin(angles.astype(np.float64))
    return (
        jnp.asarray(np.concatenate([cosine, cosine], axis=1).astype(np.float32)),
        jnp.asarray(np.concatenate([-sine, sine], axis=1).astype(np.float32)),
    )


def tuned_device(
    tokens, lengths, value_ids, out_ids, mlp_ids, w_query, w_key, w_value, w_out, sel_value, sel_out,
    gain_one, bias_one, gain_two, bias_two, w_select, w_up, w_down, cotangent,
):
    seqs, row_count, width = tokens.shape
    heads, head_dim = w_out.shape[0], w_out.shape[1]
    experts = w_out.shape[2] // width
    pair_count = seqs * heads
    span = 8 * row_count
    all_rows = seqs * row_count
    wide_out = heads * experts * LANES
    local = w_up.shape[1] // 4
    hidden = 8 * local
    own_count = w_select.shape[1]
    count = 8 * own_count
    quarter = count // 4
    tall = row_count + quarter
    place = Place()
    first_row = place.wide * row_count
    row = lambda v: v.reshape(1, -1)
    smem = pl.BlockSpec(memory_space=pltpu.SMEM)
    vmem = pl.BlockSpec(memory_space=pltpu.VMEM)
    hbm = pl.BlockSpec(memory_space=pl.ANY)
    by_seq = lambda shape: pl.BlockSpec((1,) + tuple(shape[1:]), lambda s, *_: (s,) + (0,) * (len(shape) - 1))
    split = lambda shape: pl.BlockSpec((shape[0] // seqs,) + tuple(shape[1:]), lambda s, *_: (s,) + (0,) * (len(shape) - 1))
    token_cols = lambda n: pl.BlockSpec((n, row_count), lambda s: (0, s))

    own_select = jnp.transpose(w_select).reshape(own_count, 8, -1).swapaxes(0, 1).reshape(-1, LANES)

    mine_peer = jnp.stack([place.narrow, place.narrow + 1 - 2 * place.c]).astype(jnp.int32)
    weights_mine, weights_peer = call(
        weights_kernel,
        (shaped((2, width, local)), shaped((2, width, local))),
        mine_peer, w_up, w_down,
        grid=(2,), prefetch=1,
        in_specs=[
            pl.BlockSpec((width, local), lambda s, spots: (0, spots[s])),
            pl.BlockSpec((local, width), lambda s, spots: (spots[s], 0)),
        ],
        out_specs=(full((2, width, local)), full((2, width, local))),
    )

    cot_own = cotangent.reshape(all_rows, width)
    cots = [cot_own, place.swap_y(cot_own)]
    tokens_x = place.swap_x(tokens)

    cosine, sine = turn_tables(span, head_dim)
    sel = jnp.concatenate(
        [
            jnp.zeros((SELV, width), HALF_TYPE), sel_value.T, sel_out.T,
            jnp.zeros((LANES - SELO - heads * experts, width), HALF_TYPE),
        ],
        axis=0,
    )
    value_flat = jnp.transpose(value_ids, (0, 2, 3, 1)).reshape(seqs, -1, row_count)
    out_flat = jnp.transpose(out_ids, (0, 2, 3, 1)).reshape(seqs, -1, row_count)
    payload = 3 * row_count + own_select.shape[0] + 16
    qkv, projected, gate = call(
        pre_kernel,
        (
            shaped((pair_count, payload, head_dim)),
            shaped((seqs, row_count, wide_out)),
            shaped((seqs, row_count, LANES), FULL_TYPE),
        ),
        place.wide.reshape(1).astype(jnp.int32), tokens, row(gain_one), row(bias_one), w_query, w_key, w_value, sel,
        value_flat, out_flat, cosine, sine, own_select,
        grid=(seqs,), prefetch=1,
        in_specs=[
            by_seq(tokens.shape), full((1, width)), full((1, width)), full(w_query.shape), full(w_key.shape),
            full(w_value.shape), full(sel.shape), by_seq(value_flat.shape), by_seq(out_flat.shape),
            pl.BlockSpec((row_count, head_dim), lambda s, spot: (spot[0], 0)),
            pl.BlockSpec((row_count, head_dim), lambda s, spot: (spot[0], 0)),
            full(own_select.shape),
        ],
        out_specs=(
            split((pair_count, payload, head_dim)), by_seq((seqs, row_count, wide_out)),
            by_seq((seqs, row_count, LANES)),
        ),
        flops=2 * all_rows * width * 3712,
    )
    qkv = lax.all_to_all(qkv, "wide", 0, 0, tiled=True)
    qkv, cots[1], tokens_x, weights_mine = lax.optimization_barrier((qkv, cots[1], tokens_x, weights_mine))
    weights_far, weights_near = place.swap_high(weights_mine), place.swap_low(weights_mine)
    cot_later = tie(cot_own, qkv)
    cots += [place.swap_x(cot_later), place.swap_xy(cot_later)]
    seq_here = place.wide // heads
    length = pick(lengths, seq_here).reshape(1)
    mixed, out_t, lse = call(
        attend_kernel,
        (
            shaped((8, row_count, head_dim)), shaped((head_dim, span), FULL_TYPE), shaped((1, span), FULL_TYPE),
        ),
        length, qkv,
        in_specs=[smem, vmem],
        flops=2 * span * span * head_dim,
    )
    mixed = lax.all_to_all(mixed, "wide", 0, 0, tiled=True)
    mixed, weights_far, weights_near, cots[2], cots[3] = lax.optimization_barrier(
        (mixed, weights_far, weights_near, cots[2], cots[3])
    )
    weights_last = place.swap_low(weights_far)

    kinds = (place.x * 2 + place.y) ^ jnp.arange(4)
    kx, ky = (kinds // 2)[:, None, None, None], (kinds % 2)[:, None, None, None]
    kz = (place.z ^ jnp.arange(4))[None, :, None, None]
    kc = (place.c ^ jnp.arange(2))[None, None, :, None]
    ki = jnp.arange(2)[None, None, None, :]
    sent_ids = ((kz * 2 + kx) * own_count + ky * 4 + kc * 2 + ki).reshape(-1)
    places = (sent_ids[:, None] == jnp.arange(count)[None, :]).astype(HALF_TYPE)

    own_mlp = lax.dynamic_slice_in_dim(mlp_ids, first_row, row_count, 1)
    own_mlp = jnp.swapaxes(own_mlp, 1, 2)
    after, gates, rows_own, select = call(
        post_kernel,
        (
            shaped((all_rows, width), FULL_TYPE), shaped((count, all_rows), FULL_TYPE), shaped((seqs, tall, width)),
            shaped((count, width)),
        ),
        mixed, gate, w_out, tokens, row(gain_two), row(bias_two), qkv, own_mlp, places,
        grid=(seqs,),
        in_specs=[
            split(mixed.shape), by_seq(gate.shape), full(w_out.shape), by_seq(tokens.shape), full((1, width)),
            full((1, width)), pl.BlockSpec((8, 8 * own_count, LANES), lambda s: (0, 3 * row_count // (8 * own_count), 0)),
            by_seq(own_mlp.shape), full(places.shape),
        ],
        out_specs=(
            split((all_rows, width)), token_cols(count), by_seq((seqs, tall, width)), full((count, width)),
        ),
        flops=2 * all_rows * width * wide_out,
    )

    rows_y, rows_x = place.swap_y(rows_own), place.swap_x(rows_own)
    rows_d = (place.swap_x(rows_y[0]), place.swap_y(rows_x[1]))
    rows_in = [(rows_own,), (rows_y,), (rows_x,), rows_d]
    weights = [weights_mine, weights_peer]
    for piece in (weights_near, weights_far, weights_last):
        weights += [piece, place.swap_c(piece)]
    own_two = jnp.stack([pick(tokens, seq_here), pick(tokens_x, seq_here)])
    other_two = jnp.stack([pick(tokens, 1 - seq_here), pick(tokens_x, 1 - seq_here)])
    other_two = place.swap_high(tie(other_two, rows_own))
    results = {}
    for i, before in ((1, None), (2, 1), (3, 2), (0, 3)):
        if before is not None:
            cots[i] = tie(cots[i], results[before][1])
        results[i] = call(
                functools.partial(experts_kernel, i, len(rows_in[i])),
                (
                    shaped((seqs, tall, width)), shaped((8, all_rows, local)), shaped((8, all_rows, local)),
                ),
                *rows_in[i], cots[i], *weights,
                flops=8 * all_rows * width * hidden,
            )
    swaps = (lambda v: v, place.swap_y, place.swap_x, place.swap_xy)
    d_rows = [swaps[i](results[i][0]) for i in range(4)]
    inners = [results[i][1] for i in range(4)]
    near_four = jnp.concatenate([own_two, tie(other_two, results[2][1])])
    far_four = place.swap_low(near_four)

    whole = lambda shape: pl.BlockSpec(tuple(shape), lambda p: (0,) * len(shape))
    piece = lambda: pl.BlockSpec((1, all_rows, local), lambda p: (2 * (2 * (p % 2) + (p // 2) % 2) + p // 4, 0, 0))
    grad_near, grad_far, peer_near, peer_far = call(
        expert_grads_kernel,
        (shaped((2, 2, width, local)),) * 4,
        rows_own, rows_y, rows_x, *rows_d, *cots, *[results[i][2] for i in range(4)], *inners,
        grid=(8,),
        in_specs=[whole((seqs, tall, width))] * 3 + [whole((tall, width))] * 2 + [whole((all_rows, width))] * 4
        + [piece() for _ in range(8)],
        out_specs=tuple(
            pl.BlockSpec((1, 2, width, local), lambda p, j=j: (jnp.clip(p - 2 * j, 0, 1), 0, 0, 0)) for j in range(4)
        ),
        flops=16 * all_rows * width * hidden,
    )
    d_rows[1], d_rows[2], d_rows[3], peer_far, peer_near, far_four = lax.optimization_barrier(
        (d_rows[1], d_rows[2], tie(d_rows[3], grad_near), peer_far, peer_near, far_four)
    )
    came_far, came_near = place.swap_c(peer_far), place.swap_c(peer_near)

    live_info = jnp.concatenate([jnp.zeros((1,), jnp.int32), first_row.reshape(1).astype(jnp.int32), lengths])
    d_after, d_att, d_gate_out, small = call(
        mid_kernel,
        (
            shaped((all_rows, width), FULL_TYPE), shaped((pair_count, row_count, head_dim)),
            shaped((seqs, row_count, LANES), FULL_TYPE), shaped((width, LANES), FULL_TYPE),
        ),
        live_info, *d_rows, cotangent, after, gates, row(gain_two), row(bias_two), select, places,
        w_out, gate, mixed,
        grid=(seqs,),
        in_specs=[smem] + [by_seq((seqs, tall, width))] * 4 + [
            by_seq(cotangent.shape), split((all_rows, width)), token_cols(count), full((1, width)), full((1, width)),
            full(select.shape), full(places.shape), full(w_out.shape), by_seq(gate.shape),
            split(mixed.shape),
        ],
        out_specs=(
            split((all_rows, width)), split((pair_count, row_count, head_dim)),
            by_seq((seqs, row_count, LANES)), full((width, LANES)),
        ),
        scratch=[pltpu.VMEM((LANES, width), FULL_TYPE)],
        flops=2 * all_rows * width * wide_out,
    )
    d_att_all = lax.all_to_all(d_att, "wide", 0, 0, tiled=True)

    to_low = [add(grad_far[a], came_far[a]) for a in range(2)]
    passed = [None, place.swap_low(to_low[1])]
    near_four = tie(near_four, d_att, *to_low)
    tok_t, norm_t = call(
        turn_kernel,
        (shaped((8, width, row_count)), shaped((8, width, row_count))),
        near_four, far_four, row(gain_one), row(bias_one),
        grid=(8,),
        in_specs=[
            pl.BlockSpec((1, row_count, width), lambda i: (jnp.minimum(i, 3), 0, 0)),
            pl.BlockSpec((1, row_count, width), lambda i: (jnp.maximum(i - 4, 0), 0, 0)),
            full((1, width)), full((1, width)),
        ],
        out_specs=(
            pl.BlockSpec((1, width, row_count), lambda i: (i, 0, 0)),
            pl.BlockSpec((1, width, row_count), lambda i: (i, 0, 0)),
        ),
    )
    grad_out = call(
        out_grad_kernel, shaped((heads * head_dim, experts * width)), tie(mixed, d_att, tok_t), gate, d_after,
        flops=2 * all_rows * width * wide_out,
    )
    rows_out, cols_out = grad_out.shape
    flat = ((place.y, place.swap_y), (place.x, place.swap_x))
    d_att_all, tok_t, grad_out = lax.optimization_barrier((d_att_all, tok_t, grad_out))
    out_parts = halve(place.c, place.swap_c, grad_out.reshape(2, 2, 2, 2, 2, 2, rows_out // 64, cols_out))

    d_qkv = call(
        attend_back_kernel,
        shaped((8, 3 * row_count, head_dim)),
        length, qkv, d_att_all, out_t, lse, cosine, sine,
        in_specs=[smem] + [vmem] * 6,
        scratch=[pltpu.VMEM((span, head_dim), FULL_TYPE), pltpu.VMEM((span, head_dim), FULL_TYPE)],
        flops=5 * span * span * head_dim,
    )

    d_qkv, out_parts = lax.optimization_barrier((d_qkv, out_parts))
    out_parts = [halve(*flat[i], out_parts[i]) for i in range(2)]

    block_of = lambda i, spot: spot[0] ^ ((i & 1) | ((i & 2) << 1) | ((i & 4) >> 1))
    head_cols = (2 + experts) * LANES
    head_grads = call(
        head_grads_kernel,
        shaped((width, head_cols)),
        place.wide.reshape(1).astype(jnp.int32), tok_t, norm_t, d_qkv, qkv,
        grid=(8,), prefetch=1,
        in_specs=[
            pl.BlockSpec((1, width, row_count), lambda i, spot: (i, 0, 0)),
            pl.BlockSpec((1, width, row_count), lambda i, spot: (i, 0, 0)),
            pl.BlockSpec((1, 3 * row_count, head_dim), lambda i, spot: (block_of(i, spot), 0, 0)),
            pl.BlockSpec((1, 16, head_dim), lambda i, spot: (block_of(i, spot), payload // 16 - 1, 0)),
        ],
        out_specs=pl.BlockSpec((width, head_cols), lambda i, spot: (0, 0)),
        scratch=[pltpu.VMEM((width, head_cols), FULL_TYPE)],
        flops=2 * span * width * head_cols,
    )
    d_qkv_rows = lax.all_to_all(d_qkv, "wide", 0, 0, tiled=True)
    bits = ((place.y, place.swap_y), (place.high, place.swap_high))
    rows_head = width // 16
    head_grads, out_parts[0], out_parts[1] = lax.optimization_barrier((head_grads, *out_parts))
    out_parts = [halve(*flat[1 - i], out_parts[i]) for i in range(2)]
    kept = halve(place.c, place.swap_c, head_grads.reshape(2, 2, 2, 2, rows_head, head_cols))
    branches = call(
        branch_kernel,
        (shaped((all_rows, width)),) * 4,
        tie(inners[0], head_grads), *inners[1:], *weights,
        flops=8 * all_rows * width * hidden,
    )
    b0, b1, b2, b3 = branches
    kept, out_sum, b1, b2, b3 = lax.optimization_barrier((kept, jnp.stack(out_parts, axis=2), b1, b2, b3))
    b3 = place.swap_x(b3)
    out_sum = halve(place.low, place.swap_low, out_sum)
    value = [halve(*bits[i], kept[i]) for i in range(2)]
    value[0], value[1], d_qkv_rows, out_sum = lax.optimization_barrier((value[0], value[1], d_qkv_rows, out_sum))
    value = [halve(*bits[1 - i], value[i]) for i in range(2)]
    out_sum = halve(place.high, place.swap_high, out_sum)
    grad_tokens, small = call(
        last_kernel,
        (shaped((all_rows, width)), shaped((width, LANES))),
        d_qkv_rows, tokens, row(gain_one), row(bias_one), w_query, w_key, w_value, sel, projected, gate, d_gate_out,
        small, d_after,
        grid=(seqs,),
        in_specs=[
            split(d_qkv.shape), by_seq(tokens.shape), full((1, width)), full((1, width)), full(w_query.shape),
            full(w_key.shape), full(w_value.shape), full(sel.shape), by_seq(projected.shape), by_seq(gate.shape),
            by_seq(d_gate_out.shape), full(small.shape), split(d_after.shape),
        ],
        out_specs=(split((all_rows, width)), full((width, LANES))),
        scratch=[pltpu.VMEM((row_count, wide_out), HALF_TYPE), pltpu.VMEM((width, LANES), FULL_TYPE)],
        flops=2 * all_rows * width * 3712,
    )
    done, small, out_sum, b3 = lax.optimization_barrier((jnp.stack(value), small, out_sum, b3))
    b1 = place.swap_y(add(b1, b3))
    b2 = place.swap_x(tie(b2, b3))
    far = place.swap_high(done)
    out_sum = in_order(place.high, out_sum, place.swap_high(out_sum))
    everywhere = ("wide", "narrow")
    small = lax.all_to_all(small, everywhere, 0, 0, tiled=True).reshape(32, -1, LANES)
    far, out_sum = lax.optimization_barrier((far, out_sum))
    out_sum = in_order(place.low, out_sum, place.swap_low(out_sum))
    near = [place.swap_low(done), place.swap_low(far)]
    sets = [
        jnp.stack([jnp.stack([done[i], far[i]]), jnp.stack([near[0][i], near[1][i]])]) for i in range(2)
    ]
    passed[0] = place.swap_low(tie(to_low[0], near[1]))
    to_high = add(grad_near[1], came_near[1], tie(passed[1], done))
    sets[0], sets[1], small, out_sum, b1, b2, to_high = lax.optimization_barrier(
        (sets[0], sets[1], small, out_sum, b1, b2, to_high)
    )
    mine_far = place.swap_high(to_high)
    small = jnp.sum(small.astype(FULL_TYPE), axis=0).astype(HALF_TYPE)
    small = lax.all_to_all(jnp.broadcast_to(small[None], (32,) + small.shape), everywhere, 0, 0, tiled=True)
    back = [in_order(flat[1 - i][0], out_sum[:, :, i], flat[1 - i][1](out_sum[:, :, i])) for i in range(2)]
    first = jnp.stack([sets[0], place.swap_x(sets[0])])
    second = jnp.stack([sets[1], place.swap_y(sets[1])])
    output = call(output_kernel, shaped((all_rows, width)), after, b0, b2, b1)
    first, second, back[0], back[1], output = lax.optimization_barrier((first, second, *back, output))
    sources = [first, place.swap_y(first), second, place.swap_x(second)]
    back = [in_order(flat[i][0], back[i], flat[i][1](back[i])) for i in range(2)]
    out_half = jnp.stack(back).reshape(rows_out // 2, cols_out)
    sources[1], sources[3], output, out_half, mine_far, small, passed[0] = lax.optimization_barrier(
        (sources[1], sources[3], output, out_half, mine_far, small, passed[0])
    )
    mine = add(grad_near[0], came_near[0], passed[0], mine_far)
    mine_y = place.swap_y(mine)
    peers = [place.swap_c(first), None, place.swap_c(second), None]
    peers[1], peers[3] = place.swap_c(sources[1]), place.swap_c(sources[3])
    out_peer = place.swap_c(out_half)
    grad_heads = place_heads(place, sources, 0, heads, width, None)
    grad_out = place_out(place, out_half, 0, heads, None)
    grad_heads = lax.optimization_barrier((*grad_heads, grad_out, *peers, out_peer))
    grad_heads, grad_out, peers, out_peer = grad_heads[:3], grad_heads[3], grad_heads[4:8], grad_heads[8]
    small = small.reshape(width, LANES)
    grad_select, grad_sel_value, grad_sel_out, rows_four = call(
        place_small_kernel,
        (
            shaped((own_count, width), FULL_TYPE), shaped((heads * experts, width), FULL_TYPE),
            shaped((heads * experts, width), FULL_TYPE), shaped((8, width), FULL_TYPE),
        ),
        (place.wide * own_count).reshape(1).astype(jnp.int32), small,
        in_specs=[smem, vmem],
    )
    grad_query, grad_key, grad_value = place_heads(place, list(peers), 1, heads, width, grad_heads)
    grad_out = place_out(place, out_peer, 1, heads, (grad_out,))
    mine, mine_y, grad_query, grad_out, rows_four = lax.optimization_barrier((mine, mine_y, grad_query, grad_out, rows_four))
    mine_c, mine_yc = place.swap_c(mine), place.swap_c(mine_y)
    grad_experts = place_experts(place, mine, mine_y, 0, None)
    grad_up, grad_down = place_experts(place, mine_c, mine_yc, 1, grad_experts)
    grad_select, grad_sel_value, grad_sel_out = grad_select.T, grad_sel_value.T, grad_sel_out.T
    grad_gain_two, grad_bias_two, grad_gain_one, grad_bias_one = (rows_four[i] for i in range(4))
    return (
        output.reshape(tokens.shape), grad_tokens.reshape(tokens.shape), grad_query, grad_key, grad_value, grad_out,
        grad_sel_value, grad_sel_out, grad_gain_one, grad_bias_one, grad_gain_two, grad_bias_two, grad_select,
        grad_up, grad_down,
    )


def fits(mesh):
    return dict(mesh.shape) == {"wide": 8, "narrow": 4}


def solution(mesh):
    placed = (
        P("narrow", "wide", None),
        P("narrow"),
        P("narrow", "wide", None, None),
        P("narrow", "wide", None, None),
        P("narrow", None, None),
        P(),
        P(),
        P(),
        P(),
        P(),
        P(),
        P(),
        P(),
        P(),
        P(),
        P(None, "wide"),
        P(None, "wide"),
        P("wide", None),
        P("narrow", "wide", None),
    )
    return jax.shard_map(
        tuned_device if fits(mesh) else per_device,
        mesh=mesh,
        in_specs=placed,
        out_specs=(
            P("narrow", "wide", None),
            P("narrow", "wide", None),
            P(),
            P(),
            P(),
            P(),
            P(),
            P(),
            P(),
            P(),
            P(),
            P(),
            P(None, "wide"),
            P(None, "wide"),
            P("wide", None),
        ),
        check_vma=False,
    )
```

```python
import functools

import jax
import jax.numpy as jnp
import numpy as np
from jax import lax
from jax.experimental import pallas as pl
from jax.experimental.pallas import tpu as pltpu
from jax.sharding import PartitionSpec as P

EPSILON = 1e-05
FULL_TYPE = jnp.float32
HALF_TYPE = jnp.bfloat16


def for_sending(value):

    def short(part):
        return part.astype(jnp.bfloat16) if part.dtype == jnp.float32 else part

    return jax.tree.map(short, value)


def norm_parts(values_in, gain, bias):
    row_mean = jnp.mean(values_in, axis=-1, keepdims=True)
    centred = values_in - row_mean
    inv_scale = lax.rsqrt(jnp.mean(centred * centred, axis=-1, keepdims=True) + EPSILON)
    normal = centred * inv_scale
    return (normal * gain + bias, normal, inv_scale)


def norm_back(grad_in, normal, inv_scale, gain):
    scaled = grad_in * gain
    return inv_scale * (
        scaled
        - jnp.mean(scaled, axis=-1, keepdims=True)
        - normal * jnp.mean(scaled * normal, axis=-1, keepdims=True)
    )


def rotate(values_in, positions, turn):
    half_dim = values_in.shape[-1] // 2
    frequency = 10000.0 ** (-(jnp.arange(half_dim).astype(FULL_TYPE) * 2.0 / values_in.shape[-1]))
    angles = positions.astype(FULL_TYPE)[:, None] * frequency[None, :]
    cosine = jnp.cos(angles)[:, None, :]
    sine_part = turn * jnp.sin(angles)[:, None, :]
    front_half = values_in[..., :half_dim]
    back_half = values_in[..., half_dim:]
    return jnp.concatenate(
        [front_half * cosine - back_half * sine_part, front_half * sine_part + back_half * cosine],
        axis=-1,
    )


def one_hot_sum(ids, wanted):
    return jnp.sum((ids[..., None] == wanted).astype(FULL_TYPE), axis=-2)


def matmul(left_op, right_op):
    return jnp.dot(left_op, right_op, preferred_element_type=FULL_TYPE)


def contract_rows(left_op, right_op):
    left_flat = left_op.reshape(-1, left_op.shape[-1])
    right_flat = right_op.reshape(-1, right_op.shape[-1])
    return lax.dot_general(
        left_flat, right_flat, (((0,), (0,)), ((), ())), preferred_element_type=FULL_TYPE
    )


def times_transpose(grad_in, weight):
    return lax.dot_general(
        grad_in, weight, (((grad_in.ndim - 1,), (1,)), ((), ())), preferred_element_type=FULL_TYPE
    )


def attend_forward(
    tokens,
    lengths,
    value_ids,
    out_ids,
    w_query,
    w_key,
    w_value,
    w_out,
    sel_value,
    sel_out,
    gain_one,
    bias_one,
    gain_two,
    bias_two,
):
    seq_count, row_count, model_width = tokens.shape
    head_count = w_out.shape[0]
    head_dim = w_out.shape[1]
    value_experts = sel_value.shape[1] // head_count
    positions = lax.axis_index("wide") * row_count + jnp.arange(row_count, dtype=jnp.int32)
    inputs = tokens.astype(FULL_TYPE)
    normed, normal_one, scale_one = norm_parts(inputs, gain_one, bias_one)
    normed_low = normed.astype(HALF_TYPE)
    query_pre = matmul(normed_low, w_query).reshape(seq_count, row_count, head_count, head_dim)
    key_pre = matmul(normed_low, w_key).reshape(seq_count, row_count, head_count, head_dim)
    queries = rotate(query_pre, positions, 1.0).astype(HALF_TYPE)
    key_low = rotate(key_pre, positions, 1.0).astype(HALF_TYPE)
    expert_ids = jnp.arange(value_experts, dtype=jnp.int32)
    value_choice = one_hot_sum(value_ids, expert_ids)
    value_sig = jax.nn.sigmoid(
        matmul(normed_low, sel_value).reshape(seq_count, row_count, head_count, value_experts)
    )
    value_gate = value_sig * value_choice
    projected = matmul(tokens, w_value).reshape(
        seq_count, row_count, head_count, value_experts, head_dim
    )
    values = jnp.sum(value_gate[..., None] * projected, axis=3).astype(HALF_TYPE)
    keys_all, values_all = (
        lax.all_gather(key_low, "wide", axis=1, tiled=True),
        lax.all_gather(values, "wide", axis=1, tiled=True),
    )
    span = keys_all.shape[1]
    key_pos = jnp.arange(span, dtype=jnp.int32)
    allowed = (key_pos[None, None, None, :] <= positions[None, None, :, None]) & (
        key_pos[None, None, None, :] < lengths[:, None, None, None]
    )
    scores = jnp.einsum(
        "bphc,bshc->bhps", queries, keys_all, preferred_element_type=FULL_TYPE
    ) * head_dim ** (-0.5)
    masked = jnp.where(allowed, scores, -1e30)
    row_max = jnp.max(masked, axis=-1, keepdims=True)
    exponent = jnp.exp(masked - row_max)
    row_total = jnp.sum(exponent, axis=-1, keepdims=True)
    attn_probs = exponent / row_total
    log_total = row_max + jnp.log(row_total)
    attended = jnp.einsum(
        "bhps,bshc->bphc",
        attn_probs.astype(HALF_TYPE),
        values_all,
        preferred_element_type=FULL_TYPE,
    )
    live_rows = (positions[None, :] < lengths[:, None]).astype(FULL_TYPE)[:, :, None, None]
    mixed_out = (attended * live_rows).astype(HALF_TYPE)
    out_choice = one_hot_sum(out_ids, expert_ids)
    out_sig = jax.nn.sigmoid(
        matmul(normed_low, sel_out).reshape(seq_count, row_count, head_count, value_experts)
    )
    out_gate = out_sig * out_choice
    expert_out = jnp.einsum(
        "bphc,hcf->bphf", mixed_out, w_out, preferred_element_type=FULL_TYPE
    ).reshape(seq_count, row_count, head_count, value_experts, model_width)
    after_attn = inputs + jnp.sum(out_gate[..., None] * expert_out, axis=(2, 3))
    normed_two, normal_two, scale_two = norm_parts(after_attn, gain_two, bias_two)
    return dict(
        positions=positions,
        normal_one=normal_one,
        scale_one=scale_one,
        normed_low=normed_low,
        queries=queries,
        keys_all=keys_all,
        values_all=values_all,
        allowed=allowed,
        log_total=log_total,
        live_rows=live_rows,
        mixed_out=mixed_out,
        value_choice=value_choice,
        value_sig=value_sig,
        value_gate=value_gate,
        projected=projected,
        out_choice=out_choice,
        out_sig=out_sig,
        out_gate=out_gate,
        expert_out=expert_out,
        after_attn=after_attn,
        normed_two=normed_two,
        normal_two=normal_two,
        scale_two=scale_two,
    )


def expert_forward(after_attn, normed_two, mlp_ids, w_select, w_up):
    rows_all, normed_all = (
        lax.all_gather(for_sending(after_attn.astype(HALF_TYPE)), "wide", axis=1, tiled=True),
        lax.all_gather(for_sending(normed_two.astype(HALF_TYPE)), "wide", axis=1, tiled=True),
    )
    local_count = w_select.shape[1]
    hidden = w_up.shape[1] // local_count
    seq_count, span = (rows_all.shape[0], rows_all.shape[1])
    owned_ids = lax.axis_index("wide") * local_count + jnp.arange(local_count, dtype=jnp.int32)
    chosen = one_hot_sum(mlp_ids, owned_ids)
    sigmoid_gate = jax.nn.sigmoid(matmul(normed_all, w_select))
    mlp_gate = sigmoid_gate * chosen
    pre_act = matmul(rows_all, w_up)
    activated = jax.nn.gelu(pre_act).reshape(seq_count, span, local_count, hidden)
    inner_low = (
        (activated * mlp_gate[..., None])
        .reshape(seq_count, span, local_count * hidden)
        .astype(HALF_TYPE)
    )
    return dict(
        rows_all=rows_all,
        normed_all=normed_all,
        chosen=chosen,
        sigmoid_gate=sigmoid_gate,
        mlp_gate=mlp_gate,
        pre_act=pre_act,
        activated=activated,
        inner_low=inner_low,
    )


def per_device(
    tokens,
    lengths,
    value_ids,
    out_ids,
    mlp_ids,
    w_query,
    w_key,
    w_value,
    w_out,
    sel_value,
    sel_out,
    gain_one,
    bias_one,
    gain_two,
    bias_two,
    w_select,
    w_up,
    w_down,
    cotangent,
):
    seq_count, row_count, model_width = tokens.shape
    head_count = w_out.shape[0]
    head_dim = w_out.shape[1]
    value_experts = sel_value.shape[1] // head_count
    saved = attend_forward(
        tokens,
        lengths,
        value_ids,
        out_ids,
        w_query,
        w_key,
        w_value,
        w_out,
        sel_value,
        sel_out,
        gain_one,
        bias_one,
        gain_two,
        bias_two,
    )
    expert_state = expert_forward(saved["after_attn"], saved["normed_two"], mlp_ids, w_select, w_up)
    branch_part = matmul(expert_state["inner_low"], w_down)
    branch_sum = lax.psum_scatter(
        branch_part.astype(jnp.bfloat16), "wide", scatter_dimension=1, tiled=True
    ).astype(jnp.float32)
    output = (saved["after_attn"] + branch_sum).astype(HALF_TYPE)
    saved = attend_forward(
        tokens,
        lengths,
        value_ids,
        out_ids,
        w_query,
        w_key,
        w_value,
        w_out,
        sel_value,
        sel_out,
        gain_one,
        bias_one,
        gain_two,
        bias_two,
    )
    expert_state = expert_forward(saved["after_attn"], saved["normed_two"], mlp_ids, w_select, w_up)
    cot_all = lax.all_gather(cotangent, "wide", axis=1, tiled=True)
    grad_down = contract_rows(expert_state["inner_low"], cot_all)
    d_inner = times_transpose(cot_all, w_down)
    activated = expert_state["activated"]
    d_inner_four = d_inner.reshape(activated.shape)
    d_mlp_gate = jnp.sum(d_inner_four * activated, axis=-1)
    mlp_gate = expert_state["mlp_gate"]
    gated_grad = (d_inner_four * mlp_gate[..., None]).reshape(expert_state["pre_act"].shape)
    unused_value, gelu_pull = jax.vjp(jax.nn.gelu, expert_state["pre_act"])
    d_pre = gelu_pull(gated_grad)[0].astype(HALF_TYPE)
    sigmoid_gate = expert_state["sigmoid_gate"]
    d_logit = (d_mlp_gate * expert_state["chosen"] * sigmoid_gate * (1.0 - sigmoid_gate)).astype(
        HALF_TYPE
    )
    grad_up = contract_rows(expert_state["rows_all"], d_pre)
    grad_select = contract_rows(expert_state["normed_all"], d_logit)
    row_part = times_transpose(d_pre, w_up)
    norm_part = times_transpose(d_logit, w_select)
    row_grad, norm_grad = (
        lax.psum_scatter(row_part, "wide", scatter_dimension=1, tiled=True),
        lax.psum_scatter(norm_part, "wide", scatter_dimension=1, tiled=True),
    )
    grad_gain_two = jnp.sum(norm_grad * saved["normal_two"], axis=(0, 1))
    grad_bias_two = jnp.sum(norm_grad, axis=(0, 1))
    d_after = (
        cotangent.astype(FULL_TYPE)
        + row_grad
        + norm_back(norm_grad, saved["normal_two"], saved["scale_two"], gain_two)
    )
    out_gate = saved["out_gate"]
    d_expert = (out_gate[..., None] * d_after[:, :, None, None, :]).astype(HALF_TYPE)
    d_out_gate = jnp.sum(saved["expert_out"] * d_after[:, :, None, None, :], axis=-1)
    d_expert_flat = d_expert.reshape(seq_count, row_count, head_count, value_experts * model_width)
    grad_out = jnp.einsum(
        "bphc,bphf->hcf", saved["mixed_out"], d_expert_flat, preferred_element_type=FULL_TYPE
    )
    d_mixed = jnp.einsum("bphf,hcf->bphc", d_expert_flat, w_out, preferred_element_type=FULL_TYPE)
    d_attended = (d_mixed * saved["live_rows"]).astype(HALF_TYPE)
    out_sig = saved["out_sig"]
    d_out_logit = (
        (d_out_gate * saved["out_choice"] * out_sig * (1.0 - out_sig))
        .astype(HALF_TYPE)
        .reshape(seq_count, row_count, head_count * value_experts)
    )
    queries = saved["queries"]
    keys_all = saved["keys_all"]
    values_all = saved["values_all"]
    score_scale = head_dim ** (-0.5)
    scores = (
        jnp.einsum("bphc,bshc->bhps", queries, keys_all, preferred_element_type=FULL_TYPE)
        * score_scale
    )
    attn_probs = jnp.where(saved["allowed"], jnp.exp(scores - saved["log_total"]), 0.0)
    d_values_part = jnp.einsum(
        "bhps,bphc->bshc",
        attn_probs.astype(HALF_TYPE),
        d_attended,
        preferred_element_type=FULL_TYPE,
    )
    d_probs = jnp.einsum(
        "bphc,bshc->bhps", d_attended, values_all, preferred_element_type=FULL_TYPE
    )
    row_inner = jnp.sum(attn_probs * d_probs, axis=-1, keepdims=True)
    d_scores = (attn_probs * (d_probs - row_inner)).astype(HALF_TYPE)
    d_queries = (
        jnp.einsum("bhps,bshc->bphc", d_scores, keys_all, preferred_element_type=FULL_TYPE)
        * score_scale
    )
    d_keys_part = (
        jnp.einsum("bhps,bphc->bshc", d_scores, queries, preferred_element_type=FULL_TYPE)
        * score_scale
    )
    d_keys, d_values = (
        lax.psum_scatter(
            d_keys_part.astype(jnp.bfloat16), "wide", scatter_dimension=1, tiled=True
        ).astype(jnp.float32),
        lax.psum_scatter(
            d_values_part.astype(jnp.bfloat16), "wide", scatter_dimension=1, tiled=True
        ).astype(jnp.float32),
    )
    positions = saved["positions"]
    d_query_pre = (
        rotate(d_queries, positions, -1.0)
        .astype(HALF_TYPE)
        .reshape(seq_count, row_count, head_count * head_dim)
    )
    d_key_pre = (
        rotate(d_keys, positions, -1.0)
        .astype(HALF_TYPE)
        .reshape(seq_count, row_count, head_count * head_dim)
    )
    d_projected = (
        (saved["value_gate"][..., None] * d_values[:, :, :, None, :])
        .astype(HALF_TYPE)
        .reshape(seq_count, row_count, head_count * value_experts * head_dim)
    )
    d_value_gate = jnp.sum(saved["projected"] * d_values[:, :, :, None, :], axis=-1)
    value_sig = saved["value_sig"]
    d_value_logit = (
        (d_value_gate * saved["value_choice"] * value_sig * (1.0 - value_sig))
        .astype(HALF_TYPE)
        .reshape(seq_count, row_count, head_count * value_experts)
    )
    normed_low = saved["normed_low"]
    grad_query = contract_rows(normed_low, d_query_pre)
    grad_key = contract_rows(normed_low, d_key_pre)
    grad_sel_value = contract_rows(normed_low, d_value_logit)
    grad_sel_out = contract_rows(normed_low, d_out_logit)
    grad_value = contract_rows(tokens, d_projected)
    d_normed = (
        times_transpose(d_query_pre, w_query)
        + times_transpose(d_key_pre, w_key)
        + times_transpose(d_value_logit, sel_value)
        + times_transpose(d_out_logit, sel_out)
    )
    grad_gain_one = jnp.sum(d_normed * saved["normal_one"], axis=(0, 1))
    grad_bias_one = jnp.sum(d_normed, axis=(0, 1))
    grad_tokens = (
        d_after
        + times_transpose(d_projected, w_value)
        + norm_back(d_normed, saved["normal_one"], saved["scale_one"], gain_one)
    ).astype(HALF_TYPE)
    (
        grad_query,
        grad_key,
        grad_value,
        grad_out,
        grad_sel_value,
        grad_sel_out,
        grad_gain_one,
        grad_bias_one,
        grad_gain_two,
        grad_bias_two,
    ) = lax.psum(
        (
            grad_query,
            grad_key,
            grad_value,
            grad_out,
            grad_sel_value,
            grad_sel_out,
            grad_gain_one,
            grad_bias_one,
            grad_gain_two,
            grad_bias_two,
        ),
        ("wide", "narrow"),
    )
    grad_select, grad_up, grad_down = (
        lax.psum(grad_select.astype(jnp.bfloat16), "narrow").astype(jnp.float32),
        lax.psum(grad_up.astype(jnp.bfloat16), "narrow").astype(jnp.float32),
        lax.psum(grad_down.astype(jnp.bfloat16), "narrow").astype(jnp.float32),
    )
    return (
        output,
        grad_tokens,
        grad_query,
        grad_key,
        grad_value,
        grad_out,
        grad_sel_value,
        grad_sel_out,
        grad_gain_one,
        grad_bias_one,
        grad_gain_two,
        grad_bias_two,
        grad_select,
        grad_up,
        grad_down,
    )


SELV = 72
SELO = 92
LANES = 128


def call(
    kernel, out_shape, *args, grid=None, in_specs=None, out_specs=None, scratch=(), flops=0, limit=56, prefetch=0, aliases=None
):
    moved = sum(a.size * a.dtype.itemsize for a in jax.tree.leaves((args, out_shape)))
    extra = {}
    if prefetch:
        extra["grid_spec"] = pltpu.PrefetchScalarGridSpec(
            num_scalar_prefetch=prefetch, grid=grid, in_specs=in_specs, out_specs=out_specs, scratch_shapes=list(scratch)
        )
    else:
        extra["scratch_shapes"] = list(scratch)
        if grid is not None:
            extra["grid"] = grid
        if in_specs is not None:
            extra["in_specs"] = in_specs
        if out_specs is not None:
            extra["out_specs"] = out_specs
    return pl.pallas_call(
        kernel,
        out_shape=out_shape,
        input_output_aliases=aliases or {},
        compiler_params=pltpu.CompilerParams(vmem_limit_bytes=limit * 1024 * 1024),
        cost_estimate=pl.CostEstimate(flops=int(flops), bytes_accessed=int(moved), transcendentals=0),
        **extra,
    )(*args)


def full(shape):
    rank = len(shape)
    return pl.BlockSpec(tuple(shape), lambda *s: (0,) * rank)


def shaped(shape, dtype=HALF_TYPE):
    return jax.ShapeDtypeStruct(tuple(shape), dtype)


def nn(a, b):
    return lax.dot_general(a, b, (((1,), (0,)), ((), ())), preferred_element_type=FULL_TYPE)


def nt(a, b):
    return lax.dot_general(a, b, (((1,), (1,)), ((), ())), preferred_element_type=FULL_TYPE)


def tn(a, b):
    return lax.dot_general(a, b, (((0,), (0,)), ((), ())), preferred_element_type=FULL_TYPE)


def layer_stats(v):
    centred = v - jnp.mean(v, axis=-1, keepdims=True)
    inv = lax.rsqrt(jnp.mean(centred * centred, axis=-1, keepdims=True) + EPSILON)
    return centred * inv, inv


def turned(v, cos, sin):
    return v * cos + pltpu.roll(v, v.shape[-1] // 2, axis=v.ndim - 1) * sin


def lane_ids(shape, dim):
    return lax.broadcasted_iota(jnp.int32, shape, dim)


def pre_kernel(spot, tok, gain, bias, wq, wk, wv, sel, vid, oid, cos, sin, select, qkv, proj, gate):
    heads = qkv.shape[0]
    experts = wv.shape[1] // (heads * LANES)
    low = tok[0]
    rows = low.shape[0]
    normal, _ = layer_stats(low.astype(FULL_TYPE))
    normed = (normal * gain[...] + bias[...]).astype(HALF_TYPE)
    for part, weight in ((0, wq), (1, wk)):
        pre = nn(normed, weight[...])
        for h in range(heads):
            head = turned(pre[:, h * LANES:(h + 1) * LANES], cos[...], sin[...])
            qkv[h, part * rows:(part + 1) * rows] = head.astype(HALF_TYPE)
    ids = lane_ids((LANES, rows), 0)
    chosen = jnp.zeros((LANES, rows), FULL_TYPE)
    tops = vid.shape[1] // heads
    for h in range(heads):
        for k in range(tops):
            j = h * tops + k
            chosen += (ids == vid[0, j:j + 1, :] + (SELV + experts * h)).astype(FULL_TYPE)
            chosen += (ids == oid[0, j:j + 1, :] + (SELO + experts * h)).astype(FULL_TYPE)
    gates = jax.nn.sigmoid(nt(normed, sel[...])) * jnp.transpose(chosen)
    gate[0] = gates
    gates_low = gates.astype(HALF_TYPE)
    for h in range(heads):
        at = h * experts * LANES
        block = nn(low, wv[:, at:at + experts * LANES])
        proj[0, :, at:at + experts * LANES] = block.astype(HALF_TYPE)
        total = None
        for e in range(experts):
            col = SELV + h * experts + e
            term = gates[:, col:col + 1] * block[:, e * LANES:(e + 1) * LANES]
            total = term if total is None else total + term
        qkv[h, 2 * rows:3 * rows] = total.astype(HALF_TYPE)
        first = SELV + h * experts
        row_id = lane_ids((8, LANES), 0)
        spot = (lane_ids((8, LANES), 1) == row_id + first) & (row_id < experts)
        turned_gates = nt(spot.astype(FULL_TYPE).astype(HALF_TYPE), gates_low)
        tail = jnp.concatenate([turned_gates[:, i * LANES:(i + 1) * LANES] for i in range(rows // LANES)], axis=0)
        last = 3 * rows + select.shape[0]
        qkv[h, 3 * rows:last] = select[...]
        qkv[h, last:last + tail.shape[0]] = tail.astype(HALF_TYPE)


def limits_of(i, rows, length):
    position = i * rows + lane_ids((1, rows), 1)
    return jnp.minimum(position + 1, length), position


def parts_of(ref, first, last, part, rows):
    block = ref[first:last, part * rows:(part + 1) * rows]
    return block.reshape((last - first) * rows, block.shape[2])


def attend_kernel(length, qkv, mixed, out_t, lse):
    blocks, rows, width = mixed.shape
    scale = width ** (-0.5)
    values_t = jnp.transpose(parts_of(qkv, 0, blocks, 2, rows).astype(FULL_TYPE)).astype(HALF_TYPE)
    for i in range(blocks):
        n = (i + 1) * rows
        keys = parts_of(qkv, 0, i + 1, 1, rows)
        limit, position = limits_of(i, rows, length[0])
        scores = nt(keys, qkv[i, 0:rows]) * scale
        scores = jnp.where(lane_ids((n, rows), 0) < limit, scores, -1e30)
        top = jnp.max(scores, axis=0, keepdims=True)
        weights = jnp.exp(scores - top)
        total = jnp.sum(weights, axis=0, keepdims=True)
        attended = nn(values_t[:, :n], weights.astype(HALF_TYPE)) / total
        out_t[:, i * rows:(i + 1) * rows] = attended
        lse[:, i * rows:(i + 1) * rows] = top + jnp.log(total)
        live = (position < length[0]).astype(FULL_TYPE)
        mixed[i] = jnp.transpose(attended * live).astype(HALF_TYPE)


def attend_back_kernel(length, qkv, d_out, out_t, lse, cos, sin, d_qkv, d_keys, d_values):
    blocks, rows, width = d_out.shape
    scale = width ** (-0.5)
    keys_t = jnp.transpose(parts_of(qkv, 0, blocks, 1, rows).astype(FULL_TYPE)).astype(HALF_TYPE)
    d_keys[...] = jnp.zeros_like(d_keys)
    d_values[...] = jnp.zeros_like(d_values)
    for i in range(blocks):
        n = (i + 1) * rows
        here = slice(i * rows, (i + 1) * rows)
        limit, _ = limits_of(i, rows, length[0])
        query = qkv[i, 0:rows]
        d_att = d_out[i]
        delta = jnp.sum(jnp.transpose(d_att.astype(FULL_TYPE)) * out_t[:, here], axis=0, keepdims=True)
        scores = nt(parts_of(qkv, 0, i + 1, 1, rows), query) * scale
        probs = jnp.where(lane_ids((n, rows), 0) < limit, jnp.exp(scores - lse[:, here]), 0.0)
        d_probs = nt(parts_of(qkv, 0, i + 1, 2, rows), d_att)
        d_scores = (probs * (d_probs - delta)).astype(HALF_TYPE)
        d_values[0:n, :] += nn(probs.astype(HALF_TYPE), d_att)
        d_keys[0:n, :] += nn(d_scores, query)
        d_query = jnp.transpose(nn(keys_t[:, :n], d_scores)) * scale
        d_qkv[i, 0:rows] = turned(d_query, cos[here, :], -sin[here, :]).astype(HALF_TYPE)
    for i in range(blocks):
        here = slice(i * rows, (i + 1) * rows)
        d_qkv[i, rows:2 * rows] = turned(d_keys[here, :] * scale, cos[here, :], -sin[here, :]).astype(HALF_TYPE)
        d_qkv[i, 2 * rows:3 * rows] = d_values[here, :].astype(HALF_TYPE)


def gated(mixed, gate, hp, e, experts):
    parts = []
    for h in (2 * hp, 2 * hp + 1):
        col = SELO + h * experts + e
        parts.append((gate[:, col:col + 1] * mixed[h].astype(FULL_TYPE)).astype(HALF_TYPE))
    return jnp.concatenate(parts, axis=1)


def out_block(w_out, hp, e, width):
    block = w_out[2 * hp:2 * hp + 2, :, e * width:(e + 1) * width]
    return block.reshape(2 * block.shape[1], width)


def post_kernel(mixed, gate, w_out, tok, gain, bias, columns, ids, places, after, gates, sent, select):
    width = tok.shape[2]
    heads = w_out.shape[0]
    experts = w_out.shape[2] // width
    row_count = tok.shape[1]
    total = tok[0].astype(FULL_TYPE)
    gate_here = gate[0]
    mixed_here = mixed[...]
    for hp in range(heads // 2):
        for e in range(experts):
            total += nn(gated(mixed_here, gate_here, hp, e, experts), out_block(w_out, hp, e, width))
    after[...] = total
    sent[0, 0:row_count] = total.astype(HALF_TYPE)
    normal, _ = layer_stats(total)
    normed = (normal * gain[...] + bias[...]).astype(HALF_TYPE)
    every = columns[...].astype(FULL_TYPE)
    count = every.shape[1]
    each = count // 8
    w_sel = jnp.concatenate(
        [every[:, j * each:(j + 1) * each].reshape(count, LANES) for j in range(8)], axis=1
    ).astype(HALF_TYPE)
    select[...] = w_sel
    row_id = lane_ids((count, row_count), 0)
    chosen = jnp.zeros((count, row_count), FULL_TYPE)
    for k in range(ids.shape[1]):
        chosen += (row_id == ids[0, k:k + 1, :]).astype(FULL_TYPE)
    values = jax.nn.sigmoid(nt(w_sel, normed)) * chosen
    gates[...] = values
    moved = nn(places[...], values.astype(HALF_TYPE)).astype(HALF_TYPE)
    quarter = count // 4
    for i in range(4):
        sent[0, row_count:row_count + quarter, i * row_count:(i + 1) * row_count] = moved[i * quarter:(i + 1) * quarter]


def weights_kernel(spots, up, down, mine, peer):
    for s, out in enumerate((mine, peer)):

        @pl.when(pl.program_id(0) == s)
        def _(out=out):
            out[0] = up[...]
            out[1] = jnp.transpose(down[...].astype(FULL_TYPE)).astype(HALF_TYPE)


def expand(count, cols, first):
    rows = lane_ids((count, cols), 0)
    cut = lane_ids((count, cols), 1)
    hit = None
    for i in range(cols // LANES):
        inside = (cut >= i * LANES) & (cut < (i + 1) * LANES) & (rows == first + i)
        hit = inside if hit is None else hit | inside
    return hit.astype(FULL_TYPE).astype(HALF_TYPE)


def gate_lanes(rows, first):
    row = lane_ids((rows, LANES), 0)
    lane = lane_ids((rows, LANES), 1)
    hit = None
    for i in range(rows // LANES):
        inside = (row >= i * LANES) & (row < (i + 1) * LANES) & (lane == first + i)
        hit = inside if hit is None else hit | inside
    return hit.astype(FULL_TYPE).astype(HALF_TYPE)


def experts_kernel(kind, halves, *refs):
    rows_in, cot, pieces = refs[:halves], refs[halves], refs[halves + 1:halves + 9]
    back, inner, d_pre = refs[halves + 9:]
    seqs, tall, width = back.shape
    row_count = width // 4
    cols = pieces[0].shape[2]
    quarter = tall - row_count
    picked = [rows_in[0][s] if halves == 1 else rows_in[s][...] for s in range(seqs)]
    low = jnp.concatenate([block[0:row_count] for block in picked], axis=0)
    gates = jnp.concatenate(
        [block[row_count:tall, kind * row_count:(kind + 1) * row_count] for block in picked], axis=1
    )
    cot_low = cot[...]
    row_total = gate_total = None
    weight = lambda p, u: pieces[p][u]
    root, cube = 0.7978845608028654, 0.044715
    for p in range(8):
        spread = expand(quarter, cols, p * (cols // LANES))
        gate_wide = tn(gates, spread)
        pre = nn(low, weight(p, 0))
        d_in = nn(cot_low, weight(p, 1))
        square = pre * pre
        tanh = jnp.tanh(pre * (root + (root * cube) * square))
        half = 0.5 + 0.5 * tanh
        act = pre * half
        slope = half + act * (1.0 - tanh) * (root + (3 * root * cube) * square)
        d_pre[p] = (slope * gate_wide * d_in).astype(HALF_TYPE)
        inner[p] = (act * gate_wide).astype(HALF_TYPE)
        g = nn((d_in * act).astype(HALF_TYPE), gate_lanes(cols, p * (cols // LANES)))
        gate_total = g if p == 0 else gate_total + g
    for p in range(8):
        r = nt(d_pre[p], weight(p, 0))
        row_total = r if p == 0 else row_total + r
    gate_total = jnp.transpose(gate_total)[0:quarter]
    for s in range(seqs):
        here = slice(s * row_count, (s + 1) * row_count)
        back[s, 0:row_count] = row_total[here].astype(HALF_TYPE)
        back[s, row_count:tall] = jnp.zeros((quarter, width), HALF_TYPE)
        back[s, row_count:tall, 0:row_count] = gate_total[:, here].astype(HALF_TYPE)


def branch_kernel(*refs):
    inners, pieces, outs = refs[0:4], refs[4:12], refs[12:16]
    downs = [ref[1] for ref in pieces]
    for i in range(4):
        total = None
        for p in range(8):
            term = nt(inners[i][p], downs[p])
            total = term if p == 0 else total + term
        outs[i][...] = total.astype(HALF_TYPE)


def expert_grads_kernel(*refs):
    rows, cots, pres, inners = refs[0:5], refs[5:9], refs[9:13], refs[13:17]
    outs = refs[17:21]
    step = pl.program_id(0)
    row_count = pres[0].shape[1] // 2
    up = down = None
    for i in range(4):
        for s in range(2):
            block = rows[i][s, 0:row_count] if i < 3 else rows[3 + s][0:row_count]
            term = tn(block, pres[i][0, s * row_count:(s + 1) * row_count])
            up = term if up is None else up + term
        term = tn(cots[i][...], inners[i][0])
        down = term if down is None else down + term
    results = (up.astype(HALF_TYPE), down.astype(HALF_TYPE))
    for j in range(4):

        @pl.when(step // 2 == j)
        def _(j=j):
            for u in range(2):
                outs[j][0, u] = results[u]


def mid_kernel(length, r0, r1, r2, r3, cot, after, gates, gain, bias, w_sel, places, w_out, gate, mixed,
               d_after, d_att, d_gate_out, small, acc):
    step = pl.program_id(0)
    width = cot.shape[2]
    heads = w_out.shape[0]
    experts = w_out.shape[2] // width
    row_count = cot.shape[1]
    tall = r0.shape[1]
    d_rel = jnp.concatenate([r[0, row_count:tall, 0:row_count] for r in (r0, r1, r2, r3)], axis=0)
    d_gate = tn(places[...], d_rel)
    values = gates[...]
    d_logit = (d_gate * values * (1.0 - values)).astype(HALF_TYPE)
    normal, inv = layer_stats(after[...])
    normed = (normal * gain[...] + bias[...]).astype(HALF_TYPE)
    d_normed = tn(d_logit, w_sel[...])
    sel_part = nn(d_logit, normed)
    gain_part = jnp.sum(d_normed * normal, axis=0, keepdims=True)
    bias_part = jnp.sum(d_normed, axis=0, keepdims=True)
    count = sel_part.shape[0]

    @pl.when(step == 0)
    def _():
        acc[...] = jnp.zeros_like(acc)

    acc[0:count, :] += sel_part
    acc[count:count + 1, :] += gain_part
    acc[count + 1:count + 2, :] += bias_part
    d_row = sum(r[0, 0:row_count].astype(FULL_TYPE) for r in (r0, r1, r2, r3))
    total = cot[0].astype(FULL_TYPE) + d_row + norm_back(d_normed, normal, inv, gain[...])
    d_after[...] = total
    total_low = total.astype(HALF_TYPE)
    mixed_here = mixed[...]
    gate_here = gate[0]
    lanes = lane_ids((2 * LANES, LANES), 1)
    second = (lane_ids((2 * LANES, LANES), 0) >= LANES).astype(jnp.int32)
    d_gates = jnp.zeros((row_count, LANES), FULL_TYPE)
    for hp in range(heads // 2):
        both = jnp.concatenate([mixed_here[2 * hp], mixed_here[2 * hp + 1]], axis=1).astype(FULL_TYPE)
        sums = [None, None]
        for e in range(experts):
            d_mixed = nt(total_low, out_block(w_out, hp, e, width))
            hit = (lanes == SELO + 2 * hp * experts + e + second * experts).astype(FULL_TYPE).astype(HALF_TYPE)
            d_gates += nn((both * d_mixed).astype(HALF_TYPE), hit)
            for i in range(2):
                col = SELO + (2 * hp + i) * experts + e
                term = gate_here[:, col:col + 1] * d_mixed[:, i * LANES:(i + 1) * LANES]
                sums[i] = term if e == 0 else sums[i] + term
        for i in range(2):
            position = length[1] + lane_ids((row_count, 1), 0)
            live = (position < length[2 + step]).astype(FULL_TYPE)
            d_att[2 * hp + i] = (sums[i] * live).astype(HALF_TYPE)
    d_gate_out[0] = d_gates

    @pl.when(step == pl.num_programs(0) - 1)
    def _():
        spots = (lane_ids((LANES, LANES), 0) == lanes[0:LANES]).astype(FULL_TYPE).astype(HALF_TYPE)
        small[...] = tn(acc[...].astype(HALF_TYPE), spots)


def out_grad_kernel(mixed, gate, d_after, out):
    heads, experts = 4, out.shape[1] // d_after.shape[1]
    width = d_after.shape[1]
    seqs, row_count = gate.shape[0], gate.shape[1]
    low = d_after[...].astype(HALF_TYPE)
    for hp in range(heads // 2):
        for e in range(experts):
            total = None
            for s in range(seqs):
                left = gated([mixed[s * heads + h] for h in range(heads)], gate[s], hp, e, experts)
                term = tn(left, low[s * row_count:(s + 1) * row_count, :])
                total = term if total is None else total + term
            out[2 * hp * LANES:(2 * hp + 2) * LANES, e * width:(e + 1) * width] = total.astype(HALF_TYPE)


def last_kernel(d_qkv, tok, gain, bias, wq, wk, wv, sel, proj, gate, d_gate_out, small, d_after,
                out, sums, d_proj, acc):
    step = pl.program_id(0)
    row_count, width = tok.shape[1], tok.shape[2]
    heads = d_qkv.shape[0]
    experts = proj.shape[2] // (heads * LANES)
    lanes = lane_ids((LANES, LANES), 1)
    low = tok[0]
    normal, inv = layer_stats(low.astype(FULL_TYPE))
    normed = (normal * gain[...] + bias[...]).astype(HALF_TYPE)
    d_gates = d_gate_out[0]
    gate_here = gate[0]
    d_query = jnp.concatenate([d_qkv[h, 0:row_count] for h in range(heads)], axis=1)
    d_key = jnp.concatenate([d_qkv[h, row_count:2 * row_count] for h in range(heads)], axis=1)
    for h in range(heads):
        d_value = d_qkv[h, 2 * row_count:3 * row_count].astype(FULL_TYPE)
        for e in range(experts):
            col = SELV + h * experts + e
            at = (h * experts + e) * LANES
            d_proj[:, at:at + LANES] = (gate_here[:, col:col + 1] * d_value).astype(HALF_TYPE)
            hit = (lanes == col).astype(FULL_TYPE).astype(HALF_TYPE)
            product = (proj[0, :, at:at + LANES].astype(FULL_TYPE) * d_value).astype(HALF_TYPE)
            d_gates += nn(product, hit)
    d_logit = (d_gates * gate_here * (1.0 - gate_here)).astype(HALF_TYPE)
    d_normed = nt(d_query, wq[...]) + nt(d_key, wk[...]) + nn(d_logit, sel[...])
    total = d_after[...] + norm_back(d_normed, normal, inv, gain[...]) + nt(d_proj[...], wv[...])
    out[...] = total.astype(HALF_TYPE)
    gain_sum = jnp.sum(d_normed * normal, axis=0, keepdims=True)
    bias_sum = jnp.sum(d_normed, axis=0, keepdims=True)
    rows = jnp.concatenate([gain_sum, bias_sum, jnp.zeros((14, width), FULL_TYPE)], axis=0).astype(HALF_TYPE)
    spot = (lane_ids((16, LANES), 1) == lane_ids((16, LANES), 0) + 66) & (lane_ids((16, LANES), 0) < 2)
    spread = tn(rows, spot.astype(FULL_TYPE).astype(HALF_TYPE))
    part = tn(normed, d_logit) + spread

    @pl.when(step == 0)
    def _():
        acc[...] = small[...] + part

    @pl.when(step > 0)
    def _():
        acc[...] += part

    sums[...] = acc[...].astype(HALF_TYPE)


def turn_kernel(near, far, gain, bias, tok_t, norm_t):
    step = pl.program_id(0)

    def turn(low):
        normal, _ = layer_stats(low.astype(FULL_TYPE))
        tok_t[0] = jnp.transpose(low.astype(FULL_TYPE)).astype(HALF_TYPE)
        normed = (normal * gain[...] + bias[...]).astype(HALF_TYPE)
        norm_t[0] = jnp.transpose(normed.astype(FULL_TYPE)).astype(HALF_TYPE)

    @pl.when(step < 4)
    def _():
        turn(near[0])

    @pl.when(step >= 4)
    def _():
        turn(far[0])


def head_grads_kernel(spot, tok_t, norm_t, d_qkv, gate, out, acc):
    step = pl.program_id(0)
    rows = tok_t.shape[2]
    experts = out.shape[1] // LANES - 2
    both = jnp.concatenate([d_qkv[0, 0:rows], d_qkv[0, rows:2 * rows]], axis=1)
    wide = experts * LANES
    spread = expand(8, wide, 0)
    tail = gate[0]
    gates = jnp.concatenate([tn(tail[i * 8:(i + 1) * 8], spread) for i in range(rows // LANES)], axis=0)
    d_value = d_qkv[0, 2 * rows:3 * rows].astype(FULL_TYPE)
    d_proj = (gates * jnp.concatenate([d_value] * experts, axis=1)).astype(HALF_TYPE)
    first = nn(norm_t[0], both)
    second = nn(tok_t[0], d_proj)

    @pl.when(step == 0)
    def _():
        acc[:, 0:2 * LANES] = first
        acc[:, 2 * LANES:] = second

    @pl.when(step > 0)
    def _():
        acc[:, 0:2 * LANES] += first
        acc[:, 2 * LANES:] += second

    @pl.when(step == pl.num_programs(0) - 1)
    def _():
        out[...] = acc[...].astype(HALF_TYPE)


def place_heads_kernel(bits, *refs):
    sources = refs[:4]
    query, key, value = refs[-3:]
    step = pl.program_id(0)
    y, x, high, low = bits[0], bits[1], bits[2], bits[3]
    wide = value.shape[1] // 4
    size = value.shape[0] // 2

    def put(block, head, place):
        here = pl.ds(pl.multiple_of(place * size, size), size)
        at = pl.multiple_of(head * LANES, LANES)
        query[here, pl.ds(at, LANES)] = block[:, 0:LANES].astype(FULL_TYPE)
        key[here, pl.ds(at, LANES)] = block[:, LANES:2 * LANES].astype(FULL_TYPE)
        value[here, pl.ds(pl.multiple_of(head * wide, LANES), wide)] = block[:, 2 * LANES:].astype(FULL_TYPE)

    for j in range(2):

        @pl.when(step == j)
        def _(j=j):
            for i in range(2):
                for b in range(2):
                    for a in range(2):
                        put(sources[j][i, b, a], (low ^ b) * 2 + (x ^ i), high ^ a)

    @pl.when(step >= 2)
    def _():
        for j in range(2):
            for i in range(2):
                for b in range(2):
                    put(sources[2 + j][i, b, 0], (low ^ b) * 2 + (x ^ j), y ^ i)


def place_out_kernel(spot, mine, *rest):
    rest[-1][0] = mine[...].astype(FULL_TYPE)


def place_small_kernel(first, small, select, value, out, rows):
    low = small[...]

    def rows_of(count, start):
        hit = lane_ids((count, LANES), 1) == lane_ids((count, LANES), 0) + start
        return nt(hit.astype(FULL_TYPE).astype(HALF_TYPE), low)

    select[...] = rows_of(select.shape[0], first[0])
    value[...] = rows_of(value.shape[0], SELV)
    out[...] = rows_of(out.shape[0], SELO)
    spots = (lane_ids((8, LANES), 1) == lane_ids((8, LANES), 0) + 64) & (lane_ids((8, LANES), 0) < 4)
    rows[...] = nt(spots.astype(FULL_TYPE).astype(HALF_TYPE), low)


def place_experts_kernel(spots, mine, mine_y, *rest):
    up, down = rest[-2:]
    for i, ref in enumerate((mine, mine_y)):

        @pl.when(pl.program_id(0) == i)
        def _(ref=ref):
            up[...] = ref[0].astype(FULL_TYPE)
            down[...] = jnp.transpose(ref[1].astype(FULL_TYPE))


def output_kernel(after, own, first, last, out):
    out[...] = (
        after[...] + own[...].astype(FULL_TYPE) + first[...].astype(FULL_TYPE) + last[...].astype(FULL_TYPE)
    ).astype(HALF_TYPE)


class Place:
    def __init__(self):
        self.wide = lax.axis_index("wide")
        self.narrow = lax.axis_index("narrow")
        self.z, self.x = self.wide // 2, self.wide % 2
        self.y, self.c = self.narrow // 2, self.narrow % 2
        self.high, self.low = self.z // 2, self.z % 2

    @staticmethod
    def pairs(move):
        every = []
        for z in range(4):
            for x in range(2):
                for y in range(2):
                    for c in range(2):
                        tz, tx, ty, tc = move(z, x, y, c)
                        every.append(((z * 2 + x) * 4 + y * 2 + c, (tz * 2 + tx) * 4 + ty * 2 + tc))
        return every

    def send(self, value, move):
        return lax.ppermute(value, ("wide", "narrow"), self.pairs(move))

    def swap_x(self, value):
        return self.send(value, lambda z, x, y, c: (z, 1 - x, y, c))

    def swap_y(self, value):
        return self.send(value, lambda z, x, y, c: (z, x, 1 - y, c))

    def swap_xy(self, value):
        return self.send(value, lambda z, x, y, c: (z, 1 - x, 1 - y, c))

    def swap_c(self, value):
        return self.send(value, lambda z, x, y, c: (z, x, y, 1 - c))

    def swap_low(self, value):
        return self.send(value, lambda z, x, y, c: (z ^ 1, x, y, c))

    def swap_high(self, value):
        return self.send(value, lambda z, x, y, c: (z ^ 2, x, y, c))


def pick(array, index):
    return lax.dynamic_index_in_dim(array, index, 0, keepdims=False)


def add(*terms):
    total = terms[0].astype(FULL_TYPE)
    for term in terms[1:]:
        total = total + term.astype(FULL_TYPE)
    return total.astype(HALF_TYPE)


def in_order(bit, mine, other):
    return jnp.stack([jnp.where(bit == 0, mine, other), jnp.where(bit == 0, other, mine)])


def tie(value, *others):
    return lax.optimization_barrier((value,) + others)[0]


def halve(bit, swap, value):
    return add(pick(value, bit), swap(pick(value, 1 - bit)))


def place_out(place, half, core, heads, begun):
    rows, cols = half.shape
    size = 2 * rows // heads
    more = begun or ()
    return call(
        place_out_kernel,
        shaped((heads, size, cols), FULL_TYPE),
        (place.c ^ core).reshape(1).astype(jnp.int32), half, *more,
        grid=(heads // 2,), prefetch=1,
        in_specs=[pl.BlockSpec((size, cols), lambda s, spot: (s, 0))] + [pl.BlockSpec(memory_space=pl.ANY)] * len(more),
        out_specs=pl.BlockSpec((1, size, cols), lambda s, spot: (spot[0] * (heads // 2) + s, 0, 0)),
        aliases={2 + i: i for i in range(len(more))},
    )


def place_experts(place, mine, mine_y, core, begun):
    width, local = mine.shape[1:]
    more = begun or ()
    return call(
        place_experts_kernel,
        (shaped((width, 4 * local), FULL_TYPE), shaped((4 * local, width), FULL_TYPE)),
        jnp.stack([place.narrow ^ core, place.narrow ^ core ^ 2]).astype(jnp.int32), mine, mine_y, *more,
        grid=(2,), prefetch=1,
        in_specs=[full(mine.shape)] * 2 + [pl.BlockSpec(memory_space=pl.ANY)] * len(more),
        out_specs=(
            pl.BlockSpec((width, local), lambda s, spots: (0, spots[s])),
            pl.BlockSpec((local, width), lambda s, spots: (spots[s], 0)),
        ),
        aliases={3 + i: i for i in range(len(more))},
    )


def place_heads(place, sources, core, heads, rows, begun):
    size, cols = sources[0].shape[3:]

    def block(j):
        if j < 2:
            return pl.BlockSpec((2, 2, 2, size, cols), lambda s, bits: (0, 0, 0, 0, 0))
        return pl.BlockSpec((2, 2, 1, size, cols), lambda s, bits: (0, 0, jnp.where(s < 2, 0, s % 2), 0, 0))

    def row_block(s, bits):
        inside = jnp.where(s < 2, bits[0], bits[2]) ^ (s % 2)
        return (((bits[4] ^ core) * 2 + s // 2) * 2 + inside, 0)

    wide = cols - 2 * LANES
    more = () if begun is None else tuple(begun)
    return call(
        place_heads_kernel,
        (
            shaped((rows, heads * LANES), FULL_TYPE), shaped((rows, heads * LANES), FULL_TYPE),
            shaped((rows, heads * wide), FULL_TYPE),
        ),
        jnp.stack([place.y, place.x, place.high, place.low, place.c]).astype(jnp.int32), *sources, *more,
        grid=(4,), prefetch=1,
        in_specs=[block(j) for j in range(4)] + [pl.BlockSpec(memory_space=pl.ANY)] * len(more),
        out_specs=(
            pl.BlockSpec((2 * size, heads * LANES), row_block), pl.BlockSpec((2 * size, heads * LANES), row_block),
            pl.BlockSpec((2 * size, heads * wide), row_block),
        ),
        aliases={5 + i: i for i in range(len(more))},
    )


def turn_tables(span, head_dim):
    half = head_dim // 2
    frequency = np.float32(10000.0) ** (-(np.arange(half).astype(np.float32) * np.float32(2.0) / np.float32(head_dim)))
    angles = np.arange(span).astype(np.float32)[:, None] * frequency[None, :].astype(np.float32)
    cosine, sine = np.cos(angles.astype(np.float64)), np.sin(angles.astype(np.float64))
    return (
        jnp.asarray(np.concatenate([cosine, cosine], axis=1).astype(np.float32)),
        jnp.asarray(np.concatenate([-sine, sine], axis=1).astype(np.float32)),
    )


def tuned_device(
    tokens, lengths, value_ids, out_ids, mlp_ids, w_query, w_key, w_value, w_out, sel_value, sel_out,
    gain_one, bias_one, gain_two, bias_two, w_select, w_up, w_down, cotangent,
):
    seqs, row_count, width = tokens.shape
    heads, head_dim = w_out.shape[0], w_out.shape[1]
    experts = w_out.shape[2] // width
    pair_count = seqs * heads
    span = 8 * row_count
    all_rows = seqs * row_count
    wide_out = heads * experts * LANES
    local = w_up.shape[1] // 4
    hidden = 8 * local
    own_count = w_select.shape[1]
    count = 8 * own_count
    quarter = count // 4
    tall = row_count + quarter
    place = Place()
    first_row = place.wide * row_count
    row = lambda v: v.reshape(1, -1)
    smem = pl.BlockSpec(memory_space=pltpu.SMEM)
    vmem = pl.BlockSpec(memory_space=pltpu.VMEM)
    hbm = pl.BlockSpec(memory_space=pl.ANY)
    by_seq = lambda shape: pl.BlockSpec((1,) + tuple(shape[1:]), lambda s, *_: (s,) + (0,) * (len(shape) - 1))
    split = lambda shape: pl.BlockSpec((shape[0] // seqs,) + tuple(shape[1:]), lambda s, *_: (s,) + (0,) * (len(shape) - 1))
    token_cols = lambda n: pl.BlockSpec((n, row_count), lambda s: (0, s))

    own_select = jnp.transpose(w_select).reshape(own_count, 8, -1).swapaxes(0, 1).reshape(-1, LANES)

    mine_peer = jnp.stack([place.narrow, place.narrow + 1 - 2 * place.c]).astype(jnp.int32)
    weights_mine, weights_peer = call(
        weights_kernel,
        (shaped((2, width, local)), shaped((2, width, local))),
        mine_peer, w_up, w_down,
        grid=(2,), prefetch=1,
        in_specs=[
            pl.BlockSpec((width, local), lambda s, spots: (0, spots[s])),
            pl.BlockSpec((local, width), lambda s, spots: (spots[s], 0)),
        ],
        out_specs=(full((2, width, local)), full((2, width, local))),
    )

    cot_own = cotangent.reshape(all_rows, width)
    cots = [cot_own, place.swap_y(cot_own)]
    tokens_x = place.swap_x(tokens)

    cosine, sine = turn_tables(span, head_dim)
    sel = jnp.concatenate(
        [
            jnp.zeros((SELV, width), HALF_TYPE), sel_value.T, sel_out.T,
            jnp.zeros((LANES - SELO - heads * experts, width), HALF_TYPE),
        ],
        axis=0,
    )
    value_flat = jnp.transpose(value_ids, (0, 2, 3, 1)).reshape(seqs, -1, row_count)
    out_flat = jnp.transpose(out_ids, (0, 2, 3, 1)).reshape(seqs, -1, row_count)
    payload = 3 * row_count + own_select.shape[0] + 16
    qkv, projected, gate = call(
        pre_kernel,
        (
            shaped((pair_count, payload, head_dim)),
            shaped((seqs, row_count, wide_out)),
            shaped((seqs, row_count, LANES), FULL_TYPE),
        ),
        place.wide.reshape(1).astype(jnp.int32), tokens, row(gain_one), row(bias_one), w_query, w_key, w_value, sel,
        value_flat, out_flat, cosine, sine, own_select,
        grid=(seqs,), prefetch=1,
        in_specs=[
            by_seq(tokens.shape), full((1, width)), full((1, width)), full(w_query.shape), full(w_key.shape),
            full(w_value.shape), full(sel.shape), by_seq(value_flat.shape), by_seq(out_flat.shape),
            pl.BlockSpec((row_count, head_dim), lambda s, spot: (spot[0], 0)),
            pl.BlockSpec((row_count, head_dim), lambda s, spot: (spot[0], 0)),
            full(own_select.shape),
        ],
        out_specs=(
            split((pair_count, payload, head_dim)), by_seq((seqs, row_count, wide_out)),
            by_seq((seqs, row_count, LANES)),
        ),
        flops=2 * all_rows * width * 3712,
    )
    qkv = lax.all_to_all(qkv, "wide", 0, 0, tiled=True)
    qkv, cots[1], tokens_x, weights_mine = lax.optimization_barrier((qkv, cots[1], tokens_x, weights_mine))
    weights_far, weights_near = place.swap_high(weights_mine), place.swap_low(weights_mine)
    cot_later = tie(cot_own, qkv)
    cots += [place.swap_x(cot_later), place.swap_xy(cot_later)]
    seq_here = place.wide // heads
    length = pick(lengths, seq_here).reshape(1)
    mixed, out_t, lse = call(
        attend_kernel,
        (
            shaped((8, row_count, head_dim)), shaped((head_dim, span), FULL_TYPE), shaped((1, span), FULL_TYPE),
        ),
        length, qkv,
        in_specs=[smem, vmem],
        flops=2 * span * span * head_dim,
    )
    mixed = lax.all_to_all(mixed, "wide", 0, 0, tiled=True)
    mixed, weights_far, weights_near, cots[2], cots[3] = lax.optimization_barrier(
        (mixed, weights_far, weights_near, cots[2], cots[3])
    )
    weights_last = place.swap_low(weights_far)

    kinds = (place.x * 2 + place.y) ^ jnp.arange(4)
    kx, ky = (kinds // 2)[:, None, None, None], (kinds % 2)[:, None, None, None]
    kz = (place.z ^ jnp.arange(4))[None, :, None, None]
    kc = (place.c ^ jnp.arange(2))[None, None, :, None]
    ki = jnp.arange(2)[None, None, None, :]
    sent_ids = ((kz * 2 + kx) * own_count + ky * 4 + kc * 2 + ki).reshape(-1)
    places = (sent_ids[:, None] == jnp.arange(count)[None, :]).astype(HALF_TYPE)

    own_mlp = lax.dynamic_slice_in_dim(mlp_ids, first_row, row_count, 1)
    own_mlp = jnp.swapaxes(own_mlp, 1, 2)
    after, gates, rows_own, select = call(
        post_kernel,
        (
            shaped((all_rows, width), FULL_TYPE), shaped((count, all_rows), FULL_TYPE), shaped((seqs, tall, width)),
            shaped((count, width)),
        ),
        mixed, gate, w_out, tokens, row(gain_two), row(bias_two), qkv, own_mlp, places,
        grid=(seqs,),
        in_specs=[
            split(mixed.shape), by_seq(gate.shape), full(w_out.shape), by_seq(tokens.shape), full((1, width)),
            full((1, width)), pl.BlockSpec((8, 8 * own_count, LANES), lambda s: (0, 3 * row_count // (8 * own_count), 0)),
            by_seq(own_mlp.shape), full(places.shape),
        ],
        out_specs=(
            split((all_rows, width)), token_cols(count), by_seq((seqs, tall, width)), full((count, width)),
        ),
        flops=2 * all_rows * width * wide_out,
    )

    rows_y, rows_x = place.swap_y(rows_own), place.swap_x(rows_own)
    rows_d = (place.swap_x(rows_y[0]), place.swap_y(rows_x[1]))
    rows_in = [(rows_own,), (rows_y,), (rows_x,), rows_d]
    weights = [weights_mine, weights_peer]
    for piece in (weights_near, weights_far, weights_last):
        weights += [piece, place.swap_c(piece)]
    own_two = jnp.stack([pick(tokens, seq_here), pick(tokens_x, seq_here)])
    other_two = jnp.stack([pick(tokens, 1 - seq_here), pick(tokens_x, 1 - seq_here)])
    other_two = place.swap_high(tie(other_two, rows_own))
    results = {}
    for i, before in ((1, None), (2, 1), (3, 2), (0, 3)):
        if before is not None:
            cots[i] = tie(cots[i], results[before][1])
        results[i] = call(
                functools.partial(experts_kernel, i, len(rows_in[i])),
                (
                    shaped((seqs, tall, width)), shaped((8, all_rows, local)), shaped((8, all_rows, local)),
                ),
                *rows_in[i], cots[i], *weights,
                flops=8 * all_rows * width * hidden,
            )
    swaps = (lambda v: v, place.swap_y, place.swap_x, place.swap_xy)
    d_rows = [swaps[i](results[i][0]) for i in range(4)]
    inners = [results[i][1] for i in range(4)]
    near_four = jnp.concatenate([own_two, tie(other_two, results[2][1])])
    far_four = place.swap_low(near_four)

    whole = lambda shape: pl.BlockSpec(tuple(shape), lambda p: (0,) * len(shape))
    piece = lambda: pl.BlockSpec((1, all_rows, local), lambda p: (2 * (2 * (p % 2) + (p // 2) % 2) + p // 4, 0, 0))
    grad_near, grad_far, peer_near, peer_far = call(
        expert_grads_kernel,
        (shaped((2, 2, width, local)),) * 4,
        rows_own, rows_y, rows_x, *rows_d, *cots, *[results[i][2] for i in range(4)], *inners,
        grid=(8,),
        in_specs=[whole((seqs, tall, width))] * 3 + [whole((tall, width))] * 2 + [whole((all_rows, width))] * 4
        + [piece() for _ in range(8)],
        out_specs=tuple(
            pl.BlockSpec((1, 2, width, local), lambda p, j=j: (jnp.clip(p - 2 * j, 0, 1), 0, 0, 0)) for j in range(4)
        ),
        flops=16 * all_rows * width * hidden,
    )
    d_rows[1], d_rows[2], d_rows[3], peer_far, peer_near, far_four = lax.optimization_barrier(
        (d_rows[1], d_rows[2], tie(d_rows[3], grad_near), peer_far, peer_near, far_four)
    )
    came_far, came_near = place.swap_c(peer_far), place.swap_c(peer_near)

    live_info = jnp.concatenate([jnp.zeros((1,), jnp.int32), first_row.reshape(1).astype(jnp.int32), lengths])
    d_after, d_att, d_gate_out, small = call(
        mid_kernel,
        (
            shaped((all_rows, width), FULL_TYPE), shaped((pair_count, row_count, head_dim)),
            shaped((seqs, row_count, LANES), FULL_TYPE), shaped((width, LANES), FULL_TYPE),
        ),
        live_info, *d_rows, cotangent, after, gates, row(gain_two), row(bias_two), select, places,
        w_out, gate, mixed,
        grid=(seqs,),
        in_specs=[smem] + [by_seq((seqs, tall, width))] * 4 + [
            by_seq(cotangent.shape), split((all_rows, width)), token_cols(count), full((1, width)), full((1, width)),
            full(select.shape), full(places.shape), full(w_out.shape), by_seq(gate.shape),
            split(mixed.shape),
        ],
        out_specs=(
            split((all_rows, width)), split((pair_count, row_count, head_dim)),
            by_seq((seqs, row_count, LANES)), full((width, LANES)),
        ),
        scratch=[pltpu.VMEM((LANES, width), FULL_TYPE)],
        flops=2 * all_rows * width * wide_out,
    )
    d_att_all = lax.all_to_all(d_att, "wide", 0, 0, tiled=True)

    to_low = [add(grad_far[a], came_far[a]) for a in range(2)]
    passed = [None, place.swap_low(to_low[1])]
    near_four = tie(near_four, d_att, *to_low)
    tok_t, norm_t = call(
        turn_kernel,
        (shaped((8, width, row_count)), shaped((8, width, row_count))),
        near_four, far_four, row(gain_one), row(bias_one),
        grid=(8,),
        in_specs=[
            pl.BlockSpec((1, row_count, width), lambda i: (jnp.minimum(i, 3), 0, 0)),
            pl.BlockSpec((1, row_count, width), lambda i: (jnp.maximum(i - 4, 0), 0, 0)),
            full((1, width)), full((1, width)),
        ],
        out_specs=(
            pl.BlockSpec((1, width, row_count), lambda i: (i, 0, 0)),
            pl.BlockSpec((1, width, row_count), lambda i: (i, 0, 0)),
        ),
    )
    grad_out = call(
        out_grad_kernel, shaped((heads * head_dim, experts * width)), tie(mixed, d_att, tok_t), gate, d_after,
        flops=2 * all_rows * width * wide_out,
    )
    rows_out, cols_out = grad_out.shape
    flat = ((place.y, place.swap_y), (place.x, place.swap_x))
    d_att_all, tok_t, grad_out = lax.optimization_barrier((d_att_all, tok_t, grad_out))
    out_parts = halve(place.c, place.swap_c, grad_out.reshape(2, 2, 2, 2, 2, 2, rows_out // 64, cols_out))

    d_qkv = call(
        attend_back_kernel,
        shaped((8, 3 * row_count, head_dim)),
        length, qkv, d_att_all, out_t, lse, cosine, sine,
        in_specs=[smem] + [vmem] * 6,
        scratch=[pltpu.VMEM((span, head_dim), FULL_TYPE), pltpu.VMEM((span, head_dim), FULL_TYPE)],
        flops=5 * span * span * head_dim,
    )

    d_qkv, out_parts = lax.optimization_barrier((d_qkv, out_parts))
    out_parts = [halve(*flat[i], out_parts[i]) for i in range(2)]

    block_of = lambda i, spot: spot[0] ^ ((i & 1) | ((i & 2) << 1) | ((i & 4) >> 1))
    head_cols = (2 + experts) * LANES
    head_grads = call(
        head_grads_kernel,
        shaped((width, head_cols)),
        place.wide.reshape(1).astype(jnp.int32), tok_t, norm_t, d_qkv, qkv,
        grid=(8,), prefetch=1,
        in_specs=[
            pl.BlockSpec((1, width, row_count), lambda i, spot: (i, 0, 0)),
            pl.BlockSpec((1, width, row_count), lambda i, spot: (i, 0, 0)),
            pl.BlockSpec((1, 3 * row_count, head_dim), lambda i, spot: (block_of(i, spot), 0, 0)),
            pl.BlockSpec((1, 16, head_dim), lambda i, spot: (block_of(i, spot), payload // 16 - 1, 0)),
        ],
        out_specs=pl.BlockSpec((width, head_cols), lambda i, spot: (0, 0)),
        scratch=[pltpu.VMEM((width, head_cols), FULL_TYPE)],
        flops=2 * span * width * head_cols,
    )
    d_qkv_rows = lax.all_to_all(d_qkv, "wide", 0, 0, tiled=True)
    bits = ((place.y, place.swap_y), (place.high, place.swap_high))
    rows_head = width // 16
    head_grads, out_parts[0], out_parts[1] = lax.optimization_barrier((head_grads, *out_parts))
    out_parts = [halve(*flat[1 - i], out_parts[i]) for i in range(2)]
    kept = halve(place.c, place.swap_c, head_grads.reshape(2, 2, 2, 2, rows_head, head_cols))
    branches = call(
        branch_kernel,
        (shaped((all_rows, width)),) * 4,
        tie(inners[0], head_grads), *inners[1:], *weights,
        flops=8 * all_rows * width * hidden,
    )
    b0, b1, b2, b3 = branches
    kept, out_sum, b1, b2, b3 = lax.optimization_barrier((kept, jnp.stack(out_parts, axis=2), b1, b2, b3))
    b3 = place.swap_x(b3)
    out_sum = halve(place.low, place.swap_low, out_sum)
    value = [halve(*bits[i], kept[i]) for i in range(2)]
    value[0], value[1], d_qkv_rows, out_sum = lax.optimization_barrier((value[0], value[1], d_qkv_rows, out_sum))
    value = [halve(*bits[1 - i], value[i]) for i in range(2)]
    out_sum = halve(place.high, place.swap_high, out_sum)
    grad_tokens, small = call(
        last_kernel,
        (shaped((all_rows, width)), shaped((width, LANES))),
        d_qkv_rows, tokens, row(gain_one), row(bias_one), w_query, w_key, w_value, sel, projected, gate, d_gate_out,
        small, d_after,
        grid=(seqs,),
        in_specs=[
            split(d_qkv.shape), by_seq(tokens.shape), full((1, width)), full((1, width)), full(w_query.shape),
            full(w_key.shape), full(w_value.shape), full(sel.shape), by_seq(projected.shape), by_seq(gate.shape),
            by_seq(d_gate_out.shape), full(small.shape), split(d_after.shape),
        ],
        out_specs=(split((all_rows, width)), full((width, LANES))),
        scratch=[pltpu.VMEM((row_count, wide_out), HALF_TYPE), pltpu.VMEM((width, LANES), FULL_TYPE)],
        flops=2 * all_rows * width * 3712,
    )
    done, small, out_sum, b3 = lax.optimization_barrier((jnp.stack(value), small, out_sum, b3))
    b1 = place.swap_y(add(b1, b3))
    b2 = place.swap_x(tie(b2, b3))
    far = place.swap_high(done)
    out_sum = in_order(place.high, out_sum, place.swap_high(out_sum))
    everywhere = ("wide", "narrow")
    small = lax.all_to_all(small, everywhere, 0, 0, tiled=True).reshape(32, -1, LANES)
    far, out_sum = lax.optimization_barrier((far, out_sum))
    out_sum = in_order(place.low, out_sum, place.swap_low(out_sum))
    near = [place.swap_low(done), place.swap_low(far)]
    sets = [
        jnp.stack([jnp.stack([done[i], far[i]]), jnp.stack([near[0][i], near[1][i]])]) for i in range(2)
    ]
    passed[0] = place.swap_low(tie(to_low[0], near[1]))
    to_high = add(grad_near[1], came_near[1], tie(passed[1], done))
    sets[0], sets[1], small, out_sum, b1, b2, to_high = lax.optimization_barrier(
        (sets[0], sets[1], small, out_sum, b1, b2, to_high)
    )
    mine_far = place.swap_high(to_high)
    small = jnp.sum(small.astype(FULL_TYPE), axis=0).astype(HALF_TYPE)
    small = lax.all_to_all(jnp.broadcast_to(small[None], (32,) + small.shape), everywhere, 0, 0, tiled=True)
    back = [in_order(flat[1 - i][0], out_sum[:, :, i], flat[1 - i][1](out_sum[:, :, i])) for i in range(2)]
    first = jnp.stack([sets[0], place.swap_x(sets[0])])
    second = jnp.stack([sets[1], place.swap_y(sets[1])])
    output = call(output_kernel, shaped((all_rows, width)), after, b0, b2, b1)
    first, second, back[0], back[1], output = lax.optimization_barrier((first, second, *back, output))
    sources = [first, place.swap_y(first), second, place.swap_x(second)]
    back = [in_order(flat[i][0], back[i], flat[i][1](back[i])) for i in range(2)]
    out_half = jnp.stack(back).reshape(rows_out // 2, cols_out)
    sources[1], sources[3], output, out_half, mine_far, small, passed[0] = lax.optimization_barrier(
        (sources[1], sources[3], output, out_half, mine_far, small, passed[0])
    )
    mine = add(grad_near[0], came_near[0], passed[0], mine_far)
    mine_y = place.swap_y(mine)
    peers = [place.swap_c(first), None, place.swap_c(second), None]
    peers[1], peers[3] = place.swap_c(sources[1]), place.swap_c(sources[3])
    out_peer = place.swap_c(out_half)
    grad_heads = place_heads(place, sources, 0, heads, width, None)
    grad_out = place_out(place, out_half, 0, heads, None)
    grad_heads = lax.optimization_barrier((*grad_heads, grad_out, *peers, out_peer))
    grad_heads, grad_out, peers, out_peer = grad_heads[:3], grad_heads[3], grad_heads[4:8], grad_heads[8]
    small = small.reshape(width, LANES)
    grad_select, grad_sel_value, grad_sel_out, rows_four = call(
        place_small_kernel,
        (
            shaped((own_count, width), FULL_TYPE), shaped((heads * experts, width), FULL_TYPE),
            shaped((heads * experts, width), FULL_TYPE), shaped((8, width), FULL_TYPE),
        ),
        (place.wide * own_count).reshape(1).astype(jnp.int32), small,
        in_specs=[smem, vmem],
    )
    grad_query, grad_key, grad_value = place_heads(place, list(peers), 1, heads, width, grad_heads)
    grad_out = place_out(place, out_peer, 1, heads, (grad_out,))
    mine, mine_y, grad_query, grad_out, rows_four = lax.optimization_barrier((mine, mine_y, grad_query, grad_out, rows_four))
    mine_c, mine_yc = place.swap_c(mine), place.swap_c(mine_y)
    grad_experts = place_experts(place, mine, mine_y, 0, None)
    grad_up, grad_down = place_experts(place, mine_c, mine_yc, 1, grad_experts)
    grad_select, grad_sel_value, grad_sel_out = grad_select.T, grad_sel_value.T, grad_sel_out.T
    grad_gain_two, grad_bias_two, grad_gain_one, grad_bias_one = (rows_four[i] for i in range(4))
    return (
        output.reshape(tokens.shape), grad_tokens.reshape(tokens.shape), grad_query, grad_key, grad_value, grad_out,
        grad_sel_value, grad_sel_out, grad_gain_one, grad_bias_one, grad_gain_two, grad_bias_two, grad_select,
        grad_up, grad_down,
    )


def fits(mesh):
    return dict(mesh.shape) == {"wide": 8, "narrow": 4}


def solution(mesh):
    placed = (
        P("narrow", "wide", None),
        P("narrow"),
        P("narrow", "wide", None, None),
        P("narrow", "wide", None, None),
        P("narrow", None, None),
        P(),
        P(),
        P(),
        P(),
        P(),
        P(),
        P(),
        P(),
        P(),
        P(),
        P(None, "wide"),
        P(None, "wide"),
        P("wide", None),
        P("narrow", "wide", None),
    )
    return jax.shard_map(
        tuned_device if fits(mesh) else per_device,
        mesh=mesh,
        in_specs=placed,
        out_specs=(
            P("narrow", "wide", None),
            P("narrow", "wide", None),
            P(),
            P(),
            P(),
            P(),
            P(),
            P(),
            P(),
            P(),
            P(),
            P(),
            P(None, "wide"),
            P(None, "wide"),
            P("wide", None),
        ),
        check_vma=False,
    )
```
